32 devices in a mesh: block: 8 (over z, y), dp: 4 (over x, core).
Axes of the slice: x: 2, y: 2, z: 4, core: 2. Of those that a mesh axis runs over, the one named last changes fastest.
Arguments:
- mixture: float32 [32, 9600], P('dp', 'block'), may hold values from -6 to 6
- target: float32 [32, 9600], P('dp', 'block'), may hold values from -6 to 6
- lengths: int32 [32], P('dp'), may hold values from 1200 to 9600, as said below
- input_gates: float32 [4, 2, 64, 512], replicated, may hold values from -0.75 to 0.75
- recur_gates: float32 [4, 2, 128, 512], replicated, may hold values from -0.5 to 0.5
- projections: float32 [1184, 64], replicated
- vectors: float32 [5120], replicated
- moment_input: float32 [4, 2, 64, 512], replicated, may hold values from -7.1525574e-07 to 7.1525574e-07
- moment_recur: float32 [4, 2, 128, 512], replicated, may hold values from -7.1525574e-07 to 7.1525574e-07
- moment_proj: float32 [1184, 64], replicated, may hold values from -7.1525574e-07 to 7.1525574e-07
- moment_vecs: float32 [5120], replicated, may hold values from -1.9073486e-06 to 1.9073486e-06
- square_input: float32 [4, 2, 64, 512], replicated, may hold values from 1.1529663e-15 to 4.6118653e-15
- square_recur: float32 [4, 2, 128, 512], replicated, may hold values from 1.1529663e-15 to 4.6118653e-15
- square_proj: float32 [1184, 64], replicated, may hold values from 1.1529663e-15 to 4.6118653e-15
- square_vecs: float32 [5120], replicated, may hold values from 1.0376697e-14 to 4.150679e-14
- average_input: float32 [4, 2, 64, 512], replicated, may hold values from -0.3125 to 0.3125
- average_recur: float32 [4, 2, 128, 512], replicated, may hold values from -0.3125 to 0.3125
- average_proj: float32 [1184, 64], replicated, may hold values from -0.3125 to 0.3125
- average_vecs: float32 [5120], replicated, may hold values from -1.75 to 1.75
Outputs:
- loss_sum: float32 [], replicated
- valid_count: float32 [], replicated
- grad_norm: float32 [], replicated
- moments_input: float32 [4, 2, 64, 512], replicated
- moments_recur: float32 [4, 2, 128, 512], replicated
- moments_proj: float32 [1184, 64], replicated
- moments_vecs: float32 [5120], replicated
- squares_input: float32 [4, 2, 64, 512], replicated
- squares_recur: float32 [4, 2, 128, 512], replicated
- squares_proj: float32 [1184, 64], replicated
- squares_vecs: float32 [5120], replicated
- master_input: float32 [4, 2, 64, 512], replicated
- master_recur: float32 [4, 2, 128, 512], replicated
- master_proj: float32 [1184, 64], replicated
- master_vecs: float32 [5120], replicated
- smooth_input: float32 [4, 2, 64, 512], replicated
- smooth_recur: float32 [4, 2, 128, 512], replicated
- smooth_proj: float32 [1184, 64], replicated
- smooth_vecs: float32 [5120], replicated
- lowcopy_input: bfloat16 [4, 2, 64, 512], replicated
- lowcopy_recur: bfloat16 [4, 2, 128, 512], replicated
- lowcopy_proj: bfloat16 [1184, 64], replicated
- lowcopy_vecs: bfloat16 [5120], replicated
The draws below stay inside these ranges and needn't reach their ends.
Inputs may be any that keep to these rules, and one draw needn't show every extreme that they name: `lengths`: in each aligned group of 8 mixtures (one index of dp) one mixture, which one drawn from the seed, has length 9600.
All inputs are finite; a program needn't handle non-finite values.
Results may differ from the reference program's by a relative error of at most 0.0015.
The reference program's roundings to bfloat16 on the way count: a program that leaves them out, or rounds other values in their place, can miss the bound.
Values may be sent and summed in bfloat16 or wider, within the bound.
No kernel may reach another device: no remote copies, remote signals or barrier semaphores. Data moves between devices by JAX's collectives and lax.ppermute only.
A program may use at most 384 MiB of HBM per device.

```python
import math
import jax
import jax.numpy as jnp
from jax import lax

N = 64
B = 64
H = 128
STRIDE = 8
LAYERS = 2
STEP = 10
MIX = 8
HOP = 50
TILES = 24
FRAMES = 1200
SAMPLES = 9600
MIXES = 32
MROWS = 1184
NV = 5120
PTOT = 867328


def draw_lengths(key, part):
    key = jax.random.fold_in(key, 1)
    key_len, key_pick = jax.random.split(key)
    values = jax.random.randint(key_len, (MIXES,), SAMPLES // 8, SAMPLES + 1)
    picked = jax.random.randint(key_pick, (MIXES // MIX,), 0, MIX)
    full = jnp.arange(MIXES) % MIX == jnp.repeat(picked, MIX)
    return jnp.where(full, SAMPLES, values).astype(jnp.int32)


def draw_projections(key, part):
    key = jax.random.fold_in(key, 2)
    total_rows = 4 * LAYERS * H + N + B + 4 * STRIDE
    noise = jax.random.normal(key, (total_rows, N), jnp.float32)
    row_index = jnp.arange(total_rows)[:, None]
    base = 4 * LAYERS * H
    scales = jnp.where(row_index < base, (2.0 * H) ** (-0.5), jnp.where(row_index < base + N, N ** (-0.5), jnp.where(row_index < base + N + B, B ** (-0.5), jnp.where(row_index < base + N + B + 2 * STRIDE, 2.0 * (2.0 * STRIDE) ** (-0.5), 2.0 * N ** (-0.5)))))
    return noise * scales


def draw_vectors(key, part):
    key = jax.random.fold_in(key, 3)
    period = 8 * H + 3 * B
    total = 3 * N + B + 2 * LAYERS * period
    noise = jax.random.normal(key, (total,), jnp.float32) * 0.3
    position = jnp.arange(total)
    within = (position - 2 * N - B) % period
    inside = (position >= 2 * N + B) & (position < 2 * N + B + 2 * LAYERS * period)
    gains = (position < N) | inside & (within >= 8 * H + B) & (within < 8 * H + 2 * B)
    return noise + jnp.where(gains, 1.0, 0.0)


def steps_of(stream_key, extent, cuts, low, high):
    loudness, own = 1.0, jax.random.fold_in(stream_key, 6)
    for dim, parts in cuts:
        steps = jnp.exp(jax.random.uniform(jax.random.fold_in(own, dim), (parts,), jnp.float32, low / len(cuts), high / len(cuts)))
        loudness = loudness * jnp.repeat(steps, extent[dim] // parts).reshape([-1 if axis == dim else 1 for axis in range(len(extent))])
    return loudness


def bell_draw(key, extent, width, limit, cuts=(), dtype=jnp.bfloat16):
    entries = width * jax.random.normal(key, extent, jnp.float32)
    if cuts:
        entries = entries * steps_of(key, extent, cuts, -0.22, 0.18)
    return jnp.clip(entries, -limit, limit).astype(dtype)


def setup_inputs(seed: int = 0) -> dict:
    arg_keys = jax.random.split(jax.random.key(seed), 20)
    mixture = bell_draw(arg_keys[0], (MIXES, SAMPLES), 1.0, 6.0, ((0, 4), (1, 8)), jnp.float32)
    target = bell_draw(arg_keys[1], (MIXES, SAMPLES), 1.0, 6.0, ((0, 4), (1, 8)), jnp.float32)
    lengths = draw_lengths(jax.random.fold_in(arg_keys[19], 71), 0)
    input_gates = bell_draw(arg_keys[3], (2 * LAYERS, 2, B, 4 * H), B ** -0.5, 0.75, (), jnp.float32)
    recur_gates = bell_draw(arg_keys[4], (2 * LAYERS, 2, H, 4 * H), H ** -0.5, 0.5, (), jnp.float32)
    projections = draw_projections(jax.random.fold_in(arg_keys[19], 71), 0)
    vectors = draw_vectors(jax.random.fold_in(arg_keys[19], 71), 0)
    moment_input = bell_draw(arg_keys[7], (2 * LAYERS, 2, B, 4 * H), (0.00011 / PTOT ** 0.5), 7.152557373046875e-07, (), jnp.float32)
    moment_recur = bell_draw(arg_keys[8], (2 * LAYERS, 2, H, 4 * H), (0.00011 / PTOT ** 0.5), 7.152557373046875e-07, (), jnp.float32)
    moment_proj = bell_draw(arg_keys[9], (MROWS, N), (0.00011 / PTOT ** 0.5), 7.152557373046875e-07, (), jnp.float32)
    moment_vecs = bell_draw(arg_keys[10], (NV,), (0.00033 / PTOT ** 0.5), 1.9073486328125e-06, (), jnp.float32)
    square_input = jnp.clip(jnp.exp(jax.random.uniform(arg_keys[11], (2 * LAYERS, 2, B, 4 * H), jnp.float32, math.log(1.1529663188468583e-15), math.log(4.611865275387433e-15))), 1.1529663188468583e-15, 4.611865275387433e-15)
    square_recur = jnp.clip(jnp.exp(jax.random.uniform(arg_keys[12], (2 * LAYERS, 2, H, 4 * H), jnp.float32, math.log(1.1529663188468583e-15), math.log(4.611865275387433e-15))), 1.1529663188468583e-15, 4.611865275387433e-15)
    square_proj = jnp.clip(jnp.exp(jax.random.uniform(arg_keys[13], (MROWS, N), jnp.float32, math.log(1.1529663188468583e-15), math.log(4.611865275387433e-15))), 1.1529663188468583e-15, 4.611865275387433e-15)
    square_vecs = jnp.clip(jnp.exp(jax.random.uniform(arg_keys[14], (NV,), jnp.float32, math.log(1.0376697399017316e-14), math.log(4.1506789596069266e-14))), 1.0376697399017316e-14, 4.1506789596069266e-14)
    average_input = bell_draw(arg_keys[15], (2 * LAYERS, 2, B, 4 * H), 0.05, 0.3125, (), jnp.float32)
    average_recur = bell_draw(arg_keys[16], (2 * LAYERS, 2, H, 4 * H), 0.05, 0.3125, (), jnp.float32)
    average_proj = bell_draw(arg_keys[17], (MROWS, N), 0.05, 0.3125, (), jnp.float32)
    average_vecs = bell_draw(arg_keys[18], (NV,), 0.3, 1.75, (), jnp.float32)
    return dict(mixture=mixture, target=target, lengths=lengths, input_gates=input_gates, recur_gates=recur_gates, projections=projections, vectors=vectors, moment_input=moment_input, moment_recur=moment_recur, moment_proj=moment_proj, moment_vecs=moment_vecs, square_input=square_input, square_recur=square_recur, square_proj=square_proj, square_vecs=square_vecs, average_input=average_input, average_recur=average_recur, average_proj=average_proj, average_vecs=average_vecs)


HIGH = lax.Precision.HIGHEST
EPS_NORM = 1e-05
CLIP = 0.001
RATE = 0.1
BETA_ONE = 0.9
BETA_TWO = 0.999
ADAM_EPS = 1e-08
DECAY = 0.01
KEEP = 0.9

@jax.custom_vjp
def low(v):
    return lax.optimization_barrier(v.astype(jnp.bfloat16)).astype(jnp.float32)

@jax.custom_vjp
def low_back(v):
    return v

def low_keep(v):
    return (low(v), None)

def low_pass(kept, grad):
    return (grad,)

def back_keep(v):
    return (v, None)

def back_low(kept, grad):
    return (low(grad),)
low.defvjp(low_keep, low_pass)
low_back.defvjp(back_keep, back_low)

def layer_norm(value, gain, beta):
    center = value - lax.optimization_barrier(jnp.mean(value, -1, keepdims=True))
    spread = lax.optimization_barrier(jnp.mean(center * center, -1, keepdims=True))
    return center * lax.rsqrt(spread + EPS_NORM) * gain + beta

def matmul(left, right):
    return jnp.matmul(left, right, precision=HIGH)

def rnn_vectors(vectors, layer_index):
    offset = 2 * N + B + layer_index * (8 * H + 3 * B)
    lstm_bias = vectors[offset:offset + 8 * H].reshape(2, 4 * H)
    others = vectors[offset + 8 * H:offset + 8 * H + 3 * B].reshape(3, B)
    return (lstm_bias, others[0], others[1], others[2])

def direction(inputs, weight_in, weight_rec, lstm_bias, backwards):
    pregate = matmul(inputs, weight_in) + lstm_bias

    def stepper(carry, pre_step):
        hidden, memory = carry
        summed = low_back(pre_step + matmul(hidden, weight_rec))
        gate_i, gate_f, gate_g, gate_o = jnp.split(summed, 4, -1)
        memory = jax.nn.sigmoid(gate_f) * memory + jax.nn.sigmoid(gate_i) * jnp.tanh(gate_g)
        hidden = low(jax.nn.sigmoid(gate_o) * jnp.tanh(memory))
        return ((hidden, memory), hidden)
    zeros = jnp.zeros(inputs.shape[1:-1] + (H,), jnp.float32)
    return lax.scan(stepper, (zeros, zeros), pregate, reverse=backwards)[1]

def branch(inputs, layer_index, gates_in, gates_rec, projections, vectors):
    lstm_bias, out_bias, gain, beta = rnn_vectors(vectors, layer_index)
    forward = direction(inputs, gates_in[layer_index, 0], gates_rec[layer_index, 0], lstm_bias[0], False)
    reverse = direction(inputs, gates_in[layer_index, 1], gates_rec[layer_index, 1], lstm_bias[1], True)
    joined = jnp.concatenate([forward, reverse], -1)
    weight_out = projections[layer_index * 2 * H:(layer_index + 1) * 2 * H]
    linear = low_back(matmul(joined, weight_out) + out_bias)
    return layer_norm(linear, gain, beta)

def mixture_loss(wave, goal, length, gates_in, gates_rec, projections, vectors):
    base = 4 * LAYERS * H
    w_bn = projections[base:base + N]
    w_mask = projections[base + N:base + N + B]
    w_enc = projections[base + N + B:base + N + B + 2 * STRIDE]
    w_dec = projections[base + N + B + 2 * STRIDE:base + N + B + 4 * STRIDE]
    padded = jnp.concatenate([wave.reshape(FRAMES, STRIDE), jnp.zeros((HOP + 1, STRIDE), jnp.float32)], 0)
    windows = low(jnp.concatenate([padded[:-1], padded[1:]], -1))
    frame_valid = (jnp.arange(FRAMES + HOP) * STRIDE < length).astype(jnp.float32)[:, None]
    pre_enc = low_back(matmul(windows, w_enc))
    encoded = jax.nn.softplus(pre_enc)
    normed = low(layer_norm(encoded, vectors[:N], vectors[N:2 * N]))
    bottle = low_back(matmul(normed, w_bn) + vectors[2 * N:2 * N + B]) * frame_valid

    def to_tiles(rows):
        return jnp.concatenate([rows[:FRAMES].reshape(TILES, HOP, -1), rows[HOP:].reshape(TILES, HOP, -1)], 1)
    residual = to_tiles(bottle)
    tile_valid = to_tiles(frame_valid)
    for layer in range(LAYERS):
        intra = branch(jnp.swapaxes(low(residual), 0, 1), 2 * layer, gates_in, gates_rec, projections, vectors)
        residual = (residual + jnp.swapaxes(intra, 0, 1)) * tile_valid
        inter = branch(low(low_back(residual)), 2 * layer + 1, gates_in, gates_rec, projections, vectors)
        residual = (residual + low(low_back(inter))) * tile_valid
    first_half = residual[:, :HOP].reshape(FRAMES, B)
    second_half = residual[:, HOP:].reshape(FRAMES, B)
    features = first_half + jnp.concatenate([jnp.zeros((HOP, B), jnp.float32), second_half[:FRAMES - HOP]], 0)
    activated = low(jax.nn.gelu(features))
    logits = low_back(matmul(activated, w_mask) + vectors[-N:])
    mask_gate = jax.nn.sigmoid(logits)
    source = low(mask_gate * encoded[:FRAMES])
    decoded = low_back(matmul(source, w_dec.T))
    estimate = decoded[:, :STRIDE] + jnp.concatenate([jnp.zeros((1, STRIDE), jnp.float32), decoded[:-1, STRIDE:]], 0)
    error = estimate.reshape(SAMPLES) - goal
    sample_valid = (jnp.arange(SAMPLES) < length).astype(jnp.float32)
    return jnp.sum(sample_valid * (jnp.sqrt(error * error + 1.0) - 1.0))

def adam_step(grad, moment, square, weight, average, decay):
    moment = BETA_ONE * moment + (1.0 - BETA_ONE) * grad
    square = BETA_TWO * square + (1.0 - BETA_TWO) * grad * grad
    corrected = moment / (1.0 - BETA_ONE ** STEP)
    scaled = square / (1.0 - BETA_TWO ** STEP)
    weight = weight - RATE * (corrected / (jnp.sqrt(scaled) + ADAM_EPS) + decay * weight)
    average = KEEP * average + (1.0 - KEEP) * weight
    return (moment, square, weight, average)

def reference(mixture, target, lengths, input_gates, recur_gates, projections, vectors, moment_input, moment_recur, moment_proj, moment_vecs, square_input, square_recur, square_proj, square_vecs, average_input, average_recur, average_proj, average_vecs):
    params = (input_gates, recur_gates, projections, vectors)

    def add_one(totals, item):
        wave, goal, length = item

        def loss_fn(weights):
            return mixture_loss(wave, goal, length, low(weights[0]), low(weights[1]), low(weights[2]), weights[3])
        value, pullback = jax.vjp(loss_fn, params)
        grads = pullback(jnp.ones_like(value))[0]
        return ((jax.tree.map(jnp.add, totals[0], grads), totals[1] + value), None)
    start = (jax.tree.map(jnp.zeros_like, params), jnp.zeros((), jnp.float32))
    (grads, loss_sum), _ = lax.scan(add_one, start, (mixture, target, lengths))
    valid_count = jnp.sum(lengths).astype(jnp.float32)
    squares = sum((jnp.sum(g * g) for g in grads))
    grad_norm = jnp.sqrt(squares) / valid_count
    factor = jnp.minimum(1.0, CLIP / grad_norm) / valid_count
    moments = (moment_input, moment_recur, moment_proj, moment_vecs)
    seconds = (square_input, square_recur, square_proj, square_vecs)
    averages = (average_input, average_recur, average_proj, average_vecs)
    decays = (DECAY, DECAY, DECAY, 0.0)
    results = [adam_step(grads[i] * factor, moments[i], seconds[i], params[i], averages[i], decays[i]) for i in range(4)]
    news = [r[0] for r in results]
    squares_new = [r[1] for r in results]
    masters = [r[2] for r in results]
    smooths = [r[3] for r in results]
    copies = [m.astype(jnp.bfloat16) for m in masters]
    return (loss_sum, valid_count, grad_norm, news[0], news[1], news[2], news[3], squares_new[0], squares_new[1], squares_new[2], squares_new[3], masters[0], masters[1], masters[2], masters[3], smooths[0], smooths[1], smooths[2], smooths[3], copies[0], copies[1], copies[2], copies[3])
```

```python
import functools

import jax
import jax.numpy as jnp
from jax import lax
from jax.experimental import pallas as pl
from jax.experimental.pallas import tpu as pltpu
from jax.sharding import PartitionSpec as P

N = 64
B = 64
H = 128
K = 100
STRIDE = 8
LAYERS = 2
STEP = 10
HOP = 50
TILES = 3
M = 8
FRAMES = 150
BASE = 4 * LAYERS * H
PERIOD = 8 * H + 3 * B
ROWS_G = 424
BLOCKS = 208
PADDED = 216
CHUNK = 416

EPS_NORM = 1e-05
CLIP = 0.001
RATE = 0.1
BETA_ONE = 0.9
BETA_TWO = 0.999
ADAM_EPS = 1e-08
DECAY = 0.01
KEEP = 0.9

BF = jnp.bfloat16
F32 = jnp.float32
SDS = jax.ShapeDtypeStruct


def dot(left, right):
    return jnp.dot(left, right, preferred_element_type=F32)


def dot_rows(left, right):
    return lax.dot_general(left, right, (((0,), (0,)), ((), ())), preferred_element_type=F32)


def half_scale():
    lane = lax.broadcasted_iota(jnp.int32, (1, 4 * H), 1)
    return jnp.where((lane >= 2 * H) & (lane < 3 * H), 1.0, 0.5)


def gate_acts(z):
    act = jnp.tanh(z)
    sig_i = 0.5 * act[:, :H] + 0.5
    sig_f = 0.5 * act[:, H : 2 * H] + 0.5
    sig_o = 0.5 * act[:, 3 * H :] + 0.5
    return sig_i, sig_f, act[:, 2 * H : 3 * H], sig_o


def norm_parts(value):
    center = value - jnp.mean(value, -1, keepdims=True)
    spread = jnp.mean(center * center, -1, keepdims=True)
    scale = lax.rsqrt(spread + EPS_NORM)
    return center * scale, scale


def norm_back(grad, unit, scale, gain):
    inner = grad * gain
    return scale * (
        inner
        - jnp.mean(inner, -1, keepdims=True)
        - unit * jnp.mean(inner * unit, -1, keepdims=True)
    )


def live(lim, start, count):
    pos = lax.broadcasted_iota(jnp.int32, (count, M, B), 0) + start
    return jnp.where(pos * STRIDE < lim[None], 1.0, 0.0).reshape(count * M, B)


def own(start, count):
    pos = lax.broadcasted_iota(jnp.int32, (count, M, B), 0) + start
    return jnp.where(pos < FRAMES, 1.0, 0.0).reshape(count * M, B)


def chunk_of(steps, rows):
    best = 1
    for size in range(1, steps + 1):
        if steps % size == 0 and size * rows <= 512 and size * rows % 16 == 0:
            best = size
    return best


class Shape:
    def __init__(self, groups, steps, rows):
        self.groups, self.steps, self.rows = groups, steps, rows
        self.size = steps * rows
        self.chunk = chunk_of(steps, rows)
        self.crows = self.chunk * rows
        self.chunks = steps // self.chunk
        self.wide = (steps + 2) * rows
        self.unroll = 4 if steps % 4 == 0 else 1


def chunk_loop(shape, fn):
    for g in range(shape.groups):

        def step(i, _, g=g):
            fn(g, i, pl.multiple_of(i * shape.crows, 8))
            return 0

        lax.fori_loop(0, shape.chunks, step, 0)


def forward_weights(gi, gr, wi, wr):
    half = half_scale()
    for d in range(2):
        wi[d] = (gi[0, d].astype(BF).astype(F32) * half).astype(BF)
        wr[d] = (gr[0, d].astype(BF).astype(F32) * half).astype(BF)


def lstm_scan(shape, pg, wr, h_ref, c_ref):
    G, S, R = shape.groups, shape.steps, shape.rows
    pad = jnp.zeros((R, 2 * H), F32)
    for g in range(G):
        for ref in (h_ref, c_ref):
            ref[g, :R] = pad
            ref[g, (S + 1) * R :] = pad

    def one(d, t, hidden, memory):
        at = pl.multiple_of(t * R, 8)
        pre = jnp.concatenate([pg[d, g, pl.ds(at, R), :] for g in range(G)], 0)
        z = pre + dot(hidden, wr[d])
        sig_i, sig_f, tan_g, sig_o = gate_acts(z)
        memory = sig_f * memory + sig_i * tan_g
        hidden = (sig_o * jnp.tanh(memory)).astype(BF)
        full = hidden.astype(F32)
        after = pl.multiple_of(t * R + R, 8)
        for g in range(G):
            h_ref[g, pl.ds(after, R), d * H : (d + 1) * H] = full[g * R : (g + 1) * R]
            c_ref[g, pl.ds(after, R), d * H : (d + 1) * H] = memory[g * R : (g + 1) * R]
        return hidden, memory

    def step(s, carry):
        hf, cf, hb, cb = carry
        hf, cf = one(0, s, hf, cf)
        hb, cb = one(1, S - 1 - s, hb, cb)
        return hf, cf, hb, cb

    zero = jnp.zeros((G * R, H), F32)
    start = (zero.astype(BF), zero, zero.astype(BF), zero)
    lax.fori_loop(0, S, step, start, unroll=shape.unroll)


def lstm_scan_back(shape, z, dh, c_ref, wrt):
    G, S, R = shape.groups, shape.steps, shape.rows

    def one(d, t, rec_hidden, rec_memory):
        def take(ref, at, lanes):
            at = pl.multiple_of(at, 8)
            return jnp.concatenate([ref[g, pl.ds(at, R), lanes] for g in range(G)], 0)

        lanes = slice(d * H, (d + 1) * H)
        at = pl.multiple_of(t * R, 8)
        zt = jnp.concatenate([z[d, g, pl.ds(at, R), :] for g in range(G)], 0)
        sig_i, sig_f, tan_g, sig_o = gate_acts(zt)
        tan_c = jnp.tanh(take(c_ref, t * R + R, lanes))
        before = take(c_ref, t * R + 2 * R * d, lanes)
        grad_h = take(dh, t * R, lanes) + rec_hidden
        grad_c = rec_memory + grad_h * (sig_o * (1.0 - tan_c * tan_c))
        grad_pre = jnp.concatenate(
            [
                grad_c * (tan_g * sig_i * (1.0 - sig_i)),
                grad_c * (before * sig_f * (1.0 - sig_f)),
                grad_c * (sig_i * (1.0 - tan_g * tan_g)),
                grad_h * (tan_c * sig_o * (1.0 - sig_o)),
            ],
            -1,
        ).astype(BF)
        full = grad_pre.astype(F32)
        for g in range(G):
            z[d, g, pl.ds(at, R), :] = full[g * R : (g + 1) * R]
        return dot(grad_pre, wrt[d]), grad_c * sig_f

    def step(s, carry):
        hf, cf, hb, cb = carry
        hf, cf = one(0, S - 1 - s, hf, cf)
        hb, cb = one(1, s, hb, cb)
        return hf, cf, hb, cb

    zero = jnp.zeros((G * R, H), F32)
    lax.fori_loop(0, S, step, (zero,) * 4, unroll=shape.unroll)


def branch_pregates(shape, xs, wi, bias, pg):
    half = half_scale()

    def fill(g, i, r0):
        x = xs[g, pl.ds(r0, shape.crows), :].astype(BF)
        for d in range(2):
            pg[d, g, pl.ds(r0, shape.crows), :] = dot(x, wi[d]) + bias[0, d : d + 1] * half

    chunk_loop(shape, fill)


def branch_back(shape, grads, xs, h_ref, c_ref, weights, bias, others, wout, out, scratch):
    gi, gr = weights
    wi, wr, wit, wrt, wo, wot, z, dh = scratch
    n, R = shape.crows, shape.rows
    forward_weights(gi, gr, wi, wr)
    for d in range(2):
        wit[d] = jnp.transpose(gi[0, d]).astype(BF)
        wrt[d] = jnp.transpose(gr[0, d]).astype(BF)
    wo[...] = wout.astype(BF)
    wot[...] = jnp.transpose(wout).astype(BF)
    out[...] = jnp.zeros_like(out)
    half = half_scale()
    o_bias, gain = others[0, 0:1], others[0, 1:2]

    def first(g, i, r0):
        now = h_ref[g, pl.ds(pl.multiple_of(r0 + R, 8), n), :].astype(BF)
        unit, scale = norm_parts(dot(now, wo[...]) + o_bias)
        grad = grads(g, i, r0)
        low = norm_back(grad, unit, scale, gain).astype(BF)
        dh[g, pl.ds(r0, n), :] = dot(low, wot[...])
        turned = dot_rows(low, now)
        out[384:416] += jnp.concatenate([turned[:32], turned[32:]], 1)
        for row, value in ((418, low.astype(F32)), (419, grad * unit), (420, grad)):
            out[row : row + 1, :B] += jnp.sum(value, 0, keepdims=True)
        x = xs[g, pl.ds(r0, n), :].astype(BF)
        for d in range(2):
            before = h_ref[
                g, pl.ds(pl.multiple_of(r0 + 2 * R * d, 8), n), d * H : (d + 1) * H
            ].astype(BF)
            z[d, g, pl.ds(r0, n), :] = dot(before, wr[d]) + dot(x, wi[d]) + bias[0, d : d + 1] * half

    chunk_loop(shape, first)
    lstm_scan_back(shape, z, dh, c_ref, wrt)

    def last(use):
        def fn(g, i, r0):
            x = xs[g, pl.ds(r0, n), :].astype(BF)
            total = None
            for d in range(2):
                full = z[d, g, pl.ds(r0, n), :]
                low = full.astype(BF)
                before = h_ref[
                    g, pl.ds(pl.multiple_of(r0 + 2 * R * d, 8), n), d * H : (d + 1) * H
                ].astype(BF)
                out[d * B : (d + 1) * B] += dot_rows(x, low)
                out[128 + d * H : 128 + (d + 1) * H] += dot_rows(before, low)
                out[416 + d : 417 + d] += jnp.sum(full, 0, keepdims=True)
                part = dot(low, wit[d])
                total = part if total is None else total + part
            use(g, i, r0, total)

        chunk_loop(shape, fn)

    return last


def back_scratch(shape):
    return [
        pltpu.VMEM((2, B, 4 * H), BF),
        pltpu.VMEM((2, H, 4 * H), BF),
        pltpu.VMEM((2, 4 * H, B), BF),
        pltpu.VMEM((2, 4 * H, H), BF),
        pltpu.VMEM((2 * H, B), BF),
        pltpu.VMEM((B, 2 * H), BF),
        pltpu.VMEM((2, shape.groups, shape.size, 4 * H), F32),
        pltpu.VMEM((shape.groups, shape.size, 2 * H), F32),
    ]


def send_tiles(res, send, nb, RI):
    for d in range(nb):
        for c in range(TILES):
            send[d, c] = res[c, d * RI : (d + 1) * RI].astype(BF)


def add_tiles(res, back, nb, RI, lim, pads):
    for d in range(nb):
        for c in range(TILES):
            lo, hi = d * RI, min((d + 1) * RI, K * M)
            if lo >= hi:
                continue
            value = back[d, c].astype(F32)[: hi - lo]
            mask = live(lim, c * HOP + lo // M, (hi - lo) // M)
            res[c, lo:hi] = (res[c, lo:hi] + value) * mask
    del pads


def windows_of(mix, win):
    for i in range(BLOCKS):
        win[i * M : (i + 1) * M] = mix[:, STRIDE * i : STRIDE * (i + 2)]


def proj_rows(proj, start, count):
    return proj[start : start + count]


def intra_forward(shape, res, lim, gi, gr, bias, others, wout, x_out, h_out, c_out, scratch):
    wi, wr, pg = scratch
    forward_weights(gi, gr, wi, wr)
    n = shape.crows

    def keep(g, i, r0):
        x_out[g, pl.ds(pl.multiple_of(r0, 16), n), :] = res[g, pl.ds(r0, n), :].astype(BF)

    chunk_loop(shape, keep)
    branch_pregates(shape, res, wi, bias, pg)
    lstm_scan(shape, pg, wr, h_out, c_out)
    low_out = wout.astype(BF)
    o_bias, gain, beta = others[0, 0:1], others[0, 1:2], others[0, 2:3]

    def close(g, i, r0):
        now = h_out[g, pl.ds(pl.multiple_of(r0 + shape.rows, 8), n), :].astype(BF)
        unit, _ = norm_parts(dot(now, low_out) + o_bias)
        mask = live(lim[...], g * HOP + i * shape.chunk, shape.chunk)
        res[g, pl.ds(r0, n), :] = (res[g, pl.ds(r0, n), :] + (unit * gain + beta)) * mask

    chunk_loop(shape, close)


def first_kernel(shape, nb, RI, mix, lim, proj, vec, gi, gr, bias, others, res, send, x_out, h_out, c_out, win, wi, wr, pg, flat, bottle):
    windows_of(mix, flat)
    win[...] = flat[...].astype(BF)
    w_enc = proj_rows(proj, BASE + N + B, 2 * STRIDE).astype(BF)
    w_bn = proj_rows(proj, BASE, N).astype(BF)
    gain, beta, b_bias = vec[0:1], vec[1:2], vec[2:3]
    for i in range(BLOCKS * M // CHUNK):
        at = i * CHUNK
        pre = dot(win[at : at + CHUNK], w_enc)
        unit, _ = norm_parts(softplus(pre))
        normed = (unit * gain + beta).astype(BF)
        mask = live(lim[...], i * (CHUNK // M) - 1, CHUNK // M)
        bottle[at : at + CHUNK] = (dot(normed, w_bn) + b_bias) * mask
    for c in range(TILES):
        res[c, : K * M] = bottle[(c * HOP + 1) * M : (c * HOP + 1 + K) * M]
        if nb * RI > K * M:
            res[c, K * M :] = jnp.zeros((nb * RI - K * M, B), F32)
    wout = proj_rows(proj, 0, 2 * H)
    intra_forward(shape, res, lim, gi, gr, bias, others, wout, x_out, h_out, c_out, (wi, wr, pg))
    send_tiles(res, send, nb, RI)


def softplus(value):
    return jnp.maximum(value, 0.0) + jnp.log1p(jnp.exp(-jnp.abs(value)))


def third_kernel(shape, nb, RI, index, res_in, back, lim, proj, gi, gr, bias, others, res, send, x_out, h_out, c_out, wi, wr, pg):
    res[...] = res_in[...]
    add_tiles(res, back, nb, RI, lim[...], None)
    wout = proj_rows(proj, index * 2 * H, 2 * H)
    intra_forward(shape, res, lim, gi, gr, bias, others, wout, x_out, h_out, c_out, (wi, wr, pg))
    send_tiles(res, send, nb, RI)


def inter_kernel(shape, RI, index, rows, proj, gi, gr, bias, others, normed, h_out, c_out, wi, wr, pg, xs):
    T = shape.steps
    forward_weights(gi, gr, wi, wr)

    def widen(t, _):
        xs[0, pl.ds(pl.multiple_of(t * RI, 8), RI), :] = rows[t].astype(F32)
        return 0

    lax.fori_loop(0, T, widen, 0)
    branch_pregates(shape, xs, wi, bias, pg)
    lstm_scan(shape, pg, wr, h_out, c_out)
    low_out = proj_rows(proj, index * 2 * H, 2 * H).astype(BF)
    o_bias, gain, beta = others[0, 0:1], others[0, 1:2], others[0, 2:3]

    def close(g, i, r0):
        now = h_out[g, pl.ds(pl.multiple_of(r0 + RI, 8), shape.crows), :].astype(BF)
        unit, _ = norm_parts(dot(now, low_out) + o_bias)
        value = unit * gain + beta
        for j in range(shape.chunk):
            normed[i * shape.chunk + j] = value[j * RI : (j + 1) * RI].astype(BF)

    chunk_loop(shape, close)


def part_kernel(nb, RI, res_in, back, lim, part, up, down, res):
    res[...] = res_in[...]
    add_tiles(res, back, nb, RI, lim[...], None)
    half = HOP * M
    part[:half] = res[0, :half]
    for c in range(1, TILES):
        part[c * half : (c + 1) * half] = res[c, :half] + res[c - 1, half : 2 * half]
    part[TILES * half :] = res[TILES - 1, half : 2 * half]
    up[...] = part[TILES * half - M :]
    down[...] = part[: half + M]


def middle_kernel(nb, RI, part, before, after, lim, edge, win, goal, proj, vec, send, gres, genc, gm, feats, dec, tgt, gest, enc, gate, src, act):
    half = HOP * M
    top = M + TILES * half
    feats[...] = jnp.zeros_like(feats)
    feats[:M] = before[:M]
    feats[M : M + half] = part[:half] + before[M:]
    feats[M + half : top] = part[half : TILES * half]
    feats[top : top + half] = part[TILES * half :] + after[:half]
    feats[top + half : top + half + M] = after[half:]
    w_mask = proj_rows(proj, BASE + N, B)
    w_enc = proj_rows(proj, BASE + N + B, 2 * STRIDE).astype(BF)
    w_dec = proj_rows(proj, BASE + N + B + 2 * STRIDE, 2 * STRIDE)
    low_mask = w_mask.astype(BF)
    turned_mask = jnp.transpose(w_mask).astype(BF)
    low_dec = w_dec.astype(BF)
    m_bias = vec[3:4]
    root = 0.7978845608028654
    cube = 0.044715
    total = BLOCKS * M
    dec[total:] = jnp.zeros((PADDED * M - total, 2 * STRIDE), F32)
    for i in range(total // CHUNK):
        rows = slice(i * CHUNK, (i + 1) * CHUNK)
        x = feats[rows]
        low = (0.5 * x * (1.0 + jnp.tanh(root * (x + cube * x * x * x)))).astype(BF)
        encoded = softplus(dot(win[rows], w_enc))
        mask = 0.5 * jnp.tanh(0.5 * (dot(low, low_mask) + m_bias)) + 0.5
        source = (mask * encoded).astype(BF)
        enc[rows] = encoded
        gate[rows] = mask
        src[rows] = source.astype(F32)
        act[rows] = low.astype(F32)
        dec[rows] = lax.dot_general(
            source, low_dec, (((1,), (1,)), ((), ())), preferred_element_type=F32
        )
    dec[:M] = dec[:M] * edge[:, : 2 * STRIDE]
    for ref in (feats, enc, gate, src, act):
        ref[total:] = jnp.zeros((PADDED * M - total, B), F32)
    for i in range(BLOCKS):
        tgt[i * M : (i + 1) * M] = goal[:, STRIDE * i : STRIDE * (i + 1)]
    estimate = dec[M:total, :STRIDE] + dec[: total - M, STRIDE:]
    count = BLOCKS - 1
    spot = lax.broadcasted_iota(jnp.int32, (count, M, STRIDE), 0)
    late = lax.broadcasted_iota(jnp.int32, (count, M, STRIDE), 2)
    valid = jnp.where(spot * STRIDE + late < lim[:, :STRIDE][None], 1.0, 0.0)
    inside = jnp.where(spot < FRAMES, valid, 0.0).reshape(count * M, STRIDE)
    valid = valid.reshape(count * M, STRIDE)
    error = estimate - tgt[M:total]
    smoothed = jnp.sqrt(error * error + 1.0)
    gest[:M] = jnp.zeros((M, STRIDE), F32)
    gest[M:total] = valid * error / smoothed
    gest[total:] = jnp.zeros((PADDED * M - total, STRIDE), F32)
    loss = jnp.sum(jnp.sum(inside * (smoothed - 1.0), 0, keepdims=True), 1, keepdims=True)
    seen = jnp.sum(jnp.sum(inside, 0, keepdims=True), 1, keepdims=True)
    gm[...] = jnp.zeros_like(gm)
    gm[81:82] = jnp.broadcast_to(loss, (1, B))
    gm[82:83] = jnp.broadcast_to(seen, (1, B))
    for i in range(total // CHUNK):
        at = i * CHUNK + M
        rows = slice(at, at + CHUNK)
        grad_dec = jnp.concatenate(
            [gest[rows], gest[at + M : at + M + CHUNK]], 1
        ).astype(BF)
        mine = own(i * (CHUNK // M), CHUNK // M)
        mine_low = mine.astype(BF)
        gm[64:80] += dot_rows(grad_dec, src[rows].astype(BF) * mine_low)
        grad_source = dot(grad_dec, low_dec)
        mask = gate[rows]
        grad_logit = (grad_source * enc[rows] * mask * (1.0 - mask)).astype(BF)
        enc[rows] = grad_source * mask
        gm[:64] += dot_rows(act[rows].astype(BF), grad_logit * mine_low)
        gm[80:81] += jnp.sum(grad_logit.astype(F32) * mine, 0, keepdims=True)
        x = feats[rows]
        curve = jnp.tanh(root * (x + cube * x * x * x))
        slope = 0.5 * (1.0 + curve) + (0.5 * root) * x * (1.0 - curve * curve) * (
            1.0 + (3.0 * cube) * x * x
        )
        feats[rows] = slope * dot(grad_logit, turned_mask)
    genc[...] = enc[M : M + FRAMES * M]
    for c in range(TILES):
        gres[c, : K * M] = feats[M + c * half : M + c * half + K * M] * live(lim[...], c * HOP, K)
        if nb * RI > K * M:
            gres[c, K * M :] = jnp.zeros((nb * RI - K * M, B), F32)
    send_tiles(gres, send, nb, RI)


def inter_back_kernel(shape, RI, index, grad_rows, rows, h_ref, c_ref, proj, gi, gr, bias, others, send, out, *scratch):
    xs, core = scratch[0], scratch[1:]

    def widen(t, _):
        xs[0, pl.ds(pl.multiple_of(t * RI, 8), RI), :] = rows[t].astype(F32)
        return 0

    lax.fori_loop(0, shape.steps, widen, 0)

    def grads(g, i, r0):
        return jnp.concatenate(
            [grad_rows[i * shape.chunk + j].astype(F32) for j in range(shape.chunk)], 0
        )

    wout = proj_rows(proj, index * 2 * H, 2 * H)
    last = branch_back(shape, grads, xs, h_ref, c_ref, (gi, gr), bias, others, wout, out, core)

    def use(g, i, r0, total):
        for j in range(shape.chunk):
            send[i * shape.chunk + j] = total[j * RI : (j + 1) * RI].astype(BF)

    last(use)


def intra_back(shape, nb, RI, index, gres, lim, x_ref, h_ref, c_ref, proj, gi, gr, bias, others, out, core):
    n = shape.crows

    def grads(g, i, r0):
        return gres[g, pl.ds(r0, n), :]

    wout = proj_rows(proj, index * 2 * H, 2 * H)
    last = branch_back(shape, grads, x_ref, h_ref, c_ref, (gi, gr), bias, others, wout, out, core)

    def use(g, i, r0, total):
        gres[g, pl.ds(r0, n), :] = gres[g, pl.ds(r0, n), :] + total

    last(use)


def third_back_kernel(shape, nb, RI, index, gres_in, back, lim, x_ref, h_ref, c_ref, proj, gi, gr, bias, others, gres, send, out, *core):
    gres[...] = gres_in[...]
    add_tiles(gres, back, nb, RI, lim[...], None)
    intra_back(shape, nb, RI, index, gres, lim, x_ref, h_ref, c_ref, proj, gi, gr, bias, others, out, core)
    for c in range(TILES):
        gres[c, : K * M] = gres[c, : K * M] * live(lim[...], c * HOP, K)
    send_tiles(gres, send, nb, RI)


def first_back_kernel(shape, nb, RI, gres_in, back, lim, x_ref, h_ref, c_ref, proj, gi, gr, bias, others, vec, win, genc, out, gm, gres, bottle, *core):
    gres[...] = gres_in[...]
    add_tiles(gres, back, nb, RI, lim[...], None)
    intra_back(shape, nb, RI, 0, gres, lim, x_ref, h_ref, c_ref, proj, gi, gr, bias, others, out, core)
    half = HOP * M
    bottle[...] = jnp.zeros_like(bottle)
    for c in range(TILES):
        at = (c * HOP + 1) * M
        bottle[at : at + K * M] += gres[c, : K * M]
    w_enc = proj_rows(proj, BASE + N + B, 2 * STRIDE).astype(BF)
    turned_bn = jnp.transpose(proj_rows(proj, BASE, N)).astype(BF)
    gain, beta = vec[0:1], vec[1:2]
    gm[...] = jnp.zeros_like(gm)
    own_rows = FRAMES * M
    for i in range(BLOCKS * M // CHUNK):
        at = i * CHUNK
        rows = slice(at, at + CHUNK)
        pre = dot(win[rows], w_enc)
        unit, scale = norm_parts(softplus(pre))
        normed = (unit * gain + beta).astype(BF)
        low = (bottle[rows] * live(lim[...], i * (CHUNK // M) - 1, CHUNK // M)).astype(BF)
        gm[:64] += dot_rows(normed, low)
        gm[80:81] += jnp.sum(low.astype(F32), 0, keepdims=True)
        grad_normed = dot(low, turned_bn)
        gm[81:82] += jnp.sum(grad_normed * unit, 0, keepdims=True)
        gm[82:83] += jnp.sum(grad_normed, 0, keepdims=True)
        grad_enc = norm_back(grad_normed, unit, scale, gain)
        lo, hi = max(at - M, 0), min(at + CHUNK - M, own_rows)
        if lo < hi:
            piece = genc[lo:hi]
            above, below = lo + M - at, at + CHUNK - M - hi
            if above:
                piece = jnp.concatenate([jnp.zeros((above, B), F32), piece], 0)
            if below:
                piece = jnp.concatenate([piece, jnp.zeros((below, B), F32)], 0)
            grad_enc = grad_enc + piece
        grad_pre = (grad_enc * (0.5 * jnp.tanh(0.5 * pre) + 0.5)).astype(BF)
        gm[64:80] += dot_rows(win[rows], grad_pre)


def call(kernel, outs, ins, scratch, index=None):
    if index is None:
        specs = [pl.BlockSpec(memory_space=pltpu.VMEM)] * len(ins)
        extra = []
        wrapped = kernel
    else:
        big = [i for i, a in enumerate(ins) if a.ndim == 4 and a.shape[:2] == (2 * LAYERS, 2)]
        small = [i for i, a in enumerate(ins) if a.ndim == 3 and a.shape[0] == 2 * LAYERS]
        specs = [
            pl.BlockSpec(memory_space=pl.ANY if i in big else pltpu.VMEM) for i in range(len(ins))
        ]
        extra = [pltpu.VMEM((1,) + ins[i].shape[1:], F32) for i in big]
        extra.append(pltpu.SemaphoreType.DMA((len(big),)))

        def wrapped(*refs):
            refs = list(refs)
            held, sem = refs[len(refs) - len(extra) : -1], refs[-1]
            copies = []
            for j, i in enumerate(big):
                copies.append(pltpu.make_async_copy(refs[i].at[pl.ds(index, 1)], held[j], sem.at[j]))
                copies[-1].start()
            for copy in copies:
                copy.wait()
            for j, i in enumerate(big):
                refs[i] = held[j]
            for i in small:
                refs[i] = refs[i].at[pl.ds(index, 1)]
            kernel(*refs[: len(refs) - len(extra)])

    return pl.pallas_call(
        wrapped,
        out_shape=outs,
        in_specs=specs,
        out_specs=[pl.BlockSpec(memory_space=pltpu.VMEM)] * len(outs),
        scratch_shapes=list(scratch) + extra,
        compiler_params=pltpu.CompilerParams(vmem_limit_bytes=56 * 1024 * 1024),
    )(*ins)


def shift(block, axis, distance):
    size = lax.axis_size(axis)
    route = [(i, i + distance) for i in range(size) if 0 <= i + distance < size]
    return lax.ppermute(block, axis, route)


def exchange(block):
    return lax.all_to_all(block, "block", split_axis=0, concat_axis=0, tiled=True)


def adam_step(grad, moment, square, weight, average, decay):
    moment = BETA_ONE * moment + (1.0 - BETA_ONE) * grad
    square = BETA_TWO * square + (1.0 - BETA_TWO) * grad * grad
    corrected = moment / (1.0 - BETA_ONE**STEP)
    scaled = square / (1.0 - BETA_TWO**STEP)
    weight = weight - RATE * (corrected / (jnp.sqrt(scaled) + ADAM_EPS) + decay * weight)
    average = KEEP * average + (1.0 - KEEP) * weight
    return (moment, square, weight, average)


def body(
    mixture,
    target,
    lengths,
    input_gates,
    recur_gates,
    projections,
    vectors,
    moment_input,
    moment_recur,
    moment_proj,
    moment_vecs,
    square_input,
    square_recur,
    square_proj,
    square_vecs,
    average_input,
    average_recur,
    average_proj,
    average_vecs,
):
    nb = lax.axis_size("block")
    place = lax.axis_index("block")
    RI = -(-K // nb) * M
    intra = Shape(TILES, K, M)
    inter = Shape(1, TILES * nb, RI)
    T = inter.steps
    gi, gr, proj = input_gates, recur_gates, projections
    lim = jnp.broadcast_to((lengths - place * (FRAMES * STRIDE))[:, None], (M, B))
    edge = jnp.broadcast_to((place > 0).astype(F32), (M, B))
    periods = vectors[2 * N + B : 2 * N + B + 2 * LAYERS * PERIOD].reshape(2 * LAYERS, PERIOD)
    bias = periods[:, : 8 * H].reshape(2 * LAYERS, 2, 4 * H)
    others = periods[:, 8 * H :].reshape(2 * LAYERS, 3, B)
    vec = jnp.concatenate([vectors[: 2 * N + B], vectors[-N:]]).reshape(4, N)
    waves = jnp.stack([mixture, target])
    reach = (HOP + 2) * STRIDE
    following = shift(waves[:, :, :reach], "block", -1)
    leading = shift(mixture[:, -STRIDE:], "block", 1)
    rest = jnp.zeros((2, M, 14 * 128 - STRIDE - FRAMES * STRIDE - reach), F32)
    leading = jnp.stack([leading, jnp.zeros_like(leading)])
    waves = jnp.concatenate([leading, waves, following, rest], 2)

    res_shape = SDS((TILES, nb * RI, B), F32)
    send_shape = SDS((nb, TILES, RI, B), BF)
    x_shape = SDS((TILES, K * M, B), BF)

    def state(shape):
        return SDS((shape.groups, shape.wide, 2 * H), F32)

    def fwd_scratch(shape):
        return [
            pltpu.VMEM((2, B, 4 * H), BF),
            pltpu.VMEM((2, H, 4 * H), BF),
            pltpu.VMEM((2, shape.groups, shape.size, 4 * H), F32),
        ]

    res0, send, x0, h0, c0, win = call(
        functools.partial(first_kernel, intra, nb, RI),
        [res_shape, send_shape, x_shape, state(intra), state(intra), SDS((BLOCKS * M, 2 * STRIDE), BF)],
        [waves[0], lim, proj, vec, gi, gr, bias, others],
        fwd_scratch(intra)
        + [pltpu.VMEM((BLOCKS * M, 2 * STRIDE), F32), pltpu.VMEM((BLOCKS * M, B), F32)],
        0,
    )

    def inter_step(send, index):
        rows = exchange(send).reshape(T, RI, B)
        normed, h, c = call(
            functools.partial(inter_kernel, inter, RI, index),
            [SDS((T, RI, B), BF), state(inter), state(inter)],
            [rows, proj, gi, gr, bias, others],
            fwd_scratch(inter) + [pltpu.VMEM((1, inter.size, B), F32)],
            index,
        )
        return rows, h, c, exchange(normed.reshape(nb, TILES, RI, B))

    rows1, h1, c1, back = inter_step(send, 1)
    res2, send, x2, h2, c2 = call(
        functools.partial(third_kernel, intra, nb, RI, 2),
        [res_shape, send_shape, x_shape, state(intra), state(intra)],
        [res0, back, lim, proj, gi, gr, bias, others],
        fwd_scratch(intra),
        2,
    )
    rows3, h3, c3, back = inter_step(send, 3)
    edge_shape = SDS(((HOP + 1) * M, B), F32)
    part, up, down = call(
        functools.partial(part_kernel, nb, RI),
        [SDS(((FRAMES + HOP) * M, B), F32), edge_shape, edge_shape],
        [res2, back, lim],
        [pltpu.VMEM(res_shape.shape, F32)],
    )
    before = shift(up, "block", 1)
    after = shift(down, "block", -1)
    tall = PADDED * M
    send, gres, genc, gm_mid = call(
        functools.partial(middle_kernel, nb, RI),
        [send_shape, res_shape, SDS((FRAMES * M, B), F32), SDS((88, B), F32)],
        [part, before, after, lim, edge, win, waves[1], proj, vec],
        [
            pltpu.VMEM((tall, B), F32),
            pltpu.VMEM((tall, 2 * STRIDE), F32),
            pltpu.VMEM((tall, STRIDE), F32),
            pltpu.VMEM((tall, STRIDE), F32),
            pltpu.VMEM((tall, B), F32),
            pltpu.VMEM((tall, B), F32),
            pltpu.VMEM((tall, B), F32),
            pltpu.VMEM((tall, B), F32),
        ],
    )
    out_shape = SDS((ROWS_G, 4 * H), F32)

    def inter_back(send, rows, h, c, index):
        grad_rows = exchange(send).reshape(T, RI, B)
        send, out = call(
            functools.partial(inter_back_kernel, inter, RI, index),
            [SDS((T, RI, B), BF), out_shape],
            [grad_rows, rows, h, c, proj, gi, gr, bias, others],
            [pltpu.VMEM((1, inter.size, B), F32)] + back_scratch(inter),
            index,
        )
        return exchange(send.reshape(nb, TILES, RI, B)), out

    back, out3 = inter_back(send, rows3, h3, c3, 3)
    gres, send, out2 = call(
        functools.partial(third_back_kernel, intra, nb, RI, 2),
        [res_shape, send_shape, out_shape],
        [gres, back, lim, x2, h2, c2, proj, gi, gr, bias, others],
        back_scratch(intra),
        2,
    )
    back, out1 = inter_back(send, rows1, h1, c1, 1)
    out0, gm_first = call(
        functools.partial(first_back_kernel, intra, nb, RI),
        [out_shape, SDS((88, B), F32)],
        [gres, back, lim, x0, h0, c0, proj, gi, gr, bias, others, vec, win, genc],
        [pltpu.VMEM(res_shape.shape, F32), pltpu.VMEM((BLOCKS * M, B), F32)] + back_scratch(intra),
        0,
    )
    outs = jnp.stack([out0, out1, out2, out3])
    outs, gm_mid, gm_first = lax.psum((outs, gm_mid, gm_first), ("block", "dp"))
    total_loss, total_count = gm_mid[81, 0], gm_mid[82, 0]
    grad_input = outs[:, :128].reshape(2 * LAYERS, 2, B, 4 * H)
    grad_recur = outs[:, 128:384].reshape(2 * LAYERS, 2, H, 4 * H)
    turned = outs[:, 384:416].reshape(2 * LAYERS, 32, 2, 2 * H)
    turned = jnp.transpose(turned, (0, 3, 2, 1)).reshape(4 * LAYERS * H, B)
    grad_proj = jnp.concatenate(
        [turned, gm_first[:64], gm_mid[:64], gm_first[64:80], gm_mid[64:80]], 0
    )
    rows = jnp.concatenate(
        [outs[:, 416:418].reshape(2 * LAYERS, 8 * H), outs[:, 418:421, :B].reshape(2 * LAYERS, 3 * B)], 1
    )
    grad_vecs = jnp.concatenate(
        [gm_first[81], gm_first[82], gm_first[80], rows.reshape(-1), gm_mid[80]]
    )
    grads = (grad_input, grad_recur, grad_proj, grad_vecs)
    params = (input_gates, recur_gates, projections, vectors)
    moments = (moment_input, moment_recur, moment_proj, moment_vecs)
    seconds = (square_input, square_recur, square_proj, square_vecs)
    averages = (average_input, average_recur, average_proj, average_vecs)
    squared = sum((jnp.sum(g * g) for g in grads))
    grad_norm = jnp.sqrt(squared) / total_count
    factor = jnp.minimum(1.0, CLIP / grad_norm) / total_count
    decays = (DECAY, DECAY, DECAY, 0.0)
    results = [
        adam_step(grads[i] * factor, moments[i], seconds[i], params[i], averages[i], decays[i])
        for i in range(4)
    ]
    kinds = [[r[j] for r in results] for j in range(4)]
    copies = [m.astype(BF) for m in kinds[2]]
    return (total_loss, total_count, grad_norm, *kinds[0], *kinds[1], *kinds[2], *kinds[3], *copies)


def solution(mesh):
    in_specs = (P("dp", "block"), P("dp", "block"), P("dp")) + (P(),) * 16
    return jax.shard_map(
        body, mesh=mesh, in_specs=in_specs, out_specs=(P(),) * 23, check_vma=False
    )
```

```python
import functools

import jax
import jax.numpy as jnp
from jax import lax
from jax.experimental import pallas as pl
from jax.experimental.pallas import tpu as pltpu
from jax.sharding import PartitionSpec as P

N = 64
B = 64
H = 128
K = 100
STRIDE = 8
LAYERS = 2
STEP = 10
HOP = 50
TILES = 3
M = 8
FRAMES = 150
BASE = 4 * LAYERS * H
PERIOD = 8 * H + 3 * B
ROWS_MAPS = 1536
ROWS_VECS = 1664
ROWS_G = 1696
ROWS_FIRST = 1856
LANES = 128
BLOCKS = 208
PADDED = 216
CHUNK = 416

EPS_NORM = 1e-05
CLIP = 0.001
RATE = 0.1
BETA_ONE = 0.9
BETA_TWO = 0.999
ADAM_EPS = 1e-08
DECAY = 0.01
KEEP = 0.9

BF = jnp.bfloat16
F32 = jnp.float32
SDS = jax.ShapeDtypeStruct


def dot(left, right):
    return jnp.dot(left, right, preferred_element_type=F32)


def dot_turned(left, right):
    return lax.dot_general(left, right, (((1,), (1,)), ((), ())), preferred_element_type=F32)


def dot_rows(left, right):
    return lax.dot_general(left, right, (((0,), (0,)), ((), ())), preferred_element_type=F32)


def half_scale():
    lane = lax.broadcasted_iota(jnp.int32, (1, 4 * H), 1)
    return jnp.where((lane >= 2 * H) & (lane < 3 * H), 1.0, 0.5)


def gate_acts(z):
    act = jnp.tanh(z)
    sig_i = 0.5 * act[:, :H] + 0.5
    sig_f = 0.5 * act[:, H : 2 * H] + 0.5
    sig_o = 0.5 * act[:, 3 * H :] + 0.5
    return sig_i, sig_f, act[:, 2 * H : 3 * H], sig_o


def norm_parts(value):
    center = value - jnp.mean(value, -1, keepdims=True)
    spread = jnp.mean(center * center, -1, keepdims=True)
    scale = lax.rsqrt(spread + EPS_NORM)
    return center * scale, scale


def norm_back(grad, unit, scale, gain):
    inner = grad * gain
    return scale * (
        inner
        - jnp.mean(inner, -1, keepdims=True)
        - unit * jnp.mean(inner * unit, -1, keepdims=True)
    )


def live(lim, start, count):
    pos = lax.broadcasted_iota(jnp.int32, (count, M, B), 0) + start
    return jnp.where(pos * STRIDE < lim[None], 1.0, 0.0).reshape(count * M, B)


def limits(lengths):
    row = lax.broadcasted_iota(jnp.int32, (M, B), 0)
    total = jnp.zeros((M, B), jnp.int32)
    for m in range(M):
        total = jnp.where(row == m, lengths[m], total)
    return total - lax.axis_index("block") * (FRAMES * STRIDE)


def pieces(vectors, start, count):
    parts = []
    at = start
    while at < start + count:
        wide = at % 2 == 0 and at + 2 <= start + count
        lane = (at % 2) * N
        parts.append(vectors[at // 2 : at // 2 + 1, lane : lane + (2 * N if wide else N)])
        at += 2 if wide else 1
    return parts[0] if len(parts) == 1 else jnp.concatenate(parts, 1)


def branch_vectors(vectors, index):
    first = (2 * N + B + index * PERIOD) // N
    half = half_scale()
    bias = [pieces(vectors, first + 8 * d, 8) * half for d in range(2)]
    return bias, [pieces(vectors, first + 16 + j, 1) for j in range(3)]


def own(start, count):
    pos = lax.broadcasted_iota(jnp.int32, (count, M, B), 0) + start
    return jnp.where(pos < FRAMES, 1.0, 0.0).reshape(count * M, B)


def chunk_of(steps, rows):
    best = 1
    for size in range(1, steps + 1):
        if steps % size == 0 and size * rows <= 512 and size * rows % 16 == 0:
            best = size
    return best


class Shape:
    def __init__(self, groups, steps, rows):
        self.groups, self.steps, self.rows = groups, steps, rows
        self.size = steps * rows
        self.chunk = chunk_of(steps, rows)
        self.crows = self.chunk * rows
        self.chunks = steps // self.chunk
        self.wide = (steps + 2) * rows
        self.unroll = 4 if steps % 4 == 0 else 1


def chunk_loop(shape, fn):
    for g in range(shape.groups):

        def step(i, _, g=g):
            fn(g, i, pl.multiple_of(i * shape.crows, 8))
            return 0

        lax.fori_loop(0, shape.chunks, step, 0)


def forward_weights(gi, gr, wi, wr):
    half = half_scale()
    for d in range(2):
        wi[d] = (gi[0, d].astype(BF).astype(F32) * half).astype(BF)
        wr[d] = (gr[0, d].astype(BF).astype(F32) * half).astype(BF)


def lstm_scan(shape, pg, wr, h_ref, c_ref):
    G, S, R = shape.groups, shape.steps, shape.rows
    pad = jnp.zeros((R, 2 * H), F32)
    for g in range(G):
        for ref in (h_ref, c_ref):
            ref[g, :R] = pad
            ref[g, (S + 1) * R :] = pad

    def one(d, t, hidden, memory):
        at = pl.multiple_of(t * R, 8)
        pre = jnp.concatenate([pg[d, g, pl.ds(at, R), :] for g in range(G)], 0)
        z = pre + dot(hidden, wr[d])
        sig_i, sig_f, tan_g, sig_o = gate_acts(z)
        memory = sig_f * memory + sig_i * tan_g
        hidden = (sig_o * jnp.tanh(memory)).astype(BF)
        full = hidden.astype(F32)
        after = pl.multiple_of(t * R + R, 8)
        for g in range(G):
            h_ref[g, pl.ds(after, R), d * H : (d + 1) * H] = full[g * R : (g + 1) * R]
            c_ref[g, pl.ds(after, R), d * H : (d + 1) * H] = memory[g * R : (g + 1) * R]
        return hidden, memory

    def step(s, carry):
        hf, cf, hb, cb = carry
        hf, cf = one(0, s, hf, cf)
        hb, cb = one(1, S - 1 - s, hb, cb)
        return hf, cf, hb, cb

    zero = jnp.zeros((G * R, H), F32)
    start = (zero.astype(BF), zero, zero.astype(BF), zero)
    lax.fori_loop(0, S, step, start, unroll=shape.unroll)


def lstm_scan_back(shape, z, dh, c_ref, wrt):
    G, S, R = shape.groups, shape.steps, shape.rows

    def one(d, t, rec_hidden, rec_memory):
        def take(ref, at, lanes):
            at = pl.multiple_of(at, 8)
            return jnp.concatenate([ref[g, pl.ds(at, R), lanes] for g in range(G)], 0)

        lanes = slice(d * H, (d + 1) * H)
        at = pl.multiple_of(t * R, 8)
        zt = jnp.concatenate([z[d, g, pl.ds(at, R), :] for g in range(G)], 0)
        sig_i, sig_f, tan_g, sig_o = gate_acts(zt)
        tan_c = jnp.tanh(take(c_ref, t * R + R, lanes))
        before = take(c_ref, t * R + 2 * R * d, lanes)
        grad_h = take(dh, t * R, lanes) + rec_hidden
        grad_c = rec_memory + grad_h * (sig_o * (1.0 - tan_c * tan_c))
        grad_pre = jnp.concatenate(
            [
                grad_c * (tan_g * sig_i * (1.0 - sig_i)),
                grad_c * (before * sig_f * (1.0 - sig_f)),
                grad_c * (sig_i * (1.0 - tan_g * tan_g)),
                grad_h * (tan_c * sig_o * (1.0 - sig_o)),
            ],
            -1,
        ).astype(BF)
        full = grad_pre.astype(F32)
        for g in range(G):
            z[d, g, pl.ds(at, R), :] = full[g * R : (g + 1) * R]
        return dot(grad_pre, wrt[d]), grad_c * sig_f

    def step(s, carry):
        hf, cf, hb, cb = carry
        hf, cf = one(0, S - 1 - s, hf, cf)
        hb, cb = one(1, s, hb, cb)
        return hf, cf, hb, cb

    zero = jnp.zeros((G * R, H), F32)
    lax.fori_loop(0, S, step, (zero,) * 4, unroll=shape.unroll)


def branch_pregates(shape, xs, wi, bias, pg):
    def fill(g, i, r0):
        x = xs[g, pl.ds(r0, shape.crows), :].astype(BF)
        for d in range(2):
            pg[d, g, pl.ds(r0, shape.crows), :] = dot(x, wi[d]) + bias[d]

    chunk_loop(shape, fill)


def branch_back(shape, grads, xs, h_ref, c_ref, weights, vecs, turned_out, out, scratch):
    gi, gr = weights
    wi, wr, wit, wrt, wot, z, dh = scratch
    n, R = shape.crows, shape.rows
    forward_weights(gi, gr, wi, wr)
    for d in range(2):
        wit[d] = jnp.transpose(gi[0, d]).astype(BF)
        wrt[d] = jnp.transpose(gr[0, d]).astype(BF)
    wot[...] = turned_out.astype(BF)
    out[...] = jnp.zeros_like(out)
    bias, (o_bias, gain, _) = vecs

    def earlier(g, r0, d):
        at = pl.multiple_of(r0 + 2 * R * d, 8)
        return h_ref[g, pl.ds(at, n), d * H : (d + 1) * H].astype(BF)

    def first(g, i, r0):
        now = h_ref[g, pl.ds(pl.multiple_of(r0 + R, 8), n), :].astype(BF)
        unit, scale = norm_parts(dot_turned(now, wot[...]) + o_bias)
        grad = grads(g, i, r0)
        low = norm_back(grad, unit, scale, gain).astype(BF)
        dh[g, pl.ds(r0, n), :] = dot(low, wot[...])
        turned = dot_rows(low, now)
        for j in range(2):
            at = ROWS_MAPS + j * B
            out[at : at + B] += turned[:, j * LANES : (j + 1) * LANES]
        for j, value in enumerate((low.astype(F32), grad * unit, grad)):
            at = ROWS_VECS + 8 + j
            out[at : at + 1, :B] += jnp.sum(value, 0, keepdims=True)
        x = xs[g, pl.ds(r0, n), :].astype(BF)
        for d in range(2):
            z[d, g, pl.ds(r0, n), :] = dot(earlier(g, r0, d), wr[d]) + dot(x, wi[d]) + bias[d]

    chunk_loop(shape, first)
    lstm_scan_back(shape, z, dh, c_ref, wrt)

    def last(use):
        def fn(g, i, r0):
            x = xs[g, pl.ds(r0, n), :].astype(BF)
            total = None
            for d in range(2):
                full = z[d, g, pl.ds(r0, n), :]
                low = full.astype(BF)
                grad_in = dot_rows(x, low)
                grad_rec = dot_rows(earlier(g, r0, d), low)
                grad_bias = jnp.sum(full, 0, keepdims=True)
                for j in range(4):
                    lanes = slice(j * LANES, (j + 1) * LANES)
                    at = j * 384 + d * B
                    out[at : at + B] += grad_in[:, lanes]
                    at = j * 384 + 128 + d * H
                    out[at : at + H] += grad_rec[:, lanes]
                    at = ROWS_VECS + 4 * d + j
                    out[at : at + 1] += grad_bias[:, lanes]
                part = dot(low, wit[d])
                total = part if total is None else total + part
            use(g, i, r0, total)

        chunk_loop(shape, fn)

    return last


def back_scratch(shape):
    return [
        pltpu.VMEM((2, B, 4 * H), BF),
        pltpu.VMEM((2, H, 4 * H), BF),
        pltpu.VMEM((2, 4 * H, B), BF),
        pltpu.VMEM((2, 4 * H, H), BF),
        pltpu.VMEM((B, 2 * H), BF),
        pltpu.VMEM((2, shape.groups, shape.size, 4 * H), F32),
        pltpu.VMEM((shape.groups, shape.size, 2 * H), F32),
    ]


def packed(value, RP):
    rest = value[RP:]
    if rest.shape[0] < RP:
        rest = jnp.concatenate([rest, jnp.zeros((RP - rest.shape[0], B), F32)], 0)
    return jnp.concatenate([value[:RP], rest], 1).astype(BF)


def send_tiles(res, send, nb, RI):
    RP = send.shape[2]
    for d in range(nb):
        for c in range(TILES):
            send[d, c] = packed(res[c, d * RI : (d + 1) * RI], RP)


def add_tiles(res, back, nb, RI, lim):
    RP = back.shape[2]
    for d in range(nb):
        for c in range(TILES):
            both = back[d, c].astype(F32)
            for lo, hi, value in (
                (0, RP, both[:, :B]),
                (RP, RI, both[:, B:]),
            ):
                lo, hi = d * RI + lo, min(d * RI + hi, K * M)
                if lo >= hi:
                    continue
                mask = live(lim, c * HOP + lo // M, (hi - lo) // M)
                res[c, lo:hi] = (res[c, lo:hi] + value[: hi - lo]) * mask


def unpack_steps(rows, xs, T, RI):
    RP = rows.shape[1]

    def widen(t, _):
        both = rows[t].astype(F32)
        xs[0, pl.ds(pl.multiple_of(t * RI, 8), RP), :] = both[:, :B]
        if RI > RP:
            xs[0, pl.ds(pl.multiple_of(t * RI + RP, 8), RI - RP), :] = both[: RI - RP, B:]
        return 0

    lax.fori_loop(0, T, widen, 0, unroll=4 if T % 4 == 0 else 1)


def windows_of(mix, following, win):
    last = FRAMES + HOP + 1
    for i in range(1, BLOCKS):
        at = STRIDE * (i - 1)
        if at + 2 * STRIDE <= FRAMES * STRIDE:
            win[i * M : (i + 1) * M] = mix[:, at : at + 2 * STRIDE]
        elif at < FRAMES * STRIDE:
            win[i * M : (i + 1) * M] = jnp.concatenate([mix[:, at:], following[0, :, :STRIDE]], 1)
        elif i <= last:
            at -= FRAMES * STRIDE
            win[i * M : (i + 1) * M] = following[0, :, at : at + 2 * STRIDE]
        else:
            win[i * M :] = jnp.zeros(((BLOCKS - i) * M, 2 * STRIDE), F32)
            break


def softplus(value):
    return jnp.maximum(value, 0.0) + jnp.log1p(jnp.exp(-jnp.abs(value)))


def turned_out(proj, index):
    return proj[:, index * 2 * H : (index + 1) * 2 * H]


def intra_forward(shape, index, res, lim, gi, gr, vectors, proj, x_out, h_out, c_out, scratch):
    wi, wr, pg = scratch
    forward_weights(gi, gr, wi, wr)
    bias, (o_bias, gain, beta) = branch_vectors(vectors, index)
    n = shape.crows

    def keep(g, i, r0):
        x_out[g, pl.ds(pl.multiple_of(r0, 16), n), :] = res[g, pl.ds(r0, n), :].astype(BF)

    chunk_loop(shape, keep)
    branch_pregates(shape, res, wi, bias, pg)
    lstm_scan(shape, pg, wr, h_out, c_out)
    low_out = turned_out(proj, index).astype(BF)

    def close(g, i, r0):
        now = h_out[g, pl.ds(pl.multiple_of(r0 + shape.rows, 8), n), :].astype(BF)
        unit, _ = norm_parts(dot_turned(now, low_out) + o_bias)
        mask = live(lim, g * HOP + i * shape.chunk, shape.chunk)
        res[g, pl.ds(r0, n), :] = (res[g, pl.ds(r0, n), :] + (unit * gain + beta)) * mask

    chunk_loop(shape, close)


def zero_tail(res, c):
    if res.shape[1] > K * M:
        res[c, K * M :] = jnp.zeros((res.shape[1] - K * M, B), F32)


def first_kernel(shape, nb, RI, mix, following, leading, lengths, proj, vectors, gi, gr, res, send, x_out, h_out, c_out, win, wi, wr, pg, flat, bottle):
    lim = limits(lengths)
    flat[:M] = jnp.concatenate([leading[...], mix[:, :STRIDE]], 1)
    windows_of(mix, following, flat)
    win[...] = flat[...].astype(BF)
    w_enc = proj[:, BASE + N + B : BASE + N + B + 2 * STRIDE].astype(BF)
    w_bn = proj[:, BASE : BASE + N].astype(BF)
    gain, beta, b_bias = (pieces(vectors, j, 1) for j in range(3))
    for i in range(BLOCKS * M // CHUNK):
        at = i * CHUNK
        pre = dot_turned(win[at : at + CHUNK], w_enc)
        unit, _ = norm_parts(softplus(pre))
        normed = (unit * gain + beta).astype(BF)
        mask = live(lim, i * (CHUNK // M) - 1, CHUNK // M)
        bottle[at : at + CHUNK] = (dot_turned(normed, w_bn) + b_bias) * mask
    for c in range(TILES):
        res[c, : K * M] = bottle[(c * HOP + 1) * M : (c * HOP + 1 + K) * M]
        zero_tail(res, c)
    intra_forward(shape, 0, res, lim, gi, gr, vectors, proj, x_out, h_out, c_out, (wi, wr, pg))
    send_tiles(res, send, nb, RI)


def third_kernel(shape, nb, RI, res_in, back, lengths, proj, vectors, gi, gr, res, send, x_out, h_out, c_out, wi, wr, pg):
    lim = limits(lengths)
    res[...] = res_in[...]
    add_tiles(res, back, nb, RI, lim)
    intra_forward(shape, 2, res, lim, gi, gr, vectors, proj, x_out, h_out, c_out, (wi, wr, pg))
    send_tiles(res, send, nb, RI)


def inter_kernel(shape, RI, index, rows, proj, vectors, gi, gr, normed, h_out, c_out, wi, wr, pg, xs):
    forward_weights(gi, gr, wi, wr)
    unpack_steps(rows, xs, shape.steps, RI)
    bias, (o_bias, gain, beta) = branch_vectors(vectors, index)
    branch_pregates(shape, xs, wi, bias, pg)
    lstm_scan(shape, pg, wr, h_out, c_out)
    low_out = turned_out(proj, index).astype(BF)
    RP = normed.shape[1]

    def close(g, i, r0):
        now = h_out[g, pl.ds(pl.multiple_of(r0 + RI, 8), shape.crows), :].astype(BF)
        unit, _ = norm_parts(dot_turned(now, low_out) + o_bias)
        value = unit * gain + beta
        for j in range(shape.chunk):
            normed[i * shape.chunk + j] = packed(value[j * RI : (j + 1) * RI], RP)

    chunk_loop(shape, close)


EDGE = (HOP + 1) * M
EDGE_TOP = 208


def edge_pack(value):
    rest = jnp.concatenate([value[EDGE_TOP:], jnp.zeros((2 * EDGE_TOP - EDGE, B), F32)], 0)
    return jnp.concatenate([value[:EDGE_TOP], rest], 1)


def edge_unpack(ref):
    return jnp.concatenate([ref[:, :B], ref[: EDGE - EDGE_TOP, B:]], 0)


def part_kernel(nb, RI, res_in, back, lengths, part, up, down, res):
    res[...] = res_in[...]
    add_tiles(res, back, nb, RI, limits(lengths))
    half = HOP * M
    part[:half] = res[0, :half]
    for c in range(1, TILES):
        part[c * half : (c + 1) * half] = res[c, :half] + res[c - 1, half : 2 * half]
    part[TILES * half :] = res[TILES - 1, half : 2 * half]
    up[...] = edge_pack(part[TILES * half - M :])
    down[...] = edge_pack(part[: half + M])


def middle_kernel(nb, RI, part, before, after, lengths, win, goal, following, proj, vectors, send, gres, genc, gm, feats, dec, tgt, gest, enc, gate, src, act):
    lim = limits(lengths)
    half = HOP * M
    top = M + TILES * half
    total = BLOCKS * M
    early, late = edge_unpack(before), edge_unpack(after)
    feats[:M] = early[:M]
    feats[M : M + half] = part[:half] + early[M:]
    feats[M + half : top] = part[half : TILES * half]
    feats[top : top + half] = part[TILES * half :] + late[:half]
    feats[top + half : top + half + M] = late[half:]
    feats[top + half + M :] = jnp.zeros((PADDED * M - top - half - M, B), F32)
    low_mask = proj[:, BASE + N : BASE + N + B].astype(BF)
    w_enc = proj[:, BASE + N + B : BASE + N + B + 2 * STRIDE].astype(BF)
    low_dec = proj[:, BASE + N + B + 2 * STRIDE : BASE + N + B + 4 * STRIDE].astype(BF)
    m_bias = pieces(vectors, vectors.shape[0] * 2 - 1, 1)
    root = 0.7978845608028654
    cube = 0.044715
    dec[total:] = jnp.zeros((PADDED * M - total, 2 * STRIDE), F32)
    for i in range(total // CHUNK):
        rows = slice(i * CHUNK, (i + 1) * CHUNK)
        x = feats[rows]
        low = (0.5 * x * (1.0 + jnp.tanh(root * (x + cube * x * x * x)))).astype(BF)
        encoded = softplus(dot_turned(win[rows], w_enc))
        mask = 0.5 * jnp.tanh(0.5 * (dot_turned(low, low_mask) + m_bias)) + 0.5
        source = (mask * encoded).astype(BF)
        enc[rows] = encoded
        gate[rows] = mask
        src[rows] = source.astype(F32)
        act[rows] = low.astype(F32)
        dec[rows] = dot(source, low_dec)
    dec[:M] = dec[:M] * jnp.where(lax.axis_index("block") > 0, 1.0, 0.0)
    for ref in (enc, gate, src, act):
        ref[total:] = jnp.zeros((PADDED * M - total, B), F32)
    for i in range(1, FRAMES + 1):
        tgt[i * M : (i + 1) * M] = goal[:, STRIDE * (i - 1) : STRIDE * i]
    for i in range(FRAMES + 1, FRAMES + HOP + 2):
        at = STRIDE * (i - 1 - FRAMES)
        tgt[i * M : (i + 1) * M] = following[1, :, at : at + STRIDE]
    tgt[(FRAMES + HOP + 2) * M :] = jnp.zeros(((PADDED - FRAMES - HOP - 2) * M, STRIDE), F32)
    estimate = dec[M:total, :STRIDE] + dec[: total - M, STRIDE:]
    count = BLOCKS - 1
    spot = lax.broadcasted_iota(jnp.int32, (count, M, STRIDE), 0)
    phase = lax.broadcasted_iota(jnp.int32, (count, M, STRIDE), 2)
    near = spot < FRAMES + HOP + 1
    valid = jnp.where(near & (spot * STRIDE + phase < lim[:, :STRIDE][None]), 1.0, 0.0)
    inside = jnp.where(spot < FRAMES, valid, 0.0).reshape(count * M, STRIDE)
    valid = valid.reshape(count * M, STRIDE)
    error = estimate - tgt[M:total]
    smoothed = jnp.sqrt(error * error + 1.0)
    gest[:M] = jnp.zeros((M, STRIDE), F32)
    gest[M:total] = valid * error / smoothed
    gest[total:] = jnp.zeros((PADDED * M - total, STRIDE), F32)
    loss = jnp.sum(jnp.sum(inside * (smoothed - 1.0), 0, keepdims=True), 1, keepdims=True)
    seen = jnp.sum(jnp.sum(inside, 0, keepdims=True), 1, keepdims=True)
    gm[...] = jnp.zeros_like(gm)
    gm[132:133] = jnp.broadcast_to(loss, (1, LANES))
    gm[133:134] = jnp.broadcast_to(seen, (1, LANES))
    for i in range(total // CHUNK):
        at = i * CHUNK + M
        rows = slice(at, at + CHUNK)
        grad_dec = jnp.concatenate([gest[rows], gest[at + M : at + M + CHUNK]], 1).astype(BF)
        mine = own(i * (CHUNK // M), CHUNK // M)
        mine_low = mine.astype(BF)
        gm[64:128, 16:32] += dot_rows(src[rows].astype(BF) * mine_low, grad_dec)
        grad_source = dot_turned(grad_dec, low_dec)
        mask = gate[rows]
        grad_logit = (grad_source * enc[rows] * mask * (1.0 - mask)).astype(BF)
        enc[rows] = grad_source * mask
        gm[:64, 64:] += dot_rows(grad_logit * mine_low, act[rows].astype(BF))
        gm[131:132, :B] += jnp.sum(grad_logit.astype(F32) * mine, 0, keepdims=True)
        x = feats[rows]
        curve = jnp.tanh(root * (x + cube * x * x * x))
        slope = 0.5 * (1.0 + curve) + (0.5 * root) * x * (1.0 - curve * curve) * (
            1.0 + (3.0 * cube) * x * x
        )
        feats[rows] = slope * dot(grad_logit, low_mask)
    genc[...] = enc[M : M + FRAMES * M]
    for c in range(TILES):
        gres[c, : K * M] = feats[M + c * half : M + c * half + K * M] * live(lim, c * HOP, K)
        zero_tail(gres, c)
    send_tiles(gres, send, nb, RI)


def inter_back_kernel(shape, RI, index, grad_rows, rows, h_ref, c_ref, proj, vectors, gi, gr, send, out, *scratch):
    xs, gs, core = scratch[0], scratch[1], scratch[2:]
    unpack_steps(rows, xs, shape.steps, RI)
    unpack_steps(grad_rows, gs, shape.steps, RI)
    RP = send.shape[1]

    def grads(g, i, r0):
        return gs[g, pl.ds(r0, shape.crows), :]

    last = branch_back(
        shape, grads, xs, h_ref, c_ref, (gi, gr), branch_vectors(vectors, index), turned_out(proj, index), out, core
    )

    def use(g, i, r0, total):
        for j in range(shape.chunk):
            send[i * shape.chunk + j] = packed(total[j * RI : (j + 1) * RI], RP)

    last(use)


def intra_back(shape, index, gres, x_ref, h_ref, c_ref, proj, vectors, gi, gr, out, core):
    n = shape.crows

    def grads(g, i, r0):
        return gres[g, pl.ds(r0, n), :]

    last = branch_back(
        shape, grads, x_ref, h_ref, c_ref, (gi, gr), branch_vectors(vectors, index), turned_out(proj, index), out, core
    )

    def use(g, i, r0, total):
        gres[g, pl.ds(r0, n), :] = gres[g, pl.ds(r0, n), :] + total

    last(use)


def third_back_kernel(shape, nb, RI, gres_in, back, lengths, x_ref, h_ref, c_ref, proj, vectors, gi, gr, gres, send, out, *core):
    lim = limits(lengths)
    gres[...] = gres_in[...]
    add_tiles(gres, back, nb, RI, lim)
    intra_back(shape, 2, gres, x_ref, h_ref, c_ref, proj, vectors, gi, gr, out, core)
    for c in range(TILES):
        gres[c, : K * M] = gres[c, : K * M] * live(lim, c * HOP, K)
    send_tiles(gres, send, nb, RI)


def first_back_kernel(shape, nb, RI, gres_in, back, lengths, x_ref, h_ref, c_ref, proj, vectors, gi, gr, win, genc, gm_in, out, gres, bottle, *core):
    lim = limits(lengths)
    gres[...] = gres_in[...]
    add_tiles(gres, back, nb, RI, lim)
    intra_back(shape, 0, gres, x_ref, h_ref, c_ref, proj, vectors, gi, gr, out, core)
    gm = ROWS_G
    out[gm : gm + gm_in.shape[0]] = gm_in[...]
    bottle[...] = jnp.zeros_like(bottle)
    for c in range(TILES):
        at = (c * HOP + 1) * M
        bottle[at : at + K * M] += gres[c, : K * M]
    w_enc = proj[:, BASE + N + B : BASE + N + B + 2 * STRIDE].astype(BF)
    w_bn = proj[:, BASE : BASE + N].astype(BF)
    gain, beta = (pieces(vectors, j, 1) for j in range(2))
    own_rows = FRAMES * M
    for i in range(BLOCKS * M // CHUNK):
        at = i * CHUNK
        rows = slice(at, at + CHUNK)
        pre = dot_turned(win[rows], w_enc)
        unit, scale = norm_parts(softplus(pre))
        normed = (unit * gain + beta).astype(BF)
        low = (bottle[rows] * live(lim, i * (CHUNK // M) - 1, CHUNK // M)).astype(BF)
        out[gm : gm + 64, :N] += dot_rows(low, normed)
        grad_normed = dot(low, w_bn)
        for j, value in enumerate((grad_normed * unit, grad_normed, low.astype(F32))):
            out[gm + 128 + j : gm + 129 + j, :B] += jnp.sum(value, 0, keepdims=True)
        grad_enc = norm_back(grad_normed, unit, scale, gain)
        lo, hi = max(at - M, 0), min(at + CHUNK - M, own_rows)
        if lo < hi:
            piece = genc[lo:hi]
            above, below = lo + M - at, at + CHUNK - M - hi
            if above:
                piece = jnp.concatenate([jnp.zeros((above, B), F32), piece], 0)
            if below:
                piece = jnp.concatenate([piece, jnp.zeros((below, B), F32)], 0)
            grad_enc = grad_enc + piece
        grad_pre = (grad_enc * (0.5 * jnp.tanh(0.5 * pre) + 0.5)).astype(BF)
        out[gm + 64 : gm + 128, :16] += dot_rows(grad_pre, win[rows])


def adam_parts(grad, moment, square, weight, average, decay):
    moment = BETA_ONE * moment + (1.0 - BETA_ONE) * grad
    square = BETA_TWO * square + (1.0 - BETA_TWO) * grad * grad
    corrected = moment * (1.0 / (1.0 - BETA_ONE**STEP))
    scaled = square * (1.0 / (1.0 - BETA_TWO**STEP))
    weight = weight - RATE * (corrected / (jnp.sqrt(scaled) + ADAM_EPS) + decay * weight)
    average = KEEP * average + (1.0 - KEEP) * weight
    return moment, square, weight, average, weight.astype(BF)


def adam_kernel(*refs):
    gs, old = refs[:4], refs[4:20]
    scalars, new = refs[20], refs[21:41]
    gv = refs[41]
    first = gs[0]
    gm = ROWS_G
    gv[:1] = jnp.concatenate([first[gm + 128 : gm + 129, :N], first[gm + 129 : gm + 130, :N]], 1)
    gv[1:2, :N] = first[gm + 130 : gm + 131, :N]
    gv[gv.shape[0] - 1 :, N:] = first[gm + 131 : gm + 132, :N]
    for r in range(4):
        at = 3 + 19 * r
        for j in range(8):
            row = gs[r][ROWS_VECS + j : ROWS_VECS + j + 1]
            for k in range(2):
                q = at + 2 * j + k
                gv[q // 2 : q // 2 + 1, (q % 2) * N : (q % 2 + 1) * N] = row[:, k * N : (k + 1) * N]
        for j in range(3):
            q = at + 16 + j
            gv[q // 2 : q // 2 + 1, (q % 2) * N : (q % 2 + 1) * N] = gs[r][ROWS_VECS + 8 + j : ROWS_VECS + 9 + j, :N]
    part = jnp.zeros((8, LANES), F32)
    for r in range(4):
        value = gs[r][:ROWS_VECS].reshape(ROWS_VECS // 8, 8, LANES)
        part = part + jnp.sum(value * value, 0)
    value = first[gm : gm + 128].reshape(16, 8, LANES)
    part = part + jnp.sum(value * value, 0)
    value = gv[...].reshape(5, 8, LANES)
    part = part + jnp.sum(value * value, 0)
    squared = jnp.sum(jnp.sum(part, 0, keepdims=True), 1, keepdims=True)
    loss, count = first[gm + 132 : gm + 133, :1], first[gm + 133 : gm + 134, :1]
    norm = jnp.sqrt(squared) / count
    factor = jnp.minimum(1.0, CLIP / norm) / count
    row = lax.broadcasted_iota(jnp.int32, (8, LANES), 0)
    scalars[...] = jnp.where(row == 0, loss, jnp.where(row == 1, count, norm))

    def update(kind, index, grad, decay):
        results = adam_parts(
            grad * factor,
            old[4 + kind][index],
            old[8 + kind][index],
            old[kind][index],
            old[12 + kind][index],
            decay,
        )
        for j, value in enumerate(results):
            new[4 * j + kind][index] = value

    for r in range(4):
        for d in range(2):
            for j in range(4):
                lanes = slice(j * LANES, (j + 1) * LANES)
                at = j * 384 + d * B
                update(0, (r, d, slice(None), lanes), gs[r][at : at + B], DECAY)
                at = j * 384 + 128 + d * H
                update(1, (r, d, slice(None), lanes), gs[r][at : at + H], DECAY)
        for j in range(2):
            at = ROWS_MAPS + j * B
            lanes = slice(r * 2 * H + j * LANES, r * 2 * H + (j + 1) * LANES)
            update(2, (slice(None), lanes), gs[r][at : at + B], DECAY)
    update(2, (slice(None), slice(BASE, BASE + LANES)), first[gm : gm + 64], DECAY)
    update(2, (slice(None), slice(BASE + LANES, BASE + LANES + 32)), first[gm + 64 : gm + 128, :32], DECAY)
    update(3, (slice(None), slice(None)), gv[...], 0.0)


def call(kernel, outs, ins, scratch, index=None, limit=56, micros=20):
    vmem = pl.BlockSpec(memory_space=pltpu.VMEM)
    specs = [
        pl.BlockSpec(memory_space=pltpu.SMEM) if a.ndim == 1 and a.dtype == jnp.int32 else vmem
        for a in ins
    ]
    extra = []
    wrapped = kernel
    if index is not None:
        big = [i for i, a in enumerate(ins) if a.ndim == 4 and a.shape[:2] == (2 * LAYERS, 2)]
        for i in big:
            specs[i] = pl.BlockSpec(memory_space=pl.ANY)
        extra = [pltpu.VMEM((1,) + ins[i].shape[1:], F32) for i in big]
        extra.append(pltpu.SemaphoreType.DMA((len(big),)))

        def wrapped(*refs):
            refs = list(refs)
            held, sem = refs[len(refs) - len(extra) : -1], refs[-1]
            copies = []
            for j, i in enumerate(big):
                copies.append(pltpu.make_async_copy(refs[i].at[pl.ds(index, 1)], held[j], sem.at[j]))
                copies[-1].start()
            for copy in copies:
                copy.wait()
            for j, i in enumerate(big):
                refs[i] = held[j]
            kernel(*refs[: len(refs) - len(extra)])

    return pl.pallas_call(
        wrapped,
        out_shape=outs,
        in_specs=specs,
        out_specs=[vmem] * len(outs),
        scratch_shapes=list(scratch) + extra,
        compiler_params=pltpu.CompilerParams(vmem_limit_bytes=limit * 1024 * 1024),
        cost_estimate=pl.CostEstimate(
            flops=micros * 10**9, bytes_accessed=micros * 10**6, transcendentals=0
        ),
    )(*ins)


def shift(block, axis, distance):
    size = lax.axis_size(axis)
    route = [(i, i + distance) for i in range(size) if 0 <= i + distance < size]
    return lax.ppermute(block, axis, route)


def exchange(block):
    return lax.all_to_all(block, "block", split_axis=0, concat_axis=0, tiled=True)


def flip(block, bit):
    size = lax.axis_size("dp")
    return lax.ppermute(block, "dp", [(i, i ^ (1 << bit)) for i in range(size)])


def bits():
    return lax.axis_size("dp").bit_length() - 1


def halve(block):
    for bit in range(bits()):
        half = block.shape[0] // 2
        mine = (lax.axis_index("dp") >> bit) & 1
        given = lax.dynamic_slice_in_dim(block, (1 - mine) * half, half, 0)
        block = lax.dynamic_slice_in_dim(block, mine * half, half, 0) + flip(given, bit)
    return block


def double(block):
    for bit in reversed(range(bits())):
        mine = (lax.axis_index("dp") >> bit) & 1
        other = flip(block, bit)
        block = jnp.where(
            mine == 0, jnp.concatenate([block, other], 0), jnp.concatenate([other, block], 0)
        )
    return block


def scatter_sum(block):
    nb = lax.axis_size("block")
    block = halve(block)
    rows = block.shape[0]
    part = -(-rows // (8 * nb)) * 8
    if part * nb > rows:
        block = jnp.concatenate([block, jnp.zeros((part * nb - rows, LANES), F32)], 0)
    return jnp.sum(exchange(block.reshape(nb, part, LANES)), 0)


def gather_sums(parts, sizes):
    nb, dp = lax.axis_size("block"), lax.axis_size("dp")
    mine = jnp.concatenate(parts, 0)
    all_parts = exchange(jnp.broadcast_to(mine[None], (nb,) + mine.shape))
    given, at = [], 0
    for part, size in zip(parts, sizes):
        rows = part.shape[0]
        block = all_parts[:, at : at + rows].reshape(nb * rows, LANES)
        given.append(double(block[: size // dp]))
        at += rows
    return given


def body(
    mixture,
    target,
    lengths,
    input_gates,
    recur_gates,
    projections,
    vectors,
    moment_input,
    moment_recur,
    moment_proj,
    moment_vecs,
    square_input,
    square_recur,
    square_proj,
    square_vecs,
    average_input,
    average_recur,
    average_proj,
    average_vecs,
):
    nb = lax.axis_size("block")
    RI = -(-K // nb) * M
    intra = Shape(TILES, K, M)
    inter = Shape(1, TILES * nb, RI)
    T = inter.steps
    gi, gr = input_gates, recur_gates
    proj = projections.T
    vectors_wide = vectors.reshape(-1, LANES)
    reach = (HOP + 2) * STRIDE
    following = shift(jnp.stack([mixture[:, :reach], target[:, :reach]]), "block", -1)
    leading = shift(mixture[:, -STRIDE:], "block", 1)

    RP = -(-RI // 16) * 8
    res_shape = SDS((TILES, nb * RI, B), F32)
    send_shape = SDS((nb, TILES, RP, 2 * B), BF)
    steps_shape = SDS((T, RP, 2 * B), BF)
    x_shape = SDS((TILES, K * M, B), BF)

    def state(shape):
        return SDS((shape.groups, shape.wide, 2 * H), F32)

    def fwd_scratch(shape):
        return [
            pltpu.VMEM((2, B, 4 * H), BF),
            pltpu.VMEM((2, H, 4 * H), BF),
            pltpu.VMEM((2, shape.groups, shape.size, 4 * H), F32),
        ]

    res0, send, x0, h0, c0, win = call(
        functools.partial(first_kernel, intra, nb, RI),
        [res_shape, send_shape, x_shape, state(intra), state(intra), SDS((BLOCKS * M, 2 * STRIDE), BF)],
        [mixture, following, leading, lengths, proj, vectors_wide, gi, gr],
        fwd_scratch(intra)
        + [pltpu.VMEM((BLOCKS * M, 2 * STRIDE), F32), pltpu.VMEM((BLOCKS * M, B), F32)],
        0,
    )

    def inter_step(send, index):
        rows = exchange(send).reshape(T, RP, 2 * B)
        normed, h, c = call(
            functools.partial(inter_kernel, inter, RI, index),
            [steps_shape, state(inter), state(inter)],
            [rows, proj, vectors_wide, gi, gr],
            fwd_scratch(inter) + [pltpu.VMEM((1, inter.size, B), F32)],
            index,
        )
        return rows, h, c, exchange(normed.reshape(send_shape.shape))

    rows1, h1, c1, back = inter_step(send, 1)
    res2, send, x2, h2, c2 = call(
        functools.partial(third_kernel, intra, nb, RI),
        [res_shape, send_shape, x_shape, state(intra), state(intra)],
        [res0, back, lengths, proj, vectors_wide, gi, gr],
        fwd_scratch(intra),
        2,
    )
    rows3, h3, c3, back = inter_step(send, 3)
    edge_shape = SDS((EDGE_TOP, 2 * B), F32)
    part, up, down = call(
        functools.partial(part_kernel, nb, RI),
        [SDS(((FRAMES + HOP) * M, B), F32), edge_shape, edge_shape],
        [res2, back, lengths],
        [pltpu.VMEM(res_shape.shape, F32)],
    )
    before = shift(up, "block", 1)
    after = shift(down, "block", -1)
    tall = PADDED * M
    send, gres, genc, gm = call(
        functools.partial(middle_kernel, nb, RI),
        [send_shape, res_shape, SDS((FRAMES * M, B), F32), SDS((136, LANES), F32)],
        [part, before, after, lengths, win, target, following, proj, vectors_wide],
        [
            pltpu.VMEM((tall, B), F32),
            pltpu.VMEM((tall, 2 * STRIDE), F32),
            pltpu.VMEM((tall, STRIDE), F32),
            pltpu.VMEM((tall, STRIDE), F32),
            pltpu.VMEM((tall, B), F32),
            pltpu.VMEM((tall, B), F32),
            pltpu.VMEM((tall, B), F32),
            pltpu.VMEM((tall, B), F32),
        ],
    )
    out_shape = SDS((ROWS_G, LANES), F32)

    def inter_back(send, rows, h, c, index):
        grad_rows = exchange(send).reshape(T, RP, 2 * B)
        send, out = call(
            functools.partial(inter_back_kernel, inter, RI, index),
            [steps_shape, out_shape],
            [grad_rows, rows, h, c, proj, vectors_wide, gi, gr],
            [pltpu.VMEM((1, inter.size, B), F32)] * 2 + back_scratch(inter),
            index,
        )
        return exchange(send.reshape(send_shape.shape)), out

    back, out3 = inter_back(send, rows3, h3, c3, 3)
    gres, send, out2 = call(
        functools.partial(third_back_kernel, intra, nb, RI),
        [res_shape, send_shape, out_shape],
        [gres, back, lengths, x2, h2, c2, proj, vectors_wide, gi, gr],
        back_scratch(intra),
        2,
    )
    back, out1 = inter_back(send, rows1, h1, c1, 1)
    (out0,) = call(
        functools.partial(first_back_kernel, intra, nb, RI),
        [SDS((ROWS_FIRST, LANES), F32)],
        [gres, back, lengths, x0, h0, c0, proj, vectors_wide, gi, gr, win, genc, gm],
        [pltpu.VMEM(res_shape.shape, F32), pltpu.VMEM((BLOCKS * M, B), F32)] + back_scratch(intra),
        0,
    )
    sums = gather_sums([scatter_sum(out0), scatter_sum(out1)], [ROWS_FIRST, ROWS_G])
    sums += gather_sums([scatter_sum(out2), scatter_sum(out3)], [ROWS_G, ROWS_G])
    old = [
        input_gates, recur_gates, projections, vectors,
        moment_input, moment_recur, moment_proj, moment_vecs,
        square_input, square_recur, square_proj, square_vecs,
        average_input, average_recur, average_proj, average_vecs,
    ]
    for i in range(2, 16, 4):
        old[i] = old[i].T
    for i in range(3, 16, 4):
        old[i] = old[i].reshape(-1, LANES)
    new = [SDS(a.shape, F32) for a in old[:4]] * 4 + [SDS(a.shape, BF) for a in old[:4]]
    scalars, *new = call(
        adam_kernel,
        [SDS((8, LANES), F32)] + new,
        sums + old,
        [pltpu.VMEM(old[3].shape, F32)],
    )
    for i in range(2, 20, 4):
        new[i] = new[i].T
    for i in range(3, 20, 4):
        new[i] = new[i].reshape(-1)
    return (scalars[0, 0], scalars[1, 0], scalars[2, 0], *new)


def solution(mesh):
    in_specs = (P("dp", "block"), P("dp", "block"), P("dp")) + (P(),) * 16
    return jax.shard_map(
        body, mesh=mesh, in_specs=in_specs, out_specs=(P(),) * 23, check_vma=False
    )
```

```python
import functools

import jax
import jax.numpy as jnp
from jax import lax
from jax.experimental import pallas as pl
from jax.experimental.pallas import tpu as pltpu
from jax.sharding import PartitionSpec as P

N = 64
B = 64
H = 128
K = 100
STRIDE = 8
LAYERS = 2
STEP = 10
HOP = 50
TILES = 3
M = 8
FRAMES = 150
BASE = 4 * LAYERS * H
PERIOD = 8 * H + 3 * B
ROWS_MAPS = 1536
ROWS_VECS = 1664
ROWS_G = 1696
ROWS_FIRST = 1856
LANES = 128
BLOCKS = 208
PADDED = 216
CHUNK = 416

EPS_NORM = 1e-05
CLIP = 0.001
RATE = 0.1
BETA_ONE = 0.9
BETA_TWO = 0.999
ADAM_EPS = 1e-08
DECAY = 0.01
KEEP = 0.9

BF = jnp.bfloat16
F32 = jnp.float32
SDS = jax.ShapeDtypeStruct


def dot(left, right):
    return jnp.dot(left, right, preferred_element_type=F32)


def dot_turned(left, right):
    return lax.dot_general(left, right, (((1,), (1,)), ((), ())), preferred_element_type=F32)


def dot_rows(left, right):
    return lax.dot_general(left, right, (((0,), (0,)), ((), ())), preferred_element_type=F32)


def half_scale():
    lane = lax.broadcasted_iota(jnp.int32, (1, 4 * H), 1)
    return jnp.where((lane >= 2 * H) & (lane < 3 * H), 1.0, 0.5)


def gate_acts(z):
    act = jnp.tanh(z)
    sig_i = 0.5 * act[:, :H] + 0.5
    sig_f = 0.5 * act[:, H : 2 * H] + 0.5
    sig_o = 0.5 * act[:, 3 * H :] + 0.5
    return sig_i, sig_f, act[:, 2 * H : 3 * H], sig_o


def norm_parts(value):
    center = value - jnp.mean(value, -1, keepdims=True)
    spread = jnp.mean(center * center, -1, keepdims=True)
    scale = lax.rsqrt(spread + EPS_NORM)
    return center * scale, scale


def norm_back(grad, unit, scale, gain):
    inner = grad * gain
    return scale * (
        inner
        - jnp.mean(inner, -1, keepdims=True)
        - unit * jnp.mean(inner * unit, -1, keepdims=True)
    )


def live(lim, start, count):
    pos = lax.broadcasted_iota(jnp.int32, (count, M, B), 0) + start
    return jnp.where(pos * STRIDE < lim[None], 1.0, 0.0).reshape(count * M, B)


def limits(lengths):
    row = lax.broadcasted_iota(jnp.int32, (M, B), 0)
    total = jnp.zeros((M, B), jnp.int32)
    for m in range(M):
        total = jnp.where(row == m, lengths[m], total)
    return total - lax.axis_index("block") * (FRAMES * STRIDE)


def pieces(vectors, start, count):
    parts = []
    at = start
    while at < start + count:
        wide = at % 2 == 0 and at + 2 <= start + count
        lane = (at % 2) * N
        parts.append(vectors[at // 2 : at // 2 + 1, lane : lane + (2 * N if wide else N)])
        at += 2 if wide else 1
    return parts[0] if len(parts) == 1 else jnp.concatenate(parts, 1)


def branch_vectors(vectors, index):
    first = (2 * N + B + index * PERIOD) // N
    half = half_scale()
    bias = [pieces(vectors, first + 8 * d, 8) * half for d in range(2)]
    return bias, [pieces(vectors, first + 16 + j, 1) for j in range(3)]


def own(start, count):
    pos = lax.broadcasted_iota(jnp.int32, (count, M, B), 0) + start
    return jnp.where(pos < FRAMES, 1.0, 0.0).reshape(count * M, B)


def chunk_of(steps, rows):
    best = 1
    for size in range(1, steps + 1):
        if steps % size == 0 and size * rows <= 512 and size * rows % 16 == 0:
            best = size
    return best


class Shape:
    def __init__(self, groups, steps, rows):
        self.groups, self.steps, self.rows = groups, steps, rows
        self.size = steps * rows
        self.chunk = chunk_of(steps, rows)
        self.crows = self.chunk * rows
        self.chunks = steps // self.chunk
        self.wide = (steps + 2) * rows
        self.unroll = 4 if steps % 4 == 0 else 1


def chunk_loop(shape, fn):
    for g in range(shape.groups):

        def step(i, _, g=g):
            fn(g, i, pl.multiple_of(i * shape.crows, 8))
            return 0

        lax.fori_loop(0, shape.chunks, step, 0)


def forward_weights(gi, gr, index, wc):
    half = half_scale()
    for d in range(2):
        wc[d, :H] = (gr[index, d].astype(BF).astype(F32) * half).astype(BF)
        wc[d, H:] = (gi[index, d].astype(BF).astype(F32) * half).astype(BF)


def lstm_scan(shape, pg, wc, h_ref, c_ref):
    G, S, R = shape.groups, shape.steps, shape.rows
    pad = jnp.zeros((R, 2 * H), F32)
    for g in range(G):
        for ref in (h_ref, c_ref):
            ref[g * shape.wide : g * shape.wide + R] = pad
            ref[(g + 1) * shape.wide - R : (g + 1) * shape.wide] = pad

    def one(d, t, hidden, memory):
        at = pl.multiple_of(t * R, 8)
        pre = jnp.concatenate([pg[d, pl.ds(g * shape.size + at, R), :] for g in range(G)], 0)
        z = pre + dot(hidden, wc[d, :H])
        sig_i, sig_f, tan_g, sig_o = gate_acts(z)
        memory = sig_f * memory + sig_i * tan_g
        hidden = (sig_o * jnp.tanh(memory)).astype(BF)
        full = hidden.astype(F32)
        after = pl.multiple_of(t * R + R, 8)
        for g in range(G):
            to = pl.ds(g * shape.wide + after, R)
            h_ref[to, d * H : (d + 1) * H] = full[g * R : (g + 1) * R]
            c_ref[to, d * H : (d + 1) * H] = memory[g * R : (g + 1) * R]
        return hidden, memory

    def step(s, carry):
        hf, cf, hb, cb = carry
        hf, cf = one(0, s, hf, cf)
        hb, cb = one(1, S - 1 - s, hb, cb)
        return hf, cf, hb, cb

    zero = jnp.zeros((G * R, H), F32)
    start = (zero.astype(BF), zero, zero.astype(BF), zero)
    lax.fori_loop(0, S, step, start, unroll=shape.unroll)


def lstm_scan_back(shape, z, dh, c_ref, wrt):
    G, S, R = shape.groups, shape.steps, shape.rows

    def one(d, t, rec_hidden, rec_memory):
        def take(ref, at, width, lanes):
            at = pl.multiple_of(at, 8)
            return jnp.concatenate([ref[pl.ds(g * width + at, R), lanes] for g in range(G)], 0)

        lanes = slice(d * H, (d + 1) * H)
        at = pl.multiple_of(t * R, 8)
        zt = jnp.concatenate([z[d, pl.ds(g * shape.size + at, R), :] for g in range(G)], 0)
        sig_i, sig_f, tan_g, sig_o = gate_acts(zt)
        tan_c = jnp.tanh(take(c_ref, t * R + R, shape.wide, lanes))
        before = take(c_ref, t * R + 2 * R * d, shape.wide, lanes)
        grad_h = take(dh, t * R, shape.size, lanes) + rec_hidden
        grad_c = rec_memory + grad_h * (sig_o * (1.0 - tan_c * tan_c))
        grad_pre = jnp.concatenate(
            [
                grad_c * (tan_g * sig_i * (1.0 - sig_i)),
                grad_c * (before * sig_f * (1.0 - sig_f)),
                grad_c * (sig_i * (1.0 - tan_g * tan_g)),
                grad_h * (tan_c * sig_o * (1.0 - sig_o)),
            ],
            -1,
        ).astype(BF)
        full = grad_pre.astype(F32)
        for g in range(G):
            z[d, pl.ds(g * shape.size + at, R), :] = full[g * R : (g + 1) * R]
        return dot(grad_pre, wrt[d]), grad_c * sig_f

    def step(s, carry):
        hf, cf, hb, cb = carry
        hf, cf = one(0, S - 1 - s, hf, cf)
        hb, cb = one(1, s, hb, cb)
        return hf, cf, hb, cb

    zero = jnp.zeros((G * R, H), F32)
    lax.fori_loop(0, S, step, (zero,) * 4, unroll=shape.unroll)


def branch_pregates(shape, inputs, wc, bias, pg):
    def fill(g, i, r0):
        x = inputs(g, r0).astype(BF)
        for d in range(2):
            pg[d, pl.ds(g * shape.size + r0, shape.crows), :] = dot(x, wc[d, H:]) + bias[d]

    chunk_loop(shape, fill)


def branch_back(shape, grads, inputs, h_ref, c_ref, weights, index, vecs, turned_out, out, scratch):
    gi, gr = weights
    wc, wit, wrt, wot, z, dh = scratch
    n, R = shape.crows, shape.rows
    forward_weights(gi, gr, index, wc)
    for d in range(2):
        wit[d] = jnp.transpose(gi[index, d]).astype(BF)
        wrt[d] = jnp.transpose(gr[index, d]).astype(BF)
    wot[...] = turned_out.astype(BF)
    out[...] = jnp.zeros_like(out)
    bias, (o_bias, gain, _) = vecs

    def states(g, at, lanes):
        return h_ref[pl.ds(pl.multiple_of(g * shape.wide + at, 8), n), lanes].astype(BF)

    def earlier(g, r0, d):
        before = states(g, r0 + 2 * R * d, slice(d * H, (d + 1) * H))
        return jnp.concatenate([before, inputs(g, r0).astype(BF)], 1)

    def first(g, i, r0):
        now = states(g, r0 + R, slice(0, 2 * H))
        here = pl.ds(g * shape.size + r0, n)
        unit, scale = norm_parts(dot_turned(now, wot[...]) + o_bias)
        grad = grads(g, r0)
        low = norm_back(grad, unit, scale, gain).astype(BF)
        dh[here, :] = dot(low, wot[...])
        turned = dot_rows(low, now)
        for j in range(2):
            at = ROWS_MAPS + j * B
            out[at : at + B] += turned[:, j * LANES : (j + 1) * LANES]
        for j, value in enumerate((low.astype(F32), grad * unit, grad)):
            at = ROWS_VECS + 8 + j
            out[at : at + 1, :B] += jnp.sum(value, 0, keepdims=True)
        for d in range(2):
            z[d, here, :] = dot(earlier(g, r0, d), wc[d]) + bias[d]

    chunk_loop(shape, first)
    lstm_scan_back(shape, z, dh, c_ref, wrt)

    def last(use):
        def fn(g, i, r0):
            total = None
            for d in range(2):
                full = z[d, pl.ds(g * shape.size + r0, n), :]
                low = full.astype(BF)
                maps = dot_rows(earlier(g, r0, d), low)
                grad_bias = jnp.sum(full, 0, keepdims=True)
                for j in range(4):
                    lanes = slice(j * LANES, (j + 1) * LANES)
                    at = j * 384 + d * B
                    out[at : at + B] += maps[H:, lanes]
                    at = j * 384 + 128 + d * H
                    out[at : at + H] += maps[:H, lanes]
                    at = ROWS_VECS + 4 * d + j
                    out[at : at + 1] += grad_bias[:, lanes]
                part = dot(low, wit[d])
                total = part if total is None else total + part
            use(g, i, r0, total)

        chunk_loop(shape, fn)

    return last


def fwd_scratch(shape):
    return [
        pltpu.VMEM((2, H + B, 4 * H), BF),
        pltpu.VMEM((2, shape.groups * shape.size, 4 * H), F32),
    ]


def back_scratch(shape):
    return [
        pltpu.VMEM((2, H + B, 4 * H), BF),
        pltpu.VMEM((2, 4 * H, B), BF),
        pltpu.VMEM((2, 4 * H, H), BF),
        pltpu.VMEM((B, 2 * H), BF),
        pltpu.VMEM((2, shape.groups * shape.size, 4 * H), F32),
        pltpu.VMEM((shape.groups * shape.size, 2 * H), F32),
    ]


def packed(value, RP):
    rest = value[RP:]
    if rest.shape[0] < RP:
        rest = jnp.concatenate([rest, jnp.zeros((RP - rest.shape[0], B), F32)], 0)
    return jnp.concatenate([value[:RP], rest], 1).astype(BF)


def send_tiles(res, send, nb, RI):
    RP = send.shape[2]
    for d in range(nb):
        for c in range(TILES):
            send[d, c] = packed(res[c, d * RI : (d + 1) * RI], RP)


def add_tiles(res, back, nb, RI, lim):
    RP = back.shape[2]
    for d in range(nb):
        for c in range(TILES):
            both = back[d, c].astype(F32)
            for lo, hi, value in (
                (0, RP, both[:, :B]),
                (RP, RI, both[:, B:]),
            ):
                lo, hi = d * RI + lo, min(d * RI + hi, K * M)
                if lo >= hi:
                    continue
                mask = live(lim, c * HOP + lo // M, (hi - lo) // M)
                res[c, lo:hi] = (res[c, lo:hi] + value[: hi - lo]) * mask


def unpack_steps(rows, xs, T, RI):
    RP = rows.shape[1]

    def widen(t, _):
        both = rows[t].astype(F32)
        xs[pl.ds(pl.multiple_of(t * RI, 8), RP), :] = both[:, :B]
        if RI > RP:
            xs[pl.ds(pl.multiple_of(t * RI + RP, 8), RI - RP), :] = both[: RI - RP, B:]
        return 0

    lax.fori_loop(0, T, widen, 0, unroll=4 if T % 4 == 0 else 1)


def windows_of(mix, following, win):
    last = FRAMES + HOP + 1
    for i in range(1, BLOCKS):
        at = STRIDE * (i - 1)
        if at + 2 * STRIDE <= FRAMES * STRIDE:
            win[i * M : (i + 1) * M] = mix[:, at : at + 2 * STRIDE]
        elif at < FRAMES * STRIDE:
            win[i * M : (i + 1) * M] = jnp.concatenate([mix[:, at:], following[:, :STRIDE]], 1)
        elif i <= last:
            at -= FRAMES * STRIDE
            win[i * M : (i + 1) * M] = following[:, at : at + 2 * STRIDE]
        else:
            win[i * M :] = jnp.zeros(((BLOCKS - i) * M, 2 * STRIDE), F32)
            break


def softplus(value):
    return jnp.maximum(value, 0.0) + jnp.log1p(jnp.exp(-jnp.abs(value)))


def turned_out(proj, index):
    return proj[:, index * 2 * H : (index + 1) * 2 * H]


def intra_forward(shape, index, res, lim, gi, gr, slot, vectors, proj, x_out, h_out, c_out, scratch):
    wc, pg = scratch
    forward_weights(gi, gr, slot, wc)
    bias, (o_bias, gain, beta) = branch_vectors(vectors, index)
    n = shape.crows

    def keep(g, i, r0):
        to = pl.ds(pl.multiple_of(g * shape.size + r0, 16), n)
        x_out[to, :] = res[g, pl.ds(r0, n), :].astype(BF)

    chunk_loop(shape, keep)
    branch_pregates(shape, lambda g, r0: res[g, pl.ds(r0, n), :], wc, bias, pg)
    lstm_scan(shape, pg, wc, h_out, c_out)
    low_out = turned_out(proj, index).astype(BF)

    def close(g, i, r0):
        now = h_out[pl.ds(pl.multiple_of(g * shape.wide + r0 + shape.rows, 8), n), :].astype(BF)
        unit, _ = norm_parts(dot_turned(now, low_out) + o_bias)
        mask = live(lim, g * HOP + i * shape.chunk, shape.chunk)
        res[g, pl.ds(r0, n), :] = (res[g, pl.ds(r0, n), :] + (unit * gain + beta)) * mask

    chunk_loop(shape, close)


def inter_forward(shape, index, xs, gi, gr, slot, vectors, proj, h_out, c_out, scratch, use):
    wc, pg = scratch
    forward_weights(gi, gr, slot, wc)
    bias, (o_bias, gain, beta) = branch_vectors(vectors, index)
    n = shape.crows
    branch_pregates(shape, lambda g, r0: xs[pl.ds(r0, n), :], wc, bias, pg)
    lstm_scan(shape, pg, wc, h_out, c_out)
    low_out = turned_out(proj, index).astype(BF)

    def close(g, i, r0):
        now = h_out[pl.ds(pl.multiple_of(r0 + shape.rows, 8), n), :].astype(BF)
        unit, _ = norm_parts(dot_turned(now, low_out) + o_bias)
        use(i, r0, unit * gain + beta)

    chunk_loop(shape, close)


def zero_tail(res, c):
    if res.shape[1] > K * M:
        res[c, K * M :] = jnp.zeros((res.shape[1] - K * M, B), F32)


def encode(mix, following, leading, lim, proj, vectors, win, flat, bottle, res):
    flat[:M] = jnp.concatenate([leading[...], mix[:, :STRIDE]], 1)
    windows_of(mix, following, flat)
    win[...] = flat[...].astype(BF)
    w_enc = proj[:, BASE + N + B : BASE + N + B + 2 * STRIDE].astype(BF)
    w_bn = proj[:, BASE : BASE + N].astype(BF)
    gain, beta, b_bias = (pieces(vectors, j, 1) for j in range(3))
    for i in range(BLOCKS * M // CHUNK):
        at = i * CHUNK
        pre = dot_turned(win[at : at + CHUNK], w_enc)
        unit, _ = norm_parts(softplus(pre))
        normed = (unit * gain + beta).astype(BF)
        mask = live(lim, i * (CHUNK // M) - 1, CHUNK // M)
        bottle[at : at + CHUNK] = (dot_turned(normed, w_bn) + b_bias) * mask
    for c in range(TILES):
        res[c, : K * M] = bottle[(c * HOP + 1) * M : (c * HOP + 1 + K) * M]
        zero_tail(res, c)


def first_kernel(shape, nb, RI, mix, following, leading, lengths, proj, vectors, gi, gr, res, send, x_out, h_out, c_out, win, wc, pg, flat, bottle):
    lim = limits(lengths)
    encode(mix, following.at[0], leading, lim, proj, vectors, win, flat, bottle, res)
    intra_forward(shape, 0, res, lim, gi, gr, 0, vectors, proj, x_out, h_out, c_out, (wc, pg))
    send_tiles(res, send, nb, RI)


def third_kernel(shape, nb, RI, res_in, back, lengths, proj, vectors, gi, gr, res, send, x_out, h_out, c_out, wc, pg):
    lim = limits(lengths)
    res[...] = res_in[...]
    add_tiles(res, back, nb, RI, lim)
    intra_forward(shape, 2, res, lim, gi, gr, 0, vectors, proj, x_out, h_out, c_out, (wc, pg))
    send_tiles(res, send, nb, RI)


def inter_kernel(shape, RI, index, rows, proj, vectors, gi, gr, normed, h_out, c_out, wc, pg, xs):
    unpack_steps(rows, xs, shape.steps, RI)
    RP = normed.shape[1]

    def use(i, r0, value):
        for j in range(shape.chunk):
            normed[i * shape.chunk + j] = packed(value[j * RI : (j + 1) * RI], RP)

    inter_forward(shape, index, xs, gi, gr, 0, vectors, proj, h_out, c_out, (wc, pg), use)


EDGE = (HOP + 1) * M
EDGE_TOP = 208


def edge_pack(value):
    rest = jnp.concatenate([value[EDGE_TOP:], jnp.zeros((2 * EDGE_TOP - EDGE, B), F32)], 0)
    return jnp.concatenate([value[:EDGE_TOP], rest], 1)


def edge_unpack(ref):
    return jnp.concatenate([ref[:, :B], ref[: EDGE - EDGE_TOP, B:]], 0)


def parts_of(res, part):
    half = HOP * M
    part[:half] = res[0, :half]
    for c in range(1, TILES):
        part[c * half : (c + 1) * half] = res[c, :half] + res[c - 1, half : 2 * half]
    part[TILES * half :] = res[TILES - 1, half : 2 * half]


def part_kernel(nb, RI, res_in, back, lengths, part, up, down, res):
    res[...] = res_in[...]
    add_tiles(res, back, nb, RI, limits(lengths))
    parts_of(res, part)
    half = HOP * M
    up[...] = edge_pack(part[TILES * half - M :])
    down[...] = edge_pack(part[: half + M])


def middle_kernel(nb, RI, part, before, after, lengths, win, goal, following, proj, vectors, send, gres, genc, gm, *scratch):
    edge = jnp.where(lax.axis_index("block") > 0, 1.0, 0.0)
    middle(
        part, edge_unpack(before), edge_unpack(after), limits(lengths), edge, win, goal,
        following.at[1], proj, vectors, gres, genc, gm, *scratch,
    )
    send_tiles(gres, send, nb, RI)


def middle(part, early, late, lim, edge, win, goal, following, proj, vectors, gres, genc, gm, feats, dec, tgt, gest, enc, gate, src, act):
    half = HOP * M
    top = M + TILES * half
    total = BLOCKS * M
    feats[:M] = early[:M]
    feats[M : M + half] = part[:half] + early[M:]
    feats[M + half : top] = part[half : TILES * half]
    feats[top : top + half] = part[TILES * half :] + late[:half]
    feats[top + half : top + half + M] = late[half:]
    feats[top + half + M :] = jnp.zeros((PADDED * M - top - half - M, B), F32)
    low_mask = proj[:, BASE + N : BASE + N + B].astype(BF)
    w_enc = proj[:, BASE + N + B : BASE + N + B + 2 * STRIDE].astype(BF)
    low_dec = proj[:, BASE + N + B + 2 * STRIDE : BASE + N + B + 4 * STRIDE].astype(BF)
    m_bias = pieces(vectors, vectors.shape[0] * 2 - 1, 1)
    root = 0.7978845608028654
    cube = 0.044715
    dec[total:] = jnp.zeros((PADDED * M - total, 2 * STRIDE), F32)
    for i in range(total // CHUNK):
        rows = slice(i * CHUNK, (i + 1) * CHUNK)
        x = feats[rows]
        low = (0.5 * x * (1.0 + jnp.tanh(root * (x + cube * x * x * x)))).astype(BF)
        encoded = softplus(dot_turned(win[rows], w_enc))
        mask = 0.5 * jnp.tanh(0.5 * (dot_turned(low, low_mask) + m_bias)) + 0.5
        source = (mask * encoded).astype(BF)
        enc[rows] = encoded
        gate[rows] = mask
        src[rows] = source.astype(F32)
        act[rows] = low.astype(F32)
        dec[rows] = dot(source, low_dec)
    dec[:M] = dec[:M] * edge
    for ref in (enc, gate, src, act):
        ref[total:] = jnp.zeros((PADDED * M - total, B), F32)
    for i in range(1, FRAMES + 1):
        tgt[i * M : (i + 1) * M] = goal[:, STRIDE * (i - 1) : STRIDE * i]
    for i in range(FRAMES + 1, FRAMES + HOP + 2):
        at = STRIDE * (i - 1 - FRAMES)
        tgt[i * M : (i + 1) * M] = following[:, at : at + STRIDE]
    tgt[(FRAMES + HOP + 2) * M :] = jnp.zeros(((PADDED - FRAMES - HOP - 2) * M, STRIDE), F32)
    estimate = dec[M:total, :STRIDE] + dec[: total - M, STRIDE:]
    count = BLOCKS - 1
    spot = lax.broadcasted_iota(jnp.int32, (count, M, STRIDE), 0)
    phase = lax.broadcasted_iota(jnp.int32, (count, M, STRIDE), 2)
    near = spot < FRAMES + HOP + 1
    valid = jnp.where(near & (spot * STRIDE + phase < lim[:, :STRIDE][None]), 1.0, 0.0)
    inside = jnp.where(spot < FRAMES, valid, 0.0).reshape(count * M, STRIDE)
    valid = valid.reshape(count * M, STRIDE)
    error = estimate - tgt[M:total]
    smoothed = jnp.sqrt(error * error + 1.0)
    gest[:M] = jnp.zeros((M, STRIDE), F32)
    gest[M:total] = valid * error / smoothed
    gest[total:] = jnp.zeros((PADDED * M - total, STRIDE), F32)
    loss = jnp.sum(jnp.sum(inside * (smoothed - 1.0), 0, keepdims=True), 1, keepdims=True)
    seen = jnp.sum(jnp.sum(inside, 0, keepdims=True), 1, keepdims=True)
    gm[...] = jnp.zeros_like(gm)
    gm[132:133] = jnp.broadcast_to(loss, (1, LANES))
    gm[133:134] = jnp.broadcast_to(seen, (1, LANES))
    for i in range(total // CHUNK):
        at = i * CHUNK + M
        rows = slice(at, at + CHUNK)
        grad_dec = jnp.concatenate([gest[rows], gest[at + M : at + M + CHUNK]], 1).astype(BF)
        mine = own(i * (CHUNK // M), CHUNK // M)
        mine_low = mine.astype(BF)
        gm[64:128, 16:32] += dot_rows(src[rows].astype(BF) * mine_low, grad_dec)
        grad_source = dot_turned(grad_dec, low_dec)
        mask = gate[rows]
        grad_logit = (grad_source * enc[rows] * mask * (1.0 - mask)).astype(BF)
        enc[rows] = grad_source * mask
        gm[:64, 64:] += dot_rows(grad_logit * mine_low, act[rows].astype(BF))
        gm[131:132, :B] += jnp.sum(grad_logit.astype(F32) * mine, 0, keepdims=True)
        x = feats[rows]
        curve = jnp.tanh(root * (x + cube * x * x * x))
        slope = 0.5 * (1.0 + curve) + (0.5 * root) * x * (1.0 - curve * curve) * (
            1.0 + (3.0 * cube) * x * x
        )
        feats[rows] = slope * dot(grad_logit, low_mask)
    genc[...] = enc[M : M + FRAMES * M]
    for c in range(TILES):
        gres[c, : K * M] = feats[M + c * half : M + c * half + K * M] * live(lim, c * HOP, K)
        zero_tail(gres, c)


def inter_back(shape, index, gs, xs, h_ref, c_ref, proj, vectors, gi, gr, slot, out, core, use):
    n = shape.crows
    last = branch_back(
        shape,
        lambda g, r0: gs[pl.ds(r0, n), :],
        lambda g, r0: xs[pl.ds(r0, n), :],
        h_ref, c_ref, (gi, gr), slot, branch_vectors(vectors, index), turned_out(proj, index), out, core,
    )
    last(use)


def inter_back_kernel(shape, RI, index, grad_rows, rows, h_ref, c_ref, proj, vectors, gi, gr, send, out, *scratch):
    xs, gs, core = scratch[0], scratch[1], scratch[2:]
    unpack_steps(rows, xs, shape.steps, RI)
    unpack_steps(grad_rows, gs, shape.steps, RI)
    RP = send.shape[1]

    def use(g, i, r0, total):
        for j in range(shape.chunk):
            send[i * shape.chunk + j] = packed(total[j * RI : (j + 1) * RI], RP)

    inter_back(shape, index, gs, xs, h_ref, c_ref, proj, vectors, gi, gr, 0, out, core, use)


def intra_back(shape, index, gres, x_ref, h_ref, c_ref, proj, vectors, gi, gr, slot, out, core):
    n = shape.crows

    def inputs(g, r0):
        return x_ref[pl.ds(pl.multiple_of(g * shape.size + r0, 16), n), :]

    last = branch_back(
        shape,
        lambda g, r0: gres[g, pl.ds(r0, n), :],
        inputs,
        h_ref, c_ref, (gi, gr), slot, branch_vectors(vectors, index), turned_out(proj, index), out, core,
    )

    def use(g, i, r0, total):
        gres[g, pl.ds(r0, n), :] = gres[g, pl.ds(r0, n), :] + total

    last(use)


def third_back_kernel(shape, nb, RI, gres_in, back, lengths, x_ref, h_ref, c_ref, proj, vectors, gi, gr, gres, send, out, *core):
    lim = limits(lengths)
    gres[...] = gres_in[...]
    add_tiles(gres, back, nb, RI, lim)
    intra_back(shape, 2, gres, x_ref, h_ref, c_ref, proj, vectors, gi, gr, 0, out, core)
    for c in range(TILES):
        gres[c, : K * M] = gres[c, : K * M] * live(lim, c * HOP, K)
    send_tiles(gres, send, nb, RI)


def first_back_kernel(shape, nb, RI, gres_in, back, lengths, x_ref, h_ref, c_ref, proj, vectors, gi, gr, win, genc, gm_in, out, gres, bottle, *core):
    lim = limits(lengths)
    gres[...] = gres_in[...]
    add_tiles(gres, back, nb, RI, lim)
    intra_back(shape, 0, gres, x_ref, h_ref, c_ref, proj, vectors, gi, gr, 0, out, core)
    encode_back(gres, lim, proj, vectors, win, genc, gm_in, out, bottle)


def encode_back(gres, lim, proj, vectors, win, genc, gm_in, out, bottle):
    gm = ROWS_G
    out[gm : gm + gm_in.shape[0]] = gm_in[...]
    bottle[...] = jnp.zeros_like(bottle)
    for c in range(TILES):
        at = (c * HOP + 1) * M
        bottle[at : at + K * M] += gres[c, : K * M]
    w_enc = proj[:, BASE + N + B : BASE + N + B + 2 * STRIDE].astype(BF)
    w_bn = proj[:, BASE : BASE + N].astype(BF)
    gain, beta = (pieces(vectors, j, 1) for j in range(2))
    own_rows = FRAMES * M
    for i in range(BLOCKS * M // CHUNK):
        at = i * CHUNK
        rows = slice(at, at + CHUNK)
        pre = dot_turned(win[rows], w_enc)
        unit, scale = norm_parts(softplus(pre))
        normed = (unit * gain + beta).astype(BF)
        low = (bottle[rows] * live(lim, i * (CHUNK // M) - 1, CHUNK // M)).astype(BF)
        out[gm : gm + 64, :N] += dot_rows(low, normed)
        grad_normed = dot(low, w_bn)
        for j, value in enumerate((grad_normed * unit, grad_normed, low.astype(F32))):
            out[gm + 128 + j : gm + 129 + j, :B] += jnp.sum(value, 0, keepdims=True)
        grad_enc = norm_back(grad_normed, unit, scale, gain)
        lo, hi = max(at - M, 0), min(at + CHUNK - M, own_rows)
        if lo < hi:
            piece = genc[lo:hi]
            above, below = lo + M - at, at + CHUNK - M - hi
            if above:
                piece = jnp.concatenate([jnp.zeros((above, B), F32), piece], 0)
            if below:
                piece = jnp.concatenate([piece, jnp.zeros((below, B), F32)], 0)
            grad_enc = grad_enc + piece
        grad_pre = (grad_enc * (0.5 * jnp.tanh(0.5 * pre) + 0.5)).astype(BF)
        out[gm + 64 : gm + 128, :16] += dot_rows(grad_pre, win[rows])


def turn_in(res, xs, RI, lowered=True):
    for j in range(M):
        for c in range(TILES):
            at = (TILES * j + c) * RI
            value = res[c, pl.ds(j, K, stride=M), :]
            xs[at : at + K] = value.astype(BF).astype(F32)


def turn_back(res, xs, RI, length):
    pos = lax.broadcasted_iota(jnp.int32, (K, B), 0)
    for j in range(M):
        for c in range(TILES):
            at = (TILES * j + c) * RI
            mask = jnp.where((pos + (FRAMES * j + HOP * c)) * STRIDE < length, 1.0, 0.0)
            where = (c, pl.ds(j, K, stride=M), slice(None))
            res[where] = (res[where] + xs[at : at + K]) * mask


def local_kernel(intra, inter, RI, waves, lengths, proj, vectors, gi, gr, out0, out1, out2, out3, *scratch):
    (win, flat, bottle, res, nrm, part, genc, gm, feats, dec, tgt, gest, enc, gate, src, act) = scratch[:16]
    x0, h0, c0, x1, h1, c1, x2, h2, c2, x3, h3, c3 = scratch[16:28]
    wc, wit, wrt, wot, z, dh = scratch[28:]
    core = (wc, wit, wrt, wot, z, dh)
    length = lengths[lax.axis_index("block")]
    lim = length - lax.broadcasted_iota(jnp.int32, (M, B), 0) * (FRAMES * STRIDE)
    reach = (HOP + 2) * STRIDE
    span = FRAMES * STRIDE
    goal_at = waves.shape[1] // 2
    mix = waves[:, :span]
    goal = waves[:, goal_at : goal_at + span]

    def after(value):
        return jnp.concatenate([value[1:], jnp.zeros((1, value.shape[1]), F32)], 0)

    def before(value):
        return jnp.concatenate([jnp.zeros((1, value.shape[1]), F32), value[:-1]], 0)

    for ref in (x1, x3, nrm):
        ref[...] = jnp.zeros_like(ref)
    encode(mix, after(mix[:, :reach]), before(mix[:, span - STRIDE :]), lim, proj, vectors, win, flat, bottle, res)

    def inter_layer(index, xs, h, c):
        turn_in(res, xs, RI)

        def use(i, r0, value):
            nrm[pl.ds(r0, inter.crows), :] = value.astype(BF).astype(F32)

        inter_forward(inter, index, xs, gi, gr, index, vectors, proj, h, c, (wc, z), use)
        turn_back(res, nrm, RI, length)

    intra_forward(intra, 0, res, lim, gi, gr, 0, vectors, proj, x0, h0, c0, (wc, z))
    inter_layer(1, x1, h1, c1)
    intra_forward(intra, 2, res, lim, gi, gr, 2, vectors, proj, x2, h2, c2, (wc, z))
    inter_layer(3, x3, h3, c3)

    parts_of(res, part)
    half = HOP * M
    row = lax.broadcasted_iota(jnp.int32, (EDGE, B), 0) % M
    early = jnp.where(row == 0, 0.0, before(part[TILES * half - M :]))
    late = jnp.where(row == M - 1, 0.0, after(part[: half + M]))
    edge = jnp.where(lax.broadcasted_iota(jnp.int32, (M, 2 * STRIDE), 0) == 0, 0.0, 1.0)
    middle(
        part, early, late, lim, edge, win, goal, after(goal[:, :reach]), proj, vectors, res, genc, gm,
        feats, dec, tgt, gest, enc, gate, src, act,
    )

    def inter_layer_back(index, xs, h, c, out):
        for j in range(M):
            for t in range(TILES):
                at = (TILES * j + t) * RI
                nrm[at + K : at + RI] = jnp.zeros((RI - K, B), F32)
        turn_in(res, nrm, RI)

        def use(g, i, r0, total):
            nrm[pl.ds(r0, inter.crows), :] = total.astype(BF).astype(F32)

        inter_back(inter, index, nrm, xs, h, c, proj, vectors, gi, gr, index, out, core, use)
        turn_back(res, nrm, RI, length)

    inter_layer_back(3, x3, h3, c3, out3)
    intra_back(intra, 2, res, x2, h2, c2, proj, vectors, gi, gr, 2, out2, core)
    for c in range(TILES):
        res[c, : K * M] = res[c, : K * M] * live(lim, c * HOP, K)
    inter_layer_back(1, x1, h1, c1, out1)
    intra_back(intra, 0, res, x0, h0, c0, proj, vectors, gi, gr, 0, out0, core)
    encode_back(res, lim, proj, vectors, win, genc, gm, out0, bottle)


def local_scratch(intra, inter):
    tall = PADDED * M
    narrow = [pltpu.VMEM((tall, 2 * STRIDE), F32)] + [pltpu.VMEM((tall, STRIDE), F32)] * 2
    first = [
        pltpu.VMEM((BLOCKS * M, 2 * STRIDE), BF),
        pltpu.VMEM((BLOCKS * M, 2 * STRIDE), F32),
        pltpu.VMEM((BLOCKS * M, B), F32),
        pltpu.VMEM((TILES, K * M, B), F32),
        pltpu.VMEM((inter.size, B), F32),
        pltpu.VMEM(((FRAMES + HOP) * M, B), F32),
        pltpu.VMEM((FRAMES * M, B), F32),
        pltpu.VMEM((136, LANES), F32),
        pltpu.VMEM((tall, B), F32),
        *narrow,
    ] + [pltpu.VMEM((tall, B), F32)] * 4
    kept = []
    for shape, kind in ((intra, BF), (inter, F32)) * 2:
        state = pltpu.VMEM((shape.groups * shape.wide, 2 * H), F32)
        kept += [pltpu.VMEM((shape.groups * shape.size, B), kind), state, state]
    return first + kept + back_scratch(inter)


def adam_parts(grad, moment, square, weight, average, decay):
    moment = BETA_ONE * moment + (1.0 - BETA_ONE) * grad
    square = BETA_TWO * square + (1.0 - BETA_TWO) * grad * grad
    corrected = moment * (1.0 / (1.0 - BETA_ONE**STEP))
    scaled = square * (1.0 / (1.0 - BETA_TWO**STEP))
    weight = weight - RATE * (corrected / (jnp.sqrt(scaled) + ADAM_EPS) + decay * weight)
    average = KEEP * average + (1.0 - KEEP) * weight
    return moment, square, weight, average, weight.astype(BF)


def adam_kernel(*refs):
    gs, old = refs[:4], refs[4:20]
    scalars, new = refs[20], refs[21:41]
    gv = refs[41]
    first = gs[0]
    gm = ROWS_G
    gv[:1] = jnp.concatenate([first[gm + 128 : gm + 129, :N], first[gm + 129 : gm + 130, :N]], 1)
    gv[1:2, :N] = first[gm + 130 : gm + 131, :N]
    gv[gv.shape[0] - 1 :, N:] = first[gm + 131 : gm + 132, :N]
    for r in range(4):
        at = 3 + 19 * r
        for j in range(8):
            row = gs[r][ROWS_VECS + j : ROWS_VECS + j + 1]
            for k in range(2):
                q = at + 2 * j + k
                gv[q // 2 : q // 2 + 1, (q % 2) * N : (q % 2 + 1) * N] = row[:, k * N : (k + 1) * N]
        for j in range(3):
            q = at + 16 + j
            gv[q // 2 : q // 2 + 1, (q % 2) * N : (q % 2 + 1) * N] = gs[r][ROWS_VECS + 8 + j : ROWS_VECS + 9 + j, :N]
    part = jnp.zeros((8, LANES), F32)
    for r in range(4):
        value = gs[r][:ROWS_VECS].reshape(ROWS_VECS // 8, 8, LANES)
        part = part + jnp.sum(value * value, 0)
    value = first[gm : gm + 128].reshape(16, 8, LANES)
    part = part + jnp.sum(value * value, 0)
    value = gv[...].reshape(5, 8, LANES)
    part = part + jnp.sum(value * value, 0)
    squared = jnp.sum(jnp.sum(part, 0, keepdims=True), 1, keepdims=True)
    loss, count = first[gm + 132 : gm + 133, :1], first[gm + 133 : gm + 134, :1]
    norm = jnp.sqrt(squared) / count
    factor = jnp.minimum(1.0, CLIP / norm) / count
    row = lax.broadcasted_iota(jnp.int32, (8, LANES), 0)
    scalars[...] = jnp.where(row == 0, loss, jnp.where(row == 1, count, norm))

    def update(kind, index, grad, decay):
        results = adam_parts(
            grad * factor,
            old[4 + kind][index],
            old[8 + kind][index],
            old[kind][index],
            old[12 + kind][index],
            decay,
        )
        for j, value in enumerate(results):
            new[4 * j + kind][index] = value

    for r in range(4):
        for d in range(2):
            for j in range(4):
                lanes = slice(j * LANES, (j + 1) * LANES)
                at = j * 384 + d * B
                update(0, (r, d, slice(None), lanes), gs[r][at : at + B], DECAY)
                at = j * 384 + 128 + d * H
                update(1, (r, d, slice(None), lanes), gs[r][at : at + H], DECAY)
        for j in range(2):
            at = ROWS_MAPS + j * B
            lanes = slice(r * 2 * H + j * LANES, r * 2 * H + (j + 1) * LANES)
            update(2, (slice(None), lanes), gs[r][at : at + B], DECAY)
    update(2, (slice(None), slice(BASE, BASE + LANES)), first[gm : gm + 64], DECAY)
    update(2, (slice(None), slice(BASE + LANES, BASE + LANES + 32)), first[gm + 64 : gm + 128, :32], DECAY)
    update(3, (slice(None), slice(None)), gv[...], 0.0)


def call(kernel, outs, ins, scratch, index=None, limit=56, micros=20):
    vmem = pl.BlockSpec(memory_space=pltpu.VMEM)
    specs = [
        pl.BlockSpec(memory_space=pltpu.SMEM) if a.ndim == 1 and a.dtype == jnp.int32 else vmem
        for a in ins
    ]
    extra = []
    wrapped = kernel
    if index is not None:
        big = [i for i, a in enumerate(ins) if a.ndim == 4 and a.shape[:2] == (2 * LAYERS, 2)]
        for i in big:
            specs[i] = pl.BlockSpec(memory_space=pl.ANY)
        extra = [pltpu.VMEM((1,) + ins[i].shape[1:], F32) for i in big]
        extra.append(pltpu.SemaphoreType.DMA((len(big),)))

        def wrapped(*refs):
            refs = list(refs)
            held, sem = refs[len(refs) - len(extra) : -1], refs[-1]
            copies = []
            for j, i in enumerate(big):
                copies.append(pltpu.make_async_copy(refs[i].at[pl.ds(index, 1)], held[j], sem.at[j]))
                copies[-1].start()
            for copy in copies:
                copy.wait()
            for j, i in enumerate(big):
                refs[i] = held[j]
            kernel(*refs[: len(refs) - len(extra)])

    return pl.pallas_call(
        wrapped,
        out_shape=outs,
        in_specs=specs,
        out_specs=[vmem] * len(outs),
        scratch_shapes=list(scratch) + extra,
        compiler_params=pltpu.CompilerParams(vmem_limit_bytes=limit * 1024 * 1024),
        cost_estimate=pl.CostEstimate(
            flops=micros * 10**9, bytes_accessed=micros * 10**6, transcendentals=0
        ),
    )(*ins)


def shift(block, axis, distance):
    size = lax.axis_size(axis)
    route = [(i, i + distance) for i in range(size) if 0 <= i + distance < size]
    return lax.ppermute(block, axis, route)


def exchange(block):
    return lax.all_to_all(block, "block", split_axis=0, concat_axis=0, tiled=True)


def flip(block, bit):
    size = lax.axis_size("dp")
    return lax.ppermute(block, "dp", [(i, i ^ (1 << bit)) for i in range(size)])


def bits():
    return lax.axis_size("dp").bit_length() - 1


def halve(block):
    for bit in range(bits()):
        half = block.shape[0] // 2
        mine = (lax.axis_index("dp") >> bit) & 1
        given = lax.dynamic_slice_in_dim(block, (1 - mine) * half, half, 0)
        block = lax.dynamic_slice_in_dim(block, mine * half, half, 0) + flip(given, bit)
    return block


def double(block):
    for bit in reversed(range(bits())):
        mine = (lax.axis_index("dp") >> bit) & 1
        other = flip(block, bit)
        block = jnp.where(
            mine == 0, jnp.concatenate([block, other], 0), jnp.concatenate([other, block], 0)
        )
    return block


def scatter_sum(block):
    nb = lax.axis_size("block")
    block = halve(block)
    rows = block.shape[0]
    part = -(-rows // (8 * nb)) * 8
    if part * nb > rows:
        block = jnp.concatenate([block, jnp.zeros((part * nb - rows, LANES), F32)], 0)
    return jnp.sum(exchange(block.reshape(nb, part, LANES)), 0)


def gather_sums(parts, sizes):
    nb, dp = lax.axis_size("block"), lax.axis_size("dp")
    mine = jnp.concatenate(parts, 0)
    all_parts = exchange(jnp.broadcast_to(mine[None], (nb,) + mine.shape))
    given, at = [], 0
    for part, size in zip(parts, sizes):
        rows = part.shape[0]
        block = all_parts[:, at : at + rows].reshape(nb * rows, LANES)
        given.append(double(block[: size // dp]))
        at += rows
    return given


def shared_step(mixture, target, lengths, proj, vectors_wide, gi, gr):
    nb = lax.axis_size("block")
    RI = -(-K // nb) * M
    intra = Shape(TILES, K, M)
    inter = Shape(1, TILES * nb, RI)
    T = inter.steps
    reach = (HOP + 2) * STRIDE
    following = shift(jnp.stack([mixture[:, :reach], target[:, :reach]]), "block", -1)
    leading = shift(mixture[:, -STRIDE:], "block", 1)

    RP = -(-RI // 16) * 8
    res_shape = SDS((TILES, nb * RI, B), F32)
    send_shape = SDS((nb, TILES, RP, 2 * B), BF)
    steps_shape = SDS((T, RP, 2 * B), BF)
    x_shape = SDS((TILES * K * M, B), BF)

    def state(shape):
        return SDS((shape.groups * shape.wide, 2 * H), F32)

    res0, send, x0, h0, c0, win = call(
        functools.partial(first_kernel, intra, nb, RI),
        [res_shape, send_shape, x_shape, state(intra), state(intra), SDS((BLOCKS * M, 2 * STRIDE), BF)],
        [mixture, following, leading, lengths, proj, vectors_wide, gi, gr],
        fwd_scratch(intra)
        + [pltpu.VMEM((BLOCKS * M, 2 * STRIDE), F32), pltpu.VMEM((BLOCKS * M, B), F32)],
        0,
    )

    def inter_step(send, index):
        rows = exchange(send).reshape(T, RP, 2 * B)
        normed, h, c = call(
            functools.partial(inter_kernel, inter, RI, index),
            [steps_shape, state(inter), state(inter)],
            [rows, proj, vectors_wide, gi, gr],
            fwd_scratch(inter) + [pltpu.VMEM((inter.size, B), F32)],
            index,
        )
        return rows, h, c, exchange(normed.reshape(send_shape.shape))

    rows1, h1, c1, back = inter_step(send, 1)
    res2, send, x2, h2, c2 = call(
        functools.partial(third_kernel, intra, nb, RI),
        [res_shape, send_shape, x_shape, state(intra), state(intra)],
        [res0, back, lengths, proj, vectors_wide, gi, gr],
        fwd_scratch(intra),
        2,
    )
    rows3, h3, c3, back = inter_step(send, 3)
    edge_shape = SDS((EDGE_TOP, 2 * B), F32)
    part, up, down = call(
        functools.partial(part_kernel, nb, RI),
        [SDS(((FRAMES + HOP) * M, B), F32), edge_shape, edge_shape],
        [res2, back, lengths],
        [pltpu.VMEM(res_shape.shape, F32)],
    )
    before = shift(up, "block", 1)
    after = shift(down, "block", -1)
    tall = PADDED * M
    send, gres, genc, gm = call(
        functools.partial(middle_kernel, nb, RI),
        [send_shape, res_shape, SDS((FRAMES * M, B), F32), SDS((136, LANES), F32)],
        [part, before, after, lengths, win, target, following, proj, vectors_wide],
        [
            pltpu.VMEM((tall, B), F32),
            pltpu.VMEM((tall, 2 * STRIDE), F32),
            pltpu.VMEM((tall, STRIDE), F32),
            pltpu.VMEM((tall, STRIDE), F32),
            pltpu.VMEM((tall, B), F32),
            pltpu.VMEM((tall, B), F32),
            pltpu.VMEM((tall, B), F32),
            pltpu.VMEM((tall, B), F32),
        ],
    )
    out_shape = SDS((ROWS_G, LANES), F32)

    def inter_back(send, rows, h, c, index):
        grad_rows = exchange(send).reshape(T, RP, 2 * B)
        send, out = call(
            functools.partial(inter_back_kernel, inter, RI, index),
            [steps_shape, out_shape],
            [grad_rows, rows, h, c, proj, vectors_wide, gi, gr],
            [pltpu.VMEM((inter.size, B), F32)] * 2 + back_scratch(inter),
            index,
        )
        return exchange(send.reshape(send_shape.shape)), out

    back, out3 = inter_back(send, rows3, h3, c3, 3)
    gres, send, out2 = call(
        functools.partial(third_back_kernel, intra, nb, RI),
        [res_shape, send_shape, out_shape],
        [gres, back, lengths, x2, h2, c2, proj, vectors_wide, gi, gr],
        back_scratch(intra),
        2,
    )
    back, out1 = inter_back(send, rows1, h1, c1, 1)
    (out0,) = call(
        functools.partial(first_back_kernel, intra, nb, RI),
        [SDS((ROWS_FIRST, LANES), F32)],
        [gres, back, lengths, x0, h0, c0, proj, vectors_wide, gi, gr, win, genc, gm],
        [pltpu.VMEM(res_shape.shape, F32), pltpu.VMEM((BLOCKS * M, B), F32)] + back_scratch(intra),
        0,
    )
    return out0, out1, out2, out3


def local_step(mixture, target, lengths, proj, vectors_wide, gi, gr):
    RI = -(-K // M) * M
    intra = Shape(TILES, K, M)
    inter = Shape(1, TILES * M, RI)
    pad = jnp.zeros((M, -(FRAMES * STRIDE) % LANES), F32)
    waves = jnp.concatenate([mixture, pad, target, pad], 1)
    waves = lax.all_to_all(waves.reshape(M, 1, -1), "block", split_axis=0, concat_axis=0, tiled=True)
    out_shape = SDS((ROWS_G, LANES), F32)
    return call(
        functools.partial(local_kernel, intra, inter, RI),
        [SDS((ROWS_FIRST, LANES), F32)] + [out_shape] * 3,
        [waves.reshape(M, -1), lengths, proj, vectors_wide, gi, gr],
        local_scratch(intra, inter),
        limit=62,
    )


def body(
    mixture,
    target,
    lengths,
    input_gates,
    recur_gates,
    projections,
    vectors,
    moment_input,
    moment_recur,
    moment_proj,
    moment_vecs,
    square_input,
    square_recur,
    square_proj,
    square_vecs,
    average_input,
    average_recur,
    average_proj,
    average_vecs,
):
    nb = lax.axis_size("block")
    proj = projections.T
    vectors_wide = vectors.reshape(-1, LANES)
    step = local_step if nb == M else shared_step
    out0, out1, out2, out3 = step(
        mixture, target, lengths, proj, vectors_wide, input_gates, recur_gates
    )
    sums = gather_sums([scatter_sum(out0), scatter_sum(out1)], [ROWS_FIRST, ROWS_G])
    sums += gather_sums([scatter_sum(out2), scatter_sum(out3)], [ROWS_G, ROWS_G])
    old = [
        input_gates, recur_gates, projections, vectors,
        moment_input, moment_recur, moment_proj, moment_vecs,
        square_input, square_recur, square_proj, square_vecs,
        average_input, average_recur, average_proj, average_vecs,
    ]
    for i in range(2, 16, 4):
        old[i] = old[i].T
    for i in range(3, 16, 4):
        old[i] = old[i].reshape(-1, LANES)
    new = [SDS(a.shape, F32) for a in old[:4]] * 4 + [SDS(a.shape, BF) for a in old[:4]]
    scalars, *new = call(
        adam_kernel,
        [SDS((8, LANES), F32)] + new,
        sums + old,
        [pltpu.VMEM(old[3].shape, F32)],
    )
    for i in range(2, 20, 4):
        new[i] = new[i].T
    for i in range(3, 20, 4):
        new[i] = new[i].reshape(-1)
    return (scalars[0, 0], scalars[1, 0], scalars[2, 0], *new)


def solution(mesh):
    in_specs = (P("dp", "block"), P("dp", "block"), P("dp")) + (P(),) * 16
    return jax.shard_map(
        body, mesh=mesh, in_specs=in_specs, out_specs=(P(),) * 23, check_vma=False
    )
```

```python
import functools

import jax
import jax.numpy as jnp
from jax import lax
from jax.experimental import pallas as pl
from jax.experimental.pallas import tpu as pltpu
from jax.sharding import PartitionSpec as P

N = 64
B = 64
H = 128
K = 100
STRIDE = 8
LAYERS = 2
STEP = 10
HOP = 50
TILES = 3
M = 8
FRAMES = 150
BASE = 4 * LAYERS * H
PERIOD = 8 * H + 3 * B
ROWS_MAPS = 1536
ROWS_VECS = 1664
ROWS_MORE = 1680
ROWS_G = 1792
LANES = 128
BLOCKS = 208
PADDED = 216
CHUNK = 416

EPS_NORM = 1e-05
CLIP = 0.001
RATE = 0.1
BETA_ONE = 0.9
BETA_TWO = 0.999
ADAM_EPS = 1e-08
DECAY = 0.01
KEEP = 0.9

BF = jnp.bfloat16
F32 = jnp.float32
TOP = 13.0
NOTES = 16
HALF = jnp.float16
SDS = jax.ShapeDtypeStruct


def dot(left, right):
    return jnp.dot(left, right, preferred_element_type=F32)


def dot_turned(left, right):
    return lax.dot_general(left, right, (((1,), (1,)), ((), ())), preferred_element_type=F32)


def dot_rows(left, right):
    return lax.dot_general(left, right, (((0,), (0,)), ((), ())), preferred_element_type=F32)


def half_scale():
    lane = lax.broadcasted_iota(jnp.int32, (1, 4 * H), 1)
    return jnp.where((lane >= 2 * H) & (lane < 3 * H), 1.0, 0.5)


def gate_acts(z):
    act = jnp.tanh(z)
    sig_i = 0.5 * act[:, :H] + 0.5
    sig_f = 0.5 * act[:, H : 2 * H] + 0.5
    sig_o = 0.5 * act[:, 3 * H :] + 0.5
    return sig_i, sig_f, act[:, 2 * H : 3 * H], sig_o


def norm_parts(value):
    center = value - jnp.mean(value, -1, keepdims=True)
    spread = jnp.mean(center * center, -1, keepdims=True)
    scale = lax.rsqrt(spread + EPS_NORM)
    return center * scale, scale


def norm_back(grad, unit, scale, gain):
    inner = grad * gain
    return scale * (
        inner
        - jnp.mean(inner, -1, keepdims=True)
        - unit * jnp.mean(inner * unit, -1, keepdims=True)
    )


def live(lim, start, count):
    pos = lax.broadcasted_iota(jnp.int32, (count, M, B), 0) + start
    return jnp.where(pos * STRIDE < lim[None], 1.0, 0.0).reshape(count * M, B)


def limits(lengths):
    row = lax.broadcasted_iota(jnp.int32, (M, B), 0)
    total = jnp.zeros((M, B), jnp.int32)
    for m in range(M):
        total = jnp.where(row == m, lengths[m], total)
    return total - lax.axis_index("block") * (FRAMES * STRIDE)


def pieces(vectors, start, count):
    parts = []
    at = start
    while at < start + count:
        wide = at % 2 == 0 and at + 2 <= start + count
        lane = (at % 2) * N
        parts.append(vectors[at // 2 : at // 2 + 1, lane : lane + (2 * N if wide else N)])
        at += 2 if wide else 1
    return parts[0] if len(parts) == 1 else jnp.concatenate(parts, 1)


def branch_vectors(vectors, index):
    first = (2 * N + B + index * PERIOD) // N
    half = half_scale()
    bias = [pieces(vectors, first + 8 * d, 8) * half for d in range(2)]
    return bias, [pieces(vectors, first + 16 + j, 1) for j in range(3)]


def own(start, count):
    pos = lax.broadcasted_iota(jnp.int32, (count, M, B), 0) + start
    return jnp.where(pos < FRAMES, 1.0, 0.0).reshape(count * M, B)


def chunk_of(steps, rows):
    best = 1
    for size in range(1, steps + 1):
        if steps % size == 0 and size * rows <= 512 and size * rows % 16 == 0:
            best = size
    return best


class Shape:
    def __init__(self, groups, steps, rows):
        self.groups, self.steps, self.rows = groups, steps, rows
        self.size = steps * rows
        self.chunk = chunk_of(steps, rows)
        self.crows = self.chunk * rows
        self.chunks = steps // self.chunk
        self.wide = (steps + 2) * rows
        self.unroll = 4 if steps % 4 == 0 else 1


def chunk_loop(shape, fn):
    for g in range(shape.groups):

        def step(i, _, g=g):
            fn(g, i, pl.multiple_of(i * shape.crows, 8))
            return 0

        lax.fori_loop(0, shape.chunks, step, 0)


def forward_weights(gi, gr, index, wc):
    half = half_scale()
    for d in range(2):
        wc[d, :H] = (gr[index, d].astype(BF).astype(F32) * half).astype(BF)
        wc[d, H:] = (gi[index, d].astype(BF).astype(F32) * half).astype(BF)


def lstm_scan(shape, pg, wc, h_ref, c_ref):
    G, S, R = shape.groups, shape.steps, shape.rows
    pad = jnp.zeros((R, 2 * H), F32)
    for g in range(G):
        for ref in (h_ref, c_ref):
            ref[g * shape.wide : g * shape.wide + R] = pad
            ref[(g + 1) * shape.wide - R : (g + 1) * shape.wide] = pad

    def one(d, t, hidden, memory):
        at = pl.multiple_of(t * R, 8)
        pre = jnp.concatenate([pg[d, pl.ds(g * shape.size + at, R), :] for g in range(G)], 0)
        z = pre + dot(hidden, wc[d, :H])
        sig_i, sig_f, tan_g, sig_o = gate_acts(z)
        memory = sig_f * memory + sig_i * tan_g
        hidden = (sig_o * jnp.tanh(memory)).astype(BF)
        full = hidden.astype(F32)
        after = pl.multiple_of(t * R + R, 8)
        for g in range(G):
            to = pl.ds(g * shape.wide + after, R)
            h_ref[to, d * H : (d + 1) * H] = full[g * R : (g + 1) * R]
            c_ref[to, d * H : (d + 1) * H] = memory[g * R : (g + 1) * R]
        return hidden, memory

    def step(s, carry):
        hf, cf, hb, cb = carry
        hf, cf = one(0, s, hf, cf)
        hb, cb = one(1, S - 1 - s, hb, cb)
        return hf, cf, hb, cb

    zero = jnp.zeros((G * R, H), F32)
    start = (zero.astype(BF), zero, zero.astype(BF), zero)
    lax.fori_loop(0, S, step, start, unroll=shape.unroll)


def lstm_scan_back(shape, z, dh, c_ref, wrt):
    G, S, R = shape.groups, shape.steps, shape.rows

    def one(d, t, rec_hidden, rec_memory):
        def take(ref, at, width, lanes):
            at = pl.multiple_of(at, 8)
            return jnp.concatenate([ref[pl.ds(g * width + at, R), lanes] for g in range(G)], 0)

        lanes = slice(d * H, (d + 1) * H)
        at = pl.multiple_of(t * R, 8)
        zt = jnp.concatenate([z[d, pl.ds(g * shape.size + at, R), :] for g in range(G)], 0)
        sig_i, sig_f, tan_g, sig_o = gate_acts(zt)
        tan_c = jnp.tanh(take(c_ref, t * R + R, shape.wide, lanes))
        before = take(c_ref, t * R + 2 * R * d, shape.wide, lanes)
        grad_h = take(dh, t * R, shape.size, lanes) + rec_hidden
        grad_c = rec_memory + grad_h * (sig_o * (1.0 - tan_c * tan_c))
        grad_pre = jnp.concatenate(
            [
                grad_c * (tan_g * sig_i * (1.0 - sig_i)),
                grad_c * (before * sig_f * (1.0 - sig_f)),
                grad_c * (sig_i * (1.0 - tan_g * tan_g)),
                grad_h * (tan_c * sig_o * (1.0 - sig_o)),
            ],
            -1,
        ).astype(BF)
        full = grad_pre.astype(F32)
        for g in range(G):
            z[d, pl.ds(g * shape.size + at, R), :] = full[g * R : (g + 1) * R]
        return dot(grad_pre, wrt[d]), grad_c * sig_f

    def step(s, carry):
        hf, cf, hb, cb = carry
        hf, cf = one(0, S - 1 - s, hf, cf)
        hb, cb = one(1, s, hb, cb)
        return hf, cf, hb, cb

    zero = jnp.zeros((G * R, H), F32)
    lax.fori_loop(0, S, step, (zero,) * 4, unroll=shape.unroll)


def branch_pregates(shape, inputs, wc, bias, pg):
    def fill(g, i, r0):
        x = inputs(g, r0).astype(BF)
        for d in range(2):
            pg[d, pl.ds(g * shape.size + r0, shape.crows), :] = dot(x, wc[d, H:]) + bias[d]

    chunk_loop(shape, fill)


def branch_back(shape, grads, inputs, h_ref, c_ref, weights, index, vecs, turned_out, out, scratch):
    gi, gr = weights
    wc, wit, wrt, wot, z, dh = scratch
    n, R = shape.crows, shape.rows
    forward_weights(gi, gr, index, wc)
    for d in range(2):
        wit[d] = jnp.transpose(gi[index, d]).astype(BF)
        wrt[d] = jnp.transpose(gr[index, d]).astype(BF)
    wot[...] = turned_out.astype(BF)
    out[...] = jnp.zeros_like(out)
    bias, (o_bias, gain, _) = vecs

    def states(g, at, lanes):
        return h_ref[pl.ds(pl.multiple_of(g * shape.wide + at, 8), n), lanes].astype(BF)

    def earlier(g, r0, d):
        before = states(g, r0 + 2 * R * d, slice(d * H, (d + 1) * H))
        return jnp.concatenate([before, inputs(g, r0).astype(BF)], 1)

    def first(g, i, r0):
        now = states(g, r0 + R, slice(0, 2 * H))
        here = pl.ds(g * shape.size + r0, n)
        unit, scale = norm_parts(dot_turned(now, wot[...]) + o_bias)
        grad = grads(g, r0)
        low = norm_back(grad, unit, scale, gain).astype(BF)
        dh[here, :] = dot(low, wot[...])
        turned = dot_rows(low, now)
        for j in range(2):
            at = ROWS_MAPS + j * B
            out[at : at + B] += turned[:, j * LANES : (j + 1) * LANES]
        for j, value in enumerate((low.astype(F32), grad * unit, grad)):
            at = ROWS_VECS + 8 + j
            out[at : at + 1, :B] += jnp.sum(value, 0, keepdims=True)
        for d in range(2):
            z[d, here, :] = dot(earlier(g, r0, d), wc[d]) + bias[d]

    chunk_loop(shape, first)
    lstm_scan_back(shape, z, dh, c_ref, wrt)

    def last(use):
        def fn(g, i, r0):
            total = None
            for d in range(2):
                full = z[d, pl.ds(g * shape.size + r0, n), :]
                low = full.astype(BF)
                maps = dot_rows(earlier(g, r0, d), low)
                grad_bias = jnp.sum(full, 0, keepdims=True)
                for j in range(4):
                    lanes = slice(j * LANES, (j + 1) * LANES)
                    at = j * 384 + d * B
                    out[at : at + B] += maps[H:, lanes]
                    at = j * 384 + 128 + d * H
                    out[at : at + H] += maps[:H, lanes]
                    at = ROWS_VECS + 4 * d + j
                    out[at : at + 1] += grad_bias[:, lanes]
                part = dot(low, wit[d])
                total = part if total is None else total + part
            use(g, i, r0, total)

        chunk_loop(shape, fn)

    return last


def fwd_scratch(shape):
    return [
        pltpu.VMEM((2, H + B, 4 * H), BF),
        pltpu.VMEM((2, shape.groups * shape.size, 4 * H), F32),
    ]


def back_scratch(shape):
    return [
        pltpu.VMEM((2, H + B, 4 * H), BF),
        pltpu.VMEM((2, 4 * H, B), BF),
        pltpu.VMEM((2, 4 * H, H), BF),
        pltpu.VMEM((B, 2 * H), BF),
        pltpu.VMEM((2, shape.groups * shape.size, 4 * H), F32),
        pltpu.VMEM((shape.groups * shape.size, 2 * H), F32),
    ]


def packed(value, RP):
    rest = value[RP:]
    if rest.shape[0] < RP:
        rest = jnp.concatenate([rest, jnp.zeros((RP - rest.shape[0], B), F32)], 0)
    return jnp.concatenate([value[:RP], rest], 1).astype(BF)


def send_tiles(res, send, nb, RI):
    RP = send.shape[2]
    for d in range(nb):
        for c in range(TILES):
            send[d, c] = packed(res[c, d * RI : (d + 1) * RI], RP)


def add_tiles(res, back, nb, RI, lim):
    RP = back.shape[2]
    for d in range(nb):
        for c in range(TILES):
            both = back[d, c].astype(F32)
            for lo, hi, value in (
                (0, RP, both[:, :B]),
                (RP, RI, both[:, B:]),
            ):
                lo, hi = d * RI + lo, min(d * RI + hi, K * M)
                if lo >= hi:
                    continue
                mask = live(lim, c * HOP + lo // M, (hi - lo) // M)
                res[c, lo:hi] = (res[c, lo:hi] + value[: hi - lo]) * mask


def unpack_steps(rows, xs, T, RI):
    RP = rows.shape[1]

    def widen(t, _):
        both = rows[t].astype(F32)
        xs[pl.ds(pl.multiple_of(t * RI, 8), RP), :] = both[:, :B]
        if RI > RP:
            xs[pl.ds(pl.multiple_of(t * RI + RP, 8), RI - RP), :] = both[: RI - RP, B:]
        return 0

    lax.fori_loop(0, T, widen, 0, unroll=4 if T % 4 == 0 else 1)


def windows_of(mix, following, win):
    last = FRAMES + HOP + 1
    for i in range(1, BLOCKS):
        at = STRIDE * (i - 1)
        if at + 2 * STRIDE <= FRAMES * STRIDE:
            win[i * M : (i + 1) * M] = mix[:, at : at + 2 * STRIDE]
        elif at < FRAMES * STRIDE:
            win[i * M : (i + 1) * M] = jnp.concatenate([mix[:, at:], following[:, :STRIDE]], 1)
        elif i <= last:
            at -= FRAMES * STRIDE
            win[i * M : (i + 1) * M] = following[:, at : at + 2 * STRIDE]
        else:
            win[i * M :] = jnp.zeros(((BLOCKS - i) * M, 2 * STRIDE), F32)
            break


def softplus(value):
    return jnp.maximum(value, 0.0) + jnp.log1p(jnp.exp(-jnp.abs(value)))


def turned_out(proj, index):
    return proj[:, index * 2 * H : (index + 1) * 2 * H]


def intra_forward(shape, index, res, lim, gi, gr, slot, vectors, proj, x_out, h_out, c_out, scratch):
    wc, pg = scratch
    forward_weights(gi, gr, slot, wc)
    bias, (o_bias, gain, beta) = branch_vectors(vectors, index)
    n = shape.crows

    def keep(g, i, r0):
        to = pl.ds(pl.multiple_of(g * shape.size + r0, 16), n)
        x_out[to, :] = res[g, pl.ds(r0, n), :].astype(BF)

    chunk_loop(shape, keep)
    branch_pregates(shape, lambda g, r0: res[g, pl.ds(r0, n), :], wc, bias, pg)
    lstm_scan(shape, pg, wc, h_out, c_out)
    low_out = turned_out(proj, index).astype(BF)

    def close(g, i, r0):
        now = h_out[pl.ds(pl.multiple_of(g * shape.wide + r0 + shape.rows, 8), n), :].astype(BF)
        unit, _ = norm_parts(dot_turned(now, low_out) + o_bias)
        mask = live(lim, g * HOP + i * shape.chunk, shape.chunk)
        res[g, pl.ds(r0, n), :] = (res[g, pl.ds(r0, n), :] + (unit * gain + beta)) * mask

    chunk_loop(shape, close)


def inter_forward(shape, index, xs, gi, gr, slot, vectors, proj, h_out, c_out, scratch, use):
    wc, pg = scratch
    forward_weights(gi, gr, slot, wc)
    bias, (o_bias, gain, beta) = branch_vectors(vectors, index)
    n = shape.crows
    branch_pregates(shape, lambda g, r0: xs[pl.ds(r0, n), :], wc, bias, pg)
    lstm_scan(shape, pg, wc, h_out, c_out)
    low_out = turned_out(proj, index).astype(BF)

    def close(g, i, r0):
        now = h_out[pl.ds(pl.multiple_of(r0 + shape.rows, 8), n), :].astype(BF)
        unit, _ = norm_parts(dot_turned(now, low_out) + o_bias)
        use(i, r0, unit * gain + beta)

    chunk_loop(shape, close)


def zero_tail(res, c):
    if res.shape[1] > K * M:
        res[c, K * M :] = jnp.zeros((res.shape[1] - K * M, B), F32)


def encode(mix, following, leading, lim, proj, vectors, win, flat, bottle, res):
    flat[:M] = jnp.concatenate([leading[...], mix[:, :STRIDE]], 1)
    windows_of(mix, following, flat)
    win[...] = flat[...].astype(BF)
    w_enc = proj[:, BASE + N + B : BASE + N + B + 2 * STRIDE].astype(BF)
    w_bn = proj[:, BASE : BASE + N].astype(BF)
    gain, beta, b_bias = (pieces(vectors, j, 1) for j in range(3))
    for i in range(BLOCKS * M // CHUNK):
        at = i * CHUNK
        pre = dot_turned(win[at : at + CHUNK], w_enc)
        unit, _ = norm_parts(softplus(pre))
        normed = (unit * gain + beta).astype(BF)
        mask = live(lim, i * (CHUNK // M) - 1, CHUNK // M)
        bottle[at : at + CHUNK] = (dot_turned(normed, w_bn) + b_bias) * mask
    for c in range(TILES):
        res[c, : K * M] = bottle[(c * HOP + 1) * M : (c * HOP + 1 + K) * M]
        zero_tail(res, c)


def first_kernel(shape, nb, RI, mix, following, leading, lengths, proj, vectors, gi, gr, res, send, x_out, h_out, c_out, win, wc, pg, flat, bottle):
    lim = limits(lengths)
    encode(mix, following.at[0], leading, lim, proj, vectors, win, flat, bottle, res)
    intra_forward(shape, 0, res, lim, gi, gr, 0, vectors, proj, x_out, h_out, c_out, (wc, pg))
    send_tiles(res, send, nb, RI)


def third_kernel(shape, nb, RI, res_in, back, lengths, proj, vectors, gi, gr, res, send, x_out, h_out, c_out, wc, pg):
    lim = limits(lengths)
    res[...] = res_in[...]
    add_tiles(res, back, nb, RI, lim)
    intra_forward(shape, 2, res, lim, gi, gr, 0, vectors, proj, x_out, h_out, c_out, (wc, pg))
    send_tiles(res, send, nb, RI)


def inter_kernel(shape, RI, index, rows, proj, vectors, gi, gr, normed, h_out, c_out, wc, pg, xs):
    unpack_steps(rows, xs, shape.steps, RI)
    RP = normed.shape[1]

    def use(i, r0, value):
        for j in range(shape.chunk):
            normed[i * shape.chunk + j] = packed(value[j * RI : (j + 1) * RI], RP)

    inter_forward(shape, index, xs, gi, gr, 0, vectors, proj, h_out, c_out, (wc, pg), use)


EDGE = (HOP + 1) * M
EDGE_TOP = 208


def edge_pack(value):
    rest = jnp.concatenate([value[EDGE_TOP:], jnp.zeros((2 * EDGE_TOP - EDGE, B), F32)], 0)
    return jnp.concatenate([value[:EDGE_TOP], rest], 1)


def edge_unpack(ref):
    return jnp.concatenate([ref[:, :B], ref[: EDGE - EDGE_TOP, B:]], 0)


def parts_of(res, part):
    half = HOP * M
    part[:half] = res[0, :half]
    for c in range(1, TILES):
        part[c * half : (c + 1) * half] = res[c, :half] + res[c - 1, half : 2 * half]
    part[TILES * half :] = res[TILES - 1, half : 2 * half]


def part_kernel(nb, RI, res_in, back, lengths, part, up, down, res):
    res[...] = res_in[...]
    add_tiles(res, back, nb, RI, limits(lengths))
    parts_of(res, part)
    half = HOP * M
    up[...] = edge_pack(part[TILES * half - M :])
    down[...] = edge_pack(part[: half + M])


def middle_kernel(nb, RI, part, before, after, lengths, win, goal, following, proj, vectors, send, gres, genc, gm, *scratch):
    edge = jnp.where(lax.axis_index("block") > 0, 1.0, 0.0)
    middle(
        part, edge_unpack(before), edge_unpack(after), limits(lengths), edge, win, goal,
        following.at[1], proj, vectors, gres, genc, gm, *scratch,
    )
    send_tiles(gres, send, nb, RI)


def middle(part, early, late, lim, edge, win, goal, following, proj, vectors, gres, genc, gm, feats, dec, tgt, gest, enc, gate, src, act):
    half = HOP * M
    top = M + TILES * half
    total = BLOCKS * M
    feats[:M] = early[:M]
    feats[M : M + half] = part[:half] + early[M:]
    feats[M + half : top] = part[half : TILES * half]
    feats[top : top + half] = part[TILES * half :] + late[:half]
    feats[top + half : top + half + M] = late[half:]
    feats[top + half + M :] = jnp.zeros((PADDED * M - top - half - M, B), F32)
    low_mask = proj[:, BASE + N : BASE + N + B].astype(BF)
    w_enc = proj[:, BASE + N + B : BASE + N + B + 2 * STRIDE].astype(BF)
    low_dec = proj[:, BASE + N + B + 2 * STRIDE : BASE + N + B + 4 * STRIDE].astype(BF)
    m_bias = pieces(vectors, vectors.shape[0] * 2 - 1, 1)
    root = 0.7978845608028654
    cube = 0.044715
    dec[total:] = jnp.zeros((PADDED * M - total, 2 * STRIDE), F32)
    for i in range(total // CHUNK):
        rows = slice(i * CHUNK, (i + 1) * CHUNK)
        x = feats[rows]
        low = (0.5 * x * (1.0 + jnp.tanh(root * (x + cube * x * x * x)))).astype(BF)
        encoded = softplus(dot_turned(win[rows], w_enc))
        mask = 0.5 * jnp.tanh(0.5 * (dot_turned(low, low_mask) + m_bias)) + 0.5
        source = (mask * encoded).astype(BF)
        enc[rows] = encoded
        gate[rows] = mask
        src[rows] = source.astype(F32)
        act[rows] = low.astype(F32)
        dec[rows] = dot(source, low_dec)
    dec[:M] = dec[:M] * edge
    for ref in (enc, gate, src, act):
        ref[total:] = jnp.zeros((PADDED * M - total, B), F32)
    for i in range(1, FRAMES + 1):
        tgt[i * M : (i + 1) * M] = goal[:, STRIDE * (i - 1) : STRIDE * i]
    for i in range(FRAMES + 1, FRAMES + HOP + 2):
        at = STRIDE * (i - 1 - FRAMES)
        tgt[i * M : (i + 1) * M] = following[:, at : at + STRIDE]
    tgt[(FRAMES + HOP + 2) * M :] = jnp.zeros(((PADDED - FRAMES - HOP - 2) * M, STRIDE), F32)
    estimate = dec[M:total, :STRIDE] + dec[: total - M, STRIDE:]
    count = BLOCKS - 1
    spot = lax.broadcasted_iota(jnp.int32, (count, M, STRIDE), 0)
    phase = lax.broadcasted_iota(jnp.int32, (count, M, STRIDE), 2)
    near = spot < FRAMES + HOP + 1
    valid = jnp.where(near & (spot * STRIDE + phase < lim[:, :STRIDE][None]), 1.0, 0.0)
    inside = jnp.where(spot < FRAMES, valid, 0.0).reshape(count * M, STRIDE)
    valid = valid.reshape(count * M, STRIDE)
    error = estimate - tgt[M:total]
    smoothed = jnp.sqrt(error * error + 1.0)
    gest[:M] = jnp.zeros((M, STRIDE), F32)
    gest[M:total] = valid * error / smoothed
    gest[total:] = jnp.zeros((PADDED * M - total, STRIDE), F32)
    loss = jnp.sum(jnp.sum(inside * (smoothed - 1.0), 0, keepdims=True), 1, keepdims=True)
    seen = jnp.sum(jnp.sum(inside, 0, keepdims=True), 1, keepdims=True)
    gm[...] = jnp.zeros_like(gm)
    gm[132:133] = jnp.broadcast_to(loss, (1, LANES))
    gm[133:134] = jnp.broadcast_to(seen, (1, LANES))
    for i in range(total // CHUNK):
        at = i * CHUNK + M
        rows = slice(at, at + CHUNK)
        grad_dec = jnp.concatenate([gest[rows], gest[at + M : at + M + CHUNK]], 1).astype(BF)
        mine = own(i * (CHUNK // M), CHUNK // M)
        mine_low = mine.astype(BF)
        gm[64:128, 16:32] += dot_rows(src[rows].astype(BF) * mine_low, grad_dec)
        grad_source = dot_turned(grad_dec, low_dec)
        mask = gate[rows]
        grad_logit = (grad_source * enc[rows] * mask * (1.0 - mask)).astype(BF)
        enc[rows] = grad_source * mask
        gm[:64, 64:] += dot_rows(grad_logit * mine_low, act[rows].astype(BF))
        gm[131:132, :B] += jnp.sum(grad_logit.astype(F32) * mine, 0, keepdims=True)
        x = feats[rows]
        curve = jnp.tanh(root * (x + cube * x * x * x))
        slope = 0.5 * (1.0 + curve) + (0.5 * root) * x * (1.0 - curve * curve) * (
            1.0 + (3.0 * cube) * x * x
        )
        feats[rows] = slope * dot(grad_logit, low_mask)
    genc[...] = enc[M : M + FRAMES * M]
    for c in range(TILES):
        gres[c, : K * M] = feats[M + c * half : M + c * half + K * M] * live(lim, c * HOP, K)
        zero_tail(gres, c)


def inter_back(shape, index, gs, xs, h_ref, c_ref, proj, vectors, gi, gr, slot, out, core, use):
    n = shape.crows
    last = branch_back(
        shape,
        lambda g, r0: gs[pl.ds(r0, n), :],
        lambda g, r0: xs[pl.ds(r0, n), :],
        h_ref, c_ref, (gi, gr), slot, branch_vectors(vectors, index), turned_out(proj, index), out, core,
    )
    last(use)


def inter_back_kernel(shape, RI, index, grad_rows, rows, h_ref, c_ref, proj, vectors, gi, gr, send, out, *scratch):
    xs, gs, core = scratch[0], scratch[1], scratch[2:]
    unpack_steps(rows, xs, shape.steps, RI)
    unpack_steps(grad_rows, gs, shape.steps, RI)
    RP = send.shape[1]

    def use(g, i, r0, total):
        for j in range(shape.chunk):
            send[i * shape.chunk + j] = packed(total[j * RI : (j + 1) * RI], RP)

    inter_back(shape, index, gs, xs, h_ref, c_ref, proj, vectors, gi, gr, 0, out, core, use)


def intra_back(shape, index, gres, x_ref, h_ref, c_ref, proj, vectors, gi, gr, slot, out, core):
    n = shape.crows

    def inputs(g, r0):
        return x_ref[pl.ds(pl.multiple_of(g * shape.size + r0, 16), n), :]

    last = branch_back(
        shape,
        lambda g, r0: gres[g, pl.ds(r0, n), :],
        inputs,
        h_ref, c_ref, (gi, gr), slot, branch_vectors(vectors, index), turned_out(proj, index), out, core,
    )

    def use(g, i, r0, total):
        gres[g, pl.ds(r0, n), :] = gres[g, pl.ds(r0, n), :] + total

    last(use)


def third_back_kernel(shape, nb, RI, gres_in, back, lengths, x_ref, h_ref, c_ref, proj, vectors, gi, gr, gres, send, out, *core):
    lim = limits(lengths)
    gres[...] = gres_in[...]
    add_tiles(gres, back, nb, RI, lim)
    intra_back(shape, 2, gres, x_ref, h_ref, c_ref, proj, vectors, gi, gr, 0, out, core)
    for c in range(TILES):
        gres[c, : K * M] = gres[c, : K * M] * live(lim, c * HOP, K)
    send_tiles(gres, send, nb, RI)


def first_back_kernel(shape, nb, RI, gres_in, back, lengths, x_ref, h_ref, c_ref, proj, vectors, gi, gr, win, genc, gm, more_in, out, more, gres, bottle, *core):
    lim = limits(lengths)
    more[...] = more_in[...]
    gres[...] = gres_in[...]
    add_tiles(gres, back, nb, RI, lim)
    intra_back(shape, 0, gres, x_ref, h_ref, c_ref, proj, vectors, gi, gr, 0, out, core)
    encode_back(gres, lim, proj, vectors, win, genc, gm, out, more, bottle)


def encode_back(gres, lim, proj, vectors, win, genc, gm, out, more, bottle):
    at_first, at_vecs = ROWS_MORE, ROWS_MORE + B
    out[at_first : at_first + B] = gm[:B]
    out[at_vecs : at_vecs + 8] = gm[2 * B :]
    more[at_first : at_first + B] = gm[B : 2 * B]
    bottle[...] = jnp.zeros_like(bottle)
    for c in range(TILES):
        at = (c * HOP + 1) * M
        bottle[at : at + K * M] += gres[c, : K * M]
    w_enc = proj[:, BASE + N + B : BASE + N + B + 2 * STRIDE].astype(BF)
    w_bn = proj[:, BASE : BASE + N].astype(BF)
    gain, beta = (pieces(vectors, j, 1) for j in range(2))
    own_rows = FRAMES * M
    for i in range(BLOCKS * M // CHUNK):
        at = i * CHUNK
        rows = slice(at, at + CHUNK)
        pre = dot_turned(win[rows], w_enc)
        unit, scale = norm_parts(softplus(pre))
        normed = (unit * gain + beta).astype(BF)
        low = (bottle[rows] * live(lim, i * (CHUNK // M) - 1, CHUNK // M)).astype(BF)
        out[at_first : at_first + B, :N] += dot_rows(low, normed)
        grad_normed = dot(low, w_bn)
        for j, value in enumerate((grad_normed * unit, grad_normed, low.astype(F32))):
            out[at_vecs + j : at_vecs + j + 1, :B] += jnp.sum(value, 0, keepdims=True)
        grad_enc = norm_back(grad_normed, unit, scale, gain)
        lo, hi = max(at - M, 0), min(at + CHUNK - M, own_rows)
        if lo < hi:
            piece = genc[lo:hi]
            above, below = lo + M - at, at + CHUNK - M - hi
            if above:
                piece = jnp.concatenate([jnp.zeros((above, B), F32), piece], 0)
            if below:
                piece = jnp.concatenate([piece, jnp.zeros((below, B), F32)], 0)
            grad_enc = grad_enc + piece
        grad_pre = (grad_enc * (0.5 * jnp.tanh(0.5 * pre) + 0.5)).astype(BF)
        more[at_first : at_first + B, :16] += dot_rows(grad_pre, win[rows])


def turn_in(res, xs, RI, lowered=True):
    for j in range(M):
        for c in range(TILES):
            at = (TILES * j + c) * RI
            value = res[c, pl.ds(j, K, stride=M), :]
            xs[at : at + K] = value.astype(BF).astype(F32)


def turn_back(res, xs, RI, length):
    pos = lax.broadcasted_iota(jnp.int32, (K, B), 0)
    for j in range(M):
        for c in range(TILES):
            at = (TILES * j + c) * RI
            mask = jnp.where((pos + (FRAMES * j + HOP * c)) * STRIDE < length, 1.0, 0.0)
            where = (c, pl.ds(j, K, stride=M), slice(None))
            res[where] = (res[where] + xs[at : at + K]) * mask


def local_kernel(intra, inter, RI, waves, lengths, proj, vectors, gi, gr, outs, notes, *scratch):
    (win, flat, bottle, res, nrm, part, genc, gm, feats, dec, tgt, gest, enc, gate, src, act) = scratch[:16]
    x0, h0, c0, x1, h1, c1, x2, h2, c2, x3, h3, c3 = scratch[16:28]
    wc, wit, wrt, wot, z, dh = scratch[28:]
    core = (wc, wit, wrt, wot, z, dh)
    out0, out1, out2, out3 = (outs.at[pl.ds(r * ROWS_G, ROWS_G)] for r in range(4))
    length = lengths[lax.axis_index("block")]
    lim = length - lax.broadcasted_iota(jnp.int32, (M, B), 0) * (FRAMES * STRIDE)
    reach = (HOP + 2) * STRIDE
    span = FRAMES * STRIDE
    goal_at = waves.shape[1] // 2
    mix = waves[:, :span]
    goal = waves[:, goal_at : goal_at + span]

    def after(value):
        return jnp.concatenate([value[1:], jnp.zeros((1, value.shape[1]), F32)], 0)

    def before(value):
        return jnp.concatenate([jnp.zeros((1, value.shape[1]), F32), value[:-1]], 0)

    for ref in (x1, x3, nrm):
        ref[...] = jnp.zeros_like(ref)
    encode(mix, after(mix[:, :reach]), before(mix[:, span - STRIDE :]), lim, proj, vectors, win, flat, bottle, res)

    def inter_layer(index, xs, h, c):
        turn_in(res, xs, RI)

        def use(i, r0, value):
            nrm[pl.ds(r0, inter.crows), :] = value.astype(BF).astype(F32)

        inter_forward(inter, index, xs, gi, gr, index, vectors, proj, h, c, (wc, z), use)
        turn_back(res, nrm, RI, length)

    intra_forward(intra, 0, res, lim, gi, gr, 0, vectors, proj, x0, h0, c0, (wc, z))
    inter_layer(1, x1, h1, c1)
    intra_forward(intra, 2, res, lim, gi, gr, 2, vectors, proj, x2, h2, c2, (wc, z))
    inter_layer(3, x3, h3, c3)

    parts_of(res, part)
    half = HOP * M
    row = lax.broadcasted_iota(jnp.int32, (EDGE, B), 0) % M
    early = jnp.where(row == 0, 0.0, before(part[TILES * half - M :]))
    late = jnp.where(row == M - 1, 0.0, after(part[: half + M]))
    edge = jnp.where(lax.broadcasted_iota(jnp.int32, (M, 2 * STRIDE), 0) == 0, 0.0, 1.0)
    middle(
        part, early, late, lim, edge, win, goal, after(goal[:, :reach]), proj, vectors, res, genc, gm,
        feats, dec, tgt, gest, enc, gate, src, act,
    )

    def inter_layer_back(index, xs, h, c, out):
        for j in range(M):
            for t in range(TILES):
                at = (TILES * j + t) * RI
                nrm[at + K : at + RI] = jnp.zeros((RI - K, B), F32)
        turn_in(res, nrm, RI)

        def use(g, i, r0, total):
            nrm[pl.ds(r0, inter.crows), :] = total.astype(BF).astype(F32)

        inter_back(inter, index, nrm, xs, h, c, proj, vectors, gi, gr, index, out, core, use)
        turn_back(res, nrm, RI, length)

    inter_layer_back(3, x3, h3, c3, out3)
    intra_back(intra, 2, res, x2, h2, c2, proj, vectors, gi, gr, 2, out2, core)
    for c in range(TILES):
        res[c, : K * M] = res[c, : K * M] * live(lim, c * HOP, K)
    inter_layer_back(1, x1, h1, c1, out1)
    intra_back(intra, 0, res, x0, h0, c0, proj, vectors, gi, gr, 0, out0, core)
    encode_back(res, lim, proj, vectors, win, genc, gm, out0, out1, bottle)

    def widest(i, best):
        rows = outs[pl.ds(pl.multiple_of(i * 256, 256), 256), :]
        return jnp.maximum(best, jnp.max(jnp.abs(rows).reshape(32, 8, LANES), 0))

    best = lax.fori_loop(0, outs.shape[0] // 256, widest, jnp.zeros((8, LANES), F32))
    best = jnp.max(jnp.max(best, 0, keepdims=True), 1, keepdims=True)
    notes[...] = note_rows(best, gm[132:133], gm[133:134])


def local_scratch(intra, inter):
    tall = PADDED * M
    narrow = [pltpu.VMEM((tall, 2 * STRIDE), F32)] + [pltpu.VMEM((tall, STRIDE), F32)] * 2
    first = [
        pltpu.VMEM((BLOCKS * M, 2 * STRIDE), BF),
        pltpu.VMEM((BLOCKS * M, 2 * STRIDE), F32),
        pltpu.VMEM((BLOCKS * M, B), F32),
        pltpu.VMEM((TILES, K * M, B), F32),
        pltpu.VMEM((inter.size, B), F32),
        pltpu.VMEM(((FRAMES + HOP) * M, B), F32),
        pltpu.VMEM((FRAMES * M, B), F32),
        pltpu.VMEM((136, LANES), F32),
        pltpu.VMEM((tall, B), F32),
        *narrow,
    ] + [pltpu.VMEM((tall, B), F32)] * 4
    kept = []
    for shape, kind in ((intra, BF), (inter, F32)) * 2:
        state = pltpu.VMEM((shape.groups * shape.wide, 2 * H), F32)
        kept += [pltpu.VMEM((shape.groups * shape.size, B), kind), state, state]
    return first + kept + back_scratch(inter)


def note_rows(widest, loss, count):
    row = lax.broadcasted_iota(jnp.int32, (8, LANES), 0)
    power = jnp.floor(jnp.log(jnp.maximum(widest, 1e-30)) * 1.4426950408889634)
    return jnp.where(row == 0, power, jnp.where(row == 1, loss, jnp.where(row == 2, count, 0.0)))


def adam_parts(grad, moment, square, weight, average, decay):
    moment = BETA_ONE * moment + (1.0 - BETA_ONE) * grad
    square = BETA_TWO * square + (1.0 - BETA_TWO) * grad * grad
    corrected = moment * (1.0 / (1.0 - BETA_ONE**STEP))
    scaled = square * (1.0 / (1.0 - BETA_TWO**STEP))
    weight = weight - RATE * (corrected / (jnp.sqrt(scaled) + ADAM_EPS) + decay * weight)
    average = KEEP * average + (1.0 - KEEP) * weight
    return moment, square, weight, average, weight.astype(BF)


def adam_kernel(*refs):
    near, far, totals, old = refs[0], refs[1], refs[2], refs[3:19]
    scalars, new = refs[19], refs[20:40]
    gv, sums = refs[40:]
    mine = lax.axis_index("dp") & 1
    pieces_half = (near.shape[0] - sums.shape[0] // 2) // NOTES
    size = sums.shape[0] // 2 // pieces_half
    for i in range(pieces_half):
        at = i * (size + NOTES)
        for ref, place in ((near, mine), (far, 1 - mine)):
            to = pl.multiple_of((place * pieces_half + i) * size, 16)
            scale = jnp.exp2(ref[at + size : at + size + 1, :] - TOP)
            sums[pl.ds(to, size), :] = ref[at : at + size] * scale
    gs = [sums.at[pl.ds(r * ROWS_G, ROWS_G)] for r in range(4)]
    vecs = ROWS_MORE + B
    gv[:1] = jnp.concatenate([gs[0][vecs : vecs + 1, :N], gs[0][vecs + 1 : vecs + 2, :N]], 1)
    gv[1:2, :N] = gs[0][vecs + 2 : vecs + 3, :N]
    gv[gv.shape[0] - 1 :, N:] = gs[0][vecs + 3 : vecs + 4, :N]
    for r in range(4):
        at = 3 + 19 * r
        rows = [
            gs[r][ROWS_VECS + j : ROWS_VECS + j + 1, k * N : (k + 1) * N] for j in range(8) for k in range(2)
        ]
        rows += [gs[r][ROWS_VECS + j : ROWS_VECS + j + 1, :N] for j in range(8, 11)]
        for j, row in enumerate(rows):
            q = at + j
            gv[q // 2 : q // 2 + 1, (q % 2) * N : (q % 2 + 1) * N] = row
    part = jnp.zeros((8, LANES), F32)
    pieces_of = [gs[r][:ROWS_VECS] for r in range(4)]
    pieces_of += [gs[r][ROWS_MORE : ROWS_MORE + B] for r in range(2)] + [gv[...]]
    for piece in pieces_of:
        value = piece.reshape(piece.shape[0] // 8, 8, LANES)
        part = part + jnp.sum(value * value, 0)
    squared = jnp.sum(jnp.sum(part, 0, keepdims=True), 1, keepdims=True)
    loss, count = totals[0:1, :1], totals[1:2, :1]
    norm = jnp.sqrt(squared) / count
    factor = jnp.minimum(1.0, CLIP / norm) / count
    row = lax.broadcasted_iota(jnp.int32, (8, LANES), 0)
    scalars[...] = jnp.where(row == 0, loss, jnp.where(row == 1, count, norm))

    def update(kind, index, grad, decay):
        results = adam_parts(
            grad * factor,
            old[4 + kind][index],
            old[8 + kind][index],
            old[kind][index],
            old[12 + kind][index],
            decay,
        )
        for j, value in enumerate(results):
            new[4 * j + kind][index] = value

    for r in range(4):
        for d in range(2):
            for j in range(4):
                lanes = slice(j * LANES, (j + 1) * LANES)
                at = j * 384 + d * B
                update(0, (r, d, slice(None), lanes), gs[r][at : at + B], DECAY)
                at = j * 384 + 128 + d * H
                update(1, (r, d, slice(None), lanes), gs[r][at : at + H], DECAY)
        for j in range(2):
            at = ROWS_MAPS + j * B
            lanes = slice(r * 2 * H + j * LANES, r * 2 * H + (j + 1) * LANES)
            update(2, (slice(None), lanes), gs[r][at : at + B], DECAY)
    more = slice(ROWS_MORE, ROWS_MORE + B)
    update(2, (slice(None), slice(BASE, BASE + LANES)), gs[0][more], DECAY)
    update(2, (slice(None), slice(BASE + LANES, BASE + LANES + 32)), gs[1][more, :32], DECAY)
    update(3, (slice(None), slice(None)), gv[...], 0.0)


def call(kernel, outs, ins, scratch, index=None, limit=56, micros=20):
    vmem = pl.BlockSpec(memory_space=pltpu.VMEM)
    specs = [
        pl.BlockSpec(memory_space=pltpu.SMEM) if a.ndim == 1 and a.dtype == jnp.int32 else vmem
        for a in ins
    ]
    extra = []
    wrapped = kernel
    if index is not None:
        big = [i for i, a in enumerate(ins) if a.ndim == 4 and a.shape[:2] == (2 * LAYERS, 2)]
        for i in big:
            specs[i] = pl.BlockSpec(memory_space=pl.ANY)
        extra = [pltpu.VMEM((1,) + ins[i].shape[1:], F32) for i in big]
        extra.append(pltpu.SemaphoreType.DMA((len(big),)))

        def wrapped(*refs):
            refs = list(refs)
            held, sem = refs[len(refs) - len(extra) : -1], refs[-1]
            copies = []
            for j, i in enumerate(big):
                copies.append(pltpu.make_async_copy(refs[i].at[pl.ds(index, 1)], held[j], sem.at[j]))
                copies[-1].start()
            for copy in copies:
                copy.wait()
            for j, i in enumerate(big):
                refs[i] = held[j]
            kernel(*refs[: len(refs) - len(extra)])

    return pl.pallas_call(
        wrapped,
        out_shape=outs,
        in_specs=specs,
        out_specs=[vmem] * len(outs),
        scratch_shapes=list(scratch) + extra,
        compiler_params=pltpu.CompilerParams(vmem_limit_bytes=limit * 1024 * 1024),
        cost_estimate=pl.CostEstimate(
            flops=micros * 10**9, bytes_accessed=micros * 10**6, transcendentals=0
        ),
    )(*ins)


def shift(block, axis, distance):
    size = lax.axis_size(axis)
    route = [(i, i + distance) for i in range(size) if 0 <= i + distance < size]
    return lax.ppermute(block, axis, route)


def exchange(block):
    return lax.all_to_all(block, "block", split_axis=0, concat_axis=0, tiled=True)


def flip(block, bit):
    size = lax.axis_size("dp")
    return lax.ppermute(block, "dp", [(i, i ^ (1 << bit)) for i in range(size)])


def bits():
    return lax.axis_size("dp").bit_length() - 1


def bits():
    return lax.axis_size("dp").bit_length() - 1


def noted(power, loss, count):
    row = lax.broadcasted_iota(jnp.int32, (NOTES, LANES), 0)
    rows = jnp.where(row == 0, power, 0.0)
    for first, value in ((1, loss), (5, count)):
        rest = value * (1.0 / 1024.0**2)
        for j in range(4):
            digit = jnp.floor(rest) if j < 3 else rest
            rows = jnp.where(row == first + j, digit, rows)
            rest = (rest - digit) * 1024.0
    return rows.astype(HALF)


def scaled(value, power):
    return (value * jnp.exp2(TOP - power)).astype(HALF)


def read_notes(rows):
    rows = rows.astype(F32)
    power, *digits = (rows[..., i : i + 1, :] for i in range(9))
    loss, count = (
        (d[0] * 1024.0 + d[1]) * 1024.0 + (d[2] + d[3] * (1.0 / 1024.0))
        for d in (digits[:4], digits[4:])
    )
    return power, loss, count


def cut(block, start, size):
    return lax.dynamic_slice_in_dim(block, start, size, 0)


def gradient_sums(block, notes):
    nb = lax.axis_size("block")
    size = block.shape[0] // 2
    mine = lax.axis_index("dp") & 1
    other = flip(jnp.concatenate([cut(block, (1 - mine) * size, size), notes], 0), 0)
    power = jnp.maximum(notes[0:1], other[size : size + 1]) + 1.0
    loss, count = (notes[i : i + 1] + other[size + i : size + i + 1] for i in (1, 2))
    base = mine * size

    def take(start, rows):
        return cut(block, base + start, rows) + cut(other, start, rows)

    for bit in range(1, bits()):
        size //= 2
        mine = (lax.axis_index("dp") >> bit) & 1
        given = jnp.concatenate(
            [scaled(take((1 - mine) * size, size), power), noted(power, loss, count)], 0
        )
        given = flip(given, bit)
        its_power, its_loss, its_count = read_notes(given[size:])

        def take(start, rows, take=take, given=given, base=mine * size, its_power=its_power):
            come = cut(given, start, rows).astype(F32) * jnp.exp2(its_power - TOP)
            return take(base + start, rows) + come

        loss, count = loss + its_loss, count + its_count
        power = jnp.maximum(power, its_power) + 1.0
    part = size // nb
    notes = jnp.broadcast_to(noted(power, loss, count)[None], (nb, NOTES, LANES))
    pieces = exchange(
        jnp.concatenate([scaled(take(0, size), power).reshape(nb, part, LANES), notes], 1)
    )
    powers, losses, counts = read_notes(pieces[:, part:])
    block = jnp.sum(pieces[:, :part].astype(F32) * jnp.exp2(powers - TOP), 0)
    loss, count = jnp.sum(losses, 0), jnp.sum(counts, 0)
    power = jnp.max(powers, 0) + (nb - 1).bit_length()
    mine = jnp.concatenate([scaled(block, power), noted(power, loss, count)], 0)
    block = exchange(jnp.broadcast_to(mine[None], (nb,) + mine.shape))
    for bit in reversed(range(1, bits())):
        mine = (lax.axis_index("dp") >> bit) & 1
        other = flip(block, bit)
        block = jnp.where(
            mine == 0, jnp.concatenate([block, other], 0), jnp.concatenate([other, block], 0)
        )
    other = flip(block, 0)
    row = lax.broadcasted_iota(jnp.int32, (8, LANES), 0)
    totals = jnp.where(row == 0, loss, count)
    return [half.reshape(-1, LANES).astype(F32) for half in (block, other)] + [totals]


def shared_step(mixture, target, lengths, proj, vectors_wide, gi, gr):
    nb = lax.axis_size("block")
    RI = -(-K // nb) * M
    intra = Shape(TILES, K, M)
    inter = Shape(1, TILES * nb, RI)
    T = inter.steps
    reach = (HOP + 2) * STRIDE
    following = shift(jnp.stack([mixture[:, :reach], target[:, :reach]]), "block", -1)
    leading = shift(mixture[:, -STRIDE:], "block", 1)

    RP = -(-RI // 16) * 8
    res_shape = SDS((TILES, nb * RI, B), F32)
    send_shape = SDS((nb, TILES, RP, 2 * B), BF)
    steps_shape = SDS((T, RP, 2 * B), BF)
    x_shape = SDS((TILES * K * M, B), BF)

    def state(shape):
        return SDS((shape.groups * shape.wide, 2 * H), F32)

    res0, send, x0, h0, c0, win = call(
        functools.partial(first_kernel, intra, nb, RI),
        [res_shape, send_shape, x_shape, state(intra), state(intra), SDS((BLOCKS * M, 2 * STRIDE), BF)],
        [mixture, following, leading, lengths, proj, vectors_wide, gi, gr],
        fwd_scratch(intra)
        + [pltpu.VMEM((BLOCKS * M, 2 * STRIDE), F32), pltpu.VMEM((BLOCKS * M, B), F32)],
        0,
    )

    def inter_step(send, index):
        rows = exchange(send).reshape(T, RP, 2 * B)
        normed, h, c = call(
            functools.partial(inter_kernel, inter, RI, index),
            [steps_shape, state(inter), state(inter)],
            [rows, proj, vectors_wide, gi, gr],
            fwd_scratch(inter) + [pltpu.VMEM((inter.size, B), F32)],
            index,
        )
        return rows, h, c, exchange(normed.reshape(send_shape.shape))

    rows1, h1, c1, back = inter_step(send, 1)
    res2, send, x2, h2, c2 = call(
        functools.partial(third_kernel, intra, nb, RI),
        [res_shape, send_shape, x_shape, state(intra), state(intra)],
        [res0, back, lengths, proj, vectors_wide, gi, gr],
        fwd_scratch(intra),
        2,
    )
    rows3, h3, c3, back = inter_step(send, 3)
    edge_shape = SDS((EDGE_TOP, 2 * B), F32)
    part, up, down = call(
        functools.partial(part_kernel, nb, RI),
        [SDS(((FRAMES + HOP) * M, B), F32), edge_shape, edge_shape],
        [res2, back, lengths],
        [pltpu.VMEM(res_shape.shape, F32)],
    )
    before = shift(up, "block", 1)
    after = shift(down, "block", -1)
    tall = PADDED * M
    send, gres, genc, gm = call(
        functools.partial(middle_kernel, nb, RI),
        [send_shape, res_shape, SDS((FRAMES * M, B), F32), SDS((136, LANES), F32)],
        [part, before, after, lengths, win, target, following, proj, vectors_wide],
        [
            pltpu.VMEM((tall, B), F32),
            pltpu.VMEM((tall, 2 * STRIDE), F32),
            pltpu.VMEM((tall, STRIDE), F32),
            pltpu.VMEM((tall, STRIDE), F32),
            pltpu.VMEM((tall, B), F32),
            pltpu.VMEM((tall, B), F32),
            pltpu.VMEM((tall, B), F32),
            pltpu.VMEM((tall, B), F32),
        ],
    )
    out_shape = SDS((ROWS_G, LANES), F32)

    def inter_back(send, rows, h, c, index):
        grad_rows = exchange(send).reshape(T, RP, 2 * B)
        send, out = call(
            functools.partial(inter_back_kernel, inter, RI, index),
            [steps_shape, out_shape],
            [grad_rows, rows, h, c, proj, vectors_wide, gi, gr],
            [pltpu.VMEM((inter.size, B), F32)] * 2 + back_scratch(inter),
            index,
        )
        return exchange(send.reshape(send_shape.shape)), out

    back, out3 = inter_back(send, rows3, h3, c3, 3)
    gres, send, out2 = call(
        functools.partial(third_back_kernel, intra, nb, RI),
        [res_shape, send_shape, out_shape],
        [gres, back, lengths, x2, h2, c2, proj, vectors_wide, gi, gr],
        back_scratch(intra),
        2,
    )
    back, out1 = inter_back(send, rows1, h1, c1, 1)
    out0, out1 = call(
        functools.partial(first_back_kernel, intra, nb, RI),
        [out_shape, out_shape],
        [gres, back, lengths, x0, h0, c0, proj, vectors_wide, gi, gr, win, genc, gm, out1],
        [pltpu.VMEM(res_shape.shape, F32), pltpu.VMEM((BLOCKS * M, B), F32)] + back_scratch(intra),
        0,
    )
    parts = nb * lax.axis_size("dp") * NOTES
    more = jnp.zeros((-4 * ROWS_G % parts, LANES), F32)
    outs = jnp.concatenate([out0, out1, out2, out3, more], 0)
    at = ROWS_MORE + B + 4
    return outs, note_rows(jnp.max(jnp.abs(outs)), outs[at : at + 1], outs[at + 1 : at + 2])


def local_step(mixture, target, lengths, proj, vectors_wide, gi, gr):
    RI = -(-K // M) * M
    intra = Shape(TILES, K, M)
    inter = Shape(1, TILES * M, RI)
    pad = jnp.zeros((M, -(FRAMES * STRIDE) % LANES), F32)
    waves = jnp.concatenate([mixture, pad, target, pad], 1)
    waves = lax.all_to_all(waves.reshape(M, 1, -1), "block", split_axis=0, concat_axis=0, tiled=True)
    return call(
        functools.partial(local_kernel, intra, inter, RI),
        [SDS((4 * ROWS_G, LANES), F32), SDS((8, LANES), F32)],
        [waves.reshape(M, -1), lengths, proj, vectors_wide, gi, gr],
        local_scratch(intra, inter),
        limit=62,
    )


def body(
    mixture,
    target,
    lengths,
    input_gates,
    recur_gates,
    projections,
    vectors,
    moment_input,
    moment_recur,
    moment_proj,
    moment_vecs,
    square_input,
    square_recur,
    square_proj,
    square_vecs,
    average_input,
    average_recur,
    average_proj,
    average_vecs,
):
    nb = lax.axis_size("block")
    proj = projections.T
    vectors_wide = vectors.reshape(-1, LANES)
    step = local_step if nb == M else shared_step
    outs, notes = step(mixture, target, lengths, proj, vectors_wide, input_gates, recur_gates)
    sums = gradient_sums(outs, notes)
    old = [
        input_gates, recur_gates, projections, vectors,
        moment_input, moment_recur, moment_proj, moment_vecs,
        square_input, square_recur, square_proj, square_vecs,
        average_input, average_recur, average_proj, average_vecs,
    ]
    for i in range(2, 16, 4):
        old[i] = old[i].T
    for i in range(3, 16, 4):
        old[i] = old[i].reshape(-1, LANES)
    new = [SDS(a.shape, F32) for a in old[:4]] * 4 + [SDS(a.shape, BF) for a in old[:4]]
    scalars, *new = call(
        adam_kernel,
        [SDS((8, LANES), F32)] + new,
        sums + old,
        [pltpu.VMEM(old[3].shape, F32), pltpu.VMEM(outs.shape, F32)],
        limit=48,
    )
    for i in range(2, 20, 4):
        new[i] = new[i].T
    for i in range(3, 20, 4):
        new[i] = new[i].reshape(-1)
    return (scalars[0, 0], scalars[1, 0], scalars[2, 0], *new)


def solution(mesh):
    in_specs = (P("dp", "block"), P("dp", "block"), P("dp")) + (P(),) * 16
    return jax.shard_map(
        body, mesh=mesh, in_specs=in_specs, out_specs=(P(),) * 23, check_vma=False
    )
```

```python
import functools

import jax
import jax.numpy as jnp
from jax import lax
from jax.experimental import pallas as pl
from jax.experimental.pallas import tpu as pltpu
from jax.sharding import PartitionSpec as P

N = 64
B = 64
H = 128
K = 100
STRIDE = 8
LAYERS = 2
STEP = 10
HOP = 50
TILES = 3
M = 8
FRAMES = 150
BASE = 4 * LAYERS * H
PERIOD = 8 * H + 3 * B
ROWS_MAPS = 1536
ROWS_VECS = 1664
ROWS_MORE = 1680
ROWS_G = 1792
LANES = 128
BLOCKS = 208
PADDED = 216
CHUNK = 416

EPS_NORM = 1e-05
CLIP = 0.001
RATE = 0.1
BETA_ONE = 0.9
BETA_TWO = 0.999
ADAM_EPS = 1e-08
DECAY = 0.01
KEEP = 0.9

BF = jnp.bfloat16
F32 = jnp.float32
TOP = 13.0
NOTES = 16
HALF = jnp.float16
SDS = jax.ShapeDtypeStruct


def dot(left, right):
    return jnp.dot(left, right, preferred_element_type=F32)


def dot_turned(left, right):
    return lax.dot_general(left, right, (((1,), (1,)), ((), ())), preferred_element_type=F32)


def dot_rows(left, right):
    return lax.dot_general(left, right, (((0,), (0,)), ((), ())), preferred_element_type=F32)


def half_scale():
    lane = lax.broadcasted_iota(jnp.int32, (1, 4 * H), 1)
    return jnp.where((lane >= 2 * H) & (lane < 3 * H), 1.0, 0.5)


def gate_acts(z):
    act = jnp.tanh(z)
    sig_i = 0.5 * act[:, :H] + 0.5
    sig_f = 0.5 * act[:, H : 2 * H] + 0.5
    sig_o = 0.5 * act[:, 3 * H :] + 0.5
    return sig_i, sig_f, act[:, 2 * H : 3 * H], sig_o


def norm_parts(value):
    center = value - jnp.mean(value, -1, keepdims=True)
    spread = jnp.mean(center * center, -1, keepdims=True)
    scale = lax.rsqrt(spread + EPS_NORM)
    return center * scale, scale


def norm_back(grad, unit, scale, gain):
    inner = grad * gain
    return scale * (
        inner
        - jnp.mean(inner, -1, keepdims=True)
        - unit * jnp.mean(inner * unit, -1, keepdims=True)
    )


def live(lim, start, count):
    pos = lax.broadcasted_iota(jnp.int32, (count, M, B), 0) + start
    return jnp.where(pos * STRIDE < lim[None], 1.0, 0.0).reshape(count * M, B)


def limits(lengths):
    row = lax.broadcasted_iota(jnp.int32, (M, B), 0)
    total = jnp.zeros((M, B), jnp.int32)
    for m in range(M):
        total = jnp.where(row == m, lengths[m], total)
    return total - lax.axis_index("block") * (FRAMES * STRIDE)


def pieces(vectors, start, count):
    parts = []
    at = start
    while at < start + count:
        wide = at % 2 == 0 and at + 2 <= start + count
        lane = (at % 2) * N
        parts.append(vectors[at // 2 : at // 2 + 1, lane : lane + (2 * N if wide else N)])
        at += 2 if wide else 1
    return parts[0] if len(parts) == 1 else jnp.concatenate(parts, 1)


def branch_vectors(vectors, index):
    first = (2 * N + B + index * PERIOD) // N
    half = half_scale()
    bias = [pieces(vectors, first + 8 * d, 8) * half for d in range(2)]
    return bias, [pieces(vectors, first + 16 + j, 1) for j in range(3)]


def own(start, count):
    pos = lax.broadcasted_iota(jnp.int32, (count, M, B), 0) + start
    return jnp.where(pos < FRAMES, 1.0, 0.0).reshape(count * M, B)


def chunk_of(steps, rows):
    best = 1
    for size in range(1, steps + 1):
        if steps % size == 0 and size * rows <= 1024 and size * rows % 16 == 0:
            best = size
    return best


class Shape:
    def __init__(self, groups, steps, rows):
        self.groups, self.steps, self.rows = groups, steps, rows
        self.size = steps * rows
        self.chunk = chunk_of(steps, rows)
        self.crows = self.chunk * rows
        self.chunks = steps // self.chunk
        self.wide = (steps + 2) * rows
        self.unroll = max(n for n in range(1, 26) if steps % n == 0)


def chunk_loop(shape, fn):
    for g in range(shape.groups):
        for i in range(shape.chunks):
            fn(g, i, i * shape.crows)


def forward_weights(gi, gr, index, wc):
    half = half_scale()
    for d in range(2):
        wc[d, :H] = (gr[index, d].astype(BF).astype(F32) * half).astype(BF)
        wc[d, H:] = (gi[index, d].astype(BF).astype(F32) * half).astype(BF)


def lstm_scan(shape, pg, wc, h_ref, c_ref):
    G, S, R = shape.groups, shape.steps, shape.rows
    pad = jnp.zeros((R, 2 * H), F32)
    for g in range(G):
        for ref in (h_ref, c_ref):
            ref[g * shape.wide : g * shape.wide + R] = pad
            ref[(g + 1) * shape.wide - R : (g + 1) * shape.wide] = pad

    def one(d, t, hidden, memory):
        at = pl.multiple_of(t * R, 8)
        pre = jnp.concatenate([pg[d, pl.ds(g * shape.size + at, R), :] for g in range(G)], 0)
        z = pre + dot(hidden, wc[d, :H])
        sig_i, sig_f, tan_g, sig_o = gate_acts(z)
        memory = sig_f * memory + sig_i * tan_g
        hidden = (sig_o * jnp.tanh(memory)).astype(BF)
        full = hidden.astype(F32)
        after = pl.multiple_of(t * R + R, 8)
        for g in range(G):
            to = pl.ds(g * shape.wide + after, R)
            h_ref[to, d * H : (d + 1) * H] = full[g * R : (g + 1) * R]
            c_ref[to, d * H : (d + 1) * H] = memory[g * R : (g + 1) * R]
        return hidden, memory

    def step(s, carry):
        hf, cf, hb, cb = carry
        hf, cf = one(0, s, hf, cf)
        hb, cb = one(1, S - 1 - s, hb, cb)
        return hf, cf, hb, cb

    zero = jnp.zeros((G * R, H), F32)
    start = (zero.astype(BF), zero, zero.astype(BF), zero)
    lax.fori_loop(0, S, step, start, unroll=shape.unroll)


def lstm_scan_back(shape, z, dh, c_ref, wrt):
    G, S, R = shape.groups, shape.steps, shape.rows

    def one(d, t, rec_hidden, rec_memory):
        def take(ref, at, width, lanes):
            at = pl.multiple_of(at, 8)
            return jnp.concatenate([ref[pl.ds(g * width + at, R), lanes] for g in range(G)], 0)

        lanes = slice(d * H, (d + 1) * H)
        at = pl.multiple_of(t * R, 8)
        zt = jnp.concatenate([z[d, pl.ds(g * shape.size + at, R), :] for g in range(G)], 0)
        sig_i, sig_f, tan_g, sig_o = gate_acts(zt)
        tan_c = jnp.tanh(take(c_ref, t * R + R, shape.wide, lanes))
        before = take(c_ref, t * R + 2 * R * d, shape.wide, lanes)
        grad_h = take(dh, t * R, shape.size, lanes) + rec_hidden
        grad_c = rec_memory + grad_h * (sig_o * (1.0 - tan_c * tan_c))
        grad_pre = jnp.concatenate(
            [
                grad_c * (tan_g * sig_i * (1.0 - sig_i)),
                grad_c * (before * sig_f * (1.0 - sig_f)),
                grad_c * (sig_i * (1.0 - tan_g * tan_g)),
                grad_h * (tan_c * sig_o * (1.0 - sig_o)),
            ],
            -1,
        ).astype(BF)
        full = grad_pre.astype(F32)
        for g in range(G):
            z[d, pl.ds(g * shape.size + at, R), :] = full[g * R : (g + 1) * R]
        return dot(grad_pre, wrt[d]), grad_c * sig_f

    def step(s, carry):
        hf, cf, hb, cb = carry
        hf, cf = one(0, S - 1 - s, hf, cf)
        hb, cb = one(1, s, hb, cb)
        return hf, cf, hb, cb

    zero = jnp.zeros((G * R, H), F32)
    lax.fori_loop(0, S, step, (zero,) * 4, unroll=shape.unroll)


def branch_pregates(shape, inputs, wc, bias, pg):
    def fill(g, i, r0):
        x = inputs(g, r0).astype(BF)
        for d in range(2):
            pg[d, pl.ds(g * shape.size + r0, shape.crows), :] = dot(x, wc[d, H:]) + bias[d]

    chunk_loop(shape, fill)


def branch_back(shape, grads, inputs, h_ref, c_ref, weights, index, vecs, turned_out, out, scratch):
    gi, gr = weights
    wc, wit, wrt, wot, z, dh = scratch
    n, R = shape.crows, shape.rows
    forward_weights(gi, gr, index, wc)
    for d in range(2):
        wit[d] = jnp.transpose(gi[index, d]).astype(BF)
        wrt[d] = jnp.transpose(gr[index, d]).astype(BF)
    wot[...] = turned_out.astype(BF)
    out[...] = jnp.zeros(out.shape, F32)
    bias, (o_bias, gain, _) = vecs

    def states(g, at, lanes):
        return h_ref[pl.ds(pl.multiple_of(g * shape.wide + at, 8), n), lanes].astype(BF)

    def earlier(g, r0, d):
        before = states(g, r0 + 2 * R * d, slice(d * H, (d + 1) * H))
        return jnp.concatenate([before, inputs(g, r0).astype(BF)], 1)

    def first(g, i, r0):
        now = states(g, r0 + R, slice(0, 2 * H))
        here = pl.ds(g * shape.size + r0, n)
        unit, scale = norm_parts(dot_turned(now, wot[...]) + o_bias)
        grad = grads(g, r0)
        low = norm_back(grad, unit, scale, gain).astype(BF)
        dh[here, :] = dot(low, wot[...])
        turned = dot_rows(low, now)
        for j in range(2):
            at = ROWS_MAPS + j * B
            out[at : at + B] += turned[:, j * LANES : (j + 1) * LANES]
        for j, value in enumerate((low.astype(F32), grad * unit, grad)):
            at = ROWS_VECS + 8 + j
            out[at : at + 1, :B] += jnp.sum(value, 0, keepdims=True)
        for d in range(2):
            z[d, here, :] = dot(earlier(g, r0, d), wc[d]) + bias[d]

    chunk_loop(shape, first)
    lstm_scan_back(shape, z, dh, c_ref, wrt)

    def last(use):
        def fn(g, i, r0):
            total = None
            for d in range(2):
                full = z[d, pl.ds(g * shape.size + r0, n), :]
                low = full.astype(BF)
                maps = dot_rows(earlier(g, r0, d), low)
                grad_bias = jnp.sum(full, 0, keepdims=True)
                for j in range(4):
                    lanes = slice(j * LANES, (j + 1) * LANES)
                    at = j * 384 + d * B
                    out[at : at + B] += maps[H:, lanes]
                    at = j * 384 + 128 + d * H
                    out[at : at + H] += maps[:H, lanes]
                    at = ROWS_VECS + 4 * d + j
                    out[at : at + 1] += grad_bias[:, lanes]
                part = dot(low, wit[d])
                total = part if total is None else total + part
            use(g, i, r0, total)

        chunk_loop(shape, fn)

    return last


def fwd_scratch(shape):
    return [
        pltpu.VMEM((2, H + B, 4 * H), BF),
        pltpu.VMEM((2, shape.groups * shape.size, 4 * H), F32),
    ]


def back_scratch(shape):
    return [
        pltpu.VMEM((2, H + B, 4 * H), BF),
        pltpu.VMEM((2, 4 * H, B), BF),
        pltpu.VMEM((2, 4 * H, H), BF),
        pltpu.VMEM((B, 2 * H), BF),
        pltpu.VMEM((2, shape.groups * shape.size, 4 * H), F32),
        pltpu.VMEM((shape.groups * shape.size, 2 * H), F32),
    ]


def packed(value, RP):
    rest = value[RP:]
    if rest.shape[0] < RP:
        rest = jnp.concatenate([rest, jnp.zeros((RP - rest.shape[0], B), F32)], 0)
    return jnp.concatenate([value[:RP], rest], 1).astype(BF)


def send_tiles(res, send, nb, RI):
    RP = send.shape[2]
    for d in range(nb):
        for c in range(TILES):
            send[d, c] = packed(res[c, d * RI : (d + 1) * RI], RP)


def add_tiles(res, back, nb, RI, lim):
    RP = back.shape[2]
    for d in range(nb):
        for c in range(TILES):
            both = back[d, c].astype(F32)
            for lo, hi, value in (
                (0, RP, both[:, :B]),
                (RP, RI, both[:, B:]),
            ):
                lo, hi = d * RI + lo, min(d * RI + hi, K * M)
                if lo >= hi:
                    continue
                mask = live(lim, c * HOP + lo // M, (hi - lo) // M)
                res[c, lo:hi] = (res[c, lo:hi] + value[: hi - lo]) * mask


def unpack_steps(rows, xs, T, RI):
    RP = rows.shape[1]

    def widen(t, _):
        both = rows[t].astype(F32)
        xs[pl.ds(pl.multiple_of(t * RI, 8), RP), :] = both[:, :B]
        if RI > RP:
            xs[pl.ds(pl.multiple_of(t * RI + RP, 8), RI - RP), :] = both[: RI - RP, B:]
        return 0

    lax.fori_loop(0, T, widen, 0, unroll=4 if T % 4 == 0 else 1)


def windows_of(mix, following, win):
    last = FRAMES + HOP + 1
    for i in range(1, BLOCKS):
        at = STRIDE * (i - 1)
        if at + 2 * STRIDE <= FRAMES * STRIDE:
            win[i * M : (i + 1) * M] = mix[:, at : at + 2 * STRIDE]
        elif at < FRAMES * STRIDE:
            win[i * M : (i + 1) * M] = jnp.concatenate([mix[:, at:], following[:, :STRIDE]], 1)
        elif i <= last:
            at -= FRAMES * STRIDE
            win[i * M : (i + 1) * M] = following[:, at : at + 2 * STRIDE]
        else:
            win[i * M :] = jnp.zeros(((BLOCKS - i) * M, 2 * STRIDE), F32)
            break


def softplus(value):
    return jnp.maximum(value, 0.0) + jnp.log1p(jnp.exp(-jnp.abs(value)))


def turned_out(proj, index):
    return proj[:, index * 2 * H : (index + 1) * 2 * H]


def intra_forward(shape, index, res, lim, gi, gr, slot, vectors, proj, x_out, h_out, c_out, scratch):
    wc, pg = scratch
    forward_weights(gi, gr, slot, wc)
    bias, (o_bias, gain, beta) = branch_vectors(vectors, index)
    n = shape.crows

    def inputs(g, r0):
        x = res[g, pl.ds(r0, n), :].astype(BF)
        x_out[pl.ds(pl.multiple_of(g * shape.size + r0, 16), n), :] = x
        return x

    branch_pregates(shape, inputs, wc, bias, pg)
    lstm_scan(shape, pg, wc, h_out, c_out)
    low_out = turned_out(proj, index).astype(BF)

    def close(g, i, r0):
        now = h_out[pl.ds(pl.multiple_of(g * shape.wide + r0 + shape.rows, 8), n), :].astype(BF)
        unit, _ = norm_parts(dot_turned(now, low_out) + o_bias)
        mask = live(lim, g * HOP + i * shape.chunk, shape.chunk)
        res[g, pl.ds(r0, n), :] = (res[g, pl.ds(r0, n), :] + (unit * gain + beta)) * mask

    chunk_loop(shape, close)


def inter_forward(shape, index, xs, gi, gr, slot, vectors, proj, h_out, c_out, scratch, use):
    wc, pg = scratch
    forward_weights(gi, gr, slot, wc)
    bias, (o_bias, gain, beta) = branch_vectors(vectors, index)
    n = shape.crows
    branch_pregates(shape, lambda g, r0: xs[pl.ds(r0, n), :], wc, bias, pg)
    lstm_scan(shape, pg, wc, h_out, c_out)
    low_out = turned_out(proj, index).astype(BF)

    def close(g, i, r0):
        now = h_out[pl.ds(pl.multiple_of(r0 + shape.rows, 8), n), :].astype(BF)
        unit, _ = norm_parts(dot_turned(now, low_out) + o_bias)
        use(i, r0, unit * gain + beta)

    chunk_loop(shape, close)


def zero_tail(res, c):
    if res.shape[1] > K * M:
        res[c, K * M :] = jnp.zeros((res.shape[1] - K * M, B), F32)


def encode(mix, following, leading, lim, proj, vectors, win, flat, bottle, res):
    flat[:M] = jnp.concatenate([leading[...], mix[:, :STRIDE]], 1)
    windows_of(mix, following, flat)
    win[...] = flat[...].astype(BF)
    w_enc = proj[:, BASE + N + B : BASE + N + B + 2 * STRIDE].astype(BF)
    w_bn = proj[:, BASE : BASE + N].astype(BF)
    gain, beta, b_bias = (pieces(vectors, j, 1) for j in range(3))
    for i in range(BLOCKS * M // CHUNK):
        at = i * CHUNK
        pre = dot_turned(win[at : at + CHUNK], w_enc)
        unit, _ = norm_parts(softplus(pre))
        normed = (unit * gain + beta).astype(BF)
        mask = live(lim, i * (CHUNK // M) - 1, CHUNK // M)
        bottle[at : at + CHUNK] = (dot_turned(normed, w_bn) + b_bias) * mask
    for c in range(TILES):
        res[c, : K * M] = bottle[(c * HOP + 1) * M : (c * HOP + 1 + K) * M]
        zero_tail(res, c)


def first_kernel(shape, nb, RI, mix, following, leading, lengths, proj, vectors, gi, gr, res, send, x_out, h_out, c_out, win, wc, pg, flat, bottle):
    lim = limits(lengths)
    encode(mix, following.at[0], leading, lim, proj, vectors, win, flat, bottle, res)
    intra_forward(shape, 0, res, lim, gi, gr, 0, vectors, proj, x_out, h_out, c_out, (wc, pg))
    send_tiles(res, send, nb, RI)


def third_kernel(shape, nb, RI, res_in, back, lengths, proj, vectors, gi, gr, res, send, x_out, h_out, c_out, wc, pg):
    lim = limits(lengths)
    res[...] = res_in[...]
    add_tiles(res, back, nb, RI, lim)
    intra_forward(shape, 2, res, lim, gi, gr, 0, vectors, proj, x_out, h_out, c_out, (wc, pg))
    send_tiles(res, send, nb, RI)


def inter_kernel(shape, RI, index, rows, proj, vectors, gi, gr, normed, h_out, c_out, wc, pg, xs):
    unpack_steps(rows, xs, shape.steps, RI)
    RP = normed.shape[1]

    def use(i, r0, value):
        for j in range(shape.chunk):
            normed[i * shape.chunk + j] = packed(value[j * RI : (j + 1) * RI], RP)

    inter_forward(shape, index, xs, gi, gr, 0, vectors, proj, h_out, c_out, (wc, pg), use)


EDGE = (HOP + 1) * M
EDGE_TOP = 208


def edge_pack(value):
    rest = jnp.concatenate([value[EDGE_TOP:], jnp.zeros((2 * EDGE_TOP - EDGE, B), F32)], 0)
    return jnp.concatenate([value[:EDGE_TOP], rest], 1)


def edge_unpack(ref):
    return jnp.concatenate([ref[:, :B], ref[: EDGE - EDGE_TOP, B:]], 0)


def parts_of(res, part):
    half = HOP * M
    part[:half] = res[0, :half]
    for c in range(1, TILES):
        part[c * half : (c + 1) * half] = res[c, :half] + res[c - 1, half : 2 * half]
    part[TILES * half :] = res[TILES - 1, half : 2 * half]


def part_kernel(nb, RI, res_in, back, lengths, part, up, down, res):
    res[...] = res_in[...]
    add_tiles(res, back, nb, RI, limits(lengths))
    parts_of(res, part)
    half = HOP * M
    up[...] = edge_pack(part[TILES * half - M :])
    down[...] = edge_pack(part[: half + M])


def middle_kernel(nb, RI, part, before, after, lengths, win, goal, following, proj, vectors, send, gres, genc, gm, *scratch):
    edge = jnp.where(lax.axis_index("block") > 0, 1.0, 0.0)
    middle(
        part, edge_unpack(before), edge_unpack(after), limits(lengths), edge, win, goal,
        following.at[1], proj, vectors, gres, genc, gm, *scratch,
    )
    send_tiles(gres, send, nb, RI)


def middle(part, early, late, lim, edge, win, goal, following, proj, vectors, gres, genc, gm, feats, dec, tgt, gest, enc, gate, src, act):
    half = HOP * M
    top = M + TILES * half
    total = BLOCKS * M
    feats[:M] = early[:M]
    feats[M : M + half] = part[:half] + early[M:]
    feats[M + half : top] = part[half : TILES * half]
    feats[top : top + half] = part[TILES * half :] + late[:half]
    feats[top + half : top + half + M] = late[half:]
    feats[top + half + M :] = jnp.zeros((PADDED * M - top - half - M, B), F32)
    low_mask = proj[:, BASE + N : BASE + N + B].astype(BF)
    w_enc = proj[:, BASE + N + B : BASE + N + B + 2 * STRIDE].astype(BF)
    low_dec = proj[:, BASE + N + B + 2 * STRIDE : BASE + N + B + 4 * STRIDE].astype(BF)
    m_bias = pieces(vectors, vectors.shape[0] * 2 - 1, 1)
    root = 0.7978845608028654
    cube = 0.044715
    dec[total:] = jnp.zeros((PADDED * M - total, 2 * STRIDE), F32)
    for i in range(total // CHUNK):
        rows = slice(i * CHUNK, (i + 1) * CHUNK)
        x = feats[rows]
        low = (0.5 * x * (1.0 + jnp.tanh(root * (x + cube * x * x * x)))).astype(BF)
        encoded = softplus(dot_turned(win[rows], w_enc))
        mask = 0.5 * jnp.tanh(0.5 * (dot_turned(low, low_mask) + m_bias)) + 0.5
        source = (mask * encoded).astype(BF)
        enc[rows] = encoded
        gate[rows] = mask
        src[rows] = source.astype(F32)
        act[rows] = low.astype(F32)
        dec[rows] = dot(source, low_dec)
    dec[:M] = dec[:M] * edge
    for ref in (enc, gate, src, act):
        ref[total:] = jnp.zeros((PADDED * M - total, B), F32)
    for i in range(1, FRAMES + 1):
        tgt[i * M : (i + 1) * M] = goal[:, STRIDE * (i - 1) : STRIDE * i]
    for i in range(FRAMES + 1, FRAMES + HOP + 2):
        at = STRIDE * (i - 1 - FRAMES)
        tgt[i * M : (i + 1) * M] = following[:, at : at + STRIDE]
    tgt[(FRAMES + HOP + 2) * M :] = jnp.zeros(((PADDED - FRAMES - HOP - 2) * M, STRIDE), F32)
    estimate = dec[M:total, :STRIDE] + dec[: total - M, STRIDE:]
    count = BLOCKS - 1
    spot = lax.broadcasted_iota(jnp.int32, (count, M, STRIDE), 0)
    phase = lax.broadcasted_iota(jnp.int32, (count, M, STRIDE), 2)
    near = spot < FRAMES + HOP + 1
    valid = jnp.where(near & (spot * STRIDE + phase < lim[:, :STRIDE][None]), 1.0, 0.0)
    inside = jnp.where(spot < FRAMES, valid, 0.0).reshape(count * M, STRIDE)
    valid = valid.reshape(count * M, STRIDE)
    error = estimate - tgt[M:total]
    smoothed = jnp.sqrt(error * error + 1.0)
    gest[:M] = jnp.zeros((M, STRIDE), F32)
    gest[M:total] = valid * error / smoothed
    gest[total:] = jnp.zeros((PADDED * M - total, STRIDE), F32)
    loss = jnp.sum(jnp.sum(inside * (smoothed - 1.0), 0, keepdims=True), 1, keepdims=True)
    seen = jnp.sum(jnp.sum(inside, 0, keepdims=True), 1, keepdims=True)
    gm[...] = jnp.zeros_like(gm)
    gm[132:133] = jnp.broadcast_to(loss, (1, LANES))
    gm[133:134] = jnp.broadcast_to(seen, (1, LANES))
    for i in range(total // CHUNK):
        at = i * CHUNK + M
        rows = slice(at, at + CHUNK)
        grad_dec = jnp.concatenate([gest[rows], gest[at + M : at + M + CHUNK]], 1).astype(BF)
        mine = own(i * (CHUNK // M), CHUNK // M)
        mine_low = mine.astype(BF)
        gm[64:128, 16:32] += dot_rows(src[rows].astype(BF) * mine_low, grad_dec)
        grad_source = dot_turned(grad_dec, low_dec)
        mask = gate[rows]
        grad_logit = (grad_source * enc[rows] * mask * (1.0 - mask)).astype(BF)
        enc[rows] = grad_source * mask
        gm[:64, 64:] += dot_rows(grad_logit * mine_low, act[rows].astype(BF))
        gm[131:132, :B] += jnp.sum(grad_logit.astype(F32) * mine, 0, keepdims=True)
        x = feats[rows]
        curve = jnp.tanh(root * (x + cube * x * x * x))
        slope = 0.5 * (1.0 + curve) + (0.5 * root) * x * (1.0 - curve * curve) * (
            1.0 + (3.0 * cube) * x * x
        )
        feats[rows] = slope * dot(grad_logit, low_mask)
    genc[...] = enc[M : M + FRAMES * M]
    for c in range(TILES):
        gres[c, : K * M] = feats[M + c * half : M + c * half + K * M] * live(lim, c * HOP, K)
        zero_tail(gres, c)


def inter_back(shape, index, gs, xs, h_ref, c_ref, proj, vectors, gi, gr, slot, out, core, use):
    n = shape.crows
    last = branch_back(
        shape,
        lambda g, r0: gs[pl.ds(r0, n), :],
        lambda g, r0: xs[pl.ds(r0, n), :],
        h_ref, c_ref, (gi, gr), slot, branch_vectors(vectors, index), turned_out(proj, index), out, core,
    )
    last(use)


def inter_back_kernel(shape, RI, index, grad_rows, rows, h_ref, c_ref, proj, vectors, gi, gr, send, out, *scratch):
    xs, gs, core = scratch[0], scratch[1], scratch[2:]
    unpack_steps(rows, xs, shape.steps, RI)
    unpack_steps(grad_rows, gs, shape.steps, RI)
    RP = send.shape[1]

    def use(g, i, r0, total):
        for j in range(shape.chunk):
            send[i * shape.chunk + j] = packed(total[j * RI : (j + 1) * RI], RP)

    inter_back(shape, index, gs, xs, h_ref, c_ref, proj, vectors, gi, gr, 0, out, core, use)


def intra_back(shape, index, gres, x_ref, h_ref, c_ref, proj, vectors, gi, gr, slot, out, core):
    n = shape.crows

    def inputs(g, r0):
        return x_ref[pl.ds(pl.multiple_of(g * shape.size + r0, 16), n), :]

    last = branch_back(
        shape,
        lambda g, r0: gres[g, pl.ds(r0, n), :],
        inputs,
        h_ref, c_ref, (gi, gr), slot, branch_vectors(vectors, index), turned_out(proj, index), out, core,
    )

    def use(g, i, r0, total):
        gres[g, pl.ds(r0, n), :] = gres[g, pl.ds(r0, n), :] + total

    last(use)


def third_back_kernel(shape, nb, RI, gres_in, back, lengths, x_ref, h_ref, c_ref, proj, vectors, gi, gr, gres, send, out, *core):
    lim = limits(lengths)
    gres[...] = gres_in[...]
    add_tiles(gres, back, nb, RI, lim)
    intra_back(shape, 2, gres, x_ref, h_ref, c_ref, proj, vectors, gi, gr, 0, out, core)
    for c in range(TILES):
        gres[c, : K * M] = gres[c, : K * M] * live(lim, c * HOP, K)
    send_tiles(gres, send, nb, RI)


def first_back_kernel(shape, nb, RI, gres_in, back, lengths, x_ref, h_ref, c_ref, proj, vectors, gi, gr, win, genc, gm, more_in, out, more, gres, bottle, *core):
    lim = limits(lengths)
    more[...] = more_in[...]
    gres[...] = gres_in[...]
    add_tiles(gres, back, nb, RI, lim)
    intra_back(shape, 0, gres, x_ref, h_ref, c_ref, proj, vectors, gi, gr, 0, out, core)
    encode_back(gres, lim, proj, vectors, win, genc, gm, out, more, bottle)


def encode_back(gres, lim, proj, vectors, win, genc, gm, out, more, bottle):
    at_first, at_vecs = ROWS_MORE, ROWS_MORE + B
    out[at_first : at_first + B] = gm[:B]
    out[at_vecs : at_vecs + 8] = gm[2 * B :]
    more[at_first : at_first + B] = gm[B : 2 * B]
    bottle[...] = jnp.zeros(bottle.shape, F32)
    for c in range(TILES):
        at = (c * HOP + 1) * M
        bottle[at : at + K * M] += gres[c, : K * M]
    w_enc = proj[:, BASE + N + B : BASE + N + B + 2 * STRIDE].astype(BF)
    w_bn = proj[:, BASE : BASE + N].astype(BF)
    gain, beta = (pieces(vectors, j, 1) for j in range(2))
    own_rows = FRAMES * M
    for i in range(BLOCKS * M // CHUNK):
        at = i * CHUNK
        rows = slice(at, at + CHUNK)
        pre = dot_turned(win[rows], w_enc)
        unit, scale = norm_parts(softplus(pre))
        normed = (unit * gain + beta).astype(BF)
        low = (bottle[rows] * live(lim, i * (CHUNK // M) - 1, CHUNK // M)).astype(BF)
        out[at_first : at_first + B, :N] += dot_rows(low, normed)
        grad_normed = dot(low, w_bn)
        for j, value in enumerate((grad_normed * unit, grad_normed, low.astype(F32))):
            out[at_vecs + j : at_vecs + j + 1, :B] += jnp.sum(value, 0, keepdims=True)
        grad_enc = norm_back(grad_normed, unit, scale, gain)
        lo, hi = max(at - M, 0), min(at + CHUNK - M, own_rows)
        if lo < hi:
            piece = genc[lo:hi]
            above, below = lo + M - at, at + CHUNK - M - hi
            if above:
                piece = jnp.concatenate([jnp.zeros((above, B), F32), piece], 0)
            if below:
                piece = jnp.concatenate([piece, jnp.zeros((below, B), F32)], 0)
            grad_enc = grad_enc + piece
        grad_pre = (grad_enc * (0.5 * jnp.tanh(0.5 * pre) + 0.5)).astype(BF)
        more[at_first : at_first + B, :16] += dot_rows(grad_pre, win[rows])


def turn_in(res, xs, RI, lowered=True):
    for j in range(M):
        for c in range(TILES):
            at = (TILES * j + c) * RI
            value = res[c, pl.ds(j, K, stride=M), :]
            xs[at : at + K] = value.astype(BF).astype(F32)


def turn_back(res, xs, RI, length):
    pos = lax.broadcasted_iota(jnp.int32, (K, B), 0)
    for j in range(M):
        for c in range(TILES):
            at = (TILES * j + c) * RI
            mask = jnp.where((pos + (FRAMES * j + HOP * c)) * STRIDE < length, 1.0, 0.0)
            where = (c, pl.ds(j, K, stride=M), slice(None))
            res[where] = (res[where] + xs[at : at + K]) * mask


class Strip:
    def __init__(self, ref, part, lane, rows, width):
        self.ref, self.part, self.lane, self.shape = ref, part, lane, (rows, width)

    def where(self, index):
        index = index if isinstance(index, tuple) else (index,)
        if index[0] is Ellipsis:
            index = ()
        spans = []
        for i, size in enumerate(self.shape):
            start, stop, _ = (index[i] if i < len(index) else slice(None)).indices(size)
            spans.append((start, stop))
        (top, end), (left, right) = spans
        return (self.part, slice(top, end), slice(self.lane + left, self.lane + right))

    def __getitem__(self, index):
        return self.ref[self.where(index)]

    def __setitem__(self, index, value):
        self.ref[self.where(index)] = value


def local_kernel(intra, inter, RI, waves, lengths, proj, vectors, gi_in, gr_in, outs_to, notes, *scratch):
    gi, gr, outs, sem = scratch[:4]
    scratch = scratch[4:]
    maps = [pltpu.make_async_copy(gi_in, gi, sem.at[0]), pltpu.make_async_copy(gr_in, gr, sem.at[1])]
    for copy in maps:
        copy.start()

    def leave(r):
        rows = pl.ds(r * ROWS_G, ROWS_G)
        copy = pltpu.make_async_copy(outs.at[rows], outs_to.at[rows], sem.at[2 + r])
        copy.start()
        return copy

    win, res, nrm, genc, gm = scratch[:5]
    x0, h0, c0, x1, h1, c1, x2, h2, c2, x3, h3, c3 = scratch[5:17]
    wc, wit, wrt, wot, z, dh = scratch[17:]

    def strip(d, lane, rows, width):
        return Strip(z, d, lane * LANES, rows, width)

    tall = PADDED * M
    feats, dec = strip(0, 0, tall, B), strip(0, 1, tall, 2 * STRIDE)
    tgt, gest = strip(0, 2, tall, STRIDE), strip(0, 3, tall, STRIDE)
    enc, gate, src, act = (strip(1, i, tall, B) for i in range(4))
    part = strip(1, 3, (FRAMES + HOP) * M, B)
    bottle, flat = strip(0, 0, BLOCKS * M, B), strip(0, 1, BLOCKS * M, 2 * STRIDE)
    core = (wc, wit, wrt, wot, z, dh)
    out0, out1, out2, out3 = (outs.at[pl.ds(r * ROWS_G, ROWS_G)] for r in range(4))
    length = lengths[lax.axis_index("block")]
    lim = length - lax.broadcasted_iota(jnp.int32, (M, B), 0) * (FRAMES * STRIDE)
    reach = (HOP + 2) * STRIDE
    span = FRAMES * STRIDE
    goal_at = waves.shape[1] // 2
    mix = waves[:, :span]
    goal = waves[:, goal_at : goal_at + span]

    def after(value):
        return jnp.concatenate([value[1:], jnp.zeros((1, value.shape[1]), F32)], 0)

    def before(value):
        return jnp.concatenate([jnp.zeros((1, value.shape[1]), F32), value[:-1]], 0)

    for ref in (x1, x3, nrm):
        ref[...] = jnp.zeros_like(ref)
    encode(mix, after(mix[:, :reach]), before(mix[:, span - STRIDE :]), lim, proj, vectors, win, flat, bottle, res)
    for copy in maps:
        copy.wait()

    def inter_layer(index, xs, h, c):
        turn_in(res, xs, RI)

        def use(i, r0, value):
            nrm[pl.ds(r0, inter.crows), :] = value.astype(BF).astype(F32)

        inter_forward(inter, index, xs, gi, gr, index, vectors, proj, h, c, (wc, z), use)
        turn_back(res, nrm, RI, length)

    intra_forward(intra, 0, res, lim, gi, gr, 0, vectors, proj, x0, h0, c0, (wc, z))
    inter_layer(1, x1, h1, c1)
    intra_forward(intra, 2, res, lim, gi, gr, 2, vectors, proj, x2, h2, c2, (wc, z))
    inter_layer(3, x3, h3, c3)

    parts_of(res, part)
    half = HOP * M
    row = lax.broadcasted_iota(jnp.int32, (EDGE, B), 0) % M
    early = jnp.where(row == 0, 0.0, before(part[TILES * half - M :]))
    late = jnp.where(row == M - 1, 0.0, after(part[: half + M]))
    edge = jnp.where(lax.broadcasted_iota(jnp.int32, (M, 2 * STRIDE), 0) == 0, 0.0, 1.0)
    middle(
        part, early, late, lim, edge, win, goal, after(goal[:, :reach]), proj, vectors, res, genc, gm,
        feats, dec, tgt, gest, enc, gate, src, act,
    )

    def inter_layer_back(index, xs, h, c, out):
        for j in range(M):
            for t in range(TILES):
                at = (TILES * j + t) * RI
                nrm[at + K : at + RI] = jnp.zeros((RI - K, B), F32)
        turn_in(res, nrm, RI)

        def use(g, i, r0, total):
            nrm[pl.ds(r0, inter.crows), :] = total.astype(BF).astype(F32)

        inter_back(inter, index, nrm, xs, h, c, proj, vectors, gi, gr, index, out, core, use)
        turn_back(res, nrm, RI, length)

    inter_layer_back(3, x3, h3, c3, out3)
    left = [leave(3)]
    intra_back(intra, 2, res, x2, h2, c2, proj, vectors, gi, gr, 2, out2, core)
    left.append(leave(2))
    for c in range(TILES):
        res[c, : K * M] = res[c, : K * M] * live(lim, c * HOP, K)
    inter_layer_back(1, x1, h1, c1, out1)
    intra_back(intra, 0, res, x0, h0, c0, proj, vectors, gi, gr, 0, out0, core)
    encode_back(res, lim, proj, vectors, win, genc, gm, out0, out1, bottle)
    left += [leave(1), leave(0)]

    def widest(i, best):
        rows = outs[pl.ds(pl.multiple_of(i * 256, 256), 256), :]
        return jnp.maximum(best, jnp.max(jnp.abs(rows).reshape(32, 8, LANES), 0))

    best = lax.fori_loop(0, outs.shape[0] // 256, widest, jnp.zeros((8, LANES), F32))
    best = jnp.max(jnp.max(best, 0, keepdims=True), 1, keepdims=True)
    notes[...] = note_rows(best, gm[132:133], gm[133:134])
    for copy in left:
        copy.wait()


def local_scratch(intra, inter):
    first = [
        pltpu.VMEM((2 * LAYERS, 2, B, 4 * H), F32),
        pltpu.VMEM((2 * LAYERS, 2, H, 4 * H), F32),
        pltpu.VMEM((4 * ROWS_G, LANES), F32),
        pltpu.SemaphoreType.DMA((6,)),
        pltpu.VMEM((BLOCKS * M, 2 * STRIDE), BF),
        pltpu.VMEM((TILES, K * M, B), F32),
        pltpu.VMEM((inter.size, B), F32),
        pltpu.VMEM((FRAMES * M, B), F32),
        pltpu.VMEM((136, LANES), F32),
    ]
    kept = []
    for shape, kind in ((intra, BF), (inter, F32)) * 2:
        state = pltpu.VMEM((shape.groups * shape.wide, 2 * H), F32)
        kept += [pltpu.VMEM((shape.groups * shape.size, B), kind), state, state]
    return first + kept + back_scratch(inter)


def note_rows(widest, loss, count):
    row = lax.broadcasted_iota(jnp.int32, (8, LANES), 0)
    power = jnp.floor(jnp.log(jnp.maximum(widest, 1e-30)) * 1.4426950408889634)
    return jnp.where(row == 0, power, jnp.where(row == 1, loss, jnp.where(row == 2, count, 0.0)))


def adam_parts(grad, moment, square, weight, average, decay):
    moment = BETA_ONE * moment + (1.0 - BETA_ONE) * grad
    square = BETA_TWO * square + (1.0 - BETA_TWO) * grad * grad
    corrected = moment * (1.0 / (1.0 - BETA_ONE**STEP))
    scaled = square * (1.0 / (1.0 - BETA_TWO**STEP))
    weight = weight - RATE * (corrected / (jnp.sqrt(scaled) + ADAM_EPS) + decay * weight)
    average = KEEP * average + (1.0 - KEEP) * weight
    return moment, square, weight, average, weight.astype(BF)


def adam_kernel(*refs):
    near, far, totals, old = refs[0], refs[1], refs[2], refs[3:19]
    scalars, new = refs[19], refs[20:40]
    gv, sums, sem = refs[40:43]
    ready = [refs[43 + 5 * kind : 48 + 5 * kind] for kind in range(4)]
    copies = {}
    mine = lax.axis_index("dp") & 1
    pieces_half = (near.shape[0] - sums.shape[0] // 2) // NOTES
    size = sums.shape[0] // 2 // pieces_half
    for i in range(pieces_half):
        at = i * (size + NOTES)
        for ref, place in ((near, mine), (far, 1 - mine)):
            to = pl.multiple_of((place * pieces_half + i) * size, 16)
            scale = jnp.exp2(ref[at + size : at + size + 1, :] - TOP)
            sums[pl.ds(to, size), :] = ref[at : at + size] * scale
    gs = [sums.at[pl.ds(r * ROWS_G, ROWS_G)] for r in range(4)]
    vecs = ROWS_MORE + B
    gv[:1] = jnp.concatenate([gs[0][vecs : vecs + 1, :N], gs[0][vecs + 1 : vecs + 2, :N]], 1)
    gv[1:2, :N] = gs[0][vecs + 2 : vecs + 3, :N]
    gv[gv.shape[0] - 1 :, N:] = gs[0][vecs + 3 : vecs + 4, :N]
    for r in range(4):
        at = 3 + 19 * r
        rows = [
            gs[r][ROWS_VECS + j : ROWS_VECS + j + 1, k * N : (k + 1) * N] for j in range(8) for k in range(2)
        ]
        rows += [gs[r][ROWS_VECS + j : ROWS_VECS + j + 1, :N] for j in range(8, 11)]
        for j, row in enumerate(rows):
            q = at + j
            gv[q // 2 : q // 2 + 1, (q % 2) * N : (q % 2 + 1) * N] = row
    part = jnp.zeros((8, LANES), F32)
    pieces_of = [gs[r][:ROWS_VECS] for r in range(4)]
    pieces_of += [gs[r][ROWS_MORE : ROWS_MORE + B] for r in range(2)] + [gv[...]]
    for piece in pieces_of:
        value = piece.reshape(piece.shape[0] // 8, 8, LANES)
        part = part + jnp.sum(value * value, 0)
    squared = jnp.sum(jnp.sum(part, 0, keepdims=True), 1, keepdims=True)
    loss, count = totals[0:1, :1], totals[1:2, :1]
    norm = jnp.sqrt(squared) / count
    factor = jnp.minimum(1.0, CLIP / norm) / count
    row = lax.broadcasted_iota(jnp.int32, (8, LANES), 0)
    scalars[...] = jnp.where(row == 0, loss, jnp.where(row == 1, count, norm))

    def update(kind, index, grad, decay, slot=()):
        results = adam_parts(
            grad * factor,
            old[4 + kind][index],
            old[8 + kind][index],
            old[kind][index],
            old[12 + kind][index],
            decay,
        )
        for ref, value in zip(ready[kind], results):
            ref[slot + index[1:] if slot else index] = value

    def send(kind, r=None):
        for j, ref in enumerate(ready[kind]):
            to = new[4 * j + kind]
            if r is None:
                number = 40 + 5 * (kind - 2) + j
            else:
                ref, to, number = ref.at[r % 2], to.at[r], 10 * r + 5 * kind + j
            copies[kind, r, j] = pltpu.make_async_copy(ref, to, sem.at[number])
            copies[kind, r, j].start()

    def finish(kind, r=None):
        for j in range(5):
            copies.pop((kind, r, j)).wait()

    for r in range(4):
        if r >= 2:
            finish(0, r - 2)
            finish(1, r - 2)
        for d in range(2):
            for j in range(4):
                lanes = slice(j * LANES, (j + 1) * LANES)
                at = j * 384 + d * B
                update(0, (r, d, slice(None), lanes), gs[r][at : at + B], DECAY, (r % 2,))
                at = j * 384 + 128 + d * H
                update(1, (r, d, slice(None), lanes), gs[r][at : at + H], DECAY, (r % 2,))
        send(0, r)
        send(1, r)
        for j in range(2):
            at = ROWS_MAPS + j * B
            lanes = slice(r * 2 * H + j * LANES, r * 2 * H + (j + 1) * LANES)
            update(2, (slice(None), lanes), gs[r][at : at + B], DECAY)
    more = slice(ROWS_MORE, ROWS_MORE + B)
    update(2, (slice(None), slice(BASE, BASE + LANES)), gs[0][more], DECAY)
    update(2, (slice(None), slice(BASE + LANES, BASE + LANES + 32)), gs[1][more, :32], DECAY)
    send(2)
    update(3, (slice(None), slice(None)), gv[...], 0.0)
    send(3)
    for kind in (0, 1):
        for r in (2, 3):
            finish(kind, r)
    finish(2)
    finish(3)


def call(kernel, outs, ins, scratch, index=None, limit=56, micros=20, apart=(), given=()):
    vmem = pl.BlockSpec(memory_space=pltpu.VMEM)
    specs = [
        pl.BlockSpec(memory_space=pltpu.SMEM) if a.ndim == 1 and a.dtype == jnp.int32 else vmem
        for a in ins
    ]
    for i in apart:
        specs[i] = pl.BlockSpec(memory_space=pl.ANY)
    extra = []
    wrapped = kernel
    if index is not None:
        big = [i for i, a in enumerate(ins) if a.ndim == 4 and a.shape[:2] == (2 * LAYERS, 2)]
        for i in big:
            specs[i] = pl.BlockSpec(memory_space=pl.ANY)
        extra = [pltpu.VMEM((1,) + ins[i].shape[1:], F32) for i in big]
        extra.append(pltpu.SemaphoreType.DMA((len(big),)))

        def wrapped(*refs):
            refs = list(refs)
            held, sem = refs[len(refs) - len(extra) : -1], refs[-1]
            copies = []
            for j, i in enumerate(big):
                copies.append(pltpu.make_async_copy(refs[i].at[pl.ds(index, 1)], held[j], sem.at[j]))
                copies[-1].start()
            for copy in copies:
                copy.wait()
            for j, i in enumerate(big):
                refs[i] = held[j]
            kernel(*refs[: len(refs) - len(extra)])

    return pl.pallas_call(
        wrapped,
        out_shape=outs,
        in_specs=specs,
        out_specs=[
            pl.BlockSpec(memory_space=pl.ANY) if i in given else vmem for i in range(len(outs))
        ],
        scratch_shapes=list(scratch) + extra,
        compiler_params=pltpu.CompilerParams(vmem_limit_bytes=limit * 1024 * 1024),
        cost_estimate=pl.CostEstimate(
            flops=micros * 10**9, bytes_accessed=micros * 10**6, transcendentals=0
        ),
    )(*ins)


def shift(block, axis, distance):
    size = lax.axis_size(axis)
    route = [(i, i + distance) for i in range(size) if 0 <= i + distance < size]
    return lax.ppermute(block, axis, route)


def exchange(block):
    return lax.all_to_all(block, "block", split_axis=0, concat_axis=0, tiled=True)


def flip(block, bit):
    size = lax.axis_size("dp")
    return lax.ppermute(block, "dp", [(i, i ^ (1 << bit)) for i in range(size)])


def bits():
    return lax.axis_size("dp").bit_length() - 1


def bits():
    return lax.axis_size("dp").bit_length() - 1


def noted(power, loss, count):
    row = lax.broadcasted_iota(jnp.int32, (NOTES, LANES), 0)
    rows = jnp.where(row == 0, power, 0.0)
    for first, value in ((1, loss), (5, count)):
        rest = value * (1.0 / 1024.0**2)
        for j in range(4):
            digit = jnp.floor(rest) if j < 3 else rest
            rows = jnp.where(row == first + j, digit, rows)
            rest = (rest - digit) * 1024.0
    return rows.astype(HALF)


def scaled(value, power):
    return (value * jnp.exp2(TOP - power)).astype(HALF)


def read_notes(rows):
    rows = rows.astype(F32)
    power, *digits = (rows[..., i : i + 1, :] for i in range(9))
    loss, count = (
        (d[0] * 1024.0 + d[1]) * 1024.0 + (d[2] + d[3] * (1.0 / 1024.0))
        for d in (digits[:4], digits[4:])
    )
    return power, loss, count


def cut(block, start, size):
    return lax.dynamic_slice_in_dim(block, start, size, 0)


def gradient_sums(block, notes):
    nb = lax.axis_size("block")
    size = block.shape[0] // 2
    mine = lax.axis_index("dp") & 1
    other = flip(jnp.concatenate([cut(block, (1 - mine) * size, size), notes], 0), 0)
    power = jnp.maximum(notes[0:1], other[size : size + 1]) + 1.0
    loss, count = (notes[i : i + 1] + other[size + i : size + i + 1] for i in (1, 2))
    base = mine * size

    def take(start, rows):
        return cut(block, base + start, rows) + cut(other, start, rows)

    for bit in range(1, bits()):
        size //= 2
        mine = (lax.axis_index("dp") >> bit) & 1
        given = jnp.concatenate(
            [scaled(take((1 - mine) * size, size), power), noted(power, loss, count)], 0
        )
        given = flip(given, bit)
        its_power, its_loss, its_count = read_notes(given[size:])

        def take(start, rows, take=take, given=given, base=mine * size, its_power=its_power):
            come = cut(given, start, rows).astype(F32) * jnp.exp2(its_power - TOP)
            return take(base + start, rows) + come

        loss, count = loss + its_loss, count + its_count
        power = jnp.maximum(power, its_power) + 1.0
    part = size // nb
    notes = jnp.broadcast_to(noted(power, loss, count)[None], (nb, NOTES, LANES))
    pieces = exchange(
        jnp.concatenate([scaled(take(0, size), power).reshape(nb, part, LANES), notes], 1)
    )
    powers, losses, counts = read_notes(pieces[:, part:])
    block = jnp.sum(pieces[:, :part].astype(F32) * jnp.exp2(powers - TOP), 0)
    loss, count = jnp.sum(losses, 0), jnp.sum(counts, 0)
    power = jnp.max(powers, 0) + (nb - 1).bit_length()
    mine = jnp.concatenate([scaled(block, power), noted(power, loss, count)], 0)
    block = exchange(jnp.broadcast_to(mine[None], (nb,) + mine.shape))
    for bit in reversed(range(1, bits())):
        mine = (lax.axis_index("dp") >> bit) & 1
        other = flip(block, bit)
        block = jnp.where(
            mine == 0, jnp.concatenate([block, other], 0), jnp.concatenate([other, block], 0)
        )
    other = flip(block, 0)
    row = lax.broadcasted_iota(jnp.int32, (8, LANES), 0)
    totals = jnp.where(row == 0, loss, count)
    return [half.reshape(-1, LANES).astype(F32) for half in (block, other)] + [totals]


def shared_step(mixture, target, lengths, proj, vectors_wide, gi, gr):
    nb = lax.axis_size("block")
    RI = -(-K // nb) * M
    intra = Shape(TILES, K, M)
    inter = Shape(1, TILES * nb, RI)
    T = inter.steps
    reach = (HOP + 2) * STRIDE
    following = shift(jnp.stack([mixture[:, :reach], target[:, :reach]]), "block", -1)
    leading = shift(mixture[:, -STRIDE:], "block", 1)

    RP = -(-RI // 16) * 8
    res_shape = SDS((TILES, nb * RI, B), F32)
    send_shape = SDS((nb, TILES, RP, 2 * B), BF)
    steps_shape = SDS((T, RP, 2 * B), BF)
    x_shape = SDS((TILES * K * M, B), BF)

    def state(shape):
        return SDS((shape.groups * shape.wide, 2 * H), F32)

    res0, send, x0, h0, c0, win = call(
        functools.partial(first_kernel, intra, nb, RI),
        [res_shape, send_shape, x_shape, state(intra), state(intra), SDS((BLOCKS * M, 2 * STRIDE), BF)],
        [mixture, following, leading, lengths, proj, vectors_wide, gi, gr],
        fwd_scratch(intra)
        + [pltpu.VMEM((BLOCKS * M, 2 * STRIDE), F32), pltpu.VMEM((BLOCKS * M, B), F32)],
        0,
    )

    def inter_step(send, index):
        rows = exchange(send).reshape(T, RP, 2 * B)
        normed, h, c = call(
            functools.partial(inter_kernel, inter, RI, index),
            [steps_shape, state(inter), state(inter)],
            [rows, proj, vectors_wide, gi, gr],
            fwd_scratch(inter) + [pltpu.VMEM((inter.size, B), F32)],
            index,
        )
        return rows, h, c, exchange(normed.reshape(send_shape.shape))

    rows1, h1, c1, back = inter_step(send, 1)
    res2, send, x2, h2, c2 = call(
        functools.partial(third_kernel, intra, nb, RI),
        [res_shape, send_shape, x_shape, state(intra), state(intra)],
        [res0, back, lengths, proj, vectors_wide, gi, gr],
        fwd_scratch(intra),
        2,
    )
    rows3, h3, c3, back = inter_step(send, 3)
    edge_shape = SDS((EDGE_TOP, 2 * B), F32)
    part, up, down = call(
        functools.partial(part_kernel, nb, RI),
        [SDS(((FRAMES + HOP) * M, B), F32), edge_shape, edge_shape],
        [res2, back, lengths],
        [pltpu.VMEM(res_shape.shape, F32)],
    )
    before = shift(up, "block", 1)
    after = shift(down, "block", -1)
    tall = PADDED * M
    send, gres, genc, gm = call(
        functools.partial(middle_kernel, nb, RI),
        [send_shape, res_shape, SDS((FRAMES * M, B), F32), SDS((136, LANES), F32)],
        [part, before, after, lengths, win, target, following, proj, vectors_wide],
        [
            pltpu.VMEM((tall, B), F32),
            pltpu.VMEM((tall, 2 * STRIDE), F32),
            pltpu.VMEM((tall, STRIDE), F32),
            pltpu.VMEM((tall, STRIDE), F32),
            pltpu.VMEM((tall, B), F32),
            pltpu.VMEM((tall, B), F32),
            pltpu.VMEM((tall, B), F32),
            pltpu.VMEM((tall, B), F32),
        ],
    )
    out_shape = SDS((ROWS_G, LANES), F32)

    def inter_back(send, rows, h, c, index):
        grad_rows = exchange(send).reshape(T, RP, 2 * B)
        send, out = call(
            functools.partial(inter_back_kernel, inter, RI, index),
            [steps_shape, out_shape],
            [grad_rows, rows, h, c, proj, vectors_wide, gi, gr],
            [pltpu.VMEM((inter.size, B), F32)] * 2 + back_scratch(inter),
            index,
        )
        return exchange(send.reshape(send_shape.shape)), out

    back, out3 = inter_back(send, rows3, h3, c3, 3)
    gres, send, out2 = call(
        functools.partial(third_back_kernel, intra, nb, RI),
        [res_shape, send_shape, out_shape],
        [gres, back, lengths, x2, h2, c2, proj, vectors_wide, gi, gr],
        back_scratch(intra),
        2,
    )
    back, out1 = inter_back(send, rows1, h1, c1, 1)
    out0, out1 = call(
        functools.partial(first_back_kernel, intra, nb, RI),
        [out_shape, out_shape],
        [gres, back, lengths, x0, h0, c0, proj, vectors_wide, gi, gr, win, genc, gm, out1],
        [pltpu.VMEM(res_shape.shape, F32), pltpu.VMEM((BLOCKS * M, B), F32)] + back_scratch(intra),
        0,
    )
    parts = nb * lax.axis_size("dp") * NOTES
    more = jnp.zeros((-4 * ROWS_G % parts, LANES), F32)
    outs = jnp.concatenate([out0, out1, out2, out3, more], 0)
    at = ROWS_MORE + B + 4
    return outs, note_rows(jnp.max(jnp.abs(outs)), outs[at : at + 1], outs[at + 1 : at + 2])


def local_step(mixture, target, lengths, proj, vectors_wide, gi, gr):
    RI = -(-K // M) * M
    intra = Shape(TILES, K, M)
    inter = Shape(1, TILES * M, RI)
    pad = jnp.zeros((M, -(FRAMES * STRIDE) % LANES), F32)
    waves = jnp.concatenate([mixture, pad, target, pad], 1)
    waves = lax.all_to_all(waves.reshape(M, 1, -1), "block", split_axis=0, concat_axis=0, tiled=True)
    return call(
        functools.partial(local_kernel, intra, inter, RI),
        [SDS((4 * ROWS_G, LANES), F32), SDS((8, LANES), F32)],
        [waves.reshape(M, -1), lengths, proj, vectors_wide, gi, gr],
        local_scratch(intra, inter),
        limit=62,
        apart=(4, 5),
        given=(0,),
    )


def body(
    mixture,
    target,
    lengths,
    input_gates,
    recur_gates,
    projections,
    vectors,
    moment_input,
    moment_recur,
    moment_proj,
    moment_vecs,
    square_input,
    square_recur,
    square_proj,
    square_vecs,
    average_input,
    average_recur,
    average_proj,
    average_vecs,
):
    nb = lax.axis_size("block")
    proj = projections.T
    vectors_wide = vectors.reshape(-1, LANES)
    step = local_step if nb == M else shared_step
    outs, notes = step(mixture, target, lengths, proj, vectors_wide, input_gates, recur_gates)
    sums = gradient_sums(outs, notes)
    old = [
        input_gates, recur_gates, projections, vectors,
        moment_input, moment_recur, moment_proj, moment_vecs,
        square_input, square_recur, square_proj, square_vecs,
        average_input, average_recur, average_proj, average_vecs,
    ]
    for i in range(2, 16, 4):
        old[i] = old[i].T
    for i in range(3, 16, 4):
        old[i] = old[i].reshape(-1, LANES)
    new = [SDS(a.shape, F32) for a in old[:4]] * 4 + [SDS(a.shape, BF) for a in old[:4]]
    scalars, *new = call(
        adam_kernel,
        [SDS((8, LANES), F32)] + new,
        sums + old,
        [
            pltpu.VMEM(old[3].shape, F32),
            pltpu.VMEM(outs.shape, F32),
            pltpu.SemaphoreType.DMA((50,)),
        ]
        + [
            pltpu.VMEM(((2,) if i < 2 else ()) + old[i].shape[i < 2 :], F32 if j < 4 else BF)
            for i in range(4)
            for j in range(5)
        ],
        limit=34,
        given=range(1, 21),
    )
    for i in range(2, 20, 4):
        new[i] = new[i].T
    for i in range(3, 20, 4):
        new[i] = new[i].reshape(-1)
    return (scalars[0, 0], scalars[1, 0], scalars[2, 0], *new)


def solution(mesh):
    in_specs = (P("dp", "block"), P("dp", "block"), P("dp")) + (P(),) * 16
    return jax.shard_map(
        body, mesh=mesh, in_specs=in_specs, out_specs=(P(),) * 23, check_vma=False
    )
```

```python
import functools

import jax
import jax.numpy as jnp
from jax import lax
from jax.experimental import pallas as pl
from jax.experimental.pallas import tpu as pltpu
from jax.sharding import PartitionSpec as P

N = 64
B = 64
H = 128
K = 100
STRIDE = 8
LAYERS = 2
STEP = 10
HOP = 50
TILES = 3
M = 8
FRAMES = 150
BASE = 4 * LAYERS * H
PERIOD = 8 * H + 3 * B
ROWS_MAPS = 1536
ROWS_VECS = 1664
ROWS_MORE = 1680
ROWS_G = 1792
LANES = 128
BLOCKS = 208
PADDED = 216
CHUNK = 416

EPS_NORM = 1e-05
CLIP = 0.001
RATE = 0.1
BETA_ONE = 0.9
BETA_TWO = 0.999
ADAM_EPS = 1e-08
DECAY = 0.01
KEEP = 0.9

BF = jnp.bfloat16
F32 = jnp.float32
TOP = 13.0
NOTES = 16
HALF = jnp.float16
SDS = jax.ShapeDtypeStruct


def dot(left, right):
    return jnp.dot(left, right, preferred_element_type=F32)


def dot_turned(left, right):
    return lax.dot_general(left, right, (((1,), (1,)), ((), ())), preferred_element_type=F32)


def dot_rows(left, right):
    return lax.dot_general(left, right, (((0,), (0,)), ((), ())), preferred_element_type=F32)


def half_scale():
    lane = lax.broadcasted_iota(jnp.int32, (1, 4 * H), 1)
    return jnp.where((lane >= 2 * H) & (lane < 3 * H), 1.0, 0.5)


def gate_acts(z):
    act = jnp.tanh(z)
    sig_i = 0.5 * act[:, :H] + 0.5
    sig_f = 0.5 * act[:, H : 2 * H] + 0.5
    sig_o = 0.5 * act[:, 3 * H :] + 0.5
    return sig_i, sig_f, act[:, 2 * H : 3 * H], sig_o


def norm_parts(value):
    center = value - jnp.mean(value, -1, keepdims=True)
    spread = jnp.mean(center * center, -1, keepdims=True)
    scale = lax.rsqrt(spread + EPS_NORM)
    return center * scale, scale


def norm_back(grad, unit, scale, gain):
    inner = grad * gain
    return scale * (
        inner
        - jnp.mean(inner, -1, keepdims=True)
        - unit * jnp.mean(inner * unit, -1, keepdims=True)
    )


def live(lim, start, count):
    pos = lax.broadcasted_iota(jnp.int32, (count, M, B), 0) + start
    return jnp.where(pos * STRIDE < lim[None], 1.0, 0.0).reshape(count * M, B)


def limits(lengths):
    row = lax.broadcasted_iota(jnp.int32, (M, B), 0)
    total = jnp.zeros((M, B), jnp.int32)
    for m in range(M):
        total = jnp.where(row == m, lengths[m], total)
    return total - lax.axis_index("block") * (FRAMES * STRIDE)


def pieces(vectors, start, count):
    parts = []
    at = start
    while at < start + count:
        wide = at % 2 == 0 and at + 2 <= start + count
        lane = (at % 2) * N
        parts.append(vectors[at // 2 : at // 2 + 1, lane : lane + (2 * N if wide else N)])
        at += 2 if wide else 1
    return parts[0] if len(parts) == 1 else jnp.concatenate(parts, 1)


def branch_vectors(vectors, index):
    first = (2 * N + B + index * PERIOD) // N
    half = half_scale()
    bias = [pieces(vectors, first + 8 * d, 8) * half for d in range(2)]
    return bias, [pieces(vectors, first + 16 + j, 1) for j in range(3)]


def own(start, count):
    pos = lax.broadcasted_iota(jnp.int32, (count, M, B), 0) + start
    return jnp.where(pos < FRAMES, 1.0, 0.0).reshape(count * M, B)


def chunk_of(steps, rows):
    best = 1
    for size in range(1, steps + 1):
        if steps % size == 0 and size * rows <= 1024 and size * rows % 16 == 0:
            best = size
    return best


class Shape:
    def __init__(self, groups, steps, rows):
        self.groups, self.steps, self.rows = groups, steps, rows
        self.size = steps * rows
        self.chunk = chunk_of(steps, rows)
        self.crows = self.chunk * rows
        self.chunks = steps // self.chunk
        self.wide = (steps + 2) * rows
        self.unroll = max(n for n in range(1, 26) if steps % n == 0)


def chunk_loop(shape, fn):
    for g in range(shape.groups):
        for i in range(shape.chunks):
            fn(g, i, i * shape.crows)


def forward_weights(gi, gr, index, wc):
    half = half_scale()
    for d in range(2):
        wc[d, :H] = (gr[index, d].astype(BF).astype(F32) * half).astype(BF)
        wc[d, H:] = (gi[index, d].astype(BF).astype(F32) * half).astype(BF)


def lstm_scan(shape, pg, wc, h_ref, c_ref):
    G, S, R = shape.groups, shape.steps, shape.rows
    pad = jnp.zeros((R, 2 * H), F32)
    for g in range(G):
        for ref in (h_ref, c_ref):
            ref[g * shape.wide : g * shape.wide + R] = pad
            ref[(g + 1) * shape.wide - R : (g + 1) * shape.wide] = pad

    rows = G * R
    zero = jnp.zeros((rows, H), F32)
    held = jnp.concatenate([wc[0, :H], wc[1, :H]], 0)

    def one(d, t, z, memory):
        at = pl.multiple_of(t * R, 8)
        pre = jnp.concatenate([pg[d, pl.ds(g * shape.size + at, R), :] for g in range(G)], 0)
        sig_i, sig_f, tan_g, sig_o = gate_acts(pre + z)
        memory = sig_f * memory + sig_i * tan_g
        hidden = (sig_o * jnp.tanh(memory)).astype(BF).astype(F32)
        after = pl.multiple_of(t * R + R, 8)
        for g in range(G):
            to = pl.ds(g * shape.wide + after, R)
            h_ref[to, d * H : (d + 1) * H] = hidden[g * R : (g + 1) * R]
            c_ref[to, d * H : (d + 1) * H] = memory[g * R : (g + 1) * R]
        return hidden, memory

    def step(s, carry):
        hf, cf, hb, cb = carry
        both = jnp.concatenate(
            [jnp.concatenate([hf, zero], 1), jnp.concatenate([zero, hb], 1)], 0
        ).astype(BF)
        z = dot(both, held)
        hf, cf = one(0, s, z[:rows], cf)
        hb, cb = one(1, S - 1 - s, z[rows:], cb)
        return hf, cf, hb, cb

    lax.fori_loop(0, S, step, (zero,) * 4, unroll=shape.unroll)


def lstm_scan_back(shape, z, dh, c_ref, wrt):
    G, S, R = shape.groups, shape.steps, shape.rows

    def one(d, t, rec_hidden, rec_memory):
        def take(ref, at, width, lanes):
            at = pl.multiple_of(at, 8)
            return jnp.concatenate([ref[pl.ds(g * width + at, R), lanes] for g in range(G)], 0)

        lanes = slice(d * H, (d + 1) * H)
        at = pl.multiple_of(t * R, 8)
        zt = jnp.concatenate([z[d, pl.ds(g * shape.size + at, R), :] for g in range(G)], 0)
        sig_i, sig_f, tan_g, sig_o = gate_acts(zt)
        tan_c = jnp.tanh(take(c_ref, t * R + R, shape.wide, lanes))
        before = take(c_ref, t * R + 2 * R * d, shape.wide, lanes)
        grad_h = take(dh, t * R, shape.size, lanes) + rec_hidden
        grad_c = rec_memory + grad_h * (sig_o * (1.0 - tan_c * tan_c))
        grad_pre = jnp.concatenate(
            [
                grad_c * (tan_g * sig_i * (1.0 - sig_i)),
                grad_c * (before * sig_f * (1.0 - sig_f)),
                grad_c * (sig_i * (1.0 - tan_g * tan_g)),
                grad_h * (tan_c * sig_o * (1.0 - sig_o)),
            ],
            -1,
        ).astype(BF)
        full = grad_pre.astype(F32)
        for g in range(G):
            z[d, pl.ds(g * shape.size + at, R), :] = full[g * R : (g + 1) * R]
        return dot(grad_pre, wrt[d]), grad_c * sig_f

    def step(s, carry):
        hf, cf, hb, cb = carry
        hf, cf = one(0, S - 1 - s, hf, cf)
        hb, cb = one(1, s, hb, cb)
        return hf, cf, hb, cb

    zero = jnp.zeros((G * R, H), F32)
    lax.fori_loop(0, S, step, (zero,) * 4, unroll=shape.unroll)


def branch_pregates(shape, inputs, wc, bias, pg):
    def fill(g, i, r0):
        x = inputs(g, r0).astype(BF)
        for d in range(2):
            pg[d, pl.ds(g * shape.size + r0, shape.crows), :] = dot(x, wc[d, H:]) + bias[d]

    chunk_loop(shape, fill)


def branch_back(shape, grads, inputs, h_ref, c_ref, weights, index, vecs, turned_out, out, scratch):
    gi, gr = weights
    wc, wit, wrt, wot, z, dh = scratch
    n, R = shape.crows, shape.rows
    forward_weights(gi, gr, index, wc)
    for d in range(2):
        wit[d] = jnp.transpose(gi[index, d]).astype(BF)
        wrt[d] = jnp.transpose(gr[index, d]).astype(BF)
    wot[...] = turned_out.astype(BF)
    out[...] = jnp.zeros(out.shape, F32)
    bias, (o_bias, gain, _) = vecs

    def states(g, at, lanes):
        return h_ref[pl.ds(pl.multiple_of(g * shape.wide + at, 8), n), lanes].astype(BF)

    def earlier(g, r0, d):
        before = states(g, r0 + 2 * R * d, slice(d * H, (d + 1) * H))
        return jnp.concatenate([before, inputs(g, r0).astype(BF)], 1)

    def first(g, i, r0):
        now = states(g, r0 + R, slice(0, 2 * H))
        here = pl.ds(g * shape.size + r0, n)
        unit, scale = norm_parts(dot_turned(now, wot[...]) + o_bias)
        grad = grads(g, r0)
        low = norm_back(grad, unit, scale, gain).astype(BF)
        dh[here, :] = dot(low, wot[...])
        turned = dot_rows(low, now)
        for j in range(2):
            at = ROWS_MAPS + j * B
            out[at : at + B] += turned[:, j * LANES : (j + 1) * LANES]
        for j, value in enumerate((low.astype(F32), grad * unit, grad)):
            at = ROWS_VECS + 8 + j
            out[at : at + 1, :B] += jnp.sum(value, 0, keepdims=True)
        for d in range(2):
            z[d, here, :] = dot(earlier(g, r0, d), wc[d]) + bias[d]

    chunk_loop(shape, first)
    lstm_scan_back(shape, z, dh, c_ref, wrt)

    def last(use):
        def fn(g, i, r0):
            total = None
            for d in range(2):
                full = z[d, pl.ds(g * shape.size + r0, n), :]
                low = full.astype(BF)
                maps = dot_rows(earlier(g, r0, d), low)
                grad_bias = jnp.sum(full, 0, keepdims=True)
                for j in range(4):
                    lanes = slice(j * LANES, (j + 1) * LANES)
                    at = j * 384 + d * B
                    out[at : at + B] += maps[H:, lanes]
                    at = j * 384 + 128 + d * H
                    out[at : at + H] += maps[:H, lanes]
                    at = ROWS_VECS + 4 * d + j
                    out[at : at + 1] += grad_bias[:, lanes]
                part = dot(low, wit[d])
                total = part if total is None else total + part
            use(g, i, r0, total)

        chunk_loop(shape, fn)

    return last


def fwd_scratch(shape):
    return [
        pltpu.VMEM((2, H + B, 4 * H), BF),
        pltpu.VMEM((2, shape.groups * shape.size, 4 * H), F32),
    ]


def back_scratch(shape):
    return [
        pltpu.VMEM((2, H + B, 4 * H), BF),
        pltpu.VMEM((2, 4 * H, B), BF),
        pltpu.VMEM((2, 4 * H, H), BF),
        pltpu.VMEM((B, 2 * H), BF),
        pltpu.VMEM((2, shape.groups * shape.size, 4 * H), F32),
        pltpu.VMEM((shape.groups * shape.size, 2 * H), F32),
    ]


def packed(value, RP):
    rest = value[RP:]
    if rest.shape[0] < RP:
        rest = jnp.concatenate([rest, jnp.zeros((RP - rest.shape[0], B), F32)], 0)
    return jnp.concatenate([value[:RP], rest], 1).astype(BF)


def send_tiles(res, send, nb, RI):
    RP = send.shape[2]
    for d in range(nb):
        for c in range(TILES):
            send[d, c] = packed(res[c, d * RI : (d + 1) * RI], RP)


def add_tiles(res, back, nb, RI, lim):
    RP = back.shape[2]
    for d in range(nb):
        for c in range(TILES):
            both = back[d, c].astype(F32)
            for lo, hi, value in (
                (0, RP, both[:, :B]),
                (RP, RI, both[:, B:]),
            ):
                lo, hi = d * RI + lo, min(d * RI + hi, K * M)
                if lo >= hi:
                    continue
                mask = live(lim, c * HOP + lo // M, (hi - lo) // M)
                res[c, lo:hi] = (res[c, lo:hi] + value[: hi - lo]) * mask


def unpack_steps(rows, xs, T, RI):
    RP = rows.shape[1]

    def widen(t, _):
        both = rows[t].astype(F32)
        xs[pl.ds(pl.multiple_of(t * RI, 8), RP), :] = both[:, :B]
        if RI > RP:
            xs[pl.ds(pl.multiple_of(t * RI + RP, 8), RI - RP), :] = both[: RI - RP, B:]
        return 0

    lax.fori_loop(0, T, widen, 0, unroll=4 if T % 4 == 0 else 1)


def windows_of(mix, following, win):
    last = FRAMES + HOP + 1
    for i in range(1, BLOCKS):
        at = STRIDE * (i - 1)
        if at + 2 * STRIDE <= FRAMES * STRIDE:
            win[i * M : (i + 1) * M] = mix[:, at : at + 2 * STRIDE]
        elif at < FRAMES * STRIDE:
            win[i * M : (i + 1) * M] = jnp.concatenate([mix[:, at:], following[:, :STRIDE]], 1)
        elif i <= last:
            at -= FRAMES * STRIDE
            win[i * M : (i + 1) * M] = following[:, at : at + 2 * STRIDE]
        else:
            win[i * M :] = jnp.zeros(((BLOCKS - i) * M, 2 * STRIDE), F32)
            break


def softplus(value):
    return jnp.maximum(value, 0.0) + jnp.log1p(jnp.exp(-jnp.abs(value)))


def turned_out(proj, index):
    return proj[:, index * 2 * H : (index + 1) * 2 * H]


def intra_forward(shape, index, res, lim, gi, gr, slot, vectors, proj, x_out, h_out, c_out, scratch):
    wc, pg = scratch
    forward_weights(gi, gr, slot, wc)
    bias, (o_bias, gain, beta) = branch_vectors(vectors, index)
    n = shape.crows

    def inputs(g, r0):
        x = res[g, pl.ds(r0, n), :].astype(BF)
        x_out[pl.ds(pl.multiple_of(g * shape.size + r0, 16), n), :] = x
        return x

    branch_pregates(shape, inputs, wc, bias, pg)
    lstm_scan(shape, pg, wc, h_out, c_out)
    low_out = turned_out(proj, index).astype(BF)

    def close(g, i, r0):
        now = h_out[pl.ds(pl.multiple_of(g * shape.wide + r0 + shape.rows, 8), n), :].astype(BF)
        unit, _ = norm_parts(dot_turned(now, low_out) + o_bias)
        mask = live(lim, g * HOP + i * shape.chunk, shape.chunk)
        res[g, pl.ds(r0, n), :] = (res[g, pl.ds(r0, n), :] + (unit * gain + beta)) * mask

    chunk_loop(shape, close)


def inter_forward(shape, index, xs, gi, gr, slot, vectors, proj, h_out, c_out, scratch, use):
    wc, pg = scratch
    forward_weights(gi, gr, slot, wc)
    bias, (o_bias, gain, beta) = branch_vectors(vectors, index)
    n = shape.crows
    branch_pregates(shape, lambda g, r0: xs[pl.ds(r0, n), :], wc, bias, pg)
    lstm_scan(shape, pg, wc, h_out, c_out)
    low_out = turned_out(proj, index).astype(BF)

    def close(g, i, r0):
        now = h_out[pl.ds(pl.multiple_of(r0 + shape.rows, 8), n), :].astype(BF)
        unit, _ = norm_parts(dot_turned(now, low_out) + o_bias)
        use(i, r0, unit * gain + beta)

    chunk_loop(shape, close)


def zero_tail(res, c):
    if res.shape[1] > K * M:
        res[c, K * M :] = jnp.zeros((res.shape[1] - K * M, B), F32)


def encode(mix, following, leading, lim, proj, vectors, win, flat, bottle, res):
    flat[:M] = jnp.concatenate([leading[...], mix[:, :STRIDE]], 1)
    windows_of(mix, following, flat)
    win[...] = flat[...].astype(BF)
    w_enc = proj[:, BASE + N + B : BASE + N + B + 2 * STRIDE].astype(BF)
    w_bn = proj[:, BASE : BASE + N].astype(BF)
    gain, beta, b_bias = (pieces(vectors, j, 1) for j in range(3))
    for i in range(BLOCKS * M // CHUNK):
        at = i * CHUNK
        pre = dot_turned(win[at : at + CHUNK], w_enc)
        unit, _ = norm_parts(softplus(pre))
        normed = (unit * gain + beta).astype(BF)
        mask = live(lim, i * (CHUNK // M) - 1, CHUNK // M)
        bottle[at : at + CHUNK] = (dot_turned(normed, w_bn) + b_bias) * mask
    for c in range(TILES):
        res[c, : K * M] = bottle[(c * HOP + 1) * M : (c * HOP + 1 + K) * M]
        zero_tail(res, c)


def first_kernel(shape, nb, RI, mix, following, leading, lengths, proj, vectors, gi, gr, res, send, x_out, h_out, c_out, win, wc, pg, flat, bottle):
    lim = limits(lengths)
    encode(mix, following.at[0], leading, lim, proj, vectors, win, flat, bottle, res)
    intra_forward(shape, 0, res, lim, gi, gr, 0, vectors, proj, x_out, h_out, c_out, (wc, pg))
    send_tiles(res, send, nb, RI)


def third_kernel(shape, nb, RI, res_in, back, lengths, proj, vectors, gi, gr, res, send, x_out, h_out, c_out, wc, pg):
    lim = limits(lengths)
    res[...] = res_in[...]
    add_tiles(res, back, nb, RI, lim)
    intra_forward(shape, 2, res, lim, gi, gr, 0, vectors, proj, x_out, h_out, c_out, (wc, pg))
    send_tiles(res, send, nb, RI)


def inter_kernel(shape, RI, index, rows, proj, vectors, gi, gr, normed, h_out, c_out, wc, pg, xs):
    unpack_steps(rows, xs, shape.steps, RI)
    RP = normed.shape[1]

    def use(i, r0, value):
        for j in range(shape.chunk):
            normed[i * shape.chunk + j] = packed(value[j * RI : (j + 1) * RI], RP)

    inter_forward(shape, index, xs, gi, gr, 0, vectors, proj, h_out, c_out, (wc, pg), use)


EDGE = (HOP + 1) * M
EDGE_TOP = 208


def edge_pack(value):
    rest = jnp.concatenate([value[EDGE_TOP:], jnp.zeros((2 * EDGE_TOP - EDGE, B), F32)], 0)
    return jnp.concatenate([value[:EDGE_TOP], rest], 1)


def edge_unpack(ref):
    return jnp.concatenate([ref[:, :B], ref[: EDGE - EDGE_TOP, B:]], 0)


def parts_of(res, part):
    half = HOP * M
    part[:half] = res[0, :half]
    for c in range(1, TILES):
        part[c * half : (c + 1) * half] = res[c, :half] + res[c - 1, half : 2 * half]
    part[TILES * half :] = res[TILES - 1, half : 2 * half]


def part_kernel(nb, RI, res_in, back, lengths, part, up, down, res):
    res[...] = res_in[...]
    add_tiles(res, back, nb, RI, limits(lengths))
    parts_of(res, part)
    half = HOP * M
    up[...] = edge_pack(part[TILES * half - M :])
    down[...] = edge_pack(part[: half + M])


def middle_kernel(nb, RI, part, before, after, lengths, win, goal, following, proj, vectors, send, gres, genc, gm, *scratch):
    edge = jnp.where(lax.axis_index("block") > 0, 1.0, 0.0)
    middle(
        part, edge_unpack(before), edge_unpack(after), limits(lengths), edge, win, goal,
        following.at[1], proj, vectors, gres, genc, gm, *scratch,
    )
    send_tiles(gres, send, nb, RI)


def middle(part, early, late, lim, edge, win, goal, following, proj, vectors, gres, genc, gm, feats, dec, tgt, gest, enc, gate, src, act):
    half = HOP * M
    top = M + TILES * half
    total = BLOCKS * M
    feats[:M] = early[:M]
    feats[M : M + half] = part[:half] + early[M:]
    feats[M + half : top] = part[half : TILES * half]
    feats[top : top + half] = part[TILES * half :] + late[:half]
    feats[top + half : top + half + M] = late[half:]
    feats[top + half + M :] = jnp.zeros((PADDED * M - top - half - M, B), F32)
    low_mask = proj[:, BASE + N : BASE + N + B].astype(BF)
    w_enc = proj[:, BASE + N + B : BASE + N + B + 2 * STRIDE].astype(BF)
    low_dec = proj[:, BASE + N + B + 2 * STRIDE : BASE + N + B + 4 * STRIDE].astype(BF)
    m_bias = pieces(vectors, vectors.shape[0] * 2 - 1, 1)
    root = 0.7978845608028654
    cube = 0.044715
    dec[total:] = jnp.zeros((PADDED * M - total, 2 * STRIDE), F32)
    for i in range(total // CHUNK):
        rows = slice(i * CHUNK, (i + 1) * CHUNK)
        x = feats[rows]
        low = (0.5 * x * (1.0 + jnp.tanh(root * (x + cube * x * x * x)))).astype(BF)
        encoded = softplus(dot_turned(win[rows], w_enc))
        mask = 0.5 * jnp.tanh(0.5 * (dot_turned(low, low_mask) + m_bias)) + 0.5
        source = (mask * encoded).astype(BF)
        enc[rows] = encoded
        gate[rows] = mask
        src[rows] = source.astype(F32)
        act[rows] = low.astype(F32)
        dec[rows] = dot(source, low_dec)
    dec[:M] = dec[:M] * edge
    for ref in (enc, gate, src, act):
        ref[total:] = jnp.zeros((PADDED * M - total, B), F32)
    for i in range(1, FRAMES + 1):
        tgt[i * M : (i + 1) * M] = goal[:, STRIDE * (i - 1) : STRIDE * i]
    for i in range(FRAMES + 1, FRAMES + HOP + 2):
        at = STRIDE * (i - 1 - FRAMES)
        tgt[i * M : (i + 1) * M] = following[:, at : at + STRIDE]
    tgt[(FRAMES + HOP + 2) * M :] = jnp.zeros(((PADDED - FRAMES - HOP - 2) * M, STRIDE), F32)
    estimate = dec[M:total, :STRIDE] + dec[: total - M, STRIDE:]
    count = BLOCKS - 1
    spot = lax.broadcasted_iota(jnp.int32, (count, M, STRIDE), 0)
    phase = lax.broadcasted_iota(jnp.int32, (count, M, STRIDE), 2)
    near = spot < FRAMES + HOP + 1
    valid = jnp.where(near & (spot * STRIDE + phase < lim[:, :STRIDE][None]), 1.0, 0.0)
    inside = jnp.where(spot < FRAMES, valid, 0.0).reshape(count * M, STRIDE)
    valid = valid.reshape(count * M, STRIDE)
    error = estimate - tgt[M:total]
    smoothed = jnp.sqrt(error * error + 1.0)
    gest[:M] = jnp.zeros((M, STRIDE), F32)
    gest[M:total] = valid * error / smoothed
    gest[total:] = jnp.zeros((PADDED * M - total, STRIDE), F32)
    loss = jnp.sum(jnp.sum(inside * (smoothed - 1.0), 0, keepdims=True), 1, keepdims=True)
    seen = jnp.sum(jnp.sum(inside, 0, keepdims=True), 1, keepdims=True)
    gm[...] = jnp.zeros_like(gm)
    gm[132:133] = jnp.broadcast_to(loss, (1, LANES))
    gm[133:134] = jnp.broadcast_to(seen, (1, LANES))
    for i in range(total // CHUNK):
        at = i * CHUNK + M
        rows = slice(at, at + CHUNK)
        grad_dec = jnp.concatenate([gest[rows], gest[at + M : at + M + CHUNK]], 1).astype(BF)
        mine = own(i * (CHUNK // M), CHUNK // M)
        mine_low = mine.astype(BF)
        gm[64:128, 16:32] += dot_rows(src[rows].astype(BF) * mine_low, grad_dec)
        grad_source = dot_turned(grad_dec, low_dec)
        mask = gate[rows]
        grad_logit = (grad_source * enc[rows] * mask * (1.0 - mask)).astype(BF)
        enc[rows] = grad_source * mask
        gm[:64, 64:] += dot_rows(grad_logit * mine_low, act[rows].astype(BF))
        gm[131:132, :B] += jnp.sum(grad_logit.astype(F32) * mine, 0, keepdims=True)
        x = feats[rows]
        curve = jnp.tanh(root * (x + cube * x * x * x))
        slope = 0.5 * (1.0 + curve) + (0.5 * root) * x * (1.0 - curve * curve) * (
            1.0 + (3.0 * cube) * x * x
        )
        feats[rows] = slope * dot(grad_logit, low_mask)
    genc[...] = enc[M : M + FRAMES * M]
    for c in range(TILES):
        gres[c, : K * M] = feats[M + c * half : M + c * half + K * M] * live(lim, c * HOP, K)
        zero_tail(gres, c)


def inter_back(shape, index, gs, xs, h_ref, c_ref, proj, vectors, gi, gr, slot, out, core, use):
    n = shape.crows
    last = branch_back(
        shape,
        lambda g, r0: gs[pl.ds(r0, n), :],
        lambda g, r0: xs[pl.ds(r0, n), :],
        h_ref, c_ref, (gi, gr), slot, branch_vectors(vectors, index), turned_out(proj, index), out, core,
    )
    last(use)


def inter_back_kernel(shape, RI, index, grad_rows, rows, h_ref, c_ref, proj, vectors, gi, gr, send, out, *scratch):
    xs, gs, core = scratch[0], scratch[1], scratch[2:]
    unpack_steps(rows, xs, shape.steps, RI)
    unpack_steps(grad_rows, gs, shape.steps, RI)
    RP = send.shape[1]

    def use(g, i, r0, total):
        for j in range(shape.chunk):
            send[i * shape.chunk + j] = packed(total[j * RI : (j + 1) * RI], RP)

    inter_back(shape, index, gs, xs, h_ref, c_ref, proj, vectors, gi, gr, 0, out, core, use)


def intra_back(shape, index, gres, x_ref, h_ref, c_ref, proj, vectors, gi, gr, slot, out, core):
    n = shape.crows

    def inputs(g, r0):
        return x_ref[pl.ds(pl.multiple_of(g * shape.size + r0, 16), n), :]

    last = branch_back(
        shape,
        lambda g, r0: gres[g, pl.ds(r0, n), :],
        inputs,
        h_ref, c_ref, (gi, gr), slot, branch_vectors(vectors, index), turned_out(proj, index), out, core,
    )

    def use(g, i, r0, total):
        gres[g, pl.ds(r0, n), :] = gres[g, pl.ds(r0, n), :] + total

    last(use)


def third_back_kernel(shape, nb, RI, gres_in, back, lengths, x_ref, h_ref, c_ref, proj, vectors, gi, gr, gres, send, out, *core):
    lim = limits(lengths)
    gres[...] = gres_in[...]
    add_tiles(gres, back, nb, RI, lim)
    intra_back(shape, 2, gres, x_ref, h_ref, c_ref, proj, vectors, gi, gr, 0, out, core)
    for c in range(TILES):
        gres[c, : K * M] = gres[c, : K * M] * live(lim, c * HOP, K)
    send_tiles(gres, send, nb, RI)


def first_back_kernel(shape, nb, RI, gres_in, back, lengths, x_ref, h_ref, c_ref, proj, vectors, gi, gr, win, genc, gm, more_in, out, more, gres, bottle, *core):
    lim = limits(lengths)
    more[...] = more_in[...]
    gres[...] = gres_in[...]
    add_tiles(gres, back, nb, RI, lim)
    intra_back(shape, 0, gres, x_ref, h_ref, c_ref, proj, vectors, gi, gr, 0, out, core)
    encode_back(gres, lim, proj, vectors, win, genc, gm, out, more, bottle)


def encode_back(gres, lim, proj, vectors, win, genc, gm, out, more, bottle):
    at_first, at_vecs = ROWS_MORE, ROWS_MORE + B
    out[at_first : at_first + B] = gm[:B]
    out[at_vecs : at_vecs + 8] = gm[2 * B :]
    more[at_first : at_first + B] = gm[B : 2 * B]
    bottle[...] = jnp.zeros(bottle.shape, F32)
    for c in range(TILES):
        at = (c * HOP + 1) * M
        bottle[at : at + K * M] += gres[c, : K * M]
    w_enc = proj[:, BASE + N + B : BASE + N + B + 2 * STRIDE].astype(BF)
    w_bn = proj[:, BASE : BASE + N].astype(BF)
    gain, beta = (pieces(vectors, j, 1) for j in range(2))
    own_rows = FRAMES * M
    for i in range(BLOCKS * M // CHUNK):
        at = i * CHUNK
        rows = slice(at, at + CHUNK)
        pre = dot_turned(win[rows], w_enc)
        unit, scale = norm_parts(softplus(pre))
        normed = (unit * gain + beta).astype(BF)
        low = (bottle[rows] * live(lim, i * (CHUNK // M) - 1, CHUNK // M)).astype(BF)
        out[at_first : at_first + B, :N] += dot_rows(low, normed)
        grad_normed = dot(low, w_bn)
        for j, value in enumerate((grad_normed * unit, grad_normed, low.astype(F32))):
            out[at_vecs + j : at_vecs + j + 1, :B] += jnp.sum(value, 0, keepdims=True)
        grad_enc = norm_back(grad_normed, unit, scale, gain)
        lo, hi = max(at - M, 0), min(at + CHUNK - M, own_rows)
        if lo < hi:
            piece = genc[lo:hi]
            above, below = lo + M - at, at + CHUNK - M - hi
            if above:
                piece = jnp.concatenate([jnp.zeros((above, B), F32), piece], 0)
            if below:
                piece = jnp.concatenate([piece, jnp.zeros((below, B), F32)], 0)
            grad_enc = grad_enc + piece
        grad_pre = (grad_enc * (0.5 * jnp.tanh(0.5 * pre) + 0.5)).astype(BF)
        more[at_first : at_first + B, :16] += dot_rows(grad_pre, win[rows])


def turn_in(res, xs, RI, lowered=True):
    for j in range(M):
        for c in range(TILES):
            at = (TILES * j + c) * RI
            value = res[c, pl.ds(j, K, stride=M), :]
            xs[at : at + K] = value.astype(BF).astype(F32)


def turn_back(res, xs, RI, length):
    pos = lax.broadcasted_iota(jnp.int32, (K, B), 0)
    for j in range(M):
        for c in range(TILES):
            at = (TILES * j + c) * RI
            mask = jnp.where((pos + (FRAMES * j + HOP * c)) * STRIDE < length, 1.0, 0.0)
            where = (c, pl.ds(j, K, stride=M), slice(None))
            res[where] = (res[where] + xs[at : at + K]) * mask


class Strip:
    def __init__(self, ref, part, lane, rows, width):
        self.ref, self.part, self.lane, self.shape = ref, part, lane, (rows, width)

    def where(self, index):
        index = index if isinstance(index, tuple) else (index,)
        if index[0] is Ellipsis:
            index = ()
        spans = []
        for i, size in enumerate(self.shape):
            start, stop, _ = (index[i] if i < len(index) else slice(None)).indices(size)
            spans.append((start, stop))
        (top, end), (left, right) = spans
        return (self.part, slice(top, end), slice(self.lane + left, self.lane + right))

    def __getitem__(self, index):
        return self.ref[self.where(index)]

    def __setitem__(self, index, value):
        self.ref[self.where(index)] = value


def local_kernel(intra, inter, RI, waves, lengths, proj, vectors, gi_in, gr_in, outs_to, notes, *scratch):
    gi, gr, outs, sem = scratch[:4]
    scratch = scratch[4:]
    maps = [pltpu.make_async_copy(gi_in, gi, sem.at[0]), pltpu.make_async_copy(gr_in, gr, sem.at[1])]
    for copy in maps:
        copy.start()

    def leave(r):
        rows = pl.ds(r * ROWS_G, ROWS_G)
        copy = pltpu.make_async_copy(outs.at[rows], outs_to.at[rows], sem.at[2 + r])
        copy.start()
        return copy

    win, res, nrm, genc, gm = scratch[:5]
    x0, h0, c0, x1, h1, c1, x2, h2, c2, x3, h3, c3 = scratch[5:17]
    wc, wit, wrt, wot, z, dh = scratch[17:]

    def strip(d, lane, rows, width):
        return Strip(z, d, lane * LANES, rows, width)

    tall = PADDED * M
    feats, dec = strip(0, 0, tall, B), strip(0, 1, tall, 2 * STRIDE)
    tgt, gest = strip(0, 2, tall, STRIDE), strip(0, 3, tall, STRIDE)
    enc, gate, src, act = (strip(1, i, tall, B) for i in range(4))
    part = strip(1, 3, (FRAMES + HOP) * M, B)
    bottle, flat = strip(0, 0, BLOCKS * M, B), strip(0, 1, BLOCKS * M, 2 * STRIDE)
    core = (wc, wit, wrt, wot, z, dh)
    out0, out1, out2, out3 = (outs.at[pl.ds(r * ROWS_G, ROWS_G)] for r in range(4))
    length = lengths[lax.axis_index("block")]
    lim = length - lax.broadcasted_iota(jnp.int32, (M, B), 0) * (FRAMES * STRIDE)
    reach = (HOP + 2) * STRIDE
    span = FRAMES * STRIDE
    goal_at = waves.shape[1] // 2
    mix = waves[:, :span]
    goal = waves[:, goal_at : goal_at + span]

    def after(value):
        return jnp.concatenate([value[1:], jnp.zeros((1, value.shape[1]), F32)], 0)

    def before(value):
        return jnp.concatenate([jnp.zeros((1, value.shape[1]), F32), value[:-1]], 0)

    for ref in (x1, x3, nrm):
        ref[...] = jnp.zeros_like(ref)
    encode(mix, after(mix[:, :reach]), before(mix[:, span - STRIDE :]), lim, proj, vectors, win, flat, bottle, res)
    for copy in maps:
        copy.wait()

    def inter_layer(index, xs, h, c):
        turn_in(res, xs, RI)

        def use(i, r0, value):
            nrm[pl.ds(r0, inter.crows), :] = value.astype(BF).astype(F32)

        inter_forward(inter, index, xs, gi, gr, index, vectors, proj, h, c, (wc, z), use)
        turn_back(res, nrm, RI, length)

    intra_forward(intra, 0, res, lim, gi, gr, 0, vectors, proj, x0, h0, c0, (wc, z))
    inter_layer(1, x1, h1, c1)
    intra_forward(intra, 2, res, lim, gi, gr, 2, vectors, proj, x2, h2, c2, (wc, z))
    inter_layer(3, x3, h3, c3)

    parts_of(res, part)
    half = HOP * M
    row = lax.broadcasted_iota(jnp.int32, (EDGE, B), 0) % M
    early = jnp.where(row == 0, 0.0, before(part[TILES * half - M :]))
    late = jnp.where(row == M - 1, 0.0, after(part[: half + M]))
    edge = jnp.where(lax.broadcasted_iota(jnp.int32, (M, 2 * STRIDE), 0) == 0, 0.0, 1.0)
    middle(
        part, early, late, lim, edge, win, goal, after(goal[:, :reach]), proj, vectors, res, genc, gm,
        feats, dec, tgt, gest, enc, gate, src, act,
    )

    def inter_layer_back(index, xs, h, c, out):
        for j in range(M):
            for t in range(TILES):
                at = (TILES * j + t) * RI
                nrm[at + K : at + RI] = jnp.zeros((RI - K, B), F32)
        turn_in(res, nrm, RI)

        def use(g, i, r0, total):
            nrm[pl.ds(r0, inter.crows), :] = total.astype(BF).astype(F32)

        inter_back(inter, index, nrm, xs, h, c, proj, vectors, gi, gr, index, out, core, use)
        turn_back(res, nrm, RI, length)

    inter_layer_back(3, x3, h3, c3, out3)
    left = [leave(3)]
    intra_back(intra, 2, res, x2, h2, c2, proj, vectors, gi, gr, 2, out2, core)
    left.append(leave(2))
    for c in range(TILES):
        res[c, : K * M] = res[c, : K * M] * live(lim, c * HOP, K)
    inter_layer_back(1, x1, h1, c1, out1)
    intra_back(intra, 0, res, x0, h0, c0, proj, vectors, gi, gr, 0, out0, core)
    encode_back(res, lim, proj, vectors, win, genc, gm, out0, out1, bottle)
    left += [leave(1), leave(0)]

    def widest(i, best):
        rows = outs[pl.ds(pl.multiple_of(i * 256, 256), 256), :]
        return jnp.maximum(best, jnp.max(jnp.abs(rows).reshape(32, 8, LANES), 0))

    best = lax.fori_loop(0, outs.shape[0] // 256, widest, jnp.zeros((8, LANES), F32))
    best = jnp.max(jnp.max(best, 0, keepdims=True), 1, keepdims=True)
    notes[...] = note_rows(best, gm[132:133], gm[133:134])
    for copy in left:
        copy.wait()


def local_scratch(intra, inter):
    first = [
        pltpu.VMEM((2 * LAYERS, 2, B, 4 * H), F32),
        pltpu.VMEM((2 * LAYERS, 2, H, 4 * H), F32),
        pltpu.VMEM((4 * ROWS_G, LANES), F32),
        pltpu.SemaphoreType.DMA((6,)),
        pltpu.VMEM((BLOCKS * M, 2 * STRIDE), BF),
        pltpu.VMEM((TILES, -(-K // M) * M * M, B), F32),
        pltpu.VMEM((inter.size, B), F32),
        pltpu.VMEM((FRAMES * M, B), F32),
        pltpu.VMEM((136, LANES), F32),
    ]
    kept = []
    for shape, kind in ((intra, BF), (inter, F32)) * 2:
        state = pltpu.VMEM((shape.groups * shape.wide, 2 * H), F32)
        kept += [pltpu.VMEM((shape.groups * shape.size, B), kind), state, state]
    return first + kept + back_scratch(inter)


def note_rows(widest, loss, count):
    row = lax.broadcasted_iota(jnp.int32, (8, LANES), 0)
    power = jnp.floor(jnp.log(jnp.maximum(widest, 1e-30)) * 1.4426950408889634)
    return jnp.where(row == 0, power, jnp.where(row == 1, loss, jnp.where(row == 2, count, 0.0)))


def adam_parts(grad, moment, square, weight, average, decay):
    moment = BETA_ONE * moment + (1.0 - BETA_ONE) * grad
    square = BETA_TWO * square + (1.0 - BETA_TWO) * grad * grad
    corrected = moment * (1.0 / (1.0 - BETA_ONE**STEP))
    scaled = square * (1.0 / (1.0 - BETA_TWO**STEP))
    weight = weight - RATE * (corrected / (jnp.sqrt(scaled) + ADAM_EPS) + decay * weight)
    average = KEEP * average + (1.0 - KEEP) * weight
    return moment, square, weight, average, weight.astype(BF)


def adam_kernel(*refs):
    near, far, totals, kept = refs[0], refs[1], refs[2], refs[3:19]
    scalars, new = refs[19], refs[20:40]
    gv, sums, sem = refs[40:43]
    ready = [refs[43 + 5 * kind : 48 + 5 * kind] for kind in range(4)]
    old = refs[63:79]
    arrivals = {}

    def fetch(kind, r=None):
        for j in range(4):
            source, to = kept[4 * j + kind], old[4 * j + kind]
            number = 50 + 4 * (kind if r is None else 4 + 2 * r + kind) + j
            if r is not None:
                source, to = source.at[r], to.at[r]
            arrivals[kind, r, j] = pltpu.make_async_copy(source, to, sem.at[number])
            arrivals[kind, r, j].start()

    def arrived(kind, r=None):
        for j in range(4):
            arrivals.pop((kind, r, j)).wait()

    for r in range(4):
        fetch(0, r)
        fetch(1, r)
    fetch(2)
    fetch(3)
    copies = {}
    mine = lax.axis_index("dp") & 1
    pieces_half = (near.shape[0] - sums.shape[0] // 2) // NOTES
    size = sums.shape[0] // 2 // pieces_half
    for i in range(pieces_half):
        at = i * (size + NOTES)
        for ref, place in ((near, mine), (far, 1 - mine)):
            to = pl.multiple_of((place * pieces_half + i) * size, 16)
            scale = jnp.exp2(ref[at + size : at + size + 1, :] - TOP)
            sums[pl.ds(to, size), :] = ref[at : at + size] * scale
    gs = [sums.at[pl.ds(r * ROWS_G, ROWS_G)] for r in range(4)]
    vecs = ROWS_MORE + B
    gv[:1] = jnp.concatenate([gs[0][vecs : vecs + 1, :N], gs[0][vecs + 1 : vecs + 2, :N]], 1)
    gv[1:2, :N] = gs[0][vecs + 2 : vecs + 3, :N]
    gv[gv.shape[0] - 1 :, N:] = gs[0][vecs + 3 : vecs + 4, :N]
    for r in range(4):
        at = 3 + 19 * r
        rows = [
            gs[r][ROWS_VECS + j : ROWS_VECS + j + 1, k * N : (k + 1) * N] for j in range(8) for k in range(2)
        ]
        rows += [gs[r][ROWS_VECS + j : ROWS_VECS + j + 1, :N] for j in range(8, 11)]
        for j, row in enumerate(rows):
            q = at + j
            gv[q // 2 : q // 2 + 1, (q % 2) * N : (q % 2 + 1) * N] = row
    part = jnp.zeros((8, LANES), F32)
    pieces_of = [gs[r][:ROWS_VECS] for r in range(4)]
    pieces_of += [gs[r][ROWS_MORE : ROWS_MORE + B] for r in range(2)] + [gv[...]]
    for piece in pieces_of:
        value = piece.reshape(piece.shape[0] // 8, 8, LANES)
        part = part + jnp.sum(value * value, 0)
    squared = jnp.sum(jnp.sum(part, 0, keepdims=True), 1, keepdims=True)
    loss, count = totals[0:1, :1], totals[1:2, :1]
    norm = jnp.sqrt(squared) / count
    factor = jnp.minimum(1.0, CLIP / norm) / count
    row = lax.broadcasted_iota(jnp.int32, (8, LANES), 0)
    scalars[...] = jnp.where(row == 0, loss, jnp.where(row == 1, count, norm))

    def update(kind, index, grad, decay, slot=()):
        results = adam_parts(
            grad * factor,
            old[4 + kind][index],
            old[8 + kind][index],
            old[kind][index],
            old[12 + kind][index],
            decay,
        )
        for ref, value in zip(ready[kind], results):
            ref[slot + index[1:] if slot else index] = value

    def send(kind, r=None):
        for j, ref in enumerate(ready[kind]):
            to = new[4 * j + kind]
            if r is None:
                number = 40 + 5 * (kind - 2) + j
            else:
                ref, to, number = ref.at[r % 2], to.at[r], 10 * r + 5 * kind + j
            copies[kind, r, j] = pltpu.make_async_copy(ref, to, sem.at[number])
            copies[kind, r, j].start()

    def finish(kind, r=None):
        for j in range(5):
            copies.pop((kind, r, j)).wait()

    for r in range(4):
        if r >= 2:
            finish(0, r - 2)
            finish(1, r - 2)
        arrived(0, r)
        arrived(1, r)
        for d in range(2):
            for j in range(4):
                lanes = slice(j * LANES, (j + 1) * LANES)
                at = j * 384 + d * B
                update(0, (r, d, slice(None), lanes), gs[r][at : at + B], DECAY, (r % 2,))
                at = j * 384 + 128 + d * H
                update(1, (r, d, slice(None), lanes), gs[r][at : at + H], DECAY, (r % 2,))
        send(0, r)
        send(1, r)
    arrived(2)
    arrived(3)
    for r in range(4):
        for j in range(2):
            at = ROWS_MAPS + j * B
            lanes = slice(r * 2 * H + j * LANES, r * 2 * H + (j + 1) * LANES)
            update(2, (slice(None), lanes), gs[r][at : at + B], DECAY)
    more = slice(ROWS_MORE, ROWS_MORE + B)
    update(2, (slice(None), slice(BASE, BASE + LANES)), gs[0][more], DECAY)
    update(2, (slice(None), slice(BASE + LANES, BASE + LANES + 32)), gs[1][more, :32], DECAY)
    send(2)
    update(3, (slice(None), slice(None)), gv[...], 0.0)
    send(3)
    for kind in (0, 1):
        for r in (2, 3):
            finish(kind, r)
    finish(2)
    finish(3)


def call(kernel, outs, ins, scratch, index=None, limit=56, micros=20, apart=(), given=()):
    vmem = pl.BlockSpec(memory_space=pltpu.VMEM)
    specs = [
        pl.BlockSpec(memory_space=pltpu.SMEM) if a.ndim == 1 and a.dtype == jnp.int32 else vmem
        for a in ins
    ]
    for i in apart:
        specs[i] = pl.BlockSpec(memory_space=pl.ANY)
    extra = []
    wrapped = kernel
    if index is not None:
        big = [i for i, a in enumerate(ins) if a.ndim == 4 and a.shape[:2] == (2 * LAYERS, 2)]
        for i in big:
            specs[i] = pl.BlockSpec(memory_space=pl.ANY)
        extra = [pltpu.VMEM((1,) + ins[i].shape[1:], F32) for i in big]
        extra.append(pltpu.SemaphoreType.DMA((len(big),)))

        def wrapped(*refs):
            refs = list(refs)
            held, sem = refs[len(refs) - len(extra) : -1], refs[-1]
            copies = []
            for j, i in enumerate(big):
                copies.append(pltpu.make_async_copy(refs[i].at[pl.ds(index, 1)], held[j], sem.at[j]))
                copies[-1].start()
            for copy in copies:
                copy.wait()
            for j, i in enumerate(big):
                refs[i] = held[j]
            kernel(*refs[: len(refs) - len(extra)])

    return pl.pallas_call(
        wrapped,
        out_shape=outs,
        in_specs=specs,
        out_specs=[
            pl.BlockSpec(memory_space=pl.ANY) if i in given else vmem for i in range(len(outs))
        ],
        scratch_shapes=list(scratch) + extra,
        compiler_params=pltpu.CompilerParams(vmem_limit_bytes=limit * 1024 * 1024),
        cost_estimate=pl.CostEstimate(
            flops=micros * 10**9, bytes_accessed=micros * 10**6, transcendentals=0
        ),
    )(*ins)


def shift(block, axis, distance):
    size = lax.axis_size(axis)
    route = [(i, i + distance) for i in range(size) if 0 <= i + distance < size]
    return lax.ppermute(block, axis, route)


def exchange(block):
    return lax.all_to_all(block, "block", split_axis=0, concat_axis=0, tiled=True)


def flip(block, bit):
    size = lax.axis_size("dp")
    return lax.ppermute(block, "dp", [(i, i ^ (1 << bit)) for i in range(size)])


def noted(power, loss, count):
    row = lax.broadcasted_iota(jnp.int32, (NOTES, LANES), 0)
    rows = jnp.where(row == 0, power, 0.0)
    for first, value in ((1, loss), (5, count)):
        rest = value * (1.0 / 1024.0**2)
        for j in range(4):
            digit = jnp.floor(rest) if j < 3 else rest
            rows = jnp.where(row == first + j, digit, rows)
            rest = (rest - digit) * 1024.0
    return rows.astype(HALF)


def scaled(value, power):
    return (value * jnp.exp2(TOP - power)).astype(HALF)


def read_notes(rows):
    rows = rows.astype(F32)
    power, *digits = (rows[..., i : i + 1, :] for i in range(9))
    loss, count = (
        (d[0] * 1024.0 + d[1]) * 1024.0 + (d[2] + d[3] * (1.0 / 1024.0))
        for d in (digits[:4], digits[4:])
    )
    return power, loss, count


def cut(block, start, size):
    return lax.dynamic_slice_in_dim(block, start, size, 0)


def chips(block):
    nb, dp = lax.axis_size("block"), lax.axis_size("dp")
    groups = [[i * dp + j for i in range(nb) for j in range(core, dp, 2)] for core in range(2)]
    return lax.all_to_all(
        block, ("block", "dp"), split_axis=0, concat_axis=0, tiled=True, axis_index_groups=groups
    )


def gradient_sums(block, notes):
    peers = lax.axis_size("block") * lax.axis_size("dp") // 2
    size = block.shape[0] // 2
    mine = lax.axis_index("dp") & 1
    other = flip(jnp.concatenate([cut(block, (1 - mine) * size, size), notes], 0), 0)
    power = jnp.maximum(notes[0:1], other[size : size + 1]) + 1.0
    loss, count = (notes[i : i + 1] + other[size + i : size + i + 1] for i in (1, 2))
    part = size // peers
    block = scaled(cut(block, mine * size, size) + other[:size], power)
    notes = jnp.broadcast_to(noted(power, loss, count)[None], (peers, NOTES, LANES))
    pieces = chips(jnp.concatenate([block.reshape(peers, part, LANES), notes], 1))
    powers, losses, counts = read_notes(pieces[:, part:])
    block = jnp.sum(pieces[:, :part].astype(F32) * jnp.exp2(powers - TOP), 0)
    loss, count = jnp.sum(losses, 0), jnp.sum(counts, 0)
    power = jnp.max(powers, 0) + (peers - 1).bit_length()
    mine = jnp.concatenate([scaled(block, power), noted(power, loss, count)], 0)
    block = chips(jnp.broadcast_to(mine[None], (peers,) + mine.shape))
    other = flip(block, 0)
    row = lax.broadcasted_iota(jnp.int32, (8, LANES), 0)
    totals = jnp.where(row == 0, loss, count)
    return [half.reshape(-1, LANES).astype(F32) for half in (block, other)] + [totals]


def shared_step(mixture, target, lengths, proj, vectors_wide, gi, gr):
    nb = lax.axis_size("block")
    RI = -(-K // nb) * M
    intra = Shape(TILES, K, M)
    inter = Shape(1, TILES * nb, RI)
    T = inter.steps
    reach = (HOP + 2) * STRIDE
    following = shift(jnp.stack([mixture[:, :reach], target[:, :reach]]), "block", -1)
    leading = shift(mixture[:, -STRIDE:], "block", 1)

    RP = -(-RI // 16) * 8
    res_shape = SDS((TILES, nb * RI, B), F32)
    send_shape = SDS((nb, TILES, RP, 2 * B), BF)
    steps_shape = SDS((T, RP, 2 * B), BF)
    x_shape = SDS((TILES * K * M, B), BF)

    def state(shape):
        return SDS((shape.groups * shape.wide, 2 * H), F32)

    res0, send, x0, h0, c0, win = call(
        functools.partial(first_kernel, intra, nb, RI),
        [res_shape, send_shape, x_shape, state(intra), state(intra), SDS((BLOCKS * M, 2 * STRIDE), BF)],
        [mixture, following, leading, lengths, proj, vectors_wide, gi, gr],
        fwd_scratch(intra)
        + [pltpu.VMEM((BLOCKS * M, 2 * STRIDE), F32), pltpu.VMEM((BLOCKS * M, B), F32)],
        0,
    )

    def inter_step(send, index):
        rows = exchange(send).reshape(T, RP, 2 * B)
        normed, h, c = call(
            functools.partial(inter_kernel, inter, RI, index),
            [steps_shape, state(inter), state(inter)],
            [rows, proj, vectors_wide, gi, gr],
            fwd_scratch(inter) + [pltpu.VMEM((inter.size, B), F32)],
            index,
        )
        return rows, h, c, exchange(normed.reshape(send_shape.shape))

    rows1, h1, c1, back = inter_step(send, 1)
    res2, send, x2, h2, c2 = call(
        functools.partial(third_kernel, intra, nb, RI),
        [res_shape, send_shape, x_shape, state(intra), state(intra)],
        [res0, back, lengths, proj, vectors_wide, gi, gr],
        fwd_scratch(intra),
        2,
    )
    rows3, h3, c3, back = inter_step(send, 3)
    edge_shape = SDS((EDGE_TOP, 2 * B), F32)
    part, up, down = call(
        functools.partial(part_kernel, nb, RI),
        [SDS(((FRAMES + HOP) * M, B), F32), edge_shape, edge_shape],
        [res2, back, lengths],
        [pltpu.VMEM(res_shape.shape, F32)],
    )
    before = shift(up, "block", 1)
    after = shift(down, "block", -1)
    tall = PADDED * M
    send, gres, genc, gm = call(
        functools.partial(middle_kernel, nb, RI),
        [send_shape, res_shape, SDS((FRAMES * M, B), F32), SDS((136, LANES), F32)],
        [part, before, after, lengths, win, target, following, proj, vectors_wide],
        [
            pltpu.VMEM((tall, B), F32),
            pltpu.VMEM((tall, 2 * STRIDE), F32),
            pltpu.VMEM((tall, STRIDE), F32),
            pltpu.VMEM((tall, STRIDE), F32),
            pltpu.VMEM((tall, B), F32),
            pltpu.VMEM((tall, B), F32),
            pltpu.VMEM((tall, B), F32),
            pltpu.VMEM((tall, B), F32),
        ],
    )
    out_shape = SDS((ROWS_G, LANES), F32)

    def inter_back(send, rows, h, c, index):
        grad_rows = exchange(send).reshape(T, RP, 2 * B)
        send, out = call(
            functools.partial(inter_back_kernel, inter, RI, index),
            [steps_shape, out_shape],
            [grad_rows, rows, h, c, proj, vectors_wide, gi, gr],
            [pltpu.VMEM((inter.size, B), F32)] * 2 + back_scratch(inter),
            index,
        )
        return exchange(send.reshape(send_shape.shape)), out

    back, out3 = inter_back(send, rows3, h3, c3, 3)
    gres, send, out2 = call(
        functools.partial(third_back_kernel, intra, nb, RI),
        [res_shape, send_shape, out_shape],
        [gres, back, lengths, x2, h2, c2, proj, vectors_wide, gi, gr],
        back_scratch(intra),
        2,
    )
    back, out1 = inter_back(send, rows1, h1, c1, 1)
    out0, out1 = call(
        functools.partial(first_back_kernel, intra, nb, RI),
        [out_shape, out_shape],
        [gres, back, lengths, x0, h0, c0, proj, vectors_wide, gi, gr, win, genc, gm, out1],
        [pltpu.VMEM(res_shape.shape, F32), pltpu.VMEM((BLOCKS * M, B), F32)] + back_scratch(intra),
        0,
    )
    parts = nb * lax.axis_size("dp") * NOTES
    more = jnp.zeros((-4 * ROWS_G % parts, LANES), F32)
    outs = jnp.concatenate([out0, out1, out2, out3, more], 0)
    at = ROWS_MORE + B + 4
    return outs, note_rows(jnp.max(jnp.abs(outs)), outs[at : at + 1], outs[at + 1 : at + 2])


def local_step(mixture, target, lengths, proj, vectors_wide, gi, gr):
    RI = -(-K // M) * M
    intra = Shape(TILES, K, M)
    inter = Shape(1, TILES * M, RI)
    pad = jnp.zeros((M, -(FRAMES * STRIDE) % LANES), F32)
    waves = jnp.concatenate([mixture, pad, target, pad], 1)
    waves = lax.all_to_all(waves.reshape(M, 1, -1), "block", split_axis=0, concat_axis=0, tiled=True)
    return call(
        functools.partial(local_kernel, intra, inter, RI),
        [SDS((4 * ROWS_G, LANES), F32), SDS((8, LANES), F32)],
        [waves.reshape(M, -1), lengths, proj, vectors_wide, gi, gr],
        local_scratch(intra, inter),
        limit=62,
        apart=(4, 5),
        given=(0,),
    )


def body(
    mixture,
    target,
    lengths,
    input_gates,
    recur_gates,
    projections,
    vectors,
    moment_input,
    moment_recur,
    moment_proj,
    moment_vecs,
    square_input,
    square_recur,
    square_proj,
    square_vecs,
    average_input,
    average_recur,
    average_proj,
    average_vecs,
):
    nb = lax.axis_size("block")
    proj = projections.T
    vectors_wide = vectors.reshape(-1, LANES)
    step = local_step if nb == M else shared_step
    outs, notes = step(mixture, target, lengths, proj, vectors_wide, input_gates, recur_gates)
    sums = gradient_sums(outs, notes)
    old = [
        input_gates, recur_gates, projections, vectors,
        moment_input, moment_recur, moment_proj, moment_vecs,
        square_input, square_recur, square_proj, square_vecs,
        average_input, average_recur, average_proj, average_vecs,
    ]
    for i in range(2, 16, 4):
        old[i] = old[i].T
    for i in range(3, 16, 4):
        old[i] = old[i].reshape(-1, LANES)
    new = [SDS(a.shape, F32) for a in old[:4]] * 4 + [SDS(a.shape, BF) for a in old[:4]]
    scalars, *new = call(
        adam_kernel,
        [SDS((8, LANES), F32)] + new,
        sums + old,
        [
            pltpu.VMEM(old[3].shape, F32),
            pltpu.VMEM(outs.shape, F32),
            pltpu.SemaphoreType.DMA((50 + 48,)),
        ]
        + [
            pltpu.VMEM(((2,) if i < 2 else ()) + old[i].shape[i < 2 :], F32 if j < 4 else BF)
            for i in range(4)
            for j in range(5)
        ]
        + [pltpu.VMEM(a.shape, F32) for a in old],
        limit=56,
        apart=range(3, 19),
        given=range(1, 21),
    )
    for i in range(2, 20, 4):
        new[i] = new[i].T
    for i in range(3, 20, 4):
        new[i] = new[i].reshape(-1)
    return (scalars[0, 0], scalars[1, 0], scalars[2, 0], *new)


def solution(mesh):
    in_specs = (P("dp", "block"), P("dp", "block"), P("dp")) + (P(),) * 16
    return jax.shard_map(
        body, mesh=mesh, in_specs=in_specs, out_specs=(P(),) * 23, check_vma=False
    )
```

```python
import functools

import jax
import jax.numpy as jnp
from jax import lax
from jax.experimental import pallas as pl
from jax.experimental.pallas import tpu as pltpu
from jax.sharding import PartitionSpec as P

N = 64
B = 64
H = 128
K = 100
STRIDE = 8
LAYERS = 2
STEP = 10
HOP = 50
TILES = 3
M = 8
FRAMES = 150
BASE = 4 * LAYERS * H
PERIOD = 8 * H + 3 * B
ROWS_MAPS = 1536
ROWS_VECS = 1664
ROWS_MORE = 1680
ROWS_G = 1792
LANES = 128
BLOCKS = 208
PADDED = 216
CHUNK = 416

EPS_NORM = 1e-05
CLIP = 0.001
RATE = 0.1
BETA_ONE = 0.9
BETA_TWO = 0.999
ADAM_EPS = 1e-08
DECAY = 0.01
KEEP = 0.9

BF = jnp.bfloat16
F32 = jnp.float32
TOP = 13.0
NOTES = 16
HALF = jnp.float16
SDS = jax.ShapeDtypeStruct


def dot(left, right):
    return jnp.dot(left, right, preferred_element_type=F32)


def dot_turned(left, right):
    return lax.dot_general(left, right, (((1,), (1,)), ((), ())), preferred_element_type=F32)


def dot_rows(left, right):
    return lax.dot_general(left, right, (((0,), (0,)), ((), ())), preferred_element_type=F32)


def half_scale():
    lane = lax.broadcasted_iota(jnp.int32, (1, 4 * H), 1)
    return jnp.where((lane >= 2 * H) & (lane < 3 * H), 1.0, 0.5)


def gate_acts(z):
    act = jnp.tanh(z)
    sig_i = 0.5 * act[:, :H] + 0.5
    sig_f = 0.5 * act[:, H : 2 * H] + 0.5
    sig_o = 0.5 * act[:, 3 * H :] + 0.5
    return sig_i, sig_f, act[:, 2 * H : 3 * H], sig_o


def norm_parts(value):
    center = value - jnp.mean(value, -1, keepdims=True)
    spread = jnp.mean(center * center, -1, keepdims=True)
    scale = lax.rsqrt(spread + EPS_NORM)
    return center * scale, scale


def norm_back(grad, unit, scale, gain):
    inner = grad * gain
    return scale * (
        inner
        - jnp.mean(inner, -1, keepdims=True)
        - unit * jnp.mean(inner * unit, -1, keepdims=True)
    )


def live(lim, start, count):
    pos = lax.broadcasted_iota(jnp.int32, (count, M, B), 0) + start
    return jnp.where(pos * STRIDE < lim[None], 1.0, 0.0).reshape(count * M, B)


def limits(lengths):
    row = lax.broadcasted_iota(jnp.int32, (M, B), 0)
    total = jnp.zeros((M, B), jnp.int32)
    for m in range(M):
        total = jnp.where(row == m, lengths[m], total)
    return total - lax.axis_index("block") * (FRAMES * STRIDE)


def pieces(vectors, start, count):
    parts = []
    at = start
    while at < start + count:
        wide = at % 2 == 0 and at + 2 <= start + count
        lane = (at % 2) * N
        parts.append(vectors[at // 2 : at // 2 + 1, lane : lane + (2 * N if wide else N)])
        at += 2 if wide else 1
    return parts[0] if len(parts) == 1 else jnp.concatenate(parts, 1)


def branch_vectors(vectors, index):
    first = (2 * N + B + index * PERIOD) // N
    half = half_scale()
    bias = [pieces(vectors, first + 8 * d, 8) * half for d in range(2)]
    return bias, [pieces(vectors, first + 16 + j, 1) for j in range(3)]


def own(start, count):
    pos = lax.broadcasted_iota(jnp.int32, (count, M, B), 0) + start
    return jnp.where(pos < FRAMES, 1.0, 0.0).reshape(count * M, B)


def chunk_of(steps, rows):
    best = 1
    for size in range(1, steps + 1):
        if steps % size == 0 and size * rows <= 1024 and size * rows % 16 == 0:
            best = size
    return best


class Shape:
    def __init__(self, groups, steps, rows):
        self.groups, self.steps, self.rows = groups, steps, rows
        self.size = steps * rows
        self.chunk = chunk_of(steps, rows)
        self.crows = self.chunk * rows
        self.chunks = steps // self.chunk
        self.wide = (steps + 2) * rows
        self.unroll = max(n for n in range(1, 26) if steps % n == 0)


def chunk_loop(shape, fn):
    for g in range(shape.groups):
        for i in range(shape.chunks):
            fn(g, i, i * shape.crows)


def forward_weights(gi, gr, index, wc):
    half = half_scale()
    for d in range(2):
        wc[d, :H] = (gr[index, d].astype(BF).astype(F32) * half).astype(BF)
        wc[d, H:] = (gi[index, d].astype(BF).astype(F32) * half).astype(BF)


def lstm_scan(shape, pg, wc, h_ref, c_ref):
    G, S, R = shape.groups, shape.steps, shape.rows
    pad = jnp.zeros((R, 2 * H), F32)
    for g in range(G):
        for ref in (h_ref, c_ref):
            ref[g * shape.wide : g * shape.wide + R] = pad
            ref[(g + 1) * shape.wide - R : (g + 1) * shape.wide] = pad

    rows = G * R
    zero = jnp.zeros((rows, H), F32)
    held = jnp.concatenate([wc[0, :H], wc[1, :H]], 0)

    def one(d, t, z, memory):
        at = pl.multiple_of(t * R, 8)
        pre = jnp.concatenate([pg[d, pl.ds(g * shape.size + at, R), :] for g in range(G)], 0)
        sig_i, sig_f, tan_g, sig_o = gate_acts(pre + z)
        memory = sig_f * memory + sig_i * tan_g
        hidden = (sig_o * jnp.tanh(memory)).astype(BF).astype(F32)
        after = pl.multiple_of(t * R + R, 8)
        for g in range(G):
            to = pl.ds(g * shape.wide + after, R)
            h_ref[to, d * H : (d + 1) * H] = hidden[g * R : (g + 1) * R]
            c_ref[to, d * H : (d + 1) * H] = memory[g * R : (g + 1) * R]
        return hidden, memory

    def step(s, carry):
        hf, cf, hb, cb = carry
        both = jnp.concatenate(
            [jnp.concatenate([hf, zero], 1), jnp.concatenate([zero, hb], 1)], 0
        ).astype(BF)
        z = dot(both, held)
        hf, cf = one(0, s, z[:rows], cf)
        hb, cb = one(1, S - 1 - s, z[rows:], cb)
        return hf, cf, hb, cb

    lax.fori_loop(0, S, step, (zero,) * 4, unroll=shape.unroll)


def lstm_scan_back(shape, z, dh, c_ref, wrt):
    G, S, R = shape.groups, shape.steps, shape.rows

    def one(d, t, rec_hidden, rec_memory):
        def take(ref, at, width, lanes):
            at = pl.multiple_of(at, 8)
            return jnp.concatenate([ref[pl.ds(g * width + at, R), lanes] for g in range(G)], 0)

        lanes = slice(d * H, (d + 1) * H)
        at = pl.multiple_of(t * R, 8)
        zt = jnp.concatenate([z[d, pl.ds(g * shape.size + at, R), :] for g in range(G)], 0)
        sig_i, sig_f, tan_g, sig_o = gate_acts(zt)
        tan_c = jnp.tanh(take(c_ref, t * R + R, shape.wide, lanes))
        before = take(c_ref, t * R + 2 * R * d, shape.wide, lanes)
        grad_h = take(dh, t * R, shape.size, lanes) + rec_hidden
        grad_c = rec_memory + grad_h * (sig_o * (1.0 - tan_c * tan_c))
        grad_pre = jnp.concatenate(
            [
                grad_c * (tan_g * sig_i * (1.0 - sig_i)),
                grad_c * (before * sig_f * (1.0 - sig_f)),
                grad_c * (sig_i * (1.0 - tan_g * tan_g)),
                grad_h * (tan_c * sig_o * (1.0 - sig_o)),
            ],
            -1,
        ).astype(BF)
        full = grad_pre.astype(F32)
        for g in range(G):
            z[d, pl.ds(g * shape.size + at, R), :] = full[g * R : (g + 1) * R]
        return dot(grad_pre, wrt[d]), grad_c * sig_f

    def step(s, carry):
        hf, cf, hb, cb = carry
        hf, cf = one(0, S - 1 - s, hf, cf)
        hb, cb = one(1, s, hb, cb)
        return hf, cf, hb, cb

    zero = jnp.zeros((G * R, H), F32)
    lax.fori_loop(0, S, step, (zero,) * 4, unroll=shape.unroll)


def branch_pregates(shape, inputs, wc, bias, pg):
    def fill(g, i, r0):
        x = inputs(g, r0).astype(BF)
        for d in range(2):
            pg[d, pl.ds(g * shape.size + r0, shape.crows), :] = dot(x, wc[d, H:]) + bias[d]

    chunk_loop(shape, fill)


def branch_back(shape, grads, inputs, h_ref, c_ref, weights, index, vecs, turned_out, out, scratch):
    gi, gr = weights
    wc, wit, wrt, wot, z, dh = scratch
    n, R = shape.crows, shape.rows
    forward_weights(gi, gr, index, wc)
    for d in range(2):
        wit[d] = jnp.transpose(gi[index, d]).astype(BF)
        wrt[d] = jnp.transpose(gr[index, d]).astype(BF)
    wot[...] = turned_out.astype(BF)
    out[...] = jnp.zeros(out.shape, F32)
    bias, (o_bias, gain, _) = vecs

    def states(g, at, lanes):
        return h_ref[pl.ds(pl.multiple_of(g * shape.wide + at, 8), n), lanes].astype(BF)

    def earlier(g, r0, d):
        before = states(g, r0 + 2 * R * d, slice(d * H, (d + 1) * H))
        return jnp.concatenate([before, inputs(g, r0).astype(BF)], 1)

    def first(g, i, r0):
        now = states(g, r0 + R, slice(0, 2 * H))
        here = pl.ds(g * shape.size + r0, n)
        unit, scale = norm_parts(dot_turned(now, wot[...]) + o_bias)
        grad = grads(g, r0)
        low = norm_back(grad, unit, scale, gain).astype(BF)
        dh[here, :] = dot(low, wot[...])
        turned = dot_rows(low, now)
        for j in range(2):
            at = ROWS_MAPS + j * B
            out[at : at + B] += turned[:, j * LANES : (j + 1) * LANES]
        for j, value in enumerate((low.astype(F32), grad * unit, grad)):
            at = ROWS_VECS + 8 + j
            out[at : at + 1, :B] += jnp.sum(value, 0, keepdims=True)
        for d in range(2):
            z[d, here, :] = dot(earlier(g, r0, d), wc[d]) + bias[d]

    chunk_loop(shape, first)
    lstm_scan_back(shape, z, dh, c_ref, wrt)

    def last(use):
        def fn(g, i, r0):
            total = None
            for d in range(2):
                full = z[d, pl.ds(g * shape.size + r0, n), :]
                low = full.astype(BF)
                maps = dot_rows(earlier(g, r0, d), low)
                grad_bias = jnp.sum(full, 0, keepdims=True)
                for j in range(4):
                    lanes = slice(j * LANES, (j + 1) * LANES)
                    at = j * 384 + d * B
                    out[at : at + B] += maps[H:, lanes]
                    at = j * 384 + 128 + d * H
                    out[at : at + H] += maps[:H, lanes]
                    at = ROWS_VECS + 4 * d + j
                    out[at : at + 1] += grad_bias[:, lanes]
                part = dot(low, wit[d])
                total = part if total is None else total + part
            use(g, i, r0, total)

        chunk_loop(shape, fn)

    return last


def fwd_scratch(shape):
    return [
        pltpu.VMEM((2, H + B, 4 * H), BF),
        pltpu.VMEM((2, shape.groups * shape.size, 4 * H), F32),
    ]


def back_scratch(shape):
    return [
        pltpu.VMEM((2, H + B, 4 * H), BF),
        pltpu.VMEM((2, 4 * H, B), BF),
        pltpu.VMEM((2, 4 * H, H), BF),
        pltpu.VMEM((B, 2 * H), BF),
        pltpu.VMEM((2, shape.groups * shape.size, 4 * H), F32),
        pltpu.VMEM((shape.groups * shape.size, 2 * H), F32),
    ]


def packed(value, RP):
    rest = value[RP:]
    if rest.shape[0] < RP:
        rest = jnp.concatenate([rest, jnp.zeros((RP - rest.shape[0], B), F32)], 0)
    return jnp.concatenate([value[:RP], rest], 1).astype(BF)


def send_tiles(res, send, nb, RI):
    RP = send.shape[2]
    for d in range(nb):
        for c in range(TILES):
            send[d, c] = packed(res[c, d * RI : (d + 1) * RI], RP)


def add_tiles(res, back, nb, RI, lim):
    RP = back.shape[2]
    for d in range(nb):
        for c in range(TILES):
            both = back[d, c].astype(F32)
            for lo, hi, value in (
                (0, RP, both[:, :B]),
                (RP, RI, both[:, B:]),
            ):
                lo, hi = d * RI + lo, min(d * RI + hi, K * M)
                if lo >= hi:
                    continue
                mask = live(lim, c * HOP + lo // M, (hi - lo) // M)
                res[c, lo:hi] = (res[c, lo:hi] + value[: hi - lo]) * mask


def unpack_steps(rows, xs, T, RI):
    RP = rows.shape[1]

    def widen(t, _):
        both = rows[t].astype(F32)
        xs[pl.ds(pl.multiple_of(t * RI, 8), RP), :] = both[:, :B]
        if RI > RP:
            xs[pl.ds(pl.multiple_of(t * RI + RP, 8), RI - RP), :] = both[: RI - RP, B:]
        return 0

    lax.fori_loop(0, T, widen, 0, unroll=4 if T % 4 == 0 else 1)


def windows_of(mix, following, win):
    last = FRAMES + HOP + 1
    for i in range(1, BLOCKS):
        at = STRIDE * (i - 1)
        if at + 2 * STRIDE <= FRAMES * STRIDE:
            win[i * M : (i + 1) * M] = mix[:, at : at + 2 * STRIDE]
        elif at < FRAMES * STRIDE:
            win[i * M : (i + 1) * M] = jnp.concatenate([mix[:, at:], following[:, :STRIDE]], 1)
        elif i <= last:
            at -= FRAMES * STRIDE
            win[i * M : (i + 1) * M] = following[:, at : at + 2 * STRIDE]
        else:
            win[i * M :] = jnp.zeros(((BLOCKS - i) * M, 2 * STRIDE), F32)
            break


def softplus(value):
    return jnp.maximum(value, 0.0) + jnp.log1p(jnp.exp(-jnp.abs(value)))


def turned_out(proj, index):
    return proj[:, index * 2 * H : (index + 1) * 2 * H]


def intra_forward(shape, index, res, lim, gi, gr, slot, vectors, proj, x_out, h_out, c_out, scratch):
    wc, pg = scratch
    forward_weights(gi, gr, slot, wc)
    bias, (o_bias, gain, beta) = branch_vectors(vectors, index)
    n = shape.crows

    def inputs(g, r0):
        x = res[g, pl.ds(r0, n), :].astype(BF)
        x_out[pl.ds(pl.multiple_of(g * shape.size + r0, 16), n), :] = x
        return x

    branch_pregates(shape, inputs, wc, bias, pg)
    lstm_scan(shape, pg, wc, h_out, c_out)
    low_out = turned_out(proj, index).astype(BF)

    def close(g, i, r0):
        now = h_out[pl.ds(pl.multiple_of(g * shape.wide + r0 + shape.rows, 8), n), :].astype(BF)
        unit, _ = norm_parts(dot_turned(now, low_out) + o_bias)
        mask = live(lim, g * HOP + i * shape.chunk, shape.chunk)
        res[g, pl.ds(r0, n), :] = (res[g, pl.ds(r0, n), :] + (unit * gain + beta)) * mask

    chunk_loop(shape, close)


def inter_forward(shape, index, xs, gi, gr, slot, vectors, proj, h_out, c_out, scratch, use):
    wc, pg = scratch
    forward_weights(gi, gr, slot, wc)
    bias, (o_bias, gain, beta) = branch_vectors(vectors, index)
    n = shape.crows
    branch_pregates(shape, lambda g, r0: xs[pl.ds(r0, n), :], wc, bias, pg)
    lstm_scan(shape, pg, wc, h_out, c_out)
    low_out = turned_out(proj, index).astype(BF)

    def close(g, i, r0):
        now = h_out[pl.ds(pl.multiple_of(r0 + shape.rows, 8), n), :].astype(BF)
        unit, _ = norm_parts(dot_turned(now, low_out) + o_bias)
        use(i, r0, unit * gain + beta)

    chunk_loop(shape, close)


def zero_tail(res, c):
    if res.shape[1] > K * M:
        res[c, K * M :] = jnp.zeros((res.shape[1] - K * M, B), F32)


def encode(mix, following, leading, lim, proj, vectors, win, flat, bottle, res):
    flat[:M] = jnp.concatenate([leading[...], mix[:, :STRIDE]], 1)
    windows_of(mix, following, flat)
    win[...] = flat[...].astype(BF)
    w_enc = proj[:, BASE + N + B : BASE + N + B + 2 * STRIDE].astype(BF)
    w_bn = proj[:, BASE : BASE + N].astype(BF)
    gain, beta, b_bias = (pieces(vectors, j, 1) for j in range(3))
    for i in range(BLOCKS * M // CHUNK):
        at = i * CHUNK
        pre = dot_turned(win[at : at + CHUNK], w_enc)
        unit, _ = norm_parts(softplus(pre))
        normed = (unit * gain + beta).astype(BF)
        mask = live(lim, i * (CHUNK // M) - 1, CHUNK // M)
        bottle[at : at + CHUNK] = (dot_turned(normed, w_bn) + b_bias) * mask
    for c in range(TILES):
        res[c, : K * M] = bottle[(c * HOP + 1) * M : (c * HOP + 1 + K) * M]
        zero_tail(res, c)


def first_kernel(shape, nb, RI, mix, following, leading, lengths, proj, vectors, gi, gr, res, send, x_out, h_out, c_out, win, wc, pg, flat, bottle):
    lim = limits(lengths)
    encode(mix, following.at[0], leading, lim, proj, vectors, win, flat, bottle, res)
    intra_forward(shape, 0, res, lim, gi, gr, 0, vectors, proj, x_out, h_out, c_out, (wc, pg))
    send_tiles(res, send, nb, RI)


def third_kernel(shape, nb, RI, res_in, back, lengths, proj, vectors, gi, gr, res, send, x_out, h_out, c_out, wc, pg):
    lim = limits(lengths)
    res[...] = res_in[...]
    add_tiles(res, back, nb, RI, lim)
    intra_forward(shape, 2, res, lim, gi, gr, 0, vectors, proj, x_out, h_out, c_out, (wc, pg))
    send_tiles(res, send, nb, RI)


def inter_kernel(shape, RI, index, rows, proj, vectors, gi, gr, normed, h_out, c_out, wc, pg, xs):
    unpack_steps(rows, xs, shape.steps, RI)
    RP = normed.shape[1]

    def use(i, r0, value):
        for j in range(shape.chunk):
            normed[i * shape.chunk + j] = packed(value[j * RI : (j + 1) * RI], RP)

    inter_forward(shape, index, xs, gi, gr, 0, vectors, proj, h_out, c_out, (wc, pg), use)


EDGE = (HOP + 1) * M
EDGE_TOP = 208


def edge_pack(value):
    rest = jnp.concatenate([value[EDGE_TOP:], jnp.zeros((2 * EDGE_TOP - EDGE, B), F32)], 0)
    return jnp.concatenate([value[:EDGE_TOP], rest], 1)


def edge_unpack(ref):
    return jnp.concatenate([ref[:, :B], ref[: EDGE - EDGE_TOP, B:]], 0)


def parts_of(res, part):
    half = HOP * M
    part[:half] = res[0, :half]
    for c in range(1, TILES):
        part[c * half : (c + 1) * half] = res[c, :half] + res[c - 1, half : 2 * half]
    part[TILES * half :] = res[TILES - 1, half : 2 * half]


def part_kernel(nb, RI, res_in, back, lengths, part, up, down, res):
    res[...] = res_in[...]
    add_tiles(res, back, nb, RI, limits(lengths))
    parts_of(res, part)
    half = HOP * M
    up[...] = edge_pack(part[TILES * half - M :])
    down[...] = edge_pack(part[: half + M])


def middle_kernel(nb, RI, part, before, after, lengths, win, goal, following, proj, vectors, send, gres, genc, gm, *scratch):
    edge = jnp.where(lax.axis_index("block") > 0, 1.0, 0.0)
    middle(
        part, edge_unpack(before), edge_unpack(after), limits(lengths), edge, win, goal,
        following.at[1], proj, vectors, gres, genc, gm, *scratch,
    )
    send_tiles(gres, send, nb, RI)


def middle(part, early, late, lim, edge, win, goal, following, proj, vectors, gres, genc, gm, feats, dec, tgt, gest, enc, gate, src, act):
    half = HOP * M
    top = M + TILES * half
    total = BLOCKS * M
    feats[:M] = early[:M]
    feats[M : M + half] = part[:half] + early[M:]
    feats[M + half : top] = part[half : TILES * half]
    feats[top : top + half] = part[TILES * half :] + late[:half]
    feats[top + half : top + half + M] = late[half:]
    feats[top + half + M :] = jnp.zeros((PADDED * M - top - half - M, B), F32)
    low_mask = proj[:, BASE + N : BASE + N + B].astype(BF)
    w_enc = proj[:, BASE + N + B : BASE + N + B + 2 * STRIDE].astype(BF)
    low_dec = proj[:, BASE + N + B + 2 * STRIDE : BASE + N + B + 4 * STRIDE].astype(BF)
    m_bias = pieces(vectors, vectors.shape[0] * 2 - 1, 1)
    root = 0.7978845608028654
    cube = 0.044715
    dec[total:] = jnp.zeros((PADDED * M - total, 2 * STRIDE), F32)
    for i in range(total // CHUNK):
        rows = slice(i * CHUNK, (i + 1) * CHUNK)
        x = feats[rows]
        low = (0.5 * x * (1.0 + jnp.tanh(root * (x + cube * x * x * x)))).astype(BF)
        encoded = softplus(dot_turned(win[rows], w_enc))
        mask = 0.5 * jnp.tanh(0.5 * (dot_turned(low, low_mask) + m_bias)) + 0.5
        source = (mask * encoded).astype(BF)
        enc[rows] = encoded
        gate[rows] = mask
        src[rows] = source.astype(F32)
        act[rows] = low.astype(F32)
        dec[rows] = dot(source, low_dec)
    dec[:M] = dec[:M] * edge
    for ref in (enc, gate, src, act):
        ref[total:] = jnp.zeros((PADDED * M - total, B), F32)
    for i in range(1, FRAMES + 1):
        tgt[i * M : (i + 1) * M] = goal[:, STRIDE * (i - 1) : STRIDE * i]
    for i in range(FRAMES + 1, FRAMES + HOP + 2):
        at = STRIDE * (i - 1 - FRAMES)
        tgt[i * M : (i + 1) * M] = following[:, at : at + STRIDE]
    tgt[(FRAMES + HOP + 2) * M :] = jnp.zeros(((PADDED - FRAMES - HOP - 2) * M, STRIDE), F32)
    estimate = dec[M:total, :STRIDE] + dec[: total - M, STRIDE:]
    count = BLOCKS - 1
    spot = lax.broadcasted_iota(jnp.int32, (count, M, STRIDE), 0)
    phase = lax.broadcasted_iota(jnp.int32, (count, M, STRIDE), 2)
    near = spot < FRAMES + HOP + 1
    valid = jnp.where(near & (spot * STRIDE + phase < lim[:, :STRIDE][None]), 1.0, 0.0)
    inside = jnp.where(spot < FRAMES, valid, 0.0).reshape(count * M, STRIDE)
    valid = valid.reshape(count * M, STRIDE)
    error = estimate - tgt[M:total]
    smoothed = jnp.sqrt(error * error + 1.0)
    gest[:M] = jnp.zeros((M, STRIDE), F32)
    gest[M:total] = valid * error / smoothed
    gest[total:] = jnp.zeros((PADDED * M - total, STRIDE), F32)
    loss = jnp.sum(jnp.sum(inside * (smoothed - 1.0), 0, keepdims=True), 1, keepdims=True)
    seen = jnp.sum(jnp.sum(inside, 0, keepdims=True), 1, keepdims=True)
    gm[...] = jnp.zeros_like(gm)
    gm[132:133] = jnp.broadcast_to(loss, (1, LANES))
    gm[133:134] = jnp.broadcast_to(seen, (1, LANES))
    for i in range(total // CHUNK):
        at = i * CHUNK + M
        rows = slice(at, at + CHUNK)
        grad_dec = jnp.concatenate([gest[rows], gest[at + M : at + M + CHUNK]], 1).astype(BF)
        mine = own(i * (CHUNK // M), CHUNK // M)
        mine_low = mine.astype(BF)
        gm[64:128, 16:32] += dot_rows(src[rows].astype(BF) * mine_low, grad_dec)
        grad_source = dot_turned(grad_dec, low_dec)
        mask = gate[rows]
        grad_logit = (grad_source * enc[rows] * mask * (1.0 - mask)).astype(BF)
        enc[rows] = grad_source * mask
        gm[:64, 64:] += dot_rows(grad_logit * mine_low, act[rows].astype(BF))
        gm[131:132, :B] += jnp.sum(grad_logit.astype(F32) * mine, 0, keepdims=True)
        x = feats[rows]
        curve = jnp.tanh(root * (x + cube * x * x * x))
        slope = 0.5 * (1.0 + curve) + (0.5 * root) * x * (1.0 - curve * curve) * (
            1.0 + (3.0 * cube) * x * x
        )
        feats[rows] = slope * dot(grad_logit, low_mask)
    genc[...] = enc[M : M + FRAMES * M]
    for c in range(TILES):
        gres[c, : K * M] = feats[M + c * half : M + c * half + K * M] * live(lim, c * HOP, K)
        zero_tail(gres, c)


def inter_back(shape, index, gs, xs, h_ref, c_ref, proj, vectors, gi, gr, slot, out, core, use):
    n = shape.crows
    last = branch_back(
        shape,
        lambda g, r0: gs[pl.ds(r0, n), :],
        lambda g, r0: xs[pl.ds(r0, n), :],
        h_ref, c_ref, (gi, gr), slot, branch_vectors(vectors, index), turned_out(proj, index), out, core,
    )
    last(use)


def inter_back_kernel(shape, RI, index, grad_rows, rows, h_ref, c_ref, proj, vectors, gi, gr, send, out, *scratch):
    xs, gs, core = scratch[0], scratch[1], scratch[2:]
    unpack_steps(rows, xs, shape.steps, RI)
    unpack_steps(grad_rows, gs, shape.steps, RI)
    RP = send.shape[1]

    def use(g, i, r0, total):
        for j in range(shape.chunk):
            send[i * shape.chunk + j] = packed(total[j * RI : (j + 1) * RI], RP)

    inter_back(shape, index, gs, xs, h_ref, c_ref, proj, vectors, gi, gr, 0, out, core, use)


def intra_back(shape, index, gres, x_ref, h_ref, c_ref, proj, vectors, gi, gr, slot, out, core):
    n = shape.crows

    def inputs(g, r0):
        return x_ref[pl.ds(pl.multiple_of(g * shape.size + r0, 16), n), :]

    last = branch_back(
        shape,
        lambda g, r0: gres[g, pl.ds(r0, n), :],
        inputs,
        h_ref, c_ref, (gi, gr), slot, branch_vectors(vectors, index), turned_out(proj, index), out, core,
    )

    def use(g, i, r0, total):
        gres[g, pl.ds(r0, n), :] = gres[g, pl.ds(r0, n), :] + total

    last(use)


def third_back_kernel(shape, nb, RI, gres_in, back, lengths, x_ref, h_ref, c_ref, proj, vectors, gi, gr, gres, send, out, *core):
    lim = limits(lengths)
    gres[...] = gres_in[...]
    add_tiles(gres, back, nb, RI, lim)
    intra_back(shape, 2, gres, x_ref, h_ref, c_ref, proj, vectors, gi, gr, 0, out, core)
    for c in range(TILES):
        gres[c, : K * M] = gres[c, : K * M] * live(lim, c * HOP, K)
    send_tiles(gres, send, nb, RI)


def first_back_kernel(shape, nb, RI, gres_in, back, lengths, x_ref, h_ref, c_ref, proj, vectors, gi, gr, win, genc, gm, more_in, out, more, gres, bottle, *core):
    lim = limits(lengths)
    more[...] = more_in[...]
    gres[...] = gres_in[...]
    add_tiles(gres, back, nb, RI, lim)
    intra_back(shape, 0, gres, x_ref, h_ref, c_ref, proj, vectors, gi, gr, 0, out, core)
    encode_back(gres, lim, proj, vectors, win, genc, gm, out, more, bottle)


def encode_back(gres, lim, proj, vectors, win, genc, gm, out, more, bottle):
    at_first, at_vecs = ROWS_MORE, ROWS_MORE + B
    out[at_first : at_first + B] = gm[:B]
    out[at_vecs : at_vecs + 8] = gm[2 * B :]
    more[at_first : at_first + B] = gm[B : 2 * B]
    bottle[...] = jnp.zeros(bottle.shape, F32)
    for c in range(TILES):
        at = (c * HOP + 1) * M
        bottle[at : at + K * M] += gres[c, : K * M]
    w_enc = proj[:, BASE + N + B : BASE + N + B + 2 * STRIDE].astype(BF)
    w_bn = proj[:, BASE : BASE + N].astype(BF)
    gain, beta = (pieces(vectors, j, 1) for j in range(2))
    own_rows = FRAMES * M
    for i in range(BLOCKS * M // CHUNK):
        at = i * CHUNK
        rows = slice(at, at + CHUNK)
        pre = dot_turned(win[rows], w_enc)
        unit, scale = norm_parts(softplus(pre))
        normed = (unit * gain + beta).astype(BF)
        low = (bottle[rows] * live(lim, i * (CHUNK // M) - 1, CHUNK // M)).astype(BF)
        out[at_first : at_first + B, :N] += dot_rows(low, normed)
        grad_normed = dot(low, w_bn)
        for j, value in enumerate((grad_normed * unit, grad_normed, low.astype(F32))):
            out[at_vecs + j : at_vecs + j + 1, :B] += jnp.sum(value, 0, keepdims=True)
        grad_enc = norm_back(grad_normed, unit, scale, gain)
        lo, hi = max(at - M, 0), min(at + CHUNK - M, own_rows)
        if lo < hi:
            piece = genc[lo:hi]
            above, below = lo + M - at, at + CHUNK - M - hi
            if above:
                piece = jnp.concatenate([jnp.zeros((above, B), F32), piece], 0)
            if below:
                piece = jnp.concatenate([piece, jnp.zeros((below, B), F32)], 0)
            grad_enc = grad_enc + piece
        grad_pre = (grad_enc * (0.5 * jnp.tanh(0.5 * pre) + 0.5)).astype(BF)
        more[at_first : at_first + B, :16] += dot_rows(grad_pre, win[rows])


def turn_in(res, xs, RI, lowered=True):
    for j in range(M):
        for c in range(TILES):
            at = (TILES * j + c) * RI
            value = res[c, pl.ds(j, K, stride=M), :]
            xs[at : at + K] = value.astype(BF).astype(F32)


def turn_back(res, xs, RI, length):
    pos = lax.broadcasted_iota(jnp.int32, (K, B), 0)
    for j in range(M):
        for c in range(TILES):
            at = (TILES * j + c) * RI
            mask = jnp.where((pos + (FRAMES * j + HOP * c)) * STRIDE < length, 1.0, 0.0)
            where = (c, pl.ds(j, K, stride=M), slice(None))
            res[where] = (res[where] + xs[at : at + K]) * mask


class Strip:
    def __init__(self, ref, part, lane, rows, width):
        self.ref, self.part, self.lane, self.shape = ref, part, lane, (rows, width)

    def where(self, index):
        index = index if isinstance(index, tuple) else (index,)
        if index[0] is Ellipsis:
            index = ()
        spans = []
        for i, size in enumerate(self.shape):
            start, stop, _ = (index[i] if i < len(index) else slice(None)).indices(size)
            spans.append((start, stop))
        (top, end), (left, right) = spans
        return (self.part, slice(top, end), slice(self.lane + left, self.lane + right))

    def __getitem__(self, index):
        return self.ref[self.where(index)]

    def __setitem__(self, index, value):
        self.ref[self.where(index)] = value


def local_kernel(intra, inter, RI, waves, lengths, proj, vectors, gi_in, gr_in, outs_to, notes, *scratch):
    gi, gr, outs, sem = scratch[:4]
    scratch = scratch[4:]
    maps = [pltpu.make_async_copy(gi_in, gi, sem.at[0]), pltpu.make_async_copy(gr_in, gr, sem.at[1])]
    for copy in maps:
        copy.start()

    def leave(r):
        rows = pl.ds(r * ROWS_G, ROWS_G)
        copy = pltpu.make_async_copy(outs.at[rows], outs_to.at[rows], sem.at[2 + r])
        copy.start()
        return copy

    win, res, nrm, genc, gm = scratch[:5]
    x0, h0, c0, x1, h1, c1, x2, h2, c2, x3, h3, c3 = scratch[5:17]
    wc, wit, wrt, wot, z, dh = scratch[17:]

    def strip(d, lane, rows, width):
        return Strip(z, d, lane * LANES, rows, width)

    tall = PADDED * M
    feats, dec = strip(0, 0, tall, B), strip(0, 1, tall, 2 * STRIDE)
    tgt, gest = strip(0, 2, tall, STRIDE), strip(0, 3, tall, STRIDE)
    enc, gate, src, act = (strip(1, i, tall, B) for i in range(4))
    part = strip(1, 3, (FRAMES + HOP) * M, B)
    bottle, flat = strip(0, 0, BLOCKS * M, B), strip(0, 1, BLOCKS * M, 2 * STRIDE)
    core = (wc, wit, wrt, wot, z, dh)
    out0, out1, out2, out3 = (outs.at[pl.ds(r * ROWS_G, ROWS_G)] for r in range(4))
    length = lengths[lax.axis_index("block")]
    lim = length - lax.broadcasted_iota(jnp.int32, (M, B), 0) * (FRAMES * STRIDE)
    reach = (HOP + 2) * STRIDE
    span = FRAMES * STRIDE
    goal_at = waves.shape[1] // 2
    mix = waves[:, :span]
    goal = waves[:, goal_at : goal_at + span]

    def after(value):
        return jnp.concatenate([value[1:], jnp.zeros((1, value.shape[1]), F32)], 0)

    def before(value):
        return jnp.concatenate([jnp.zeros((1, value.shape[1]), F32), value[:-1]], 0)

    for ref in (x1, x3, nrm):
        ref[...] = jnp.zeros_like(ref)
    encode(mix, after(mix[:, :reach]), before(mix[:, span - STRIDE :]), lim, proj, vectors, win, flat, bottle, res)
    for copy in maps:
        copy.wait()

    def inter_layer(index, xs, h, c):
        turn_in(res, xs, RI)

        def use(i, r0, value):
            nrm[pl.ds(r0, inter.crows), :] = value.astype(BF).astype(F32)

        inter_forward(inter, index, xs, gi, gr, index, vectors, proj, h, c, (wc, z), use)
        turn_back(res, nrm, RI, length)

    intra_forward(intra, 0, res, lim, gi, gr, 0, vectors, proj, x0, h0, c0, (wc, z))
    inter_layer(1, x1, h1, c1)
    intra_forward(intra, 2, res, lim, gi, gr, 2, vectors, proj, x2, h2, c2, (wc, z))
    inter_layer(3, x3, h3, c3)

    parts_of(res, part)
    half = HOP * M
    row = lax.broadcasted_iota(jnp.int32, (EDGE, B), 0) % M
    early = jnp.where(row == 0, 0.0, before(part[TILES * half - M :]))
    late = jnp.where(row == M - 1, 0.0, after(part[: half + M]))
    edge = jnp.where(lax.broadcasted_iota(jnp.int32, (M, 2 * STRIDE), 0) == 0, 0.0, 1.0)
    middle(
        part, early, late, lim, edge, win, goal, after(goal[:, :reach]), proj, vectors, res, genc, gm,
        feats, dec, tgt, gest, enc, gate, src, act,
    )

    def inter_layer_back(index, xs, h, c, out):
        for j in range(M):
            for t in range(TILES):
                at = (TILES * j + t) * RI
                nrm[at + K : at + RI] = jnp.zeros((RI - K, B), F32)
        turn_in(res, nrm, RI)

        def use(g, i, r0, total):
            nrm[pl.ds(r0, inter.crows), :] = total.astype(BF).astype(F32)

        inter_back(inter, index, nrm, xs, h, c, proj, vectors, gi, gr, index, out, core, use)
        turn_back(res, nrm, RI, length)

    inter_layer_back(3, x3, h3, c3, out3)
    left = [leave(3)]
    intra_back(intra, 2, res, x2, h2, c2, proj, vectors, gi, gr, 2, out2, core)
    left.append(leave(2))
    for c in range(TILES):
        res[c, : K * M] = res[c, : K * M] * live(lim, c * HOP, K)
    inter_layer_back(1, x1, h1, c1, out1)
    intra_back(intra, 0, res, x0, h0, c0, proj, vectors, gi, gr, 0, out0, core)
    encode_back(res, lim, proj, vectors, win, genc, gm, out0, out1, bottle)
    left += [leave(1), leave(0)]

    def widest(i, best):
        rows = outs[pl.ds(pl.multiple_of(i * 256, 256), 256), :]
        return jnp.maximum(best, jnp.max(jnp.abs(rows).reshape(32, 8, LANES), 0))

    best = lax.fori_loop(0, outs.shape[0] // 256, widest, jnp.zeros((8, LANES), F32))
    best = jnp.max(jnp.max(best, 0, keepdims=True), 1, keepdims=True)
    notes[...] = note_rows(best, gm[132:133], gm[133:134])
    for copy in left:
        copy.wait()


def local_scratch(intra, inter):
    first = [
        pltpu.VMEM((2 * LAYERS, 2, B, 4 * H), F32),
        pltpu.VMEM((2 * LAYERS, 2, H, 4 * H), F32),
        pltpu.VMEM((4 * ROWS_G, LANES), F32),
        pltpu.SemaphoreType.DMA((6,)),
        pltpu.VMEM((BLOCKS * M, 2 * STRIDE), BF),
        pltpu.VMEM((TILES, -(-K // M) * M * M, B), F32),
        pltpu.VMEM((inter.size, B), F32),
        pltpu.VMEM((FRAMES * M, B), F32),
        pltpu.VMEM((136, LANES), F32),
    ]
    kept = []
    for shape, kind in ((intra, BF), (inter, F32)) * 2:
        state = pltpu.VMEM((shape.groups * shape.wide, 2 * H), F32)
        kept += [pltpu.VMEM((shape.groups * shape.size, B), kind), state, state]
    return first + kept + back_scratch(inter)


def note_rows(widest, loss, count):
    row = lax.broadcasted_iota(jnp.int32, (8, LANES), 0)
    power = jnp.floor(jnp.log(jnp.maximum(widest, 1e-30)) * 1.4426950408889634)
    return jnp.where(row == 0, power, jnp.where(row == 1, loss, jnp.where(row == 2, count, 0.0)))


def adam_parts(grad, moment, square, weight, average, decay):
    moment = BETA_ONE * moment + (1.0 - BETA_ONE) * grad
    square = BETA_TWO * square + (1.0 - BETA_TWO) * grad * grad
    corrected = moment * (1.0 / (1.0 - BETA_ONE**STEP))
    scaled = square * (1.0 / (1.0 - BETA_TWO**STEP))
    weight = weight - RATE * (corrected / (jnp.sqrt(scaled) + ADAM_EPS) + decay * weight)
    average = KEEP * average + (1.0 - KEEP) * weight
    return moment, square, weight, average, weight.astype(BF)


def adam_kernel(*refs):
    near, far, totals, kept = refs[0], refs[1], refs[2], refs[3:19]
    scalars, new = refs[19], refs[20:40]
    gv, sums, sem = refs[40:43]
    ready = [refs[43 + 5 * kind : 48 + 5 * kind] for kind in range(4)]
    old = refs[63:79]
    arrivals = {}

    def fetch(kind, r=None):
        for j in range(4):
            source, to = kept[4 * j + kind], old[4 * j + kind]
            number = 50 + 4 * (kind if r is None else 4 + 2 * r + kind) + j
            if r is not None:
                source, to = source.at[r], to.at[r]
            arrivals[kind, r, j] = pltpu.make_async_copy(source, to, sem.at[number])
            arrivals[kind, r, j].start()

    def arrived(kind, r=None):
        for j in range(4):
            arrivals.pop((kind, r, j)).wait()

    for r in range(4):
        fetch(0, r)
        fetch(1, r)
    fetch(2)
    fetch(3)
    copies = {}
    mine = lax.axis_index("dp") & 1
    pieces_half = (near.shape[0] - sums.shape[0] // 2) // NOTES
    size = sums.shape[0] // 2 // pieces_half
    for i in range(pieces_half):
        at = i * (size + NOTES)
        for ref, place in ((near, mine), (far, 1 - mine)):
            to = pl.multiple_of((place * pieces_half + i) * size, 16)
            scale = jnp.exp2(ref[at + size : at + size + 1, :] - TOP)
            sums[pl.ds(to, size), :] = ref[at : at + size] * scale
    gs = [sums.at[pl.ds(r * ROWS_G, ROWS_G)] for r in range(4)]
    vecs = ROWS_MORE + B
    gv[:1] = jnp.concatenate([gs[0][vecs : vecs + 1, :N], gs[0][vecs + 1 : vecs + 2, :N]], 1)
    gv[1:2, :N] = gs[0][vecs + 2 : vecs + 3, :N]
    gv[gv.shape[0] - 1 :, N:] = gs[0][vecs + 3 : vecs + 4, :N]
    for r in range(4):
        at = 3 + 19 * r
        rows = [
            gs[r][ROWS_VECS + j : ROWS_VECS + j + 1, k * N : (k + 1) * N] for j in range(8) for k in range(2)
        ]
        rows += [gs[r][ROWS_VECS + j : ROWS_VECS + j + 1, :N] for j in range(8, 11)]
        for j, row in enumerate(rows):
            q = at + j
            gv[q // 2 : q // 2 + 1, (q % 2) * N : (q % 2 + 1) * N] = row
    part = jnp.zeros((8, LANES), F32)
    pieces_of = [gs[r][:ROWS_VECS] for r in range(4)]
    pieces_of += [gs[r][ROWS_MORE : ROWS_MORE + B] for r in range(2)] + [gv[...]]
    for piece in pieces_of:
        value = piece.reshape(piece.shape[0] // 8, 8, LANES)
        part = part + jnp.sum(value * value, 0)
    squared = jnp.sum(jnp.sum(part, 0, keepdims=True), 1, keepdims=True)
    loss, count = totals[0:1, :1], totals[1:2, :1]
    norm = jnp.sqrt(squared) / count
    factor = jnp.minimum(1.0, CLIP / norm) / count
    row = lax.broadcasted_iota(jnp.int32, (8, LANES), 0)
    scalars[...] = jnp.where(row == 0, loss, jnp.where(row == 1, count, norm))

    def update(kind, index, grad, decay, slot=()):
        results = adam_parts(
            grad * factor,
            old[4 + kind][index],
            old[8 + kind][index],
            old[kind][index],
            old[12 + kind][index],
            decay,
        )
        for ref, value in zip(ready[kind], results):
            ref[slot + index[1:] if slot else index] = value

    def send(kind, r=None):
        for j, ref in enumerate(ready[kind]):
            to = new[4 * j + kind]
            if r is None:
                number = 40 + 5 * (kind - 2) + j
            else:
                ref, to, number = ref.at[r % 2], to.at[r], 10 * r + 5 * kind + j
            copies[kind, r, j] = pltpu.make_async_copy(ref, to, sem.at[number])
            copies[kind, r, j].start()

    def finish(kind, r=None):
        for j in range(5):
            copies.pop((kind, r, j)).wait()

    for r in range(4):
        if r >= 2:
            finish(0, r - 2)
            finish(1, r - 2)
        arrived(0, r)
        arrived(1, r)
        for d in range(2):
            for j in range(4):
                lanes = slice(j * LANES, (j + 1) * LANES)
                at = j * 384 + d * B
                update(0, (r, d, slice(None), lanes), gs[r][at : at + B], DECAY, (r % 2,))
                at = j * 384 + 128 + d * H
                update(1, (r, d, slice(None), lanes), gs[r][at : at + H], DECAY, (r % 2,))
        send(0, r)
        send(1, r)
    arrived(2)
    arrived(3)
    for r in range(4):
        for j in range(2):
            at = ROWS_MAPS + j * B
            lanes = slice(r * 2 * H + j * LANES, r * 2 * H + (j + 1) * LANES)
            update(2, (slice(None), lanes), gs[r][at : at + B], DECAY)
    more = slice(ROWS_MORE, ROWS_MORE + B)
    update(2, (slice(None), slice(BASE, BASE + LANES)), gs[0][more], DECAY)
    update(2, (slice(None), slice(BASE + LANES, BASE + LANES + 32)), gs[1][more, :32], DECAY)
    send(2)
    update(3, (slice(None), slice(None)), gv[...], 0.0)
    send(3)
    for kind in (0, 1):
        for r in (2, 3):
            finish(kind, r)
    finish(2)
    finish(3)


def call(kernel, outs, ins, scratch, index=None, limit=56, micros=20, apart=(), given=()):
    vmem = pl.BlockSpec(memory_space=pltpu.VMEM)
    specs = [
        pl.BlockSpec(memory_space=pltpu.SMEM) if a.ndim == 1 and a.dtype == jnp.int32 else vmem
        for a in ins
    ]
    for i in apart:
        specs[i] = pl.BlockSpec(memory_space=pltpu.HBM)
    extra = []
    wrapped = kernel
    if index is not None:
        big = [i for i, a in enumerate(ins) if a.ndim == 4 and a.shape[:2] == (2 * LAYERS, 2)]
        for i in big:
            specs[i] = pl.BlockSpec(memory_space=pl.ANY)
        extra = [pltpu.VMEM((1,) + ins[i].shape[1:], F32) for i in big]
        extra.append(pltpu.SemaphoreType.DMA((len(big),)))

        def wrapped(*refs):
            refs = list(refs)
            held, sem = refs[len(refs) - len(extra) : -1], refs[-1]
            copies = []
            for j, i in enumerate(big):
                copies.append(pltpu.make_async_copy(refs[i].at[pl.ds(index, 1)], held[j], sem.at[j]))
                copies[-1].start()
            for copy in copies:
                copy.wait()
            for j, i in enumerate(big):
                refs[i] = held[j]
            kernel(*refs[: len(refs) - len(extra)])

    return pl.pallas_call(
        wrapped,
        out_shape=outs,
        in_specs=specs,
        out_specs=[
            pl.BlockSpec(memory_space=pl.ANY) if i in given else vmem for i in range(len(outs))
        ],
        scratch_shapes=list(scratch) + extra,
        compiler_params=pltpu.CompilerParams(vmem_limit_bytes=limit * 1024 * 1024),
        cost_estimate=pl.CostEstimate(
            flops=micros * 10**9, bytes_accessed=micros * 10**6, transcendentals=0
        ),
    )(*ins)


def shift(block, axis, distance):
    size = lax.axis_size(axis)
    route = [(i, i + distance) for i in range(size) if 0 <= i + distance < size]
    return lax.ppermute(block, axis, route)


def exchange(block):
    return lax.all_to_all(block, "block", split_axis=0, concat_axis=0, tiled=True)


def flip(block, bit):
    size = lax.axis_size("dp")
    return lax.ppermute(block, "dp", [(i, i ^ (1 << bit)) for i in range(size)])


def noted(power, loss, count):
    row = lax.broadcasted_iota(jnp.int32, (NOTES, LANES), 0)
    rows = jnp.where(row == 0, power, 0.0)
    for first, value in ((1, loss), (5, count)):
        rest = value * (1.0 / 1024.0**2)
        for j in range(4):
            digit = jnp.floor(rest) if j < 3 else rest
            rows = jnp.where(row == first + j, digit, rows)
            rest = (rest - digit) * 1024.0
    return rows.astype(HALF)


def scaled(value, power):
    return (value * jnp.exp2(TOP - power)).astype(HALF)


def read_notes(rows):
    rows = rows.astype(F32)
    power, *digits = (rows[..., i : i + 1, :] for i in range(9))
    loss, count = (
        (d[0] * 1024.0 + d[1]) * 1024.0 + (d[2] + d[3] * (1.0 / 1024.0))
        for d in (digits[:4], digits[4:])
    )
    return power, loss, count


def cut(block, start, size):
    return lax.dynamic_slice_in_dim(block, start, size, 0)


def chips(block):
    nb, dp = lax.axis_size("block"), lax.axis_size("dp")
    groups = [[i * dp + j for i in range(nb) for j in range(core, dp, 2)] for core in range(2)]
    return lax.all_to_all(
        block, ("block", "dp"), split_axis=0, concat_axis=0, tiled=True, axis_index_groups=groups
    )


def gradient_sums(block, notes):
    peers = lax.axis_size("block") * lax.axis_size("dp") // 2
    size = block.shape[0] // 2
    mine = lax.axis_index("dp") & 1
    other = flip(jnp.concatenate([cut(block, (1 - mine) * size, size), notes], 0), 0)
    power = jnp.maximum(notes[0:1], other[size : size + 1]) + 1.0
    loss, count = (notes[i : i + 1] + other[size + i : size + i + 1] for i in (1, 2))
    part = size // peers
    block = scaled(cut(block, mine * size, size) + other[:size], power)
    notes = jnp.broadcast_to(noted(power, loss, count)[None], (peers, NOTES, LANES))
    pieces = chips(jnp.concatenate([block.reshape(peers, part, LANES), notes], 1))
    powers, losses, counts = read_notes(pieces[:, part:])
    block = jnp.sum(pieces[:, :part].astype(F32) * jnp.exp2(powers - TOP), 0)
    loss, count = jnp.sum(losses, 0), jnp.sum(counts, 0)
    power = jnp.max(powers, 0) + (peers - 1).bit_length()
    mine = jnp.concatenate([scaled(block, power), noted(power, loss, count)], 0)
    block = chips(jnp.broadcast_to(mine[None], (peers,) + mine.shape))
    other = flip(block, 0)
    row = lax.broadcasted_iota(jnp.int32, (8, LANES), 0)
    totals = jnp.where(row == 0, loss, count)
    return [half.reshape(-1, LANES).astype(F32) for half in (block, other)] + [totals]


def shared_step(mixture, target, lengths, proj, vectors_wide, gi, gr):
    nb = lax.axis_size("block")
    RI = -(-K // nb) * M
    intra = Shape(TILES, K, M)
    inter = Shape(1, TILES * nb, RI)
    T = inter.steps
    reach = (HOP + 2) * STRIDE
    following = shift(jnp.stack([mixture[:, :reach], target[:, :reach]]), "block", -1)
    leading = shift(mixture[:, -STRIDE:], "block", 1)

    RP = -(-RI // 16) * 8
    res_shape = SDS((TILES, nb * RI, B), F32)
    send_shape = SDS((nb, TILES, RP, 2 * B), BF)
    steps_shape = SDS((T, RP, 2 * B), BF)
    x_shape = SDS((TILES * K * M, B), BF)

    def state(shape):
        return SDS((shape.groups * shape.wide, 2 * H), F32)

    res0, send, x0, h0, c0, win = call(
        functools.partial(first_kernel, intra, nb, RI),
        [res_shape, send_shape, x_shape, state(intra), state(intra), SDS((BLOCKS * M, 2 * STRIDE), BF)],
        [mixture, following, leading, lengths, proj, vectors_wide, gi, gr],
        fwd_scratch(intra)
        + [pltpu.VMEM((BLOCKS * M, 2 * STRIDE), F32), pltpu.VMEM((BLOCKS * M, B), F32)],
        0,
    )

    def inter_step(send, index):
        rows = exchange(send).reshape(T, RP, 2 * B)
        normed, h, c = call(
            functools.partial(inter_kernel, inter, RI, index),
            [steps_shape, state(inter), state(inter)],
            [rows, proj, vectors_wide, gi, gr],
            fwd_scratch(inter) + [pltpu.VMEM((inter.size, B), F32)],
            index,
        )
        return rows, h, c, exchange(normed.reshape(send_shape.shape))

    rows1, h1, c1, back = inter_step(send, 1)
    res2, send, x2, h2, c2 = call(
        functools.partial(third_kernel, intra, nb, RI),
        [res_shape, send_shape, x_shape, state(intra), state(intra)],
        [res0, back, lengths, proj, vectors_wide, gi, gr],
        fwd_scratch(intra),
        2,
    )
    rows3, h3, c3, back = inter_step(send, 3)
    edge_shape = SDS((EDGE_TOP, 2 * B), F32)
    part, up, down = call(
        functools.partial(part_kernel, nb, RI),
        [SDS(((FRAMES + HOP) * M, B), F32), edge_shape, edge_shape],
        [res2, back, lengths],
        [pltpu.VMEM(res_shape.shape, F32)],
    )
    before = shift(up, "block", 1)
    after = shift(down, "block", -1)
    tall = PADDED * M
    send, gres, genc, gm = call(
        functools.partial(middle_kernel, nb, RI),
        [send_shape, res_shape, SDS((FRAMES * M, B), F32), SDS((136, LANES), F32)],
        [part, before, after, lengths, win, target, following, proj, vectors_wide],
        [
            pltpu.VMEM((tall, B), F32),
            pltpu.VMEM((tall, 2 * STRIDE), F32),
            pltpu.VMEM((tall, STRIDE), F32),
            pltpu.VMEM((tall, STRIDE), F32),
            pltpu.VMEM((tall, B), F32),
            pltpu.VMEM((tall, B), F32),
            pltpu.VMEM((tall, B), F32),
            pltpu.VMEM((tall, B), F32),
        ],
    )
    out_shape = SDS((ROWS_G, LANES), F32)

    def inter_back(send, rows, h, c, index):
        grad_rows = exchange(send).reshape(T, RP, 2 * B)
        send, out = call(
            functools.partial(inter_back_kernel, inter, RI, index),
            [steps_shape, out_shape],
            [grad_rows, rows, h, c, proj, vectors_wide, gi, gr],
            [pltpu.VMEM((inter.size, B), F32)] * 2 + back_scratch(inter),
            index,
        )
        return exchange(send.reshape(send_shape.shape)), out

    back, out3 = inter_back(send, rows3, h3, c3, 3)
    gres, send, out2 = call(
        functools.partial(third_back_kernel, intra, nb, RI),
        [res_shape, send_shape, out_shape],
        [gres, back, lengths, x2, h2, c2, proj, vectors_wide, gi, gr],
        back_scratch(intra),
        2,
    )
    back, out1 = inter_back(send, rows1, h1, c1, 1)
    out0, out1 = call(
        functools.partial(first_back_kernel, intra, nb, RI),
        [out_shape, out_shape],
        [gres, back, lengths, x0, h0, c0, proj, vectors_wide, gi, gr, win, genc, gm, out1],
        [pltpu.VMEM(res_shape.shape, F32), pltpu.VMEM((BLOCKS * M, B), F32)] + back_scratch(intra),
        0,
    )
    parts = nb * lax.axis_size("dp") * NOTES
    more = jnp.zeros((-4 * ROWS_G % parts, LANES), F32)
    outs = jnp.concatenate([out0, out1, out2, out3, more], 0)
    at = ROWS_MORE + B + 4
    return outs, note_rows(jnp.max(jnp.abs(outs)), outs[at : at + 1], outs[at + 1 : at + 2])


def local_step(mixture, target, lengths, proj, vectors_wide, gi, gr):
    RI = -(-K // M) * M
    intra = Shape(TILES, K, M)
    inter = Shape(1, TILES * M, RI)
    pad = jnp.zeros((M, -(FRAMES * STRIDE) % LANES), F32)
    waves = jnp.concatenate([mixture, pad, target, pad], 1)
    waves = exchange(waves)
    return call(
        functools.partial(local_kernel, intra, inter, RI),
        [SDS((4 * ROWS_G, LANES), F32), SDS((8, LANES), F32)],
        [waves, lengths, proj, vectors_wide, gi, gr],
        local_scratch(intra, inter),
        limit=62,
        apart=(4, 5),
        given=(0,),
    )


def body(
    mixture,
    target,
    lengths,
    input_gates,
    recur_gates,
    projections,
    vectors,
    moment_input,
    moment_recur,
    moment_proj,
    moment_vecs,
    square_input,
    square_recur,
    square_proj,
    square_vecs,
    average_input,
    average_recur,
    average_proj,
    average_vecs,
):
    nb = lax.axis_size("block")
    proj = projections.T
    vectors_wide = vectors.reshape(-1, LANES)
    step = local_step if nb == M else shared_step
    outs, notes = step(mixture, target, lengths, proj, vectors_wide, input_gates, recur_gates)
    sums = gradient_sums(outs, notes)
    old = [
        input_gates, recur_gates, projections, vectors,
        moment_input, moment_recur, moment_proj, moment_vecs,
        square_input, square_recur, square_proj, square_vecs,
        average_input, average_recur, average_proj, average_vecs,
    ]
    for i in range(2, 16, 4):
        old[i] = old[i].T
    for i in range(3, 16, 4):
        old[i] = old[i].reshape(-1, LANES)
    new = [SDS(a.shape, F32) for a in old[:4]] * 4 + [SDS(a.shape, BF) for a in old[:4]]
    scalars, *new = call(
        adam_kernel,
        [SDS((8, LANES), F32)] + new,
        sums + old,
        [
            pltpu.VMEM(old[3].shape, F32),
            pltpu.VMEM(outs.shape, F32),
            pltpu.SemaphoreType.DMA((50 + 48,)),
        ]
        + [
            pltpu.VMEM(((2,) if i < 2 else ()) + old[i].shape[i < 2 :], F32 if j < 4 else BF)
            for i in range(4)
            for j in range(5)
        ]
        + [pltpu.VMEM(a.shape, F32) for a in old],
        limit=40,
        apart=range(3, 19),
        given=range(1, 21),
    )
    for i in range(2, 20, 4):
        new[i] = new[i].T
    for i in range(3, 20, 4):
        new[i] = new[i].reshape(-1)
    return (scalars[0, 0], scalars[1, 0], scalars[2, 0], *new)


def solution(mesh):
    in_specs = (P("dp", "block"), P("dp", "block"), P("dp")) + (P(),) * 16
    return jax.shard_map(
        body, mesh=mesh, in_specs=in_specs, out_specs=(P(),) * 23, check_vma=False
    )
```

```python
import functools

import jax
import jax.numpy as jnp
from jax import lax
from jax.experimental import pallas as pl
from jax.experimental.pallas import tpu as pltpu
from jax.sharding import PartitionSpec as P

N = 64
B = 64
H = 128
K = 100
STRIDE = 8
LAYERS = 2
STEP = 10
HOP = 50
TILES = 3
M = 8
FRAMES = 150
BASE = 4 * LAYERS * H
PERIOD = 8 * H + 3 * B
ROWS_MAPS = 1536
ROWS_VECS = 1664
ROWS_MORE = 1680
ROWS_G = 1792
LANES = 128
BLOCKS = 208
PADDED = 216
CHUNK = 416

EPS_NORM = 1e-05
CLIP = 0.001
RATE = 0.1
BETA_ONE = 0.9
BETA_TWO = 0.999
ADAM_EPS = 1e-08
DECAY = 0.01
KEEP = 0.9

BF = jnp.bfloat16
F32 = jnp.float32
TOP = 13.0
NOTES = 8
HALF = jnp.float16
SDS = jax.ShapeDtypeStruct


def dot(left, right):
    return jnp.dot(left, right, preferred_element_type=F32)


def dot_turned(left, right):
    return lax.dot_general(left, right, (((1,), (1,)), ((), ())), preferred_element_type=F32)


def dot_rows(left, right):
    return lax.dot_general(left, right, (((0,), (0,)), ((), ())), preferred_element_type=F32)


def half_scale():
    lane = lax.broadcasted_iota(jnp.int32, (1, 4 * H), 1)
    return jnp.where((lane >= 2 * H) & (lane < 3 * H), 1.0, 0.5)


def gate_acts(z):
    act = jnp.tanh(z)
    sig_i = 0.5 * act[:, :H] + 0.5
    sig_f = 0.5 * act[:, H : 2 * H] + 0.5
    sig_o = 0.5 * act[:, 3 * H :] + 0.5
    return sig_i, sig_f, act[:, 2 * H : 3 * H], sig_o


def norm_parts(value):
    center = value - jnp.mean(value, -1, keepdims=True)
    spread = jnp.mean(center * center, -1, keepdims=True)
    scale = lax.rsqrt(spread + EPS_NORM)
    return center * scale, scale


def norm_back(grad, unit, scale, gain):
    inner = grad * gain
    return scale * (
        inner
        - jnp.mean(inner, -1, keepdims=True)
        - unit * jnp.mean(inner * unit, -1, keepdims=True)
    )


def live(lim, start, count):
    pos = lax.broadcasted_iota(jnp.int32, (count, M, B), 0) + start
    return jnp.where(pos * STRIDE < lim[None], 1.0, 0.0).reshape(count * M, B)


def limits(lengths):
    row = lax.broadcasted_iota(jnp.int32, (M, B), 0)
    total = jnp.zeros((M, B), jnp.int32)
    for m in range(M):
        total = jnp.where(row == m, lengths[m], total)
    return total - lax.axis_index("block") * (FRAMES * STRIDE)


def pieces(vectors, start, count):
    parts = []
    at = start
    while at < start + count:
        wide = at % 2 == 0 and at + 2 <= start + count
        lane = (at % 2) * N
        parts.append(vectors[at // 2 : at // 2 + 1, lane : lane + (2 * N if wide else N)])
        at += 2 if wide else 1
    return parts[0] if len(parts) == 1 else jnp.concatenate(parts, 1)


def branch_vectors(vectors, index):
    first = (2 * N + B + index * PERIOD) // N
    half = half_scale()
    bias = [pieces(vectors, first + 8 * d, 8) * half for d in range(2)]
    return bias, [pieces(vectors, first + 16 + j, 1) for j in range(3)]


def own(start, count):
    pos = lax.broadcasted_iota(jnp.int32, (count, M, B), 0) + start
    return jnp.where(pos < FRAMES, 1.0, 0.0).reshape(count * M, B)


def chunk_of(steps, rows):
    best = 1
    for size in range(1, steps + 1):
        if steps % size == 0 and size * rows <= 1024 and size * rows % 16 == 0:
            best = size
    return best


class Shape:
    def __init__(self, groups, steps, rows):
        self.groups, self.steps, self.rows = groups, steps, rows
        self.size = steps * rows
        self.chunk = chunk_of(steps, rows)
        self.crows = self.chunk * rows
        self.chunks = steps // self.chunk
        self.wide = (steps + 2) * rows
        self.unroll = max(n for n in range(1, 26) if steps % n == 0)


def chunk_loop(shape, fn):
    for g in range(shape.groups):
        for i in range(shape.chunks):
            fn(g, i, i * shape.crows)


def forward_weights(gi, gr, index, wc):
    half = half_scale()
    for d in range(2):
        wc[d, :H] = (gr[index, d].astype(BF).astype(F32) * half).astype(BF)
        wc[d, H:] = (gi[index, d].astype(BF).astype(F32) * half).astype(BF)


def lstm_scan(shape, pg, wc, h_ref, c_ref):
    G, S, R = shape.groups, shape.steps, shape.rows
    pad = jnp.zeros((R, 2 * H), F32)
    for g in range(G):
        for ref in (h_ref, c_ref):
            ref[g * shape.wide : g * shape.wide + R] = pad
            ref[(g + 1) * shape.wide - R : (g + 1) * shape.wide] = pad

    rows = G * R
    zero = jnp.zeros((rows, H), F32)
    held = jnp.concatenate([wc[0, :H], wc[1, :H]], 0)

    def one(d, t, z, memory):
        at = pl.multiple_of(t * R, 8)
        pre = jnp.concatenate([pg[d, pl.ds(g * shape.size + at, R), :] for g in range(G)], 0)
        sig_i, sig_f, tan_g, sig_o = gate_acts(pre + z)
        memory = sig_f * memory + sig_i * tan_g
        hidden = (sig_o * jnp.tanh(memory)).astype(BF).astype(F32)
        after = pl.multiple_of(t * R + R, 8)
        for g in range(G):
            to = pl.ds(g * shape.wide + after, R)
            h_ref[to, d * H : (d + 1) * H] = hidden[g * R : (g + 1) * R]
            c_ref[to, d * H : (d + 1) * H] = memory[g * R : (g + 1) * R]
        return hidden, memory

    def step(s, carry):
        hf, cf, hb, cb = carry
        both = jnp.concatenate(
            [jnp.concatenate([hf, zero], 1), jnp.concatenate([zero, hb], 1)], 0
        ).astype(BF)
        z = dot(both, held)
        hf, cf = one(0, s, z[:rows], cf)
        hb, cb = one(1, S - 1 - s, z[rows:], cb)
        return hf, cf, hb, cb

    lax.fori_loop(0, S, step, (zero,) * 4, unroll=shape.unroll)


def lstm_scan_back(shape, z, dh, c_ref, wrt):
    G, S, R = shape.groups, shape.steps, shape.rows

    def one(d, t, rec_hidden, rec_memory):
        def take(ref, at, width, lanes):
            at = pl.multiple_of(at, 8)
            return jnp.concatenate([ref[pl.ds(g * width + at, R), lanes] for g in range(G)], 0)

        lanes = slice(d * H, (d + 1) * H)
        at = pl.multiple_of(t * R, 8)
        zt = jnp.concatenate([z[d, pl.ds(g * shape.size + at, R), :] for g in range(G)], 0)
        sig_i, sig_f, tan_g, sig_o = gate_acts(zt)
        tan_c = jnp.tanh(take(c_ref, t * R + R, shape.wide, lanes))
        before = take(c_ref, t * R + 2 * R * d, shape.wide, lanes)
        grad_h = take(dh, t * R, shape.size, lanes) + rec_hidden
        grad_c = rec_memory + grad_h * (sig_o * (1.0 - tan_c * tan_c))
        grad_pre = jnp.concatenate(
            [
                grad_c * (tan_g * sig_i * (1.0 - sig_i)),
                grad_c * (before * sig_f * (1.0 - sig_f)),
                grad_c * (sig_i * (1.0 - tan_g * tan_g)),
                grad_h * (tan_c * sig_o * (1.0 - sig_o)),
            ],
            -1,
        ).astype(BF)
        full = grad_pre.astype(F32)
        for g in range(G):
            z[d, pl.ds(g * shape.size + at, R), :] = full[g * R : (g + 1) * R]
        return dot(grad_pre, wrt[d]), grad_c * sig_f

    def step(s, carry):
        hf, cf, hb, cb = carry
        hf, cf = one(0, S - 1 - s, hf, cf)
        hb, cb = one(1, s, hb, cb)
        return hf, cf, hb, cb

    zero = jnp.zeros((G * R, H), F32)
    lax.fori_loop(0, S, step, (zero,) * 4, unroll=shape.unroll)


def branch_pregates(shape, inputs, wc, bias, pg):
    def fill(g, i, r0):
        x = inputs(g, r0).astype(BF)
        for d in range(2):
            pg[d, pl.ds(g * shape.size + r0, shape.crows), :] = dot(x, wc[d, H:]) + bias[d]

    chunk_loop(shape, fill)


def branch_back(shape, grads, inputs, h_ref, c_ref, weights, index, vecs, turned_out, out, scratch):
    gi, gr = weights
    wc, wit, wrt, wot, z, dh = scratch
    n, R = shape.crows, shape.rows
    forward_weights(gi, gr, index, wc)
    for d in range(2):
        wit[d] = jnp.transpose(gi[index, d]).astype(BF)
        wrt[d] = jnp.transpose(gr[index, d]).astype(BF)
    wot[...] = turned_out.astype(BF)
    out[...] = jnp.zeros(out.shape, F32)
    bias, (o_bias, gain, _) = vecs

    def states(g, at, lanes):
        return h_ref[pl.ds(pl.multiple_of(g * shape.wide + at, 8), n), lanes].astype(BF)

    def earlier(g, r0, d):
        before = states(g, r0 + 2 * R * d, slice(d * H, (d + 1) * H))
        return jnp.concatenate([before, inputs(g, r0).astype(BF)], 1)

    def first(g, i, r0):
        now = states(g, r0 + R, slice(0, 2 * H))
        here = pl.ds(g * shape.size + r0, n)
        unit, scale = norm_parts(dot_turned(now, wot[...]) + o_bias)
        grad = grads(g, r0)
        low = norm_back(grad, unit, scale, gain).astype(BF)
        dh[here, :] = dot(low, wot[...])
        turned = dot_rows(low, now)
        for j in range(2):
            at = ROWS_MAPS + j * B
            out[at : at + B] += turned[:, j * LANES : (j + 1) * LANES]
        for j, value in enumerate((low.astype(F32), grad * unit, grad)):
            at = ROWS_VECS + 8 + j
            out[at : at + 1, :B] += jnp.sum(value, 0, keepdims=True)
        for d in range(2):
            z[d, here, :] = dot(earlier(g, r0, d), wc[d]) + bias[d]

    chunk_loop(shape, first)
    lstm_scan_back(shape, z, dh, c_ref, wrt)

    def last(use):
        def fn(g, i, r0):
            total = None
            for d in range(2):
                full = z[d, pl.ds(g * shape.size + r0, n), :]
                low = full.astype(BF)
                maps = dot_rows(earlier(g, r0, d), low)
                grad_bias = jnp.sum(full, 0, keepdims=True)
                for j in range(4):
                    lanes = slice(j * LANES, (j + 1) * LANES)
                    at = j * 384 + d * B
                    out[at : at + B] += maps[H:, lanes]
                    at = j * 384 + 128 + d * H
                    out[at : at + H] += maps[:H, lanes]
                    at = ROWS_VECS + 4 * d + j
                    out[at : at + 1] += grad_bias[:, lanes]
                part = dot(low, wit[d])
                total = part if total is None else total + part
            use(g, i, r0, total)

        chunk_loop(shape, fn)

    return last


def fwd_scratch(shape):
    return [
        pltpu.VMEM((2, H + B, 4 * H), BF),
        pltpu.VMEM((2, shape.groups * shape.size, 4 * H), F32),
    ]


def back_scratch(shape):
    return [
        pltpu.VMEM((2, H + B, 4 * H), BF),
        pltpu.VMEM((2, 4 * H, B), BF),
        pltpu.VMEM((2, 4 * H, H), BF),
        pltpu.VMEM((B, 2 * H), BF),
        pltpu.VMEM((2, shape.groups * shape.size, 4 * H), F32),
        pltpu.VMEM((shape.groups * shape.size, 2 * H), F32),
    ]


def packed(value, RP):
    rest = value[RP:]
    if rest.shape[0] < RP:
        rest = jnp.concatenate([rest, jnp.zeros((RP - rest.shape[0], B), F32)], 0)
    return jnp.concatenate([value[:RP], rest], 1).astype(BF)


def send_tiles(res, send, nb, RI):
    RP = send.shape[2]
    for d in range(nb):
        for c in range(TILES):
            send[d, c] = packed(res[c, d * RI : (d + 1) * RI], RP)


def add_tiles(res, back, nb, RI, lim):
    RP = back.shape[2]
    for d in range(nb):
        for c in range(TILES):
            both = back[d, c].astype(F32)
            for lo, hi, value in (
                (0, RP, both[:, :B]),
                (RP, RI, both[:, B:]),
            ):
                lo, hi = d * RI + lo, min(d * RI + hi, K * M)
                if lo >= hi:
                    continue
                mask = live(lim, c * HOP + lo // M, (hi - lo) // M)
                res[c, lo:hi] = (res[c, lo:hi] + value[: hi - lo]) * mask


def unpack_steps(rows, xs, T, RI):
    RP = rows.shape[1]

    def widen(t, _):
        both = rows[t].astype(F32)
        xs[pl.ds(pl.multiple_of(t * RI, 8), RP), :] = both[:, :B]
        if RI > RP:
            xs[pl.ds(pl.multiple_of(t * RI + RP, 8), RI - RP), :] = both[: RI - RP, B:]
        return 0

    lax.fori_loop(0, T, widen, 0, unroll=4 if T % 4 == 0 else 1)


def windows_of(mix, following, win):
    last = FRAMES + HOP + 1
    for i in range(1, BLOCKS):
        at = STRIDE * (i - 1)
        if at + 2 * STRIDE <= FRAMES * STRIDE:
            win[i * M : (i + 1) * M] = mix[:, at : at + 2 * STRIDE]
        elif at < FRAMES * STRIDE:
            win[i * M : (i + 1) * M] = jnp.concatenate([mix[:, at:], following[:, :STRIDE]], 1)
        elif i <= last:
            at -= FRAMES * STRIDE
            win[i * M : (i + 1) * M] = following[:, at : at + 2 * STRIDE]
        else:
            win[i * M :] = jnp.zeros(((BLOCKS - i) * M, 2 * STRIDE), F32)
            break


def softplus(value):
    return jnp.maximum(value, 0.0) + jnp.log1p(jnp.exp(-jnp.abs(value)))


def turned_out(proj, index):
    return proj[:, index * 2 * H : (index + 1) * 2 * H]


def intra_forward(shape, index, res, lim, gi, gr, slot, vectors, proj, x_out, h_out, c_out, scratch):
    wc, pg = scratch
    forward_weights(gi, gr, slot, wc)
    bias, (o_bias, gain, beta) = branch_vectors(vectors, index)
    n = shape.crows

    def inputs(g, r0):
        x = res[g, pl.ds(r0, n), :].astype(BF)
        x_out[pl.ds(pl.multiple_of(g * shape.size + r0, 16), n), :] = x
        return x

    branch_pregates(shape, inputs, wc, bias, pg)
    lstm_scan(shape, pg, wc, h_out, c_out)
    low_out = turned_out(proj, index).astype(BF)

    def close(g, i, r0):
        now = h_out[pl.ds(pl.multiple_of(g * shape.wide + r0 + shape.rows, 8), n), :].astype(BF)
        unit, _ = norm_parts(dot_turned(now, low_out) + o_bias)
        mask = live(lim, g * HOP + i * shape.chunk, shape.chunk)
        res[g, pl.ds(r0, n), :] = (res[g, pl.ds(r0, n), :] + (unit * gain + beta)) * mask

    chunk_loop(shape, close)


def inter_forward(shape, index, xs, gi, gr, slot, vectors, proj, h_out, c_out, scratch, use):
    wc, pg = scratch
    forward_weights(gi, gr, slot, wc)
    bias, (o_bias, gain, beta) = branch_vectors(vectors, index)
    n = shape.crows
    branch_pregates(shape, lambda g, r0: xs[pl.ds(r0, n), :], wc, bias, pg)
    lstm_scan(shape, pg, wc, h_out, c_out)
    low_out = turned_out(proj, index).astype(BF)

    def close(g, i, r0):
        now = h_out[pl.ds(pl.multiple_of(r0 + shape.rows, 8), n), :].astype(BF)
        unit, _ = norm_parts(dot_turned(now, low_out) + o_bias)
        use(i, r0, unit * gain + beta)

    chunk_loop(shape, close)


def zero_tail(res, c):
    if res.shape[1] > K * M:
        res[c, K * M :] = jnp.zeros((res.shape[1] - K * M, B), F32)


def encode(mix, following, leading, lim, proj, vectors, win, flat, bottle, res):
    flat[:M] = jnp.concatenate([leading[...], mix[:, :STRIDE]], 1)
    windows_of(mix, following, flat)
    win[...] = flat[...].astype(BF)
    w_enc = proj[:, BASE + N + B : BASE + N + B + 2 * STRIDE].astype(BF)
    w_bn = proj[:, BASE : BASE + N].astype(BF)
    gain, beta, b_bias = (pieces(vectors, j, 1) for j in range(3))
    for i in range(BLOCKS * M // CHUNK):
        at = i * CHUNK
        pre = dot_turned(win[at : at + CHUNK], w_enc)
        unit, _ = norm_parts(softplus(pre))
        normed = (unit * gain + beta).astype(BF)
        mask = live(lim, i * (CHUNK // M) - 1, CHUNK // M)
        bottle[at : at + CHUNK] = (dot_turned(normed, w_bn) + b_bias) * mask
    for c in range(TILES):
        res[c, : K * M] = bottle[(c * HOP + 1) * M : (c * HOP + 1 + K) * M]
        zero_tail(res, c)


def first_kernel(shape, nb, RI, mix, following, leading, lengths, proj, vectors, gi, gr, res, send, x_out, h_out, c_out, win, wc, pg, flat, bottle):
    lim = limits(lengths)
    encode(mix, following.at[0], leading, lim, proj, vectors, win, flat, bottle, res)
    intra_forward(shape, 0, res, lim, gi, gr, 0, vectors, proj, x_out, h_out, c_out, (wc, pg))
    send_tiles(res, send, nb, RI)


def third_kernel(shape, nb, RI, res_in, back, lengths, proj, vectors, gi, gr, res, send, x_out, h_out, c_out, wc, pg):
    lim = limits(lengths)
    res[...] = res_in[...]
    add_tiles(res, back, nb, RI, lim)
    intra_forward(shape, 2, res, lim, gi, gr, 0, vectors, proj, x_out, h_out, c_out, (wc, pg))
    send_tiles(res, send, nb, RI)


def inter_kernel(shape, RI, index, rows, proj, vectors, gi, gr, normed, h_out, c_out, wc, pg, xs):
    unpack_steps(rows, xs, shape.steps, RI)
    RP = normed.shape[1]

    def use(i, r0, value):
        for j in range(shape.chunk):
            normed[i * shape.chunk + j] = packed(value[j * RI : (j + 1) * RI], RP)

    inter_forward(shape, index, xs, gi, gr, 0, vectors, proj, h_out, c_out, (wc, pg), use)


EDGE = (HOP + 1) * M
EDGE_TOP = 208


def edge_pack(value):
    rest = jnp.concatenate([value[EDGE_TOP:], jnp.zeros((2 * EDGE_TOP - EDGE, B), F32)], 0)
    return jnp.concatenate([value[:EDGE_TOP], rest], 1)


def edge_unpack(ref):
    return jnp.concatenate([ref[:, :B], ref[: EDGE - EDGE_TOP, B:]], 0)


def parts_of(res, part):
    half = HOP * M
    part[:half] = res[0, :half]
    for c in range(1, TILES):
        part[c * half : (c + 1) * half] = res[c, :half] + res[c - 1, half : 2 * half]
    part[TILES * half :] = res[TILES - 1, half : 2 * half]


def part_kernel(nb, RI, res_in, back, lengths, part, up, down, res):
    res[...] = res_in[...]
    add_tiles(res, back, nb, RI, limits(lengths))
    parts_of(res, part)
    half = HOP * M
    up[...] = edge_pack(part[TILES * half - M :])
    down[...] = edge_pack(part[: half + M])


def middle_kernel(nb, RI, part, before, after, lengths, win, goal, following, proj, vectors, send, gres, genc, gm, *scratch):
    edge = jnp.where(lax.axis_index("block") > 0, 1.0, 0.0)
    middle(
        part, edge_unpack(before), edge_unpack(after), limits(lengths), edge, win, goal,
        following.at[1], proj, vectors, gres, genc, gm, *scratch,
    )
    send_tiles(gres, send, nb, RI)


def middle(part, early, late, lim, edge, win, goal, following, proj, vectors, gres, genc, gm, feats, dec, tgt, gest, enc, gate, src, act):
    half = HOP * M
    top = M + TILES * half
    total = BLOCKS * M
    feats[:M] = early[:M]
    feats[M : M + half] = part[:half] + early[M:]
    feats[M + half : top] = part[half : TILES * half]
    feats[top : top + half] = part[TILES * half :] + late[:half]
    feats[top + half : top + half + M] = late[half:]
    feats[top + half + M :] = jnp.zeros((PADDED * M - top - half - M, B), F32)
    low_mask = proj[:, BASE + N : BASE + N + B].astype(BF)
    w_enc = proj[:, BASE + N + B : BASE + N + B + 2 * STRIDE].astype(BF)
    low_dec = proj[:, BASE + N + B + 2 * STRIDE : BASE + N + B + 4 * STRIDE].astype(BF)
    m_bias = pieces(vectors, vectors.shape[0] * 2 - 1, 1)
    root = 0.7978845608028654
    cube = 0.044715
    dec[total:] = jnp.zeros((PADDED * M - total, 2 * STRIDE), F32)
    for i in range(total // CHUNK):
        rows = slice(i * CHUNK, (i + 1) * CHUNK)
        x = feats[rows]
        low = (0.5 * x * (1.0 + jnp.tanh(root * (x + cube * x * x * x)))).astype(BF)
        encoded = softplus(dot_turned(win[rows], w_enc))
        mask = 0.5 * jnp.tanh(0.5 * (dot_turned(low, low_mask) + m_bias)) + 0.5
        source = (mask * encoded).astype(BF)
        enc[rows] = encoded
        gate[rows] = mask
        src[rows] = source.astype(F32)
        act[rows] = low.astype(F32)
        dec[rows] = dot(source, low_dec)
    dec[:M] = dec[:M] * edge
    for ref in (enc, gate, src, act):
        ref[total:] = jnp.zeros((PADDED * M - total, B), F32)
    for i in range(1, FRAMES + 1):
        tgt[i * M : (i + 1) * M] = goal[:, STRIDE * (i - 1) : STRIDE * i]
    for i in range(FRAMES + 1, FRAMES + HOP + 2):
        at = STRIDE * (i - 1 - FRAMES)
        tgt[i * M : (i + 1) * M] = following[:, at : at + STRIDE]
    tgt[(FRAMES + HOP + 2) * M :] = jnp.zeros(((PADDED - FRAMES - HOP - 2) * M, STRIDE), F32)
    estimate = dec[M:total, :STRIDE] + dec[: total - M, STRIDE:]
    count = BLOCKS - 1
    spot = lax.broadcasted_iota(jnp.int32, (count, M, STRIDE), 0)
    phase = lax.broadcasted_iota(jnp.int32, (count, M, STRIDE), 2)
    near = spot < FRAMES + HOP + 1
    valid = jnp.where(near & (spot * STRIDE + phase < lim[:, :STRIDE][None]), 1.0, 0.0)
    inside = jnp.where(spot < FRAMES, valid, 0.0).reshape(count * M, STRIDE)
    valid = valid.reshape(count * M, STRIDE)
    error = estimate - tgt[M:total]
    smoothed = jnp.sqrt(error * error + 1.0)
    gest[:M] = jnp.zeros((M, STRIDE), F32)
    gest[M:total] = valid * error / smoothed
    gest[total:] = jnp.zeros((PADDED * M - total, STRIDE), F32)
    loss = jnp.sum(jnp.sum(inside * (smoothed - 1.0), 0, keepdims=True), 1, keepdims=True)
    seen = jnp.sum(jnp.sum(inside, 0, keepdims=True), 1, keepdims=True)
    gm[...] = jnp.zeros_like(gm)
    gm[132:133] = jnp.broadcast_to(loss, (1, LANES))
    gm[133:134] = jnp.broadcast_to(seen, (1, LANES))
    for i in range(total // CHUNK):
        at = i * CHUNK + M
        rows = slice(at, at + CHUNK)
        grad_dec = jnp.concatenate([gest[rows], gest[at + M : at + M + CHUNK]], 1).astype(BF)
        mine = own(i * (CHUNK // M), CHUNK // M)
        mine_low = mine.astype(BF)
        gm[64:128, 16:32] += dot_rows(src[rows].astype(BF) * mine_low, grad_dec)
        grad_source = dot_turned(grad_dec, low_dec)
        mask = gate[rows]
        grad_logit = (grad_source * enc[rows] * mask * (1.0 - mask)).astype(BF)
        enc[rows] = grad_source * mask
        gm[:64, 64:] += dot_rows(grad_logit * mine_low, act[rows].astype(BF))
        gm[131:132, :B] += jnp.sum(grad_logit.astype(F32) * mine, 0, keepdims=True)
        x = feats[rows]
        curve = jnp.tanh(root * (x + cube * x * x * x))
        slope = 0.5 * (1.0 + curve) + (0.5 * root) * x * (1.0 - curve * curve) * (
            1.0 + (3.0 * cube) * x * x
        )
        feats[rows] = slope * dot(grad_logit, low_mask)
    genc[...] = enc[M : M + FRAMES * M]
    for c in range(TILES):
        gres[c, : K * M] = feats[M + c * half : M + c * half + K * M] * live(lim, c * HOP, K)
        zero_tail(gres, c)


def inter_back(shape, index, gs, xs, h_ref, c_ref, proj, vectors, gi, gr, slot, out, core, use):
    n = shape.crows
    last = branch_back(
        shape,
        lambda g, r0: gs[pl.ds(r0, n), :],
        lambda g, r0: xs[pl.ds(r0, n), :],
        h_ref, c_ref, (gi, gr), slot, branch_vectors(vectors, index), turned_out(proj, index), out, core,
    )
    last(use)


def inter_back_kernel(shape, RI, index, grad_rows, rows, h_ref, c_ref, proj, vectors, gi, gr, send, out, *scratch):
    xs, gs, core = scratch[0], scratch[1], scratch[2:]
    unpack_steps(rows, xs, shape.steps, RI)
    unpack_steps(grad_rows, gs, shape.steps, RI)
    RP = send.shape[1]

    def use(g, i, r0, total):
        for j in range(shape.chunk):
            send[i * shape.chunk + j] = packed(total[j * RI : (j + 1) * RI], RP)

    inter_back(shape, index, gs, xs, h_ref, c_ref, proj, vectors, gi, gr, 0, out, core, use)


def intra_back(shape, index, gres, x_ref, h_ref, c_ref, proj, vectors, gi, gr, slot, out, core):
    n = shape.crows

    def inputs(g, r0):
        return x_ref[pl.ds(pl.multiple_of(g * shape.size + r0, 16), n), :]

    last = branch_back(
        shape,
        lambda g, r0: gres[g, pl.ds(r0, n), :],
        inputs,
        h_ref, c_ref, (gi, gr), slot, branch_vectors(vectors, index), turned_out(proj, index), out, core,
    )

    def use(g, i, r0, total):
        gres[g, pl.ds(r0, n), :] = gres[g, pl.ds(r0, n), :] + total

    last(use)


def third_back_kernel(shape, nb, RI, gres_in, back, lengths, x_ref, h_ref, c_ref, proj, vectors, gi, gr, gres, send, out, *core):
    lim = limits(lengths)
    gres[...] = gres_in[...]
    add_tiles(gres, back, nb, RI, lim)
    intra_back(shape, 2, gres, x_ref, h_ref, c_ref, proj, vectors, gi, gr, 0, out, core)
    for c in range(TILES):
        gres[c, : K * M] = gres[c, : K * M] * live(lim, c * HOP, K)
    send_tiles(gres, send, nb, RI)


def first_back_kernel(shape, nb, RI, gres_in, back, lengths, x_ref, h_ref, c_ref, proj, vectors, gi, gr, win, genc, gm, more_in, out, more, gres, bottle, *core):
    lim = limits(lengths)
    more[...] = more_in[...]
    gres[...] = gres_in[...]
    add_tiles(gres, back, nb, RI, lim)
    intra_back(shape, 0, gres, x_ref, h_ref, c_ref, proj, vectors, gi, gr, 0, out, core)
    encode_back(gres, lim, proj, vectors, win, genc, gm, out, more, bottle)


def encode_back(gres, lim, proj, vectors, win, genc, gm, out, more, bottle):
    at_first, at_vecs = ROWS_MORE, ROWS_MORE + B
    out[at_first : at_first + B] = gm[:B]
    out[at_vecs : at_vecs + 8] = gm[2 * B :]
    more[at_first : at_first + B] = gm[B : 2 * B]
    bottle[...] = jnp.zeros(bottle.shape, F32)
    for c in range(TILES):
        at = (c * HOP + 1) * M
        bottle[at : at + K * M] += gres[c, : K * M]
    w_enc = proj[:, BASE + N + B : BASE + N + B + 2 * STRIDE].astype(BF)
    w_bn = proj[:, BASE : BASE + N].astype(BF)
    gain, beta = (pieces(vectors, j, 1) for j in range(2))
    own_rows = FRAMES * M
    for i in range(BLOCKS * M // CHUNK):
        at = i * CHUNK
        rows = slice(at, at + CHUNK)
        pre = dot_turned(win[rows], w_enc)
        unit, scale = norm_parts(softplus(pre))
        normed = (unit * gain + beta).astype(BF)
        low = (bottle[rows] * live(lim, i * (CHUNK // M) - 1, CHUNK // M)).astype(BF)
        out[at_first : at_first + B, :N] += dot_rows(low, normed)
        grad_normed = dot(low, w_bn)
        for j, value in enumerate((grad_normed * unit, grad_normed, low.astype(F32))):
            out[at_vecs + j : at_vecs + j + 1, :B] += jnp.sum(value, 0, keepdims=True)
        grad_enc = norm_back(grad_normed, unit, scale, gain)
        lo, hi = max(at - M, 0), min(at + CHUNK - M, own_rows)
        if lo < hi:
            piece = genc[lo:hi]
            above, below = lo + M - at, at + CHUNK - M - hi
            if above:
                piece = jnp.concatenate([jnp.zeros((above, B), F32), piece], 0)
            if below:
                piece = jnp.concatenate([piece, jnp.zeros((below, B), F32)], 0)
            grad_enc = grad_enc + piece
        grad_pre = (grad_enc * (0.5 * jnp.tanh(0.5 * pre) + 0.5)).astype(BF)
        more[at_first : at_first + B, :16] += dot_rows(grad_pre, win[rows])


def turn_in(res, xs, RI, lowered=True):
    for j in range(M):
        for c in range(TILES):
            at = (TILES * j + c) * RI
            value = res[c, pl.ds(j, K, stride=M), :]
            xs[at : at + K] = value.astype(BF).astype(F32)


def turn_back(res, xs, RI, length):
    pos = lax.broadcasted_iota(jnp.int32, (K, B), 0)
    for j in range(M):
        for c in range(TILES):
            at = (TILES * j + c) * RI
            mask = jnp.where((pos + (FRAMES * j + HOP * c)) * STRIDE < length, 1.0, 0.0)
            where = (c, pl.ds(j, K, stride=M), slice(None))
            res[where] = (res[where] + xs[at : at + K]) * mask


class Strip:
    def __init__(self, ref, part, lane, rows, width):
        self.ref, self.part, self.lane, self.shape = ref, part, lane, (rows, width)

    def where(self, index):
        index = index if isinstance(index, tuple) else (index,)
        if index[0] is Ellipsis:
            index = ()
        spans = []
        for i, size in enumerate(self.shape):
            start, stop, _ = (index[i] if i < len(index) else slice(None)).indices(size)
            spans.append((start, stop))
        (top, end), (left, right) = spans
        return (self.part, slice(top, end), slice(self.lane + left, self.lane + right))

    def __getitem__(self, index):
        return self.ref[self.where(index)]

    def __setitem__(self, index, value):
        self.ref[self.where(index)] = value


def local_kernel(intra, inter, RI, waves, lengths, proj, vectors, gi_in, gr_in, outs_to, notes, *scratch):
    gi, gr, outs, sem = scratch[:4]
    scratch = scratch[4:]
    maps = [pltpu.make_async_copy(gi_in, gi, sem.at[0]), pltpu.make_async_copy(gr_in, gr, sem.at[1])]
    for copy in maps:
        copy.start()

    def leave(r):
        rows = pl.ds(r * ROWS_G, ROWS_G)
        copy = pltpu.make_async_copy(outs.at[rows], outs_to.at[rows], sem.at[2 + r])
        copy.start()
        return copy

    win, res, nrm, genc, gm = scratch[:5]
    x0, h0, c0, x1, h1, c1, x2, h2, c2, x3, h3, c3 = scratch[5:17]
    wc, wit, wrt, wot, z, dh = scratch[17:]

    def strip(d, lane, rows, width):
        return Strip(z, d, lane * LANES, rows, width)

    tall = PADDED * M
    feats, dec = strip(0, 0, tall, B), strip(0, 1, tall, 2 * STRIDE)
    tgt, gest = strip(0, 2, tall, STRIDE), strip(0, 3, tall, STRIDE)
    enc, gate, src, act = (strip(1, i, tall, B) for i in range(4))
    part = strip(1, 3, (FRAMES + HOP) * M, B)
    bottle, flat = strip(0, 0, BLOCKS * M, B), strip(0, 1, BLOCKS * M, 2 * STRIDE)
    core = (wc, wit, wrt, wot, z, dh)
    out0, out1, out2, out3 = (outs.at[pl.ds(r * ROWS_G, ROWS_G)] for r in range(4))
    length = lengths[lax.axis_index("block")]
    lim = length - lax.broadcasted_iota(jnp.int32, (M, B), 0) * (FRAMES * STRIDE)
    reach = (HOP + 2) * STRIDE
    span = FRAMES * STRIDE
    goal_at = waves.shape[1] // 2
    mix = waves[:, :span]
    goal = waves[:, goal_at : goal_at + span]

    def after(value):
        return jnp.concatenate([value[1:], jnp.zeros((1, value.shape[1]), F32)], 0)

    def before(value):
        return jnp.concatenate([jnp.zeros((1, value.shape[1]), F32), value[:-1]], 0)

    for ref in (x1, x3, nrm):
        ref[...] = jnp.zeros_like(ref)
    encode(mix, after(mix[:, :reach]), before(mix[:, span - STRIDE :]), lim, proj, vectors, win, flat, bottle, res)
    for copy in maps:
        copy.wait()

    def inter_layer(index, xs, h, c):
        turn_in(res, xs, RI)

        def use(i, r0, value):
            nrm[pl.ds(r0, inter.crows), :] = value.astype(BF).astype(F32)

        inter_forward(inter, index, xs, gi, gr, index, vectors, proj, h, c, (wc, z), use)
        turn_back(res, nrm, RI, length)

    intra_forward(intra, 0, res, lim, gi, gr, 0, vectors, proj, x0, h0, c0, (wc, z))
    inter_layer(1, x1, h1, c1)
    intra_forward(intra, 2, res, lim, gi, gr, 2, vectors, proj, x2, h2, c2, (wc, z))
    inter_layer(3, x3, h3, c3)

    parts_of(res, part)
    half = HOP * M
    row = lax.broadcasted_iota(jnp.int32, (EDGE, B), 0) % M
    early = jnp.where(row == 0, 0.0, before(part[TILES * half - M :]))
    late = jnp.where(row == M - 1, 0.0, after(part[: half + M]))
    edge = jnp.where(lax.broadcasted_iota(jnp.int32, (M, 2 * STRIDE), 0) == 0, 0.0, 1.0)
    middle(
        part, early, late, lim, edge, win, goal, after(goal[:, :reach]), proj, vectors, res, genc, gm,
        feats, dec, tgt, gest, enc, gate, src, act,
    )

    def inter_layer_back(index, xs, h, c, out):
        for j in range(M):
            for t in range(TILES):
                at = (TILES * j + t) * RI
                nrm[at + K : at + RI] = jnp.zeros((RI - K, B), F32)
        turn_in(res, nrm, RI)

        def use(g, i, r0, total):
            nrm[pl.ds(r0, inter.crows), :] = total.astype(BF).astype(F32)

        inter_back(inter, index, nrm, xs, h, c, proj, vectors, gi, gr, index, out, core, use)
        turn_back(res, nrm, RI, length)

    inter_layer_back(3, x3, h3, c3, out3)
    left = [leave(3)]
    intra_back(intra, 2, res, x2, h2, c2, proj, vectors, gi, gr, 2, out2, core)
    left.append(leave(2))
    for c in range(TILES):
        res[c, : K * M] = res[c, : K * M] * live(lim, c * HOP, K)
    inter_layer_back(1, x1, h1, c1, out1)
    intra_back(intra, 0, res, x0, h0, c0, proj, vectors, gi, gr, 0, out0, core)
    encode_back(res, lim, proj, vectors, win, genc, gm, out0, out1, bottle)
    left += [leave(1), leave(0)]

    def widest(i, best):
        rows = outs[pl.ds(pl.multiple_of(i * 256, 256), 256), :]
        return jnp.maximum(best, jnp.max(jnp.abs(rows).reshape(32, 8, LANES), 0))

    best = lax.fori_loop(0, outs.shape[0] // 256, widest, jnp.zeros((8, LANES), F32))
    best = jnp.max(jnp.max(best, 0, keepdims=True), 1, keepdims=True)
    notes[...] = note_rows(best, gm[132:133], gm[133:134])
    for copy in left:
        copy.wait()


def local_scratch(intra, inter):
    first = [
        pltpu.VMEM((2 * LAYERS, 2, B, 4 * H), F32),
        pltpu.VMEM((2 * LAYERS, 2, H, 4 * H), F32),
        pltpu.VMEM((4 * ROWS_G, LANES), F32),
        pltpu.SemaphoreType.DMA((6,)),
        pltpu.VMEM((BLOCKS * M, 2 * STRIDE), BF),
        pltpu.VMEM((TILES, -(-K // M) * M * M, B), F32),
        pltpu.VMEM((inter.size, B), F32),
        pltpu.VMEM((FRAMES * M, B), F32),
        pltpu.VMEM((136, LANES), F32),
    ]
    kept = []
    for shape, kind in ((intra, BF), (inter, F32)) * 2:
        state = pltpu.VMEM((shape.groups * shape.wide, 2 * H), F32)
        kept += [pltpu.VMEM((shape.groups * shape.size, B), kind), state, state]
    return first + kept + back_scratch(inter)


def note_rows(widest, loss, count):
    row = lax.broadcasted_iota(jnp.int32, (8, LANES), 0)
    power = jnp.floor(jnp.log(jnp.maximum(widest, 1e-30)) * 1.4426950408889634)
    return jnp.where(row == 0, power, jnp.where(row == 1, loss, jnp.where(row == 2, count, 0.0)))


def adam_parts(grad, moment, square, weight, average, decay):
    moment = BETA_ONE * moment + (1.0 - BETA_ONE) * grad
    square = BETA_TWO * square + (1.0 - BETA_TWO) * grad * grad
    corrected = moment * (1.0 / (1.0 - BETA_ONE**STEP))
    scaled = square * (1.0 / (1.0 - BETA_TWO**STEP))
    weight = weight - RATE * (corrected / (jnp.sqrt(scaled) + ADAM_EPS) + decay * weight)
    average = KEEP * average + (1.0 - KEEP) * weight
    return moment, square, weight, average, weight.astype(BF)


def adam_kernel(*refs):
    near, far, totals, kept = refs[0], refs[1], refs[2], refs[3:19]
    scalars, new = refs[19], refs[20:40]
    gv, sums, sem = refs[40:43]
    ready = [refs[43 + 5 * kind : 48 + 5 * kind] for kind in range(4)]
    old = refs[63:79]
    arrivals = {}

    def fetch(kind, r=None):
        for j in range(4):
            source, to = kept[4 * j + kind], old[4 * j + kind]
            number = 50 + 4 * (kind if r is None else 4 + 2 * r + kind) + j
            if r is not None:
                source, to = source.at[r], to.at[r]
            arrivals[kind, r, j] = pltpu.make_async_copy(source, to, sem.at[number])
            arrivals[kind, r, j].start()

    def arrived(kind, r=None):
        for j in range(4):
            arrivals.pop((kind, r, j)).wait()

    for r in range(4):
        fetch(0, r)
        fetch(1, r)
    fetch(2)
    fetch(3)
    copies = {}
    mine = lax.axis_index("dp") & 1
    pieces_half = (near.shape[0] - sums.shape[0] // 2) // NOTES
    size = sums.shape[0] // 2 // pieces_half
    for i in range(pieces_half):
        at = i * (size + NOTES)
        for ref, place in ((near, mine), (far, 1 - mine)):
            to = pl.multiple_of((place * pieces_half + i) * size, 16)
            scale = jnp.exp2(ref[at + size : at + size + 1, :] - TOP)
            sums[pl.ds(to, size), :] = ref[at : at + size] * scale
    gs = [sums.at[pl.ds(r * ROWS_G, ROWS_G)] for r in range(4)]
    vecs = ROWS_MORE + B
    gv[:1] = jnp.concatenate([gs[0][vecs : vecs + 1, :N], gs[0][vecs + 1 : vecs + 2, :N]], 1)
    gv[1:2, :N] = gs[0][vecs + 2 : vecs + 3, :N]
    gv[gv.shape[0] - 1 :, N:] = gs[0][vecs + 3 : vecs + 4, :N]
    for r in range(4):
        at = 3 + 19 * r
        rows = [
            gs[r][ROWS_VECS + j : ROWS_VECS + j + 1, k * N : (k + 1) * N] for j in range(8) for k in range(2)
        ]
        rows += [gs[r][ROWS_VECS + j : ROWS_VECS + j + 1, :N] for j in range(8, 11)]
        for j, row in enumerate(rows):
            q = at + j
            gv[q // 2 : q // 2 + 1, (q % 2) * N : (q % 2 + 1) * N] = row
    part = jnp.zeros((8, LANES), F32)
    pieces_of = [gs[r][:ROWS_VECS] for r in range(4)]
    pieces_of += [gs[r][ROWS_MORE : ROWS_MORE + B] for r in range(2)] + [gv[...]]
    for piece in pieces_of:
        value = piece.reshape(piece.shape[0] // 8, 8, LANES)
        part = part + jnp.sum(value * value, 0)
    squared = jnp.sum(jnp.sum(part, 0, keepdims=True), 1, keepdims=True)
    loss, count = totals[0:1, :1], totals[1:2, :1]
    norm = jnp.sqrt(squared) / count
    factor = jnp.minimum(1.0, CLIP / norm) / count
    row = lax.broadcasted_iota(jnp.int32, (8, LANES), 0)
    scalars[...] = jnp.where(row == 0, loss, jnp.where(row == 1, count, norm))

    def update(kind, index, grad, decay, slot=()):
        results = adam_parts(
            grad * factor,
            old[4 + kind][index],
            old[8 + kind][index],
            old[kind][index],
            old[12 + kind][index],
            decay,
        )
        for ref, value in zip(ready[kind], results):
            ref[slot + index[1:] if slot else index] = value

    def send(kind, r=None):
        for j, ref in enumerate(ready[kind]):
            to = new[4 * j + kind]
            if r is None:
                number = 40 + 5 * (kind - 2) + j
            else:
                ref, to, number = ref.at[r % 2], to.at[r], 10 * r + 5 * kind + j
            copies[kind, r, j] = pltpu.make_async_copy(ref, to, sem.at[number])
            copies[kind, r, j].start()

    def finish(kind, r=None):
        for j in range(5):
            copies.pop((kind, r, j)).wait()

    for r in range(4):
        if r >= 2:
            finish(0, r - 2)
            finish(1, r - 2)
        arrived(0, r)
        arrived(1, r)
        for d in range(2):
            for j in range(4):
                lanes = slice(j * LANES, (j + 1) * LANES)
                at = j * 384 + d * B
                update(0, (r, d, slice(None), lanes), gs[r][at : at + B], DECAY, (r % 2,))
                at = j * 384 + 128 + d * H
                update(1, (r, d, slice(None), lanes), gs[r][at : at + H], DECAY, (r % 2,))
        send(0, r)
        send(1, r)
    arrived(2)
    arrived(3)
    for r in range(4):
        for j in range(2):
            at = ROWS_MAPS + j * B
            lanes = slice(r * 2 * H + j * LANES, r * 2 * H + (j + 1) * LANES)
            update(2, (slice(None), lanes), gs[r][at : at + B], DECAY)
    more = slice(ROWS_MORE, ROWS_MORE + B)
    update(2, (slice(None), slice(BASE, BASE + LANES)), gs[0][more], DECAY)
    update(2, (slice(None), slice(BASE + LANES, BASE + LANES + 32)), gs[1][more, :32], DECAY)
    send(2)
    update(3, (slice(None), slice(None)), gv[...], 0.0)
    send(3)
    for kind in (0, 1):
        for r in (2, 3):
            finish(kind, r)
    finish(2)
    finish(3)


def call(kernel, outs, ins, scratch, index=None, limit=56, micros=20, apart=(), given=()):
    vmem = pl.BlockSpec(memory_space=pltpu.VMEM)
    specs = [
        pl.BlockSpec(memory_space=pltpu.SMEM) if a.ndim == 1 and a.dtype == jnp.int32 else vmem
        for a in ins
    ]
    for i in apart:
        specs[i] = pl.BlockSpec(memory_space=pltpu.HBM)
    extra = []
    wrapped = kernel
    if index is not None:
        big = [i for i, a in enumerate(ins) if a.ndim == 4 and a.shape[:2] == (2 * LAYERS, 2)]
        for i in big:
            specs[i] = pl.BlockSpec(memory_space=pl.ANY)
        extra = [pltpu.VMEM((1,) + ins[i].shape[1:], F32) for i in big]
        extra.append(pltpu.SemaphoreType.DMA((len(big),)))

        def wrapped(*refs):
            refs = list(refs)
            held, sem = refs[len(refs) - len(extra) : -1], refs[-1]
            copies = []
            for j, i in enumerate(big):
                copies.append(pltpu.make_async_copy(refs[i].at[pl.ds(index, 1)], held[j], sem.at[j]))
                copies[-1].start()
            for copy in copies:
                copy.wait()
            for j, i in enumerate(big):
                refs[i] = held[j]
            kernel(*refs[: len(refs) - len(extra)])

    return pl.pallas_call(
        wrapped,
        out_shape=outs,
        in_specs=specs,
        out_specs=[
            pl.BlockSpec(memory_space=pl.ANY) if i in given else vmem for i in range(len(outs))
        ],
        scratch_shapes=list(scratch) + extra,
        compiler_params=pltpu.CompilerParams(vmem_limit_bytes=limit * 1024 * 1024),
        cost_estimate=pl.CostEstimate(
            flops=micros * 10**9, bytes_accessed=micros * 10**6, transcendentals=0
        ),
    )(*ins)


def shift(block, axis, distance):
    size = lax.axis_size(axis)
    route = [(i, i + distance) for i in range(size) if 0 <= i + distance < size]
    return lax.ppermute(block, axis, route)


def exchange(block):
    return lax.all_to_all(block, "block", split_axis=0, concat_axis=0, tiled=True)


def flip(block, bit):
    size = lax.axis_size("dp")
    return lax.ppermute(block, "dp", [(i, i ^ (1 << bit)) for i in range(size)])


def noted(power, loss, count):
    row = lax.broadcasted_iota(jnp.int32, (NOTES, LANES), 0)
    rows = jnp.where(row == 0, power, 0.0)
    for first, value, digits in ((1, loss, 4), (5, count, 3)):
        rest = value * (1.0 / 1024.0**2)
        for j in range(digits):
            digit = jnp.floor(rest) if j < 3 else rest
            rows = jnp.where(row == first + j, digit, rows)
            rest = (rest - digit) * 1024.0
    return rows.astype(HALF)


def scaled(value, power):
    return (value * jnp.exp2(TOP - power)).astype(HALF)


def read_notes(rows):
    rows = rows.astype(F32)
    power, *digits = (rows[..., i : i + 1, :] for i in range(8))
    loss, count = ((d[0] * 1024.0 + d[1]) * 1024.0 + d[2] for d in (digits[:3], digits[4:]))
    loss = loss + digits[3] * (1.0 / 1024.0)
    return power, loss, count


def cut(block, start, size):
    return lax.dynamic_slice_in_dim(block, start, size, 0)


def chips(block):
    nb, dp = lax.axis_size("block"), lax.axis_size("dp")
    groups = [[i * dp + j for i in range(nb) for j in range(core, dp, 2)] for core in range(2)]
    return lax.all_to_all(
        block, ("block", "dp"), split_axis=0, concat_axis=0, tiled=True, axis_index_groups=groups
    )


def gradient_sums(block, notes):
    peers = lax.axis_size("block") * lax.axis_size("dp") // 2
    size = block.shape[0] // 2
    mine = lax.axis_index("dp") & 1
    other = flip(jnp.concatenate([cut(block, (1 - mine) * size, size), notes], 0), 0)
    power = jnp.maximum(notes[0:1], other[size : size + 1]) + 1.0
    loss, count = (notes[i : i + 1] + other[size + i : size + i + 1] for i in (1, 2))
    part = size // peers
    block = scaled(cut(block, mine * size, size) + other[:size], power)
    notes = jnp.broadcast_to(noted(power, loss, count)[None], (peers, NOTES, LANES))
    pieces = chips(jnp.concatenate([block.reshape(peers, part, LANES), notes], 1))
    powers, losses, counts = read_notes(pieces[:, part:])
    block = jnp.sum(pieces[:, :part].astype(F32) * jnp.exp2(powers - TOP), 0)
    loss, count = jnp.sum(losses, 0), jnp.sum(counts, 0)
    power = jnp.max(powers, 0) + (peers - 1).bit_length()
    mine = jnp.concatenate([scaled(block, power), noted(power, loss, count)], 0)
    block = chips(jnp.broadcast_to(mine[None], (peers,) + mine.shape))
    other = flip(block, 0)
    row = lax.broadcasted_iota(jnp.int32, (8, LANES), 0)
    totals = jnp.where(row == 0, loss, count)
    return [half.reshape(-1, LANES).astype(F32) for half in (block, other)] + [totals]


def shared_step(mixture, target, lengths, proj, vectors_wide, gi, gr):
    nb = lax.axis_size("block")
    RI = -(-K // nb) * M
    intra = Shape(TILES, K, M)
    inter = Shape(1, TILES * nb, RI)
    T = inter.steps
    reach = (HOP + 2) * STRIDE
    following = shift(jnp.stack([mixture[:, :reach], target[:, :reach]]), "block", -1)
    leading = shift(mixture[:, -STRIDE:], "block", 1)

    RP = -(-RI // 16) * 8
    res_shape = SDS((TILES, nb * RI, B), F32)
    send_shape = SDS((nb, TILES, RP, 2 * B), BF)
    steps_shape = SDS((T, RP, 2 * B), BF)
    x_shape = SDS((TILES * K * M, B), BF)

    def state(shape):
        return SDS((shape.groups * shape.wide, 2 * H), F32)

    res0, send, x0, h0, c0, win = call(
        functools.partial(first_kernel, intra, nb, RI),
        [res_shape, send_shape, x_shape, state(intra), state(intra), SDS((BLOCKS * M, 2 * STRIDE), BF)],
        [mixture, following, leading, lengths, proj, vectors_wide, gi, gr],
        fwd_scratch(intra)
        + [pltpu.VMEM((BLOCKS * M, 2 * STRIDE), F32), pltpu.VMEM((BLOCKS * M, B), F32)],
        0,
    )

    def inter_step(send, index):
        rows = exchange(send).reshape(T, RP, 2 * B)
        normed, h, c = call(
            functools.partial(inter_kernel, inter, RI, index),
            [steps_shape, state(inter), state(inter)],
            [rows, proj, vectors_wide, gi, gr],
            fwd_scratch(inter) + [pltpu.VMEM((inter.size, B), F32)],
            index,
        )
        return rows, h, c, exchange(normed.reshape(send_shape.shape))

    rows1, h1, c1, back = inter_step(send, 1)
    res2, send, x2, h2, c2 = call(
        functools.partial(third_kernel, intra, nb, RI),
        [res_shape, send_shape, x_shape, state(intra), state(intra)],
        [res0, back, lengths, proj, vectors_wide, gi, gr],
        fwd_scratch(intra),
        2,
    )
    rows3, h3, c3, back = inter_step(send, 3)
    edge_shape = SDS((EDGE_TOP, 2 * B), F32)
    part, up, down = call(
        functools.partial(part_kernel, nb, RI),
        [SDS(((FRAMES + HOP) * M, B), F32), edge_shape, edge_shape],
        [res2, back, lengths],
        [pltpu.VMEM(res_shape.shape, F32)],
    )
    before = shift(up, "block", 1)
    after = shift(down, "block", -1)
    tall = PADDED * M
    send, gres, genc, gm = call(
        functools.partial(middle_kernel, nb, RI),
        [send_shape, res_shape, SDS((FRAMES * M, B), F32), SDS((136, LANES), F32)],
        [part, before, after, lengths, win, target, following, proj, vectors_wide],
        [
            pltpu.VMEM((tall, B), F32),
            pltpu.VMEM((tall, 2 * STRIDE), F32),
            pltpu.VMEM((tall, STRIDE), F32),
            pltpu.VMEM((tall, STRIDE), F32),
            pltpu.VMEM((tall, B), F32),
            pltpu.VMEM((tall, B), F32),
            pltpu.VMEM((tall, B), F32),
            pltpu.VMEM((tall, B), F32),
        ],
    )
    out_shape = SDS((ROWS_G, LANES), F32)

    def inter_back(send, rows, h, c, index):
        grad_rows = exchange(send).reshape(T, RP, 2 * B)
        send, out = call(
            functools.partial(inter_back_kernel, inter, RI, index),
            [steps_shape, out_shape],
            [grad_rows, rows, h, c, proj, vectors_wide, gi, gr],
            [pltpu.VMEM((inter.size, B), F32)] * 2 + back_scratch(inter),
            index,
        )
        return exchange(send.reshape(send_shape.shape)), out

    back, out3 = inter_back(send, rows3, h3, c3, 3)
    gres, send, out2 = call(
        functools.partial(third_back_kernel, intra, nb, RI),
        [res_shape, send_shape, out_shape],
        [gres, back, lengths, x2, h2, c2, proj, vectors_wide, gi, gr],
        back_scratch(intra),
        2,
    )
    back, out1 = inter_back(send, rows1, h1, c1, 1)
    out0, out1 = call(
        functools.partial(first_back_kernel, intra, nb, RI),
        [out_shape, out_shape],
        [gres, back, lengths, x0, h0, c0, proj, vectors_wide, gi, gr, win, genc, gm, out1],
        [pltpu.VMEM(res_shape.shape, F32), pltpu.VMEM((BLOCKS * M, B), F32)] + back_scratch(intra),
        0,
    )
    parts = nb * lax.axis_size("dp") * NOTES
    more = jnp.zeros((-4 * ROWS_G % parts, LANES), F32)
    outs = jnp.concatenate([out0, out1, out2, out3, more], 0)
    at = ROWS_MORE + B + 4
    return outs, note_rows(jnp.max(jnp.abs(outs)), outs[at : at + 1], outs[at + 1 : at + 2])


def local_step(mixture, target, lengths, proj, vectors_wide, gi, gr):
    RI = -(-K // M) * M
    intra = Shape(TILES, K, M)
    inter = Shape(1, TILES * M, RI)
    pad = jnp.zeros((M, -(FRAMES * STRIDE) % LANES), F32)
    waves = jnp.concatenate([mixture, pad, target, pad], 1)
    waves = exchange(waves)
    return call(
        functools.partial(local_kernel, intra, inter, RI),
        [SDS((4 * ROWS_G, LANES), F32), SDS((8, LANES), F32)],
        [waves, lengths, proj, vectors_wide, gi, gr],
        local_scratch(intra, inter),
        limit=62,
        apart=(4, 5),
        given=(0,),
    )


def body(
    mixture,
    target,
    lengths,
    input_gates,
    recur_gates,
    projections,
    vectors,
    moment_input,
    moment_recur,
    moment_proj,
    moment_vecs,
    square_input,
    square_recur,
    square_proj,
    square_vecs,
    average_input,
    average_recur,
    average_proj,
    average_vecs,
):
    nb = lax.axis_size("block")
    proj = projections.T
    vectors_wide = vectors.reshape(-1, LANES)
    step = local_step if nb == M else shared_step
    outs, notes = step(mixture, target, lengths, proj, vectors_wide, input_gates, recur_gates)
    sums = gradient_sums(outs, notes)
    old = [
        input_gates, recur_gates, projections, vectors,
        moment_input, moment_recur, moment_proj, moment_vecs,
        square_input, square_recur, square_proj, square_vecs,
        average_input, average_recur, average_proj, average_vecs,
    ]
    for i in range(2, 16, 4):
        old[i] = old[i].T
    for i in range(3, 16, 4):
        old[i] = old[i].reshape(-1, LANES)
    new = [SDS(a.shape, F32) for a in old[:4]] * 4 + [SDS(a.shape, BF) for a in old[:4]]
    scalars, *new = call(
        adam_kernel,
        [SDS((8, LANES), F32)] + new,
        sums + old,
        [
            pltpu.VMEM(old[3].shape, F32),
            pltpu.VMEM(outs.shape, F32),
            pltpu.SemaphoreType.DMA((50 + 48,)),
        ]
        + [
            pltpu.VMEM(((2,) if i < 2 else ()) + old[i].shape[i < 2 :], F32 if j < 4 else BF)
            for i in range(4)
            for j in range(5)
        ]
        + [pltpu.VMEM(a.shape, F32) for a in old],
        limit=40,
        apart=range(3, 19),
        given=range(1, 21),
    )
    for i in range(2, 20, 4):
        new[i] = new[i].T
    for i in range(3, 20, 4):
        new[i] = new[i].reshape(-1)
    return (scalars[0, 0], scalars[1, 0], scalars[2, 0], *new)


def solution(mesh):
    in_specs = (P("dp", "block"), P("dp", "block"), P("dp")) + (P(),) * 16
    return jax.shard_map(
        body, mesh=mesh, in_specs=in_specs, out_specs=(P(),) * 23, check_vma=False
    )
```
